32 devices in a mesh: ctx: 8 (over y, x, core), tp: 4 (over z).
Axes of the slice: x: 2, y: 2, z: 4, core: 2. Of those that a mesh axis runs over, the one named last changes fastest.
Arguments:
- stream: bfloat16 [3072, 8192], P('ctx', 'tp'), may hold values from -40 to 40
- pending: bfloat16 [4, 3072, 8192], P('tp', 'ctx'), may hold values from -5 to 5
- norm_gain: bfloat16 [8192], replicated, may hold values from 0.099609375 to 1.8984375
- w_query: bfloat16 [8192, 4096], P('ctx', 'tp'), may hold values from -0.0625 to 0.0625
- w_key: bfloat16 [8192, 1024], P('ctx'), may hold values from -0.375 to 0.375
- w_value: bfloat16 [8192, 1024], P('ctx'), may hold values from -0.1875 to 0.1875
- w_out: bfloat16 [4096, 8192], P('tp', 'ctx'), may hold values from -0.09375 to 0.09375
- prefix_keys: bfloat16 [8, 6144, 128], P(None, 'ctx'), may hold values from -600 to 600
- prefix_values: bfloat16 [8, 6144, 128], P(None, 'ctx'), may hold values from -6 to 6
- prefix_segments: int32 [6144], P('ctx'), may hold values from 0 to 15, never falling along the last dimension, each value on 1 to 768 neighbouring positions
- stretch_segments: int32 [3072], P('ctx'), may hold values from 0 to 15, never falling along the last dimension, each value on 1 to 384 neighbouring positions
- stretch_offset: int32 [1], replicated, may hold values from 6144 to 12287
Outputs:
- output: bfloat16 [3072, 8192], P('ctx', 'tp')
The draws below stay inside these ranges and needn't reach their ends.
Inputs may be any that keep to these rules, and one draw needn't show every extreme that they name: `prefix_segments`: never falls along the positions; every trajectory 0 to 15 occurs. `stretch_segments`: never falls along the positions; every trajectory 0 to 15 occurs.
All inputs are finite; a program needn't handle non-finite values.
Results may differ from the reference program's by a relative error of at most 0.024.
Values may be sent and summed in bfloat16 or wider, within the bound.
No kernel may reach another device: no remote copies, remote signals or barrier semaphores. Data moves between devices by JAX's collectives and lax.ppermute only.
A program may use at most 256 MiB of HBM per device.

```python
import math
import jax
import jax.numpy as jnp
import numpy as np
from jax import lax

D = 8192
HQ = 32
KVH = 8
HD = 128
NTRAJ = 16
STRETCH = 3072
PREFIX = 6144
N_TP = 4


def draw_stream(key, part):
    key = jax.random.fold_in(key, 7)
    base_key, row_key, col_key = jax.random.split(key, 3)
    column_trend = 3.0 ** (jnp.arange(D, dtype=jnp.float32) / D)
    spread = jnp.exp(math.log(3.0) * (jax.random.uniform(col_key, (D,), jnp.float32) - 0.5))
    base_draw = jnp.clip(jax.random.normal(base_key, (STRETCH, D), jnp.float32), -6.0, 6.0)
    row_scale = jnp.exp(math.log(10.0) * jax.random.uniform(row_key, (STRETCH, 1), jnp.float32))
    return (0.1 * base_draw * row_scale * column_trend * spread).astype(jnp.bfloat16)


def draw_prefix_keys(key, part):
    key = jax.random.fold_in(key, 13)
    base_key = jax.random.fold_in(key, 0)
    key_shape = (KVH, PREFIX, HD)
    return (3.0 * jnp.clip(jax.random.normal(base_key, key_shape, jnp.float32), -6.0, 6.0)).astype(jnp.bfloat16)


def with_spikes(entries, key, source, target, blocks, factor):
    owner, partner = [(jnp.arange(entries.shape[axis_at]) // (entries.shape[axis_at] // blocks)).reshape([-1 if axis == axis_at else 1 for axis in range(entries.ndim)]) for axis_at in (source, target)]
    chosen = jax.random.permutation(key, blocks)[partner]
    strong = (owner == chosen) | (owner == (partner + blocks // 2) % blocks)
    return jnp.where(strong, factor * entries, entries)


def steps_of(own_key, shape, cuts, smallest, largest):
    loudness, own = 1.0, jax.random.fold_in(own_key, 6)
    for axis_at, parts in cuts:
        steps = jnp.exp(jax.random.uniform(jax.random.fold_in(own, axis_at), (parts,), jnp.float32, smallest / len(cuts), largest / len(cuts)))
        loudness = loudness * jnp.repeat(steps, shape[axis_at] // parts).reshape([-1 if axis == axis_at else 1 for axis in range(len(shape))])
    return loudness


def length_profile(count, total, limit, skew):
    loads = [(1 << 20) // math.isqrt(rank ** skew) + 1 for rank in range(2, count + 1)]
    surplus, given = total - limit - (count - 1), [1] * (count - 1)
    while surplus > 0:
        movable = [i for i in range(count - 1) if given[i] < limit]
        mass, remaining = sum([loads[i] for i in movable]), surplus
        for i in movable:
            more = min(limit - given[i], max(1, remaining * loads[i] // mass), surplus)
            given[i] = given[i] + more
            surplus = surplus - more
    return np.array([limit] + given)


def uneven_parts(own_key, amount, total, most, slope):
    if amount == 2:
        one = jax.random.randint(own_key, (), max(1, total - most), min(most, total - 1) + 1)
        return jnp.stack([one, total - one])
    lengths = jnp.asarray(length_profile(amount, total, most, slope), jnp.int32)
    pairs = (amount - 1) // 2
    giver, sink = lengths[1:1 + 2 * pairs:2], lengths[2:2 + 2 * pairs:2]
    margin = jnp.minimum(giver - 1, most - sink)
    passed = jax.random.randint(jax.random.fold_in(own_key, 1), (pairs,), 0, 1 << 20) % (margin + 1)
    lengths = lengths.at[1:1 + 2 * pairs:2].set(giver - passed).at[2:2 + 2 * pairs:2].set(sink + passed)
    return lengths[jax.random.permutation(jax.random.fold_in(own_key, 2), amount)]


def centred(own_key, shape, scale, reach, pieces=(), kind=jnp.bfloat16):
    gain = steps_of(own_key, shape, pieces, -0.22, 0.18) if pieces else 1.0
    entries = jax.random.normal(own_key, shape, jnp.float32) * scale * gain
    return jnp.minimum(jnp.maximum(entries, -reach), reach).astype(kind)


def heavy_noise(own_key, dims, scale, bound, cuts, heavy, kind=jnp.bfloat16):
    drawn = scale * jax.random.normal(own_key, dims, jnp.float32)
    if cuts:
        drawn = drawn * steps_of(own_key, dims, cuts, -0.22, 0.18)
    return jnp.clip(with_spikes(drawn, jax.random.fold_in(own_key, 3), *heavy), -bound, bound).astype(kind)


def setup_inputs(seed: int = 0) -> dict:
    splits = jax.random.split(jax.random.key(seed), 13)
    return {
        "stream": draw_stream(jax.random.fold_in(splits[12], 71), 0),
        "pending": heavy_noise(splits[1], (N_TP, STRETCH, D), 0.25, 5.0, ((0, 4), (1, 8)), (0, 2, 4, 2.0)),
        "norm_gain": jnp.clip(1.0 + 0.18 * jax.random.normal(splits[2], (D,), jnp.float32), 0.099609375, 1.8984375).astype(jnp.bfloat16),
        "w_query": centred(splits[3], (D, HQ * HD), D ** -0.5, 0.0625, ((0, 8), (1, 4))),
        "w_key": centred(splits[4], (D, KVH * HD), (D // 36) ** -0.5, 0.375, ((0, 8),)),
        "w_value": centred(splits[5], (D, KVH * HD), (D // 9) ** -0.5, 0.1875, ((0, 8),)),
        "w_out": centred(splits[6], (HQ * HD, D), (HQ * HD) ** -0.5, 0.09375, ((0, 4), (1, 8))),
        "prefix_keys": draw_prefix_keys(jax.random.fold_in(splits[12], 71), 0),
        "prefix_values": centred(splits[8], (KVH, PREFIX, HD), 1.0, 6.0, ((1, 8),)),
        "prefix_segments": jnp.searchsorted(jnp.cumsum(uneven_parts(splits[9], NTRAJ, PREFIX, 2 * PREFIX // NTRAJ, 1)), jnp.arange(PREFIX), side="right").astype(jnp.int32),
        "stretch_segments": jnp.searchsorted(jnp.cumsum(uneven_parts(splits[10], NTRAJ, STRETCH, 2 * STRETCH // NTRAJ, 1)), jnp.arange(STRETCH), side="right").astype(jnp.int32),
        "stretch_offset": jax.random.randint(splits[11], (1,), PREFIX, 2 * PREFIX).astype(jnp.int32),
    }


ROPE_BASE = 500000.0
ROPE_FACTOR = 8.0
LOW_FREQ = 1.0
HIGH_FREQ = 4.0
INITIAL_SPAN = 8192.0
NORM_EPSILON = 1e-05
MASKED = -1e+30

def inverse_freqs(head_width):
    pair_index = jnp.arange(head_width // 2, dtype=jnp.float32)
    base_freq = ROPE_BASE ** (-2.0 * pair_index / head_width)
    wavelength = 2.0 * math.pi / base_freq
    smooth = (INITIAL_SPAN / wavelength - LOW_FREQ) / (HIGH_FREQ - LOW_FREQ)
    blended = (1.0 - smooth) * base_freq / ROPE_FACTOR + smooth * base_freq
    return jnp.where(wavelength < INITIAL_SPAN / HIGH_FREQ, base_freq, jnp.where(wavelength > INITIAL_SPAN / LOW_FREQ, base_freq / ROPE_FACTOR, blended))

def rotate(vectors, positions):
    head_width = vectors.shape[-1]
    angles = positions[..., None] * inverse_freqs(head_width)
    cosine = jnp.cos(angles)
    sinus = jnp.sin(angles)
    first_half = vectors[..., :head_width // 2]
    second_half = vectors[..., head_width // 2:]
    return jnp.concatenate([first_half * cosine - second_half * sinus, second_half * cosine + first_half * sinus], axis=-1)

def reference(stream, pending, norm_gain, w_query, w_key, w_value, w_out, prefix_keys, prefix_values, prefix_segments, stretch_segments, stretch_offset):
    stream_wide = stream.astype(jnp.float32)
    mean_square = lax.optimization_barrier(jnp.mean(stream_wide * stream_wide, axis=1, keepdims=True))
    normed = (stream_wide * lax.rsqrt(mean_square + NORM_EPSILON) * norm_gain.astype(jnp.float32)).astype(jnp.bfloat16)
    positions = stretch_offset[0].astype(jnp.float32) + jnp.arange(STRETCH, dtype=jnp.float32)
    queries = jnp.dot(normed, w_query, preferred_element_type=jnp.float32).reshape(STRETCH, HQ, HD)
    queries = rotate(queries, positions[:, None]).astype(jnp.bfloat16)
    new_keys = jnp.dot(normed, w_key, preferred_element_type=jnp.float32).reshape(STRETCH, KVH, HD)
    new_keys = rotate(new_keys, positions[:, None]).astype(jnp.bfloat16)
    new_values = jnp.dot(normed, w_value, preferred_element_type=jnp.float32).astype(jnp.bfloat16).reshape(STRETCH, KVH, HD)
    all_keys = jnp.concatenate([prefix_keys, jnp.transpose(new_keys, (1, 0, 2))], axis=1)
    all_values = jnp.concatenate([prefix_values, jnp.transpose(new_values, (1, 0, 2))], axis=1)
    stretch_index = jnp.arange(STRETCH, dtype=jnp.int32)
    earlier = prefix_segments[None, :] <= stretch_segments[:, None]
    same = (stretch_segments[None, :] == stretch_segments[:, None]) & (stretch_index[None, :] <= stretch_index[:, None])
    visible = jnp.concatenate([earlier, same], axis=1)
    group_size = HQ // KVH
    score_scale = 1.0 / math.sqrt(HD)

    def one_head(head_index):
        head_queries = lax.dynamic_index_in_dim(queries, head_index, axis=1, keepdims=False)
        kv_index = head_index // group_size
        head_keys = lax.dynamic_index_in_dim(all_keys, kv_index, axis=0, keepdims=False)
        head_values = lax.dynamic_index_in_dim(all_values, kv_index, axis=0, keepdims=False)
        scores = jnp.dot(head_queries, head_keys.T, preferred_element_type=jnp.float32) * score_scale
        scores = jnp.where(visible, scores, MASKED)
        row_max = lax.optimization_barrier(jnp.max(scores, axis=1, keepdims=True))
        weights = jnp.where(visible, jnp.exp(scores - row_max), 0.0)
        totals = lax.optimization_barrier(jnp.sum(weights, axis=1, keepdims=True))
        mixed = jnp.dot(weights.astype(jnp.bfloat16), head_values, preferred_element_type=jnp.float32)
        return (mixed / totals).astype(jnp.bfloat16)
    heads_out = lax.map(one_head, jnp.arange(HQ, dtype=jnp.int32))
    attended = jnp.transpose(heads_out, (1, 0, 2)).reshape(STRETCH, HQ * HD)
    group_cols = HQ * HD // N_TP

    def add_group(total, group_index):
        start = (group_index * group_cols).astype(jnp.int32)
        cols = lax.dynamic_slice_in_dim(attended, start, group_cols, 1)
        rows = lax.dynamic_slice_in_dim(w_out, start, group_cols, 0)
        part_low = lax.optimization_barrier(jnp.dot(cols, rows, preferred_element_type=jnp.float32).astype(jnp.bfloat16))
        return (total + part_low.astype(jnp.float32), None)
    head_sum, _ = lax.scan(add_group, jnp.zeros((STRETCH, D), jnp.float32), jnp.arange(N_TP, dtype=jnp.int32))
    carried = lax.optimization_barrier(jnp.sum(pending.astype(jnp.float32), axis=0))
    return (stream_wide + (head_sum + carried)).astype(jnp.bfloat16)
```

```python
import functools
import math

import jax
import jax.numpy as jnp
from jax import lax
from jax.experimental import pallas as pl
from jax.experimental.pallas import tpu as pltpu
from jax.sharding import PartitionSpec as P

HQ = 32
KVH = 8
HD = 128
NTRAJ = 16


ROPE_BASE = 500000.0
ROPE_FACTOR = 8.0
LOW_FREQ = 1.0
HIGH_FREQ = 4.0
INITIAL_SPAN = 8192.0
NORM_EPSILON = 1e-05
MASKED = -1e30


def inverse_freqs(head_width):
    pair_index = jnp.arange(head_width // 2, dtype=jnp.float32)
    base_freq = ROPE_BASE ** (-2.0 * pair_index / head_width)
    wavelength = 2.0 * math.pi / base_freq
    smooth = (INITIAL_SPAN / wavelength - LOW_FREQ) / (HIGH_FREQ - LOW_FREQ)
    blended = (1.0 - smooth) * base_freq / ROPE_FACTOR + smooth * base_freq
    return jnp.where(
        wavelength < INITIAL_SPAN / HIGH_FREQ,
        base_freq,
        jnp.where(wavelength > INITIAL_SPAN / LOW_FREQ, base_freq / ROPE_FACTOR, blended),
    )


def rotate(vectors, positions):
    head_width = vectors.shape[-1]
    angles = positions[..., None] * inverse_freqs(head_width)
    cosine = jnp.cos(angles)
    sinus = jnp.sin(angles)
    first_half = vectors[..., : head_width // 2]
    second_half = vectors[..., head_width // 2 :]
    return jnp.concatenate(
        [first_half * cosine - second_half * sinus, second_half * cosine + first_half * sinus],
        axis=-1,
    )


def visibility(key_labels, is_prefix, key_pos, query_segs, query_index):
    earlier = key_labels[None, :] <= query_segs[:, None]
    same = (key_labels[None, :] == query_segs[:, None]) & (key_pos[None, :] <= query_index[:, None])
    return jnp.where(is_prefix[None, :], earlier, same)


def attend_whole(grouped, key_block, value_block, seen):
    scores = jnp.einsum("hrd,hnd->hrn", grouped, key_block, preferred_element_type=jnp.float32) * (
        1.0 / math.sqrt(HD)
    )
    scores = jnp.where(seen[None], scores, MASKED)
    new_max = jnp.max(scores, axis=2)
    weights = jnp.where(seen[None], jnp.exp(scores - new_max[..., None]), 0.0)
    totals = jnp.sum(weights, axis=2)
    numerator = jnp.einsum(
        "hrn,hnd->hrd",
        weights.astype(jnp.bfloat16),
        value_block,
        preferred_element_type=jnp.float32,
    )
    return numerator / totals[..., None]


def per_device_any(
    stream,
    pending,
    norm_gain,
    w_query,
    w_key,
    w_value,
    w_out,
    prefix_keys,
    prefix_values,
    prefix_segments,
    stretch_segments,
    stretch_offset,
):
    tok_rows = stream.shape[0]
    prefix_rows = prefix_keys.shape[1]
    ctx_index = lax.axis_index("ctx")
    tp_index = lax.axis_index("tp")
    gain_wide = norm_gain.astype(jnp.float32)
    whole = lax.all_gather(stream, "tp", axis=1, tiled=True).astype(jnp.float32)
    mean_square = jnp.mean(whole * whole, axis=1, keepdims=True)
    normed = (whole * lax.rsqrt(mean_square + NORM_EPSILON) * gain_wide).astype(jnp.bfloat16)
    q_cols = w_query.shape[1]
    q_heads = q_cols // HD
    full_group = HQ // KVH
    kv_heads = max(1, q_heads // full_group)
    group_size = q_heads // kv_heads
    head_start = tp_index * q_heads // full_group
    kv_cols = kv_heads * HD
    key_slice = lax.dynamic_slice_in_dim(w_key, head_start * HD, kv_cols, 1)
    value_slice = lax.dynamic_slice_in_dim(w_value, head_start * HD, kv_cols, 1)
    pieces = (
        lax.all_gather(w_query, "ctx", axis=0, tiled=True),
        lax.all_gather(key_slice, "ctx", axis=0, tiled=True),
        lax.all_gather(value_slice, "ctx", axis=0, tiled=True),
    )
    query_raw, key_full, value_full = tuple(
        (jnp.dot(normed, piece_rows, preferred_element_type=jnp.float32) for piece_rows in pieces)
    )
    token_index = ctx_index * tok_rows + jnp.arange(tok_rows, dtype=jnp.int32)
    positions = stretch_offset[0].astype(jnp.float32) + token_index.astype(jnp.float32)
    query_rows = rotate(query_raw.reshape(tok_rows, q_heads, HD), positions[:, None]).astype(
        jnp.bfloat16
    )
    new_keys = jnp.transpose(
        rotate(key_full.reshape(tok_rows, kv_heads, HD), positions[:, None]).astype(jnp.bfloat16),
        (1, 0, 2),
    )
    new_values = jnp.transpose(
        value_full.astype(jnp.bfloat16).reshape(tok_rows, kv_heads, HD), (1, 0, 2)
    )
    old_keys = lax.dynamic_slice_in_dim(prefix_keys, head_start, kv_heads, 0)
    old_values = lax.dynamic_slice_in_dim(prefix_values, head_start, kv_heads, 0)
    local_keys = jnp.concatenate([old_keys, new_keys], 1)
    local_values = jnp.concatenate([old_values, new_values], 1)
    key_labels = jnp.concatenate([prefix_segments, stretch_segments])
    key_span = prefix_rows + tok_rows
    grouped = jnp.transpose(
        query_rows.reshape(tok_rows, kv_heads, group_size, HD), (1, 0, 2, 3)
    ).reshape(kv_heads, tok_rows * group_size, HD)
    query_index = jnp.repeat(token_index, group_size)
    query_segs = jnp.repeat(stretch_segments, group_size)
    both = jnp.stack([local_keys, local_values])
    kv_block = lax.all_gather(both, "ctx", axis=2, tiled=True)
    label_block = lax.all_gather(key_labels[None, None, :], "ctx", axis=2, tiled=True)
    key_count = kv_block.shape[2]
    absolute = jnp.arange(key_count, dtype=jnp.int32)
    within = absolute % key_span
    key_pos = absolute // key_span * tok_rows + within - prefix_rows
    seen = visibility(label_block[0, 0], within < prefix_rows, key_pos, query_segs, query_index)
    attended_heads = attend_whole(grouped, kv_block[0], kv_block[1], seen).astype(jnp.bfloat16)
    attended = jnp.transpose(
        attended_heads.reshape(kv_heads, tok_rows, group_size, HD), (1, 0, 2, 3)
    ).reshape(tok_rows, q_cols)
    head_terms = jnp.dot(
        attended,
        lax.all_gather(w_out, "ctx", axis=1, tiled=True),
        preferred_element_type=jnp.float32,
    )
    head_share, pending_share = (
        lax.psum_scatter(
            head_terms.astype(jnp.bfloat16), "tp", scatter_dimension=1, tiled=True
        ).astype(jnp.float32),
        lax.psum_scatter(
            pending[0].astype(jnp.float32).astype(jnp.bfloat16),
            "tp",
            scatter_dimension=1,
            tiled=True,
        ).astype(jnp.float32),
    )
    block_share = head_share + pending_share
    return (stream.astype(jnp.float32) + block_share).astype(jnp.bfloat16)


N_CTX = 8
N_TP = 4
VMEM = 56 * 1024 * 1024


def swap(x, bit):
    return lax.ppermute(x, "ctx", [(c, c ^ bit) for c in range(N_CTX)])


def line_gather(x, z):
    def up(v, first):
        return lax.ppermute(v, "tp", [(i, i + 1) for i in range(first, N_TP - 1)])

    def down(v, first):
        return lax.ppermute(v, "tp", [(N_TP - 1 - i, N_TP - 2 - i) for i in range(first, N_TP - 1)])

    u1, d1 = up(x, 0), down(x, 0)
    u2, d2 = up(u1, 1), down(d1, 1)
    u3, d3 = up(u2, 2), down(d2, 2)
    low = z < 2
    a = jnp.where(low, d1, u1)
    b = jnp.where(low, d2, u2)
    c = jnp.where(z == 0, d3, jnp.where(z == 1, u1, jnp.where(z == 2, d1, u3)))
    return (
        (a, jnp.where(low, z + 1, z - 1)),
        (b, jnp.where(low, z + 2, z - 2)),
        (c, jnp.where(z % 2 == 1, 0, 3)),
    )


def plane_gather(block):
    half = block.shape[0] // 2
    bx, by = swap(block, 2), swap(block, 4)
    return block, bx, by, swap(bx[:half], 4), swap(by[half:], 2)


def part_maps(steps):
    q = steps // 4

    def walk(first, count):
        return lambda i, *_: (jnp.clip(i - first, 0, count - 1), 0)

    return (
        walk(0, q),
        walk(q, q),
        walk(2 * q, q),
        walk(3 * q, q // 2),
        walk(3 * q + q // 2, q - q // 2),
    )


def choose(i, steps, refs, use):
    q = steps // 4
    edges = (0, q, 2 * q, 3 * q, 3 * q + q // 2, steps)
    for ref, lo, hi in zip(refs, edges[:-1], edges[1:]):

        @pl.when((i >= lo) & (i < hi))
        def _():
            use(ref)


def rotated(v, cosine, sinus):
    return v * cosine + pltpu.roll(v, HD // 2, 1) * sinus


def project_kernel(steps, heads, rot_heads, scale, where_ref, x_ref, gain_ref, *rest):
    weights, (cos_ref, sin_ref, out_ref, acc_ref, square_ref) = rest[:5], rest[5:]
    i = pl.program_id(0)

    @pl.when(i == 0)
    def _():
        acc_ref[...] = jnp.zeros_like(acc_ref)
        square_ref[...] = jnp.zeros_like(square_ref)

    wide = x_ref[...].astype(jnp.float32)
    squares = wide * wide
    total = square_ref[...]
    for j in range(x_ref.shape[1] // 128):
        total = total + squares[:, j * 128 : (j + 1) * 128]
    square_ref[...] = total
    scaled = (wide * gain_ref[...].astype(jnp.float32)).astype(jnp.bfloat16)

    def use(ref):
        acc_ref[...] += jnp.dot(scaled, ref[...], preferred_element_type=jnp.float32)

    choose(i, steps, weights, use)

    @pl.when(i == steps - 1)
    def _():
        width = x_ref.shape[1] * steps
        mean = jnp.sum(square_ref[...], axis=1, keepdims=True) * (1.0 / width)
        factor = lax.rsqrt(mean + NORM_EPSILON)
        for h in range(heads):
            v = acc_ref[:, h * HD : (h + 1) * HD] * factor
            if h < rot_heads:
                v = rotated(v, cos_ref[...], sin_ref[...]) * scale
            out_ref[h] = v.astype(jnp.bfloat16)


def project(where, x, gain, weights, cosine, sinus, heads, rot_heads, scale):
    rows, depth = x.shape
    steps = 16
    wide = depth // steps
    cols = heads * HD

    def x_map(i, where_ref):
        part, sub = i // 4, i % 4
        chip = where_ref[0] ^ part
        return (0, chip * 4 + ((sub // 2) ^ where_ref[1]) * 2 + sub % 2)

    maps = part_maps(steps)
    whole = lambda i, *_: (0, 0)
    return pl.pallas_call(
        functools.partial(project_kernel, steps, heads, rot_heads, scale),
        out_shape=jax.ShapeDtypeStruct((heads, rows, HD), jnp.bfloat16),
        grid_spec=pltpu.PrefetchScalarGridSpec(
            num_scalar_prefetch=1,
            grid=(steps,),
            in_specs=[
                pl.BlockSpec((rows, wide), x_map),
                pl.BlockSpec((1, wide), x_map),
            ]
            + [pl.BlockSpec((wide, cols), m) for m in maps]
            + [pl.BlockSpec((rows, HD), whole), pl.BlockSpec((rows, HD), whole)],
            out_specs=pl.BlockSpec((heads, rows, HD), lambda i, *_: (0, 0, 0)),
            scratch_shapes=[
                pltpu.VMEM((rows, cols), jnp.float32),
                pltpu.VMEM((rows, 128), jnp.float32),
            ],
        ),
        compiler_params=pltpu.CompilerParams(vmem_limit_bytes=VMEM),
        cost_estimate=pl.CostEstimate(
            flops=2 * rows * depth * cols,
            bytes_accessed=2 * depth * (rows + cols),
            transcendentals=0,
        ),
    )(where, x, gain, *weights, cosine, sinus)


BT = 256
BK = 512
CHAIN = 2


def step(q, k, v_ext, m, acc, hide):
    s = lax.dot_general(q, k, (((1,), (1,)), ((), ())), preferred_element_type=jnp.float32)
    if hide is not None:
        s = hide(s)
    new = jnp.maximum(m, jnp.max(s, axis=1, keepdims=True))
    p = jnp.exp2(s - new).astype(jnp.bfloat16)
    acc = acc * jnp.exp2(m - new) + jnp.dot(p, v_ext, preferred_element_type=jnp.float32)
    return new, acc


def prefix_kernel(bound_ref, q_ref, n_ref, kv_ref, m_out, acc_out, v_ext, m_ref, acc_ref):
    b = pl.program_id(0)
    heads, bt = q_ref.shape[0], q_ref.shape[1]
    rows = CHAIN * bt

    @pl.when(b == 0)
    def _():
        v_ext[:, :HD] = kv_ref[1]
        v_ext[:, HD:] = jnp.ones_like(kv_ref[1])

    m_ref[...] = jnp.full_like(m_ref, MASKED)
    acc_ref[...] = jnp.zeros_like(acc_ref)
    n_rows = jnp.concatenate([n_ref[:, :1]] * CHAIN, axis=0)

    def body(kb, masked):
        start = pl.multiple_of(kb * BK, BK)
        k = kv_ref[0, pl.ds(start, BK), :]
        v = v_ext[pl.ds(start, BK), :]

        def hide(s):
            col = lax.broadcasted_iota(jnp.int32, s.shape, 1) + start
            return jnp.where(col < n_rows, s, MASKED)

        for g in range(heads // CHAIN):
            q = q_ref[g * CHAIN : (g + 1) * CHAIN].reshape(rows, HD)
            new, acc = step(q, k, v, m_ref[g][:, :1], acc_ref[g], hide if masked else None)
            m_ref[g] = jnp.broadcast_to(new, (rows, 128))
            acc_ref[g] = acc

    full = bound_ref[0, b] // BK
    some = (bound_ref[1, b] + BK - 1) // BK
    lax.fori_loop(0, full, lambda kb, c: (body(kb, False), c)[1], 0)
    lax.fori_loop(full, some, lambda kb, c: (body(kb, True), c)[1], 0)
    m_out[0] = m_ref[...]
    acc_out[0] = acc_ref[...]


def attend_prefix(bounds, q, n_tok, kv):
    heads, tokens, _ = q.shape
    blocks = tokens // BT
    chains, rows = heads // CHAIN, CHAIN * BT
    keys = kv.shape[1]
    return pl.pallas_call(
        prefix_kernel,
        out_shape=(
            jax.ShapeDtypeStruct((blocks, chains, rows, 128), jnp.float32),
            jax.ShapeDtypeStruct((blocks, chains, rows, 2 * HD), jnp.float32),
        ),
        grid_spec=pltpu.PrefetchScalarGridSpec(
            num_scalar_prefetch=1,
            grid=(blocks,),
            in_specs=[
                pl.BlockSpec((heads, BT, HD), lambda b, *_: (0, b, 0)),
                pl.BlockSpec((BT, 128), lambda b, *_: (b, 0)),
                pl.BlockSpec((2, keys, HD), lambda b, *_: (0, 0, 0)),
            ],
            out_specs=(
                pl.BlockSpec((1, chains, rows, 128), lambda b, *_: (b, 0, 0, 0)),
                pl.BlockSpec((1, chains, rows, 2 * HD), lambda b, *_: (b, 0, 0, 0)),
            ),
            scratch_shapes=[
                pltpu.VMEM((keys, 2 * HD), jnp.bfloat16),
                pltpu.VMEM((chains, rows, 128), jnp.float32),
                pltpu.VMEM((chains, rows, 2 * HD), jnp.float32),
            ],
        ),
        compiler_params=pltpu.CompilerParams(vmem_limit_bytes=VMEM),
        cost_estimate=pl.CostEstimate(
            flops=8 * heads * tokens * keys * HD,
            bytes_accessed=4 * keys * HD,
            transcendentals=heads * tokens * keys,
        ),
    )(bounds, q, n_tok, kv)


def new_kernel(halo, q_ref, lo_ref, k_ref, v_ref, m_ref, acc_ref, out_ref):
    b = pl.program_id(0)
    heads, bt = q_ref.shape[0], q_ref.shape[1]
    rows = CHAIN * bt
    span = halo + bt
    start = pl.multiple_of(b * bt, bt)
    k = k_ref[pl.ds(start, span), :]
    v = v_ref[pl.ds(start, span), :]
    v_ext = jnp.concatenate([v, jnp.ones_like(v)], axis=1)
    lo = jnp.concatenate([lo_ref[:, :1]] * CHAIN, axis=0)

    def hide(s):
        col = lax.broadcasted_iota(jnp.int32, s.shape, 1)
        row = lax.broadcasted_iota(jnp.int32, s.shape, 0) % bt
        return jnp.where((col + start >= lo) & (col <= row + halo), s, MASKED)

    for g in range(heads // CHAIN):
        q = q_ref[g * CHAIN : (g + 1) * CHAIN].reshape(rows, HD)
        _, acc = step(q, k, v_ext, m_ref[0, g][:, :1], acc_ref[0, g], hide)
        mixed = (acc[:, :HD] / acc[:, HD:]).astype(jnp.bfloat16)
        for h in range(CHAIN):
            at = (g * CHAIN + h) * HD
            out_ref[:, at : at + HD] = mixed[h * bt : (h + 1) * bt]


def attend_new(q, lo_tok, k, v, m, acc):
    heads, tokens, _ = q.shape
    blocks = tokens // BT
    chains, rows = heads // CHAIN, CHAIN * BT
    halo = k.shape[0] - tokens
    whole = lambda b: (0, 0)
    return pl.pallas_call(
        functools.partial(new_kernel, halo),
        out_shape=jax.ShapeDtypeStruct((tokens, heads * HD), jnp.bfloat16),
        grid=(blocks,),
        in_specs=[
            pl.BlockSpec((heads, BT, HD), lambda b: (0, b, 0)),
            pl.BlockSpec((BT, 128), lambda b: (b, 0)),
            pl.BlockSpec(k.shape, whole),
            pl.BlockSpec(v.shape, whole),
            pl.BlockSpec((1, chains, rows, 128), lambda b: (b, 0, 0, 0)),
            pl.BlockSpec((1, chains, rows, 2 * HD), lambda b: (b, 0, 0, 0)),
        ],
        out_specs=pl.BlockSpec((BT, heads * HD), lambda b: (b, 0)),
        compiler_params=pltpu.CompilerParams(vmem_limit_bytes=VMEM),
        cost_estimate=pl.CostEstimate(
            flops=8 * heads * tokens * (halo + BT) * HD,
            bytes_accessed=4 * tokens * heads * HD * 4,
            transcendentals=heads * tokens * (halo + BT),
        ),
    )(q, lo_tok, k, v, m, acc)


def out_kernel(steps, where_ref, x_ref, *rest):
    weights, (out_ref, acc_ref) = rest[:5], rest[5:]
    i = pl.program_id(0)

    @pl.when(i == 0)
    def _():
        acc_ref[...] = jnp.zeros_like(acc_ref)

    def use(ref):
        acc_ref[...] += jnp.dot(x_ref[...], ref[...], preferred_element_type=jnp.float32)

    choose(i, steps, weights, use)

    @pl.when(i == steps - 1)
    def _():
        out_ref[...] = acc_ref[...].astype(jnp.bfloat16)


def out_project(where, x, weights):
    rows, depth = x.shape
    cols = weights[0].shape[1]
    steps = 16
    wide = depth // steps

    def x_map(i, where_ref):
        part, sub = i // 4, i % 4
        return (0, (where_ref[0] ^ part ^ sub) * 4 + sub)

    return pl.pallas_call(
        functools.partial(out_kernel, steps),
        out_shape=jax.ShapeDtypeStruct((rows, cols), jnp.bfloat16),
        grid_spec=pltpu.PrefetchScalarGridSpec(
            num_scalar_prefetch=1,
            grid=(steps,),
            in_specs=[pl.BlockSpec((rows, wide), x_map)]
            + [pl.BlockSpec((wide, cols), m) for m in part_maps(steps)],
            out_specs=pl.BlockSpec((rows, cols), lambda i, *_: (0, 0)),
            scratch_shapes=[pltpu.VMEM((rows, cols), jnp.float32)],
        ),
        compiler_params=pltpu.CompilerParams(vmem_limit_bytes=VMEM),
        cost_estimate=pl.CostEstimate(
            flops=2 * rows * depth * cols,
            bytes_accessed=2 * depth * (rows + cols),
            transcendentals=0,
        ),
    )(where, x, *weights)


def per_device(
    stream,
    pending,
    norm_gain,
    w_query,
    w_key,
    w_value,
    w_out,
    prefix_keys,
    prefix_values,
    prefix_segments,
    stretch_segments,
    stretch_offset,
):
    tok, feat = stream.shape
    chip_tok = 2 * tok
    c = lax.axis_index("ctx")
    z = lax.axis_index("tp")
    chip, core = c // 2, c % 2
    where = jnp.stack([chip, core]).astype(jnp.int32)
    depth = feat * N_TP

    labels = jnp.arange(NTRAJ, dtype=jnp.int32)
    counts = jnp.stack(
        [
            jnp.sum((prefix_segments[:, None] <= labels).astype(jnp.int32), axis=0),
            jnp.sum((stretch_segments[:, None] < labels).astype(jnp.int32), axis=0),
        ]
    )
    for bit in (1, 2, 4):
        counts = counts + swap(counts, bit)
    other_segs = swap(stretch_segments, 1)
    first = core == 0
    segs = jnp.concatenate(
        [
            jnp.where(first, stretch_segments, other_segs),
            jnp.where(first, other_segs, stretch_segments),
        ]
    )
    onehot = (segs[:, None] == labels).astype(jnp.int32)
    n_tok = jnp.sum(onehot * counts[0], axis=1)
    lo_tok = jnp.sum(onehot * counts[1], axis=1) - chip * chip_tok + tok
    blocked = n_tok.reshape(chip_tok // BT, BT)
    bounds = jnp.stack([blocked[:, 0], blocked[:, -1]])
    n_wide = jnp.broadcast_to(n_tok[:, None], (chip_tok, 128))
    lo_wide = jnp.broadcast_to(lo_tok[:, None], (chip_tok, 128))

    token_index = chip * chip_tok + jnp.arange(chip_tok, dtype=jnp.int32)
    positions = stretch_offset[0].astype(jnp.float32) + token_index.astype(jnp.float32)
    angles = positions[:, None] * inverse_freqs(HD)
    cosine, sinus = jnp.cos(angles), jnp.sin(angles)
    cosine = jnp.concatenate([cosine, cosine], axis=1)
    sinus = jnp.concatenate([-sinus, sinus], axis=1)

    def columns(w, width, base):
        mine = lax.dynamic_slice_in_dim(w, base + core * width, width, 1)
        theirs = lax.dynamic_slice_in_dim(w, base + (1 - core) * width, width, 1)
        return mine, theirs

    def chip_block(mine, theirs):
        return jnp.concatenate([mine, swap(theirs, 1)], axis=0)

    q_heads = w_query.shape[1] // HD // 2
    kv_old = jnp.stack([prefix_keys, prefix_values])
    mine_old = lax.dynamic_index_in_dim(kv_old, 2 * z + core, 1, keepdims=False)
    theirs_old = swap(lax.dynamic_index_in_dim(kv_old, 2 * z + 1 - core, 1, keepdims=False), 1)
    old = jnp.where(
        first,
        jnp.concatenate([mine_old, theirs_old], axis=1),
        jnp.concatenate([theirs_old, mine_old], axis=1),
    )
    old_parts = plane_gather(old)
    wq_parts = plane_gather(chip_block(*columns(w_query, q_heads * HD, 0)))
    mine_k, theirs_k = columns(w_key, HD, 2 * z * HD)
    mine_v, theirs_v = columns(w_value, HD, 2 * z * HD)
    wkv_parts = plane_gather(
        chip_block(
            jnp.concatenate([mine_k, mine_v], axis=1), jnp.concatenate([theirs_k, theirs_v], axis=1)
        )
    )

    span = old.shape[1]
    kv = jnp.zeros((2, 4 * span, HD), jnp.bfloat16)
    for index, part in enumerate(old_parts[:3]):
        kv = lax.dynamic_update_slice(kv, part, (0, (chip ^ index) * span, 0))
    kv = lax.dynamic_update_slice(kv, old_parts[3], (0, (chip ^ 3) * span, 0))
    kv = lax.dynamic_update_slice(kv, old_parts[4], (1, (chip ^ 3) * span, 0))

    whole = jnp.zeros((chip_tok, depth), jnp.bfloat16)
    for piece, place in ((stream, z),) + line_gather(stream, z):
        whole = lax.dynamic_update_slice(whole, piece, (core * tok, place * feat))
        whole = lax.dynamic_update_slice(whole, swap(piece, 1), ((1 - core) * tok, place * feat))

    gain = norm_gain[None, :]
    scale = math.log2(math.e) / math.sqrt(HD)
    q = project(where, whole, gain, wq_parts, cosine, sinus, q_heads, q_heads, scale)
    m, acc = attend_prefix(bounds, q, n_wide, kv)
    kv_new = project(where, whole, gain, wkv_parts, cosine, sinus, 2, 1, 1.0)
    before = lax.ppermute(kv_new[:, tok:], "ctx", [(i, i + 2) for i in range(N_CTX - 2)])
    k_near = jnp.concatenate([before[0], kv_new[0]], axis=0)
    v_near = jnp.concatenate([before[1], kv_new[1]], axis=0)
    attended = attend_new(q, lo_wide, k_near, v_near, m, acc)

    rows = w_out.shape[0] // 4
    moved = [
        lax.ppermute(
            w_out[j * rows : (j + 1) * rows],
            ("ctx", "tp"),
            [
                ((2 * k + s) * N_TP + t, (2 * (t ^ j) + s) * N_TP + k)
                for k in range(4)
                for s in range(2)
                for t in range(4)
            ],
        )
        for j in range(4)
    ]
    wo_parts = plane_gather(jnp.concatenate(moved, axis=0))

    width = attended.shape[1]
    heads_all = jnp.zeros((chip_tok, 2 * width * N_TP), jnp.bfloat16)
    for piece, place in ((attended, z),) + line_gather(attended, z):
        base = place * 2 * width
        heads_all = lax.dynamic_update_slice(heads_all, piece, (0, base + core * width))
        heads_all = lax.dynamic_update_slice(
            heads_all, swap(piece, 1), (0, base + (1 - core) * width)
        )
    projected = out_project(where, heads_all, wo_parts)
    mine = lax.dynamic_slice_in_dim(projected, core * tok, tok, 0)
    theirs = swap(lax.dynamic_slice_in_dim(projected, (1 - core) * tok, tok, 0), 1)
    head_share = jnp.where(
        first,
        jnp.concatenate([mine, theirs], axis=1),
        jnp.concatenate([theirs, mine], axis=1),
    ).astype(jnp.float32)

    pending_share = lax.psum_scatter(
        pending[0], "tp", scatter_dimension=1, tiled=True
    ).astype(jnp.float32)
    return (stream.astype(jnp.float32) + (head_share + pending_share)).astype(jnp.bfloat16)


def solution(mesh):
    in_specs = (
        P("ctx", "tp"),
        P("tp", "ctx", None),
        P(),
        P("ctx", "tp"),
        P("ctx", None),
        P("ctx", None),
        P("tp", "ctx"),
        P(None, "ctx", None),
        P(None, "ctx", None),
        P("ctx"),
        P("ctx"),
        P(),
    )
    out_specs = P("ctx", "tp")
    small = mesh.shape["ctx"] == N_CTX and mesh.shape["tp"] == N_TP
    return jax.shard_map(
        per_device if small else per_device_any,
        mesh=mesh,
        in_specs=in_specs,
        out_specs=out_specs,
        check_vma=False,
    )
```

```python
import functools
import math

import jax
import jax.numpy as jnp
from jax import lax
from jax.experimental import pallas as pl
from jax.experimental.pallas import tpu as pltpu
from jax.sharding import PartitionSpec as P

HQ = 32
KVH = 8
HD = 128
NTRAJ = 16


ROPE_BASE = 500000.0
ROPE_FACTOR = 8.0
LOW_FREQ = 1.0
HIGH_FREQ = 4.0
INITIAL_SPAN = 8192.0
NORM_EPSILON = 1e-05
MASKED = -1e30


def inverse_freqs(head_width):
    pair_index = jnp.arange(head_width // 2, dtype=jnp.float32)
    base_freq = ROPE_BASE ** (-2.0 * pair_index / head_width)
    wavelength = 2.0 * math.pi / base_freq
    smooth = (INITIAL_SPAN / wavelength - LOW_FREQ) / (HIGH_FREQ - LOW_FREQ)
    blended = (1.0 - smooth) * base_freq / ROPE_FACTOR + smooth * base_freq
    return jnp.where(
        wavelength < INITIAL_SPAN / HIGH_FREQ,
        base_freq,
        jnp.where(wavelength > INITIAL_SPAN / LOW_FREQ, base_freq / ROPE_FACTOR, blended),
    )


def rotate(vectors, positions):
    head_width = vectors.shape[-1]
    angles = positions[..., None] * inverse_freqs(head_width)
    cosine = jnp.cos(angles)
    sinus = jnp.sin(angles)
    first_half = vectors[..., : head_width // 2]
    second_half = vectors[..., head_width // 2 :]
    return jnp.concatenate(
        [first_half * cosine - second_half * sinus, second_half * cosine + first_half * sinus],
        axis=-1,
    )


def visibility(key_labels, is_prefix, key_pos, query_segs, query_index):
    earlier = key_labels[None, :] <= query_segs[:, None]
    same = (key_labels[None, :] == query_segs[:, None]) & (key_pos[None, :] <= query_index[:, None])
    return jnp.where(is_prefix[None, :], earlier, same)


def attend_whole(grouped, key_block, value_block, seen):
    scores = jnp.einsum("hrd,hnd->hrn", grouped, key_block, preferred_element_type=jnp.float32) * (
        1.0 / math.sqrt(HD)
    )
    scores = jnp.where(seen[None], scores, MASKED)
    new_max = jnp.max(scores, axis=2)
    weights = jnp.where(seen[None], jnp.exp(scores - new_max[..., None]), 0.0)
    totals = jnp.sum(weights, axis=2)
    numerator = jnp.einsum(
        "hrn,hnd->hrd",
        weights.astype(jnp.bfloat16),
        value_block,
        preferred_element_type=jnp.float32,
    )
    return numerator / totals[..., None]


def per_device_any(
    stream,
    pending,
    norm_gain,
    w_query,
    w_key,
    w_value,
    w_out,
    prefix_keys,
    prefix_values,
    prefix_segments,
    stretch_segments,
    stretch_offset,
):
    tok_rows = stream.shape[0]
    prefix_rows = prefix_keys.shape[1]
    ctx_index = lax.axis_index("ctx")
    tp_index = lax.axis_index("tp")
    gain_wide = norm_gain.astype(jnp.float32)
    whole = lax.all_gather(stream, "tp", axis=1, tiled=True).astype(jnp.float32)
    mean_square = jnp.mean(whole * whole, axis=1, keepdims=True)
    normed = (whole * lax.rsqrt(mean_square + NORM_EPSILON) * gain_wide).astype(jnp.bfloat16)
    q_cols = w_query.shape[1]
    q_heads = q_cols // HD
    full_group = HQ // KVH
    kv_heads = max(1, q_heads // full_group)
    group_size = q_heads // kv_heads
    head_start = tp_index * q_heads // full_group
    kv_cols = kv_heads * HD
    key_slice = lax.dynamic_slice_in_dim(w_key, head_start * HD, kv_cols, 1)
    value_slice = lax.dynamic_slice_in_dim(w_value, head_start * HD, kv_cols, 1)
    pieces = (
        lax.all_gather(w_query, "ctx", axis=0, tiled=True),
        lax.all_gather(key_slice, "ctx", axis=0, tiled=True),
        lax.all_gather(value_slice, "ctx", axis=0, tiled=True),
    )
    query_raw, key_full, value_full = tuple(
        (jnp.dot(normed, piece_rows, preferred_element_type=jnp.float32) for piece_rows in pieces)
    )
    token_index = ctx_index * tok_rows + jnp.arange(tok_rows, dtype=jnp.int32)
    positions = stretch_offset[0].astype(jnp.float32) + token_index.astype(jnp.float32)
    query_rows = rotate(query_raw.reshape(tok_rows, q_heads, HD), positions[:, None]).astype(
        jnp.bfloat16
    )
    new_keys = jnp.transpose(
        rotate(key_full.reshape(tok_rows, kv_heads, HD), positions[:, None]).astype(jnp.bfloat16),
        (1, 0, 2),
    )
    new_values = jnp.transpose(
        value_full.astype(jnp.bfloat16).reshape(tok_rows, kv_heads, HD), (1, 0, 2)
    )
    old_keys = lax.dynamic_slice_in_dim(prefix_keys, head_start, kv_heads, 0)
    old_values = lax.dynamic_slice_in_dim(prefix_values, head_start, kv_heads, 0)
    local_keys = jnp.concatenate([old_keys, new_keys], 1)
    local_values = jnp.concatenate([old_values, new_values], 1)
    key_labels = jnp.concatenate([prefix_segments, stretch_segments])
    key_span = prefix_rows + tok_rows
    grouped = jnp.transpose(
        query_rows.reshape(tok_rows, kv_heads, group_size, HD), (1, 0, 2, 3)
    ).reshape(kv_heads, tok_rows * group_size, HD)
    query_index = jnp.repeat(token_index, group_size)
    query_segs = jnp.repeat(stretch_segments, group_size)
    both = jnp.stack([local_keys, local_values])
    kv_block = lax.all_gather(both, "ctx", axis=2, tiled=True)
    label_block = lax.all_gather(key_labels[None, None, :], "ctx", axis=2, tiled=True)
    key_count = kv_block.shape[2]
    absolute = jnp.arange(key_count, dtype=jnp.int32)
    within = absolute % key_span
    key_pos = absolute // key_span * tok_rows + within - prefix_rows
    seen = visibility(label_block[0, 0], within < prefix_rows, key_pos, query_segs, query_index)
    attended_heads = attend_whole(grouped, kv_block[0], kv_block[1], seen).astype(jnp.bfloat16)
    attended = jnp.transpose(
        attended_heads.reshape(kv_heads, tok_rows, group_size, HD), (1, 0, 2, 3)
    ).reshape(tok_rows, q_cols)
    head_terms = jnp.dot(
        attended,
        lax.all_gather(w_out, "ctx", axis=1, tiled=True),
        preferred_element_type=jnp.float32,
    )
    head_share, pending_share = (
        lax.psum_scatter(
            head_terms.astype(jnp.bfloat16), "tp", scatter_dimension=1, tiled=True
        ).astype(jnp.float32),
        lax.psum_scatter(
            pending[0].astype(jnp.float32).astype(jnp.bfloat16),
            "tp",
            scatter_dimension=1,
            tiled=True,
        ).astype(jnp.float32),
    )
    block_share = head_share + pending_share
    return (stream.astype(jnp.float32) + block_share).astype(jnp.bfloat16)


N_CTX = 8
N_TP = 4
MIB = 1024 * 1024


def swap(x, bit):
    return lax.ppermute(x, "ctx", [(c, c ^ bit) for c in range(N_CTX)])


def hop_up(v, pairs):
    return lax.ppermute(v, "tp", [(i, i + 1) for i in pairs])


def hop_down(v, pairs):
    return lax.ppermute(v, "tp", [(N_TP - 1 - i, N_TP - 2 - i) for i in pairs])


def none_of(*arrays):
    total = jnp.float32(0)
    for a in arrays:
        total = total + jnp.minimum(jnp.abs(a.reshape(-1)[0].astype(jnp.float32)), 0.0)
    return total


def after(x, zero):
    return x + zero.astype(x.dtype)


def gather_steps(x, z):
    u1, d1 = hop_up(x, (0, 1, 2)), hop_down(x, (0, 1, 2))
    u2, d2 = hop_up(u1, (1, 2)), hop_down(d1, (1, 2))
    u3, d3 = hop_up(u2, (2,)), hop_down(d2, (2,))
    low = z < 2
    a = jnp.where(low, d1, u1)
    b = jnp.where(low, d2, u2)
    early = jnp.where(z == 1, u1, d1)
    c = jnp.where(z == 0, d3, jnp.where(z == 3, u3, early))
    places = jnp.stack(
        [z, jnp.where(low, z + 1, z - 1), jnp.where(low, z + 2, z - 2), jnp.where(z % 2 == 1, 0, 3)]
    )
    return ((u1, d1), (u2, d2), (u3, d3)), (x, a, b, c), places


def rotated(v, cosine, sinus):
    return v * cosine + pltpu.roll(v, HD // 2, 1) * sinus


def copies_of(sems, first=0):
    count = [first]

    def make(src, dst):
        copy = pltpu.make_async_copy(src, dst, sems.at[count[0]])
        count[0] += 1
        return copy

    return make


def project_kernel(heads, rot_heads, scale, ids_ref, *refs):
    xs, ws = refs[:8], refs[8:16]
    factor_ref, cos_ref, sin_ref, out_ref, x_buf, w_buf, x_sem, w_sem = refs[16:]
    chip, core = ids_ref[0], ids_ref[1]
    tok, half = xs[0].shape[0], x_buf.shape[-1]
    mine = pl.multiple_of(core * tok, 128)
    theirs = pl.multiple_of((1 - core) * tok, 128)
    for r in range(4):
        part = ids_ref[2 + r] ^ chip
        for h in range(2):
            cols = pl.ds(pl.multiple_of((core ^ h) * half, 128), half)
            at = 2 * r + h
            for m in range(4):

                @pl.when(part == m)
                def _():
                    pltpu.make_async_copy(ws[2 * m + h], w_buf.at[at], w_sem.at[at]).start()

            for s, rows in ((0, mine), (1, theirs)):
                pltpu.make_async_copy(
                    xs[2 * r + s].at[:, cols], x_buf.at[at, pl.ds(rows, tok)], x_sem.at[2 * at + s]
                ).start()
    acc = None
    for at in range(8):
        pltpu.make_async_copy(ws[0], w_buf.at[at], w_sem.at[at]).wait()
        for s in range(2):
            pltpu.make_async_copy(
                xs[0].at[:, pl.ds(0, half)], x_buf.at[at, pl.ds(0, tok)], x_sem.at[2 * at + s]
            ).wait()
        term = jnp.dot(x_buf[at], w_buf[at], preferred_element_type=jnp.float32)
        acc = term if acc is None else acc + term
    factor = factor_ref[...]
    for h in range(heads):
        v = acc[:, h * HD : (h + 1) * HD] * factor
        if h < rot_heads:
            v = rotated(v, cos_ref[...], sin_ref[...]) * scale
        out_ref[h] = v.astype(jnp.bfloat16)


def project(ids, xs, ws, factor, cosine, sinus, heads, rot_heads, scale):
    tok, feat = xs[0].shape
    cols = heads * HD
    half = feat // 2
    hbm = pl.BlockSpec(memory_space=pl.ANY)
    vmem = pl.BlockSpec(memory_space=pltpu.VMEM)
    return pl.pallas_call(
        functools.partial(project_kernel, heads, rot_heads, scale),
        out_shape=jax.ShapeDtypeStruct((heads, 2 * tok, HD), jnp.bfloat16),
        in_specs=[pl.BlockSpec(memory_space=pltpu.SMEM)] + [hbm] * 16 + [vmem] * 3,
        out_specs=vmem,
        scratch_shapes=[
            pltpu.VMEM((8, 2 * tok, half), jnp.bfloat16),
            pltpu.VMEM((8, half, cols), jnp.bfloat16),
            pltpu.SemaphoreType.DMA((16,)),
            pltpu.SemaphoreType.DMA((8,)),
        ],
        compiler_params=pltpu.CompilerParams(vmem_limit_bytes=40 * MIB),
        cost_estimate=pl.CostEstimate(
            flops=2 * 2 * tok * 4 * feat * cols,
            bytes_accessed=8 * feat * (2 * tok + cols),
            transcendentals=0,
        ),
    )(ids, *xs, *ws, factor, cosine, sinus)


BT = 256
BK = 512
UNROLL = 2
CHAIN = 2


def scores(q, k):
    return lax.dot_general(q, k, (((1,), (1,)), ((), ())), preferred_element_type=jnp.float32)


def absorb(s, v_ext, m, acc):
    new = jnp.maximum(m, jnp.max(s, axis=1, keepdims=True))
    p = jnp.exp2(s - new).astype(jnp.bfloat16)
    acc = acc * jnp.exp2(m - new) + jnp.dot(p, v_ext, preferred_element_type=jnp.float32)
    return new, acc


def prefix_kernel(bound_ref, q_ref, n_ref, kv_ref, m_out, acc_out, v_ext, s_ref, m_ref, acc_ref):
    b = pl.program_id(0)
    heads, bt = q_ref.shape[0], q_ref.shape[1]
    rows, chains = CHAIN * bt, heads // CHAIN
    big = UNROLL * BK
    last = kv_ref.shape[1] // big - 1

    @pl.when(b == 0)
    def _():
        v_ext[:, :HD] = kv_ref[1]
        v_ext[:, HD:] = jnp.ones_like(kv_ref[1])

    m_ref[...] = jnp.full_like(m_ref, MASKED)
    acc_ref[...] = jnp.zeros_like(acc_ref)
    n_rows = jnp.concatenate([n_ref[:, :1]] * CHAIN, axis=0)

    def query(g):
        return q_ref[g * CHAIN : (g + 1) * CHAIN].reshape(rows, HD)

    s_ref[...] = scores(query(0), kv_ref[0, :BK, :])
    items = [(u, g) for u in range(UNROLL) for g in range(chains)]

    def body(kb, masked):
        start = pl.multiple_of(kb * big, big)
        follow = pl.multiple_of(jnp.minimum(kb + 1, last) * big, big)
        ms = [m_ref[g][:, :1] for g in range(chains)]
        accs = [acc_ref[g] for g in range(chains)]
        s = s_ref[...]
        for t, (u, g) in enumerate(items):
            if t + 1 < len(items):
                at, who = start + items[t + 1][0] * BK, items[t + 1][1]
            else:
                at, who = follow, 0
            ahead = scores(query(who), kv_ref[0, pl.ds(at, BK), :])
            if masked:
                col = lax.broadcasted_iota(jnp.int32, s.shape, 1) + (start + u * BK)
                s = jnp.where(col < n_rows, s, MASKED)
            v = v_ext[pl.ds(start + u * BK, BK), :]
            ms[g], accs[g] = absorb(s, v, ms[g], accs[g])
            s = ahead
        s_ref[...] = s
        for g in range(chains):
            m_ref[g] = jnp.broadcast_to(ms[g], (rows, 128))
            acc_ref[g] = accs[g]

    full = bound_ref[0, b] // big
    some = (bound_ref[1, b] + big - 1) // big
    lax.fori_loop(0, full, lambda kb, c: (body(kb, False), c)[1], 0)
    lax.fori_loop(full, some, lambda kb, c: (body(kb, True), c)[1], 0)
    m_out[0] = m_ref[...]
    acc_out[0] = acc_ref[...]


def attend_prefix(bounds, q, n_tok, kv):
    heads, tokens, _ = q.shape
    blocks = tokens // BT
    chains, rows = heads // CHAIN, CHAIN * BT
    keys = kv.shape[1]
    return pl.pallas_call(
        prefix_kernel,
        out_shape=(
            jax.ShapeDtypeStruct((blocks, chains, rows, 128), jnp.float32),
            jax.ShapeDtypeStruct((blocks, chains, rows, 2 * HD), jnp.float32),
        ),
        grid_spec=pltpu.PrefetchScalarGridSpec(
            num_scalar_prefetch=1,
            grid=(blocks,),
            in_specs=[
                pl.BlockSpec((heads, BT, HD), lambda b, *_: (0, b, 0)),
                pl.BlockSpec((BT, 128), lambda b, *_: (b, 0)),
                pl.BlockSpec((2, keys, HD), lambda b, *_: (0, 0, 0)),
            ],
            out_specs=(
                pl.BlockSpec((1, chains, rows, 128), lambda b, *_: (b, 0, 0, 0)),
                pl.BlockSpec((1, chains, rows, 2 * HD), lambda b, *_: (b, 0, 0, 0)),
            ),
            scratch_shapes=[
                pltpu.VMEM((keys, 2 * HD), jnp.bfloat16),
                pltpu.VMEM((rows, BK), jnp.float32),
                pltpu.VMEM((chains, rows, 128), jnp.float32),
                pltpu.VMEM((chains, rows, 2 * HD), jnp.float32),
            ],
        ),
        compiler_params=pltpu.CompilerParams(vmem_limit_bytes=40 * MIB),
        cost_estimate=pl.CostEstimate(
            flops=8 * heads * tokens * keys * HD,
            bytes_accessed=4 * keys * HD,
            transcendentals=heads * tokens * keys,
        ),
    )(bounds, q, n_tok, kv)


def new_kernel(halo, q_ref, lo_ref, k_ref, v_ref, m_ref, acc_ref, out_ref):
    b = pl.program_id(0)
    heads, bt = q_ref.shape[0], q_ref.shape[1]
    rows = CHAIN * bt
    span = halo + bt
    start = pl.multiple_of(b * bt, bt)
    k = k_ref[pl.ds(start, span), :]
    v = v_ref[pl.ds(start, span), :]
    v_ext = jnp.concatenate([v, jnp.ones_like(v)], axis=1)
    lo = jnp.concatenate([lo_ref[:, :1]] * CHAIN, axis=0)

    def hide(s):
        col = lax.broadcasted_iota(jnp.int32, s.shape, 1)
        row = lax.broadcasted_iota(jnp.int32, s.shape, 0) % bt
        return jnp.where((col + start >= lo) & (col <= row + halo), s, MASKED)

    for g in range(heads // CHAIN):
        q = q_ref[g * CHAIN : (g + 1) * CHAIN].reshape(rows, HD)
        _, acc = absorb(hide(scores(q, k)), v_ext, m_ref[0, g][:, :1], acc_ref[0, g])
        mixed = (acc[:, :HD] / acc[:, HD:]).astype(jnp.bfloat16)
        for h in range(CHAIN):
            at = (g * CHAIN + h) * HD
            out_ref[:, at : at + HD] = mixed[h * bt : (h + 1) * bt]


def attend_new(q, lo_tok, k, v, m, acc):
    heads, tokens, _ = q.shape
    blocks = tokens // BT
    chains, rows = heads // CHAIN, CHAIN * BT
    halo = k.shape[0] - tokens
    whole = lambda b: (0, 0)
    return pl.pallas_call(
        functools.partial(new_kernel, halo),
        out_shape=jax.ShapeDtypeStruct((tokens, heads * HD), jnp.bfloat16),
        grid=(blocks,),
        in_specs=[
            pl.BlockSpec((heads, BT, HD), lambda b: (0, b, 0)),
            pl.BlockSpec((BT, 128), lambda b: (b, 0)),
            pl.BlockSpec(k.shape, whole),
            pl.BlockSpec(v.shape, whole),
            pl.BlockSpec((1, chains, rows, 128), lambda b: (b, 0, 0, 0)),
            pl.BlockSpec((1, chains, rows, 2 * HD), lambda b: (b, 0, 0, 0)),
        ],
        out_specs=pl.BlockSpec((BT, heads * HD), lambda b: (b, 0)),
        compiler_params=pltpu.CompilerParams(vmem_limit_bytes=40 * MIB),
        cost_estimate=pl.CostEstimate(
            flops=8 * heads * tokens * (halo + BT) * HD,
            bytes_accessed=4 * tokens * heads * HD * 4,
            transcendentals=heads * tokens * (halo + BT),
        ),
    )(q, lo_tok, k, v, m, acc)


def out_kernel(ids_ref, *refs):
    xs, ws = refs[:8], refs[8:13]
    out_ref, x_buf, w_buf, x_sem, w_sem = refs[13:]
    chip, core, z = ids_ref[0], ids_ref[1], ids_ref[2]
    width = xs[0].shape[1]
    rows = w_buf.shape[1] // 4
    top = ws[3].shape[0]
    for r in range(4):
        near = ids_ref[2 + r] ^ z
        for m in range(4):
            to = w_buf.at[r, pl.ds(pl.multiple_of((chip ^ m) * rows, 128), rows)]
            sem = w_sem.at[4 * r + m]
            if m < 3:
                src = ws[m].at[pl.ds(pl.multiple_of(near * rows, 128), rows)]
                pltpu.make_async_copy(src, to, sem).start()
            else:

                @pl.when(near < 2)
                def _():
                    src = ws[3].at[pl.ds(pl.multiple_of(near * rows, 128), rows)]
                    pltpu.make_async_copy(src, to, sem).start()

                @pl.when(near >= 2)
                def _():
                    src = ws[4].at[pl.ds(pl.multiple_of(near * rows - top, 128), rows)]
                    pltpu.make_async_copy(src, to, sem).start()

        for s in range(2):
            at = pl.multiple_of((core ^ s) * width, 128)
            pltpu.make_async_copy(
                xs[2 * r + s], x_buf.at[r, :, pl.ds(at, width)], x_sem.at[2 * r + s]
            ).start()
    acc = None
    for r in range(4):
        for m in range(4):
            pltpu.make_async_copy(
                ws[0].at[pl.ds(0, rows)], w_buf.at[r, pl.ds(0, rows)], w_sem.at[4 * r + m]
            ).wait()
        for s in range(2):
            pltpu.make_async_copy(
                xs[0], x_buf.at[r, :, pl.ds(0, width)], x_sem.at[2 * r + s]
            ).wait()
        term = jnp.dot(x_buf[r], w_buf[r], preferred_element_type=jnp.float32)
        acc = term if acc is None else acc + term
    out_ref[...] = acc.astype(jnp.bfloat16)


def out_project(ids, xs, ws):
    tokens, width = xs[0].shape
    depth, cols = ws[0].shape
    hbm = pl.BlockSpec(memory_space=pl.ANY)
    return pl.pallas_call(
        out_kernel,
        out_shape=jax.ShapeDtypeStruct((tokens, cols), jnp.bfloat16),
        in_specs=[pl.BlockSpec(memory_space=pltpu.SMEM)] + [hbm] * 13,
        out_specs=pl.BlockSpec(memory_space=pltpu.VMEM),
        scratch_shapes=[
            pltpu.VMEM((4, tokens, 2 * width), jnp.bfloat16),
            pltpu.VMEM((4, depth, cols), jnp.bfloat16),
            pltpu.SemaphoreType.DMA((8,)),
            pltpu.SemaphoreType.DMA((16,)),
        ],
        compiler_params=pltpu.CompilerParams(vmem_limit_bytes=40 * MIB),
        cost_estimate=pl.CostEstimate(
            flops=2 * tokens * 4 * depth * cols,
            bytes_accessed=8 * depth * (tokens + cols),
            transcendentals=0,
        ),
    )(ids, *xs, *ws)


def per_device(
    stream,
    pending,
    norm_gain,
    w_query,
    w_key,
    w_value,
    w_out,
    prefix_keys,
    prefix_values,
    prefix_segments,
    stretch_segments,
    stretch_offset,
):
    tok, feat = stream.shape
    chip_tok = 2 * tok
    c = lax.axis_index("ctx")
    z = lax.axis_index("tp")
    chip, core = c // 2, c % 2
    first = core == 0
    depth = feat * N_TP

    wide = stream.astype(jnp.float32)
    gain = lax.dynamic_slice_in_dim(norm_gain, z * feat, feat, 0).astype(jnp.float32)
    scaled = (wide * gain[None, :]).astype(jnp.bfloat16)
    arrivals, parts, places = gather_steps(scaled, z)
    ids = jnp.concatenate([jnp.stack([chip, core]), places]).astype(jnp.int32)
    step1, step2, step3 = (none_of(*pair) for pair in arrivals)
    xs = []
    for part in parts:
        xs += [part, swap(part, 1)]

    def halves(w, width, base):
        mine = lax.dynamic_slice_in_dim(w, base + core * width, width, 1)
        theirs = lax.dynamic_slice_in_dim(w, base + (1 - core) * width, width, 1)
        return mine, swap(theirs, 1)

    def plane(own, other, zero_other, zero_far):
        own_x, own_y = swap(own, 2), swap(own, 4)
        late = after(other, zero_other)
        other_x, other_y = swap(late, 2), swap(late, 4)
        far_own = swap(after(own_x, zero_far), 4)
        far_other = swap(after(other_y, zero_far), 2)
        return own, other, own_x, other_x, own_y, other_y, far_own, far_other

    q_heads = w_query.shape[1] // HD // 2
    wq_parts = plane(*halves(w_query, q_heads * HD, 0), step1, step2)
    kv_old = jnp.stack([prefix_keys, prefix_values])
    old_own = lax.dynamic_index_in_dim(kv_old, 2 * z + core, 1, keepdims=False)
    old_other = swap(lax.dynamic_index_in_dim(kv_old, 2 * z + 1 - core, 1, keepdims=False), 1)
    old_parts = plane(old_own, old_other, step1, step2)
    span = old_own.shape[1]
    kv = jnp.zeros((2, N_CTX * span, HD), jnp.bfloat16)
    for index, part in enumerate(old_parts):
        from_ctx = ((chip ^ (index // 2)) * 2 + (core ^ (index % 2))) * span
        kv = lax.dynamic_update_slice(kv, part, (0, from_ctx, 0))

    piece_rows = w_out.shape[0] // 4

    def piece(q):
        return lax.dynamic_slice_in_dim(w_out, q * piece_rows, piece_rows, 0)

    to_x, to_y = swap(piece(chip ^ 1), 2), swap(piece(chip ^ 2), 4)
    to_far = swap(after(piece(chip ^ 3), step1), 6)
    by_chip = jnp.stack([piece(chip), to_x, to_y, to_far])

    def of_chip(q):
        return lax.dynamic_index_in_dim(by_chip, q ^ chip, 0, keepdims=False)

    pieces = [of_chip(z)]
    for r in (1, 2, 3):
        pieces.append(
            lax.ppermute(after(of_chip(z ^ r), step3), "tp", [(i, i ^ r) for i in range(N_TP)])
        )
    moved = none_of(*pieces[1:])
    block = jnp.concatenate(pieces, axis=0)
    half = block.shape[0] // 2
    wo_x, wo_y = swap(block, 2), swap(block, 4)
    wo_parts = (block, wo_x, wo_y, swap(wo_x[:half], 4), swap(wo_y[half:], 2))

    def share(place):
        return lax.dynamic_slice_in_dim(pending[0], jnp.clip(place, 0, N_TP - 1) * feat, feat, 1)

    up = hop_up(after(share(z + 3), step1), (0,))
    down = hop_down(after(share(z - 3), step1), (0,))
    up = hop_up(after(share(z + 2) + up, step2), (0, 1))
    down = hop_down(after(share(z - 2) + down, step2), (0, 1))
    up = hop_up(after(share(z + 1) + up, moved), (0, 1, 2))
    down = hop_down(after(share(z - 1) + down, moved), (0, 1, 2))
    pending_share = (
        share(z).astype(jnp.float32) + up.astype(jnp.float32) + down.astype(jnp.float32)
    )

    squares = jnp.sum(wide * wide, axis=1)[None, :]
    for r in (1, 2):
        squares = squares + lax.ppermute(squares, "tp", [(i, i ^ r) for i in range(N_TP)])
    factor = lax.rsqrt(squares[0] * (1.0 / depth) + NORM_EPSILON)

    labels = jnp.arange(NTRAJ, dtype=jnp.int32)
    counts = jnp.stack(
        [
            jnp.sum((prefix_segments[:, None] <= labels).astype(jnp.int32), axis=0),
            jnp.sum((stretch_segments[:, None] < labels).astype(jnp.int32), axis=0),
        ]
    )
    for bit in (1, 2, 4):
        counts = counts + swap(counts, bit)

    def of_chip_tokens(mine):
        theirs = swap(mine, 1)
        return jnp.where(
            first, jnp.concatenate([mine, theirs], axis=0), jnp.concatenate([theirs, mine], axis=0)
        )

    factor = jnp.broadcast_to(of_chip_tokens(factor)[:, None], (chip_tok, 128))
    segs = of_chip_tokens(stretch_segments)
    onehot = (segs[:, None] == labels).astype(jnp.int32)
    n_tok = jnp.sum(onehot * counts[0], axis=1)
    lo_tok = jnp.sum(onehot * counts[1], axis=1) - chip * chip_tok + tok
    blocked = n_tok.reshape(chip_tok // BT, BT)
    bounds = jnp.stack([blocked[:, 0], blocked[:, -1]])
    n_wide = jnp.broadcast_to(n_tok[:, None], (chip_tok, 128))
    lo_wide = jnp.broadcast_to(lo_tok[:, None], (chip_tok, 128))

    token_index = chip * chip_tok + jnp.arange(chip_tok, dtype=jnp.int32)
    positions = stretch_offset[0].astype(jnp.float32) + token_index.astype(jnp.float32)
    angles = positions[:, None] * inverse_freqs(HD)
    cosine, sinus = jnp.cos(angles), jnp.sin(angles)
    cosine = jnp.concatenate([cosine, cosine], axis=1)
    sinus = jnp.concatenate([-sinus, sinus], axis=1)

    scale = math.log2(math.e) / math.sqrt(HD)
    q = project(ids, xs, wq_parts, factor, cosine, sinus, q_heads, q_heads, scale)
    m, acc = attend_prefix(bounds, q, n_wide, kv)

    mine_k, other_k = halves(w_key, HD, 2 * z * HD)
    mine_v, other_v = halves(w_value, HD, 2 * z * HD)
    wkv_parts = plane(
        after(jnp.concatenate([mine_k, mine_v], axis=1), step3),
        jnp.concatenate([other_k, other_v], axis=1),
        step3,
        step3,
    )
    kv_new = project(ids, xs, wkv_parts, factor, cosine, sinus, 2, 1, 1.0)
    before = lax.ppermute(kv_new[:, tok:], "ctx", [(i, i + 2) for i in range(N_CTX - 2)])
    k_near = jnp.concatenate([before[0], kv_new[0]], axis=0)
    v_near = jnp.concatenate([before[1], kv_new[1]], axis=0)
    attended = attend_new(q, lo_wide, k_near, v_near, m, acc)

    _, heads_parts, _ = gather_steps(attended, z)
    hs = []
    for part in heads_parts:
        hs += [part, swap(part, 1)]
    projected = out_project(ids, hs, wo_parts)
    mine = lax.dynamic_slice_in_dim(projected, core * tok, tok, 0)
    theirs = swap(lax.dynamic_slice_in_dim(projected, (1 - core) * tok, tok, 0), 1)
    head_share = jnp.where(
        first,
        jnp.concatenate([mine, theirs], axis=1),
        jnp.concatenate([theirs, mine], axis=1),
    ).astype(jnp.float32)
    return (wide + (head_share + pending_share)).astype(jnp.bfloat16)


def solution(mesh):
    in_specs = (
        P("ctx", "tp"),
        P("tp", "ctx", None),
        P(),
        P("ctx", "tp"),
        P("ctx", None),
        P("ctx", None),
        P("tp", "ctx"),
        P(None, "ctx", None),
        P(None, "ctx", None),
        P("ctx"),
        P("ctx"),
        P(),
    )
    out_specs = P("ctx", "tp")
    small = mesh.shape["ctx"] == N_CTX and mesh.shape["tp"] == N_TP
    return jax.shard_map(
        per_device if small else per_device_any,
        mesh=mesh,
        in_specs=in_specs,
        out_specs=out_specs,
        check_vma=False,
    )
```

```python
import functools
import math

import jax
import jax.numpy as jnp
from jax import lax
from jax.experimental import pallas as pl
from jax.experimental.pallas import tpu as pltpu
from jax.sharding import PartitionSpec as P

HQ = 32
KVH = 8
HD = 128
NTRAJ = 16


ROPE_BASE = 500000.0
ROPE_FACTOR = 8.0
LOW_FREQ = 1.0
HIGH_FREQ = 4.0
INITIAL_SPAN = 8192.0
NORM_EPSILON = 1e-05
MASKED = -1e30


def inverse_freqs(head_width):
    pair_index = jnp.arange(head_width // 2, dtype=jnp.float32)
    base_freq = ROPE_BASE ** (-2.0 * pair_index / head_width)
    wavelength = 2.0 * math.pi / base_freq
    smooth = (INITIAL_SPAN / wavelength - LOW_FREQ) / (HIGH_FREQ - LOW_FREQ)
    blended = (1.0 - smooth) * base_freq / ROPE_FACTOR + smooth * base_freq
    return jnp.where(
        wavelength < INITIAL_SPAN / HIGH_FREQ,
        base_freq,
        jnp.where(wavelength > INITIAL_SPAN / LOW_FREQ, base_freq / ROPE_FACTOR, blended),
    )


def rotate(vectors, positions):
    head_width = vectors.shape[-1]
    angles = positions[..., None] * inverse_freqs(head_width)
    cosine = jnp.cos(angles)
    sinus = jnp.sin(angles)
    first_half = vectors[..., : head_width // 2]
    second_half = vectors[..., head_width // 2 :]
    return jnp.concatenate(
        [first_half * cosine - second_half * sinus, second_half * cosine + first_half * sinus],
        axis=-1,
    )


def visibility(key_labels, is_prefix, key_pos, query_segs, query_index):
    earlier = key_labels[None, :] <= query_segs[:, None]
    same = (key_labels[None, :] == query_segs[:, None]) & (key_pos[None, :] <= query_index[:, None])
    return jnp.where(is_prefix[None, :], earlier, same)


def attend_whole(grouped, key_block, value_block, seen):
    scores = jnp.einsum("hrd,hnd->hrn", grouped, key_block, preferred_element_type=jnp.float32) * (
        1.0 / math.sqrt(HD)
    )
    scores = jnp.where(seen[None], scores, MASKED)
    new_max = jnp.max(scores, axis=2)
    weights = jnp.where(seen[None], jnp.exp(scores - new_max[..., None]), 0.0)
    totals = jnp.sum(weights, axis=2)
    numerator = jnp.einsum(
        "hrn,hnd->hrd",
        weights.astype(jnp.bfloat16),
        value_block,
        preferred_element_type=jnp.float32,
    )
    return numerator / totals[..., None]


def per_device_any(
    stream,
    pending,
    norm_gain,
    w_query,
    w_key,
    w_value,
    w_out,
    prefix_keys,
    prefix_values,
    prefix_segments,
    stretch_segments,
    stretch_offset,
):
    tok_rows = stream.shape[0]
    prefix_rows = prefix_keys.shape[1]
    ctx_index = lax.axis_index("ctx")
    tp_index = lax.axis_index("tp")
    gain_wide = norm_gain.astype(jnp.float32)
    whole = lax.all_gather(stream, "tp", axis=1, tiled=True).astype(jnp.float32)
    mean_square = jnp.mean(whole * whole, axis=1, keepdims=True)
    normed = (whole * lax.rsqrt(mean_square + NORM_EPSILON) * gain_wide).astype(jnp.bfloat16)
    q_cols = w_query.shape[1]
    q_heads = q_cols // HD
    full_group = HQ // KVH
    kv_heads = max(1, q_heads // full_group)
    group_size = q_heads // kv_heads
    head_start = tp_index * q_heads // full_group
    kv_cols = kv_heads * HD
    key_slice = lax.dynamic_slice_in_dim(w_key, head_start * HD, kv_cols, 1)
    value_slice = lax.dynamic_slice_in_dim(w_value, head_start * HD, kv_cols, 1)
    pieces = (
        lax.all_gather(w_query, "ctx", axis=0, tiled=True),
        lax.all_gather(key_slice, "ctx", axis=0, tiled=True),
        lax.all_gather(value_slice, "ctx", axis=0, tiled=True),
    )
    query_raw, key_full, value_full = tuple(
        (jnp.dot(normed, piece_rows, preferred_element_type=jnp.float32) for piece_rows in pieces)
    )
    token_index = ctx_index * tok_rows + jnp.arange(tok_rows, dtype=jnp.int32)
    positions = stretch_offset[0].astype(jnp.float32) + token_index.astype(jnp.float32)
    query_rows = rotate(query_raw.reshape(tok_rows, q_heads, HD), positions[:, None]).astype(
        jnp.bfloat16
    )
    new_keys = jnp.transpose(
        rotate(key_full.reshape(tok_rows, kv_heads, HD), positions[:, None]).astype(jnp.bfloat16),
        (1, 0, 2),
    )
    new_values = jnp.transpose(
        value_full.astype(jnp.bfloat16).reshape(tok_rows, kv_heads, HD), (1, 0, 2)
    )
    old_keys = lax.dynamic_slice_in_dim(prefix_keys, head_start, kv_heads, 0)
    old_values = lax.dynamic_slice_in_dim(prefix_values, head_start, kv_heads, 0)
    local_keys = jnp.concatenate([old_keys, new_keys], 1)
    local_values = jnp.concatenate([old_values, new_values], 1)
    key_labels = jnp.concatenate([prefix_segments, stretch_segments])
    key_span = prefix_rows + tok_rows
    grouped = jnp.transpose(
        query_rows.reshape(tok_rows, kv_heads, group_size, HD), (1, 0, 2, 3)
    ).reshape(kv_heads, tok_rows * group_size, HD)
    query_index = jnp.repeat(token_index, group_size)
    query_segs = jnp.repeat(stretch_segments, group_size)
    both = jnp.stack([local_keys, local_values])
    kv_block = lax.all_gather(both, "ctx", axis=2, tiled=True)
    label_block = lax.all_gather(key_labels[None, None, :], "ctx", axis=2, tiled=True)
    key_count = kv_block.shape[2]
    absolute = jnp.arange(key_count, dtype=jnp.int32)
    within = absolute % key_span
    key_pos = absolute // key_span * tok_rows + within - prefix_rows
    seen = visibility(label_block[0, 0], within < prefix_rows, key_pos, query_segs, query_index)
    attended_heads = attend_whole(grouped, kv_block[0], kv_block[1], seen).astype(jnp.bfloat16)
    attended = jnp.transpose(
        attended_heads.reshape(kv_heads, tok_rows, group_size, HD), (1, 0, 2, 3)
    ).reshape(tok_rows, q_cols)
    head_terms = jnp.dot(
        attended,
        lax.all_gather(w_out, "ctx", axis=1, tiled=True),
        preferred_element_type=jnp.float32,
    )
    head_share, pending_share = (
        lax.psum_scatter(
            head_terms.astype(jnp.bfloat16), "tp", scatter_dimension=1, tiled=True
        ).astype(jnp.float32),
        lax.psum_scatter(
            pending[0].astype(jnp.float32).astype(jnp.bfloat16),
            "tp",
            scatter_dimension=1,
            tiled=True,
        ).astype(jnp.float32),
    )
    block_share = head_share + pending_share
    return (stream.astype(jnp.float32) + block_share).astype(jnp.bfloat16)


N_CTX = 8
N_TP = 4
MIB = 1024 * 1024


def swap(x, bit):
    return lax.ppermute(x, "ctx", [(c, c ^ bit) for c in range(N_CTX)])


def hop_up(v, pairs):
    return lax.ppermute(v, "tp", [(i, i + 1) for i in pairs])


def hop_down(v, pairs):
    return lax.ppermute(v, "tp", [(N_TP - 1 - i, N_TP - 2 - i) for i in pairs])


def none_of(*arrays):
    total = jnp.float32(0)
    for a in arrays:
        total = total + jnp.minimum(jnp.abs(a.reshape(-1)[0].astype(jnp.float32)), 0.0)
    return total


def after(x, zero):
    return x + zero.astype(x.dtype)


def line_parts(z, one, two, three):
    (u1, d1), (u2, d2), (u3, d3) = one, two, three
    low = z < 2
    a = jnp.where(low, d1, u1)
    b = jnp.where(low, d2, u2)
    early = jnp.where(z == 1, u1, d1)
    c = jnp.where(z == 0, d3, jnp.where(z == 3, u3, early))
    places = jnp.stack(
        [z, jnp.where(low, z + 1, z - 1), jnp.where(low, z + 2, z - 2), jnp.where(z % 2 == 1, 0, 3)]
    )
    return (a, b, c), places


def rotated(v, cosine, sinus):
    return v * cosine + pltpu.roll(v, HD // 2, 1) * sinus


def copies_of(sems, first=0):
    count = [first]

    def make(src, dst):
        copy = pltpu.make_async_copy(src, dst, sems.at[count[0]])
        count[0] += 1
        return copy

    return make


def project_kernel(heads, rot_heads, scale, ids_ref, *refs):
    xs, ws = refs[:8], refs[8:16]
    factor_ref, cos_ref, sin_ref, out_ref, x_buf, w_buf, x_sem, w_sem = refs[16:]
    chip, core = ids_ref[0], ids_ref[1]
    tok, half = xs[0].shape[0], x_buf.shape[-1]
    mine = pl.multiple_of(core * tok, 128)
    theirs = pl.multiple_of((1 - core) * tok, 128)
    for r in range(4):
        part = ids_ref[2 + r] ^ chip
        for h in range(2):
            cols = pl.ds(pl.multiple_of((core ^ h) * half, 128), half)
            at = 2 * r + h
            for m in range(4):

                @pl.when(part == m)
                def _():
                    src = ws[2 * m + h].at[pl.ds(0, half)]
                    pltpu.make_async_copy(src, w_buf.at[at], w_sem.at[at]).start()

            for s, rows in ((0, mine), (1, theirs)):
                src = xs[2 * r + s]
                skip = tok if src.shape[0] > tok and r == 1 else 0
                pltpu.make_async_copy(
                    src.at[pl.ds(skip, tok), cols],
                    x_buf.at[at, pl.ds(rows, tok)],
                    x_sem.at[2 * at + s],
                ).start()
    acc = None
    for at in range(8):
        pltpu.make_async_copy(ws[0].at[pl.ds(0, half)], w_buf.at[at], w_sem.at[at]).wait()
        for s in range(2):
            pltpu.make_async_copy(
                xs[0].at[:, pl.ds(0, half)], x_buf.at[at, pl.ds(0, tok)], x_sem.at[2 * at + s]
            ).wait()
        term = jnp.dot(x_buf[at], w_buf[at], preferred_element_type=jnp.float32)
        acc = term if acc is None else acc + term
    factor = factor_ref[...]
    for h in range(heads):
        v = acc[:, h * HD : (h + 1) * HD] * factor
        if h < rot_heads:
            v = rotated(v, cos_ref[...], sin_ref[...]) * scale
        out_ref[h] = v.astype(jnp.bfloat16)


def project(ids, xs, ws, factor, cosine, sinus, heads, rot_heads, scale):
    tok, feat = xs[0].shape
    cols = heads * HD
    half = feat // 2
    hbm = pl.BlockSpec(memory_space=pl.ANY)
    vmem = pl.BlockSpec(memory_space=pltpu.VMEM)
    return pl.pallas_call(
        functools.partial(project_kernel, heads, rot_heads, scale),
        out_shape=jax.ShapeDtypeStruct((heads, 2 * tok, HD), jnp.bfloat16),
        in_specs=[pl.BlockSpec(memory_space=pltpu.SMEM)] + [hbm] * 16 + [vmem] * 3,
        out_specs=vmem,
        scratch_shapes=[
            pltpu.VMEM((8, 2 * tok, half), jnp.bfloat16),
            pltpu.VMEM((8, half, cols), jnp.bfloat16),
            pltpu.SemaphoreType.DMA((16,)),
            pltpu.SemaphoreType.DMA((8,)),
        ],
        compiler_params=pltpu.CompilerParams(vmem_limit_bytes=40 * MIB),
        cost_estimate=pl.CostEstimate(
            flops=2 * 2 * tok * 4 * feat * cols,
            bytes_accessed=8 * feat * (2 * tok + cols),
            transcendentals=0,
        ),
    )(ids, *xs, *ws, factor, cosine, sinus)


BT = 256
BK = 512
UNROLL = 2
CHAIN = 2


def scores(q, k):
    return lax.dot_general(q, k, (((1,), (1,)), ((), ())), preferred_element_type=jnp.float32)


def absorb(s, v_ext, m, acc):
    new = jnp.maximum(m, jnp.max(s, axis=1, keepdims=True))
    p = jnp.exp2(s - new).astype(jnp.bfloat16)
    acc = acc * jnp.exp2(m - new) + jnp.dot(p, v_ext, preferred_element_type=jnp.float32)
    return new, acc


def prefix_kernel(bound_ref, q_ref, n_ref, kv_ref, m_out, acc_out, v_ext, s_ref, m_ref, acc_ref):
    b = pl.program_id(0)
    heads, bt = q_ref.shape[0], q_ref.shape[1]
    rows, chains = CHAIN * bt, heads // CHAIN
    big = UNROLL * BK
    last = kv_ref.shape[1] // big - 1

    @pl.when(b == 0)
    def _():
        v_ext[:, :HD] = kv_ref[1]
        v_ext[:, HD:] = jnp.ones_like(kv_ref[1])

    m_ref[...] = jnp.full_like(m_ref, MASKED)
    acc_ref[...] = jnp.zeros_like(acc_ref)
    n_rows = jnp.concatenate([n_ref[:, :1]] * CHAIN, axis=0)

    def query(g):
        return q_ref[g * CHAIN : (g + 1) * CHAIN].reshape(rows, HD)

    s_ref[...] = scores(query(0), kv_ref[0, :BK, :])
    items = [(u, g) for u in range(UNROLL) for g in range(chains)]

    def body(kb, masked):
        start = pl.multiple_of(kb * big, big)
        follow = pl.multiple_of(jnp.minimum(kb + 1, last) * big, big)
        ms = [m_ref[g][:, :1] for g in range(chains)]
        accs = [acc_ref[g] for g in range(chains)]
        s = s_ref[...]
        for t, (u, g) in enumerate(items):
            if t + 1 < len(items):
                at, who = start + items[t + 1][0] * BK, items[t + 1][1]
            else:
                at, who = follow, 0
            ahead = scores(query(who), kv_ref[0, pl.ds(at, BK), :])
            if masked:
                col = lax.broadcasted_iota(jnp.int32, s.shape, 1) + (start + u * BK)
                s = jnp.where(col < n_rows, s, MASKED)
            v = v_ext[pl.ds(start + u * BK, BK), :]
            ms[g], accs[g] = absorb(s, v, ms[g], accs[g])
            s = ahead
        s_ref[...] = s
        for g in range(chains):
            m_ref[g] = jnp.broadcast_to(ms[g], (rows, 128))
            acc_ref[g] = accs[g]

    full = bound_ref[0, b] // big
    some = (bound_ref[1, b] + big - 1) // big
    lax.fori_loop(0, full, lambda kb, c: (body(kb, False), c)[1], 0)
    lax.fori_loop(full, some, lambda kb, c: (body(kb, True), c)[1], 0)
    m_out[0] = m_ref[...]
    acc_out[0] = acc_ref[...]


def attend_prefix(bounds, q, group, n_tok, kv):
    heads, tokens = CHAIN, q.shape[1]
    blocks = tokens // BT
    chains, rows = heads // CHAIN, CHAIN * BT
    keys = kv.shape[1]
    return pl.pallas_call(
        prefix_kernel,
        out_shape=(
            jax.ShapeDtypeStruct((blocks, chains, rows, 128), jnp.float32),
            jax.ShapeDtypeStruct((blocks, chains, rows, 2 * HD), jnp.float32),
        ),
        grid_spec=pltpu.PrefetchScalarGridSpec(
            num_scalar_prefetch=1,
            grid=(blocks,),
            in_specs=[
                pl.BlockSpec((heads, BT, HD), lambda b, *_: (group, b, 0)),
                pl.BlockSpec((BT, 128), lambda b, *_: (b, 0)),
                pl.BlockSpec((2, keys, HD), lambda b, *_: (0, 0, 0)),
            ],
            out_specs=(
                pl.BlockSpec((1, chains, rows, 128), lambda b, *_: (b, 0, 0, 0)),
                pl.BlockSpec((1, chains, rows, 2 * HD), lambda b, *_: (b, 0, 0, 0)),
            ),
            scratch_shapes=[
                pltpu.VMEM((keys, 2 * HD), jnp.bfloat16),
                pltpu.VMEM((rows, BK), jnp.float32),
                pltpu.VMEM((chains, rows, 128), jnp.float32),
                pltpu.VMEM((chains, rows, 2 * HD), jnp.float32),
            ],
        ),
        compiler_params=pltpu.CompilerParams(vmem_limit_bytes=40 * MIB),
        cost_estimate=pl.CostEstimate(
            flops=heads * tokens * HD, bytes_accessed=4 * keys * HD, transcendentals=0
        ),
    )(bounds, q, n_tok, kv)


def new_kernel(halo, q_ref, lo_ref, k_ref, v_ref, *refs):
    states, out_ref = refs[:-1], refs[-1]
    b = pl.program_id(0)
    heads, bt = q_ref.shape[0], q_ref.shape[1]
    rows = CHAIN * bt
    span = halo + bt
    start = pl.multiple_of(b * bt, bt)
    k = k_ref[pl.ds(start, span), :]
    v = v_ref[pl.ds(start, span), :]
    v_ext = jnp.concatenate([v, jnp.ones_like(v)], axis=1)
    lo = jnp.concatenate([lo_ref[:, :1]] * CHAIN, axis=0)

    def hide(s):
        col = lax.broadcasted_iota(jnp.int32, s.shape, 1)
        row = lax.broadcasted_iota(jnp.int32, s.shape, 0) % bt
        return jnp.where((col + start >= lo) & (col <= row + halo), s, MASKED)

    for g in range(heads // CHAIN):
        q = q_ref[g * CHAIN : (g + 1) * CHAIN].reshape(rows, HD)
        _, acc = absorb(
            hide(scores(q, k)), v_ext, states[2 * g][0, 0][:, :1], states[2 * g + 1][0, 0]
        )
        mixed = (acc[:, :HD] / acc[:, HD:]).astype(jnp.bfloat16)
        for h in range(CHAIN):
            at = (g * CHAIN + h) * HD
            out_ref[:, at : at + HD] = mixed[h * bt : (h + 1) * bt]


def attend_new(q, lo_tok, k, v, states):
    heads, tokens, _ = q.shape
    blocks = tokens // BT
    chains, rows = heads // CHAIN, CHAIN * BT
    halo = k.shape[0] - tokens
    whole = lambda b: (0, 0)
    return pl.pallas_call(
        functools.partial(new_kernel, halo),
        out_shape=jax.ShapeDtypeStruct((tokens, heads * HD), jnp.bfloat16),
        grid=(blocks,),
        in_specs=[
            pl.BlockSpec((heads, BT, HD), lambda b: (0, b, 0)),
            pl.BlockSpec((BT, 128), lambda b: (b, 0)),
            pl.BlockSpec(k.shape, whole),
            pl.BlockSpec(v.shape, whole),
        ]
        + [
            pl.BlockSpec((1, 1, rows, 128), lambda b: (b, 0, 0, 0)),
            pl.BlockSpec((1, 1, rows, 2 * HD), lambda b: (b, 0, 0, 0)),
        ]
        * chains,
        out_specs=pl.BlockSpec((BT, heads * HD), lambda b: (b, 0)),
        compiler_params=pltpu.CompilerParams(vmem_limit_bytes=40 * MIB),
        cost_estimate=pl.CostEstimate(
            flops=heads * tokens * HD, bytes_accessed=4 * tokens * heads * HD, transcendentals=0
        ),
    )(q, lo_tok, k, v, *states)


def out_kernel(ids_ref, *refs):
    xs, ws = refs[:8], refs[8:13]
    out_ref, x_buf, w_buf, x_sem, w_sem = refs[13:]
    chip, core, z = ids_ref[0], ids_ref[1], ids_ref[2]
    width = xs[0].shape[1]
    rows = w_buf.shape[1] // 4
    top = ws[3].shape[0]
    for r in range(4):
        near = ids_ref[2 + r] ^ z
        for m in range(4):
            to = w_buf.at[r, pl.ds(pl.multiple_of((chip ^ m) * rows, 128), rows)]
            sem = w_sem.at[4 * r + m]
            if m < 3:
                src = ws[m].at[pl.ds(pl.multiple_of(near * rows, 128), rows)]
                pltpu.make_async_copy(src, to, sem).start()
            else:

                @pl.when(near < 2)
                def _():
                    src = ws[3].at[pl.ds(pl.multiple_of(near * rows, 128), rows)]
                    pltpu.make_async_copy(src, to, sem).start()

                @pl.when(near >= 2)
                def _():
                    src = ws[4].at[pl.ds(pl.multiple_of(near * rows - top, 128), rows)]
                    pltpu.make_async_copy(src, to, sem).start()

        for s in range(2):
            at = pl.multiple_of((core ^ s) * width, 128)
            pltpu.make_async_copy(
                xs[2 * r + s], x_buf.at[r, :, pl.ds(at, width)], x_sem.at[2 * r + s]
            ).start()
    acc = None
    for r in range(4):
        for m in range(4):
            pltpu.make_async_copy(
                ws[0].at[pl.ds(0, rows)], w_buf.at[r, pl.ds(0, rows)], w_sem.at[4 * r + m]
            ).wait()
        for s in range(2):
            pltpu.make_async_copy(
                xs[0], x_buf.at[r, :, pl.ds(0, width)], x_sem.at[2 * r + s]
            ).wait()
        term = jnp.dot(x_buf[r], w_buf[r], preferred_element_type=jnp.float32)
        acc = term if acc is None else acc + term
    out_ref[...] = acc.astype(jnp.bfloat16)


def out_project(ids, xs, ws):
    tokens, width = xs[0].shape
    depth, cols = ws[0].shape
    hbm = pl.BlockSpec(memory_space=pl.ANY)
    return pl.pallas_call(
        out_kernel,
        out_shape=jax.ShapeDtypeStruct((tokens, cols), jnp.bfloat16),
        in_specs=[pl.BlockSpec(memory_space=pltpu.SMEM)] + [hbm] * 13,
        out_specs=pl.BlockSpec(memory_space=pltpu.VMEM),
        scratch_shapes=[
            pltpu.VMEM((4, tokens, 2 * width), jnp.bfloat16),
            pltpu.VMEM((4, depth, cols), jnp.bfloat16),
            pltpu.SemaphoreType.DMA((8,)),
            pltpu.SemaphoreType.DMA((16,)),
        ],
        compiler_params=pltpu.CompilerParams(vmem_limit_bytes=40 * MIB),
        cost_estimate=pl.CostEstimate(
            flops=2 * tokens * 4 * depth * cols,
            bytes_accessed=8 * depth * (tokens + cols),
            transcendentals=0,
        ),
    )(ids, *xs, *ws)


def per_device(
    stream,
    pending,
    norm_gain,
    w_query,
    w_key,
    w_value,
    w_out,
    prefix_keys,
    prefix_values,
    prefix_segments,
    stretch_segments,
    stretch_offset,
):
    tok, feat = stream.shape
    chip_tok = 2 * tok
    c = lax.axis_index("ctx")
    z = lax.axis_index("tp")
    chip, core = c // 2, c % 2
    first = core == 0
    depth = feat * N_TP

    wide = stream.astype(jnp.float32)
    labels = jnp.arange(NTRAJ, dtype=jnp.int32)
    seen_counts = jnp.sum((prefix_segments[:, None] <= labels).astype(jnp.float32), axis=0)
    start_counts = jnp.sum((stretch_segments[:, None] < labels).astype(jnp.float32), axis=0)
    here = (jnp.arange(N_CTX) == c).astype(jnp.float32)[:, None]
    lead = (z == 0).astype(jnp.float32)
    sums = lax.psum(
        jnp.concatenate(
            [
                (here * jnp.sum(wide * wide, axis=1)[None, :]).reshape(-1),
                (here * stretch_segments.astype(jnp.float32)[None, :]).reshape(-1) * lead,
                seen_counts * lead,
                start_counts * lead,
            ]
        ),
        ("ctx", "tp"),
    )
    all_tok = N_CTX * tok
    squares = lax.dynamic_slice_in_dim(sums[:all_tok], chip * chip_tok, chip_tok, 0)
    segs = lax.dynamic_slice_in_dim(sums[all_tok : 2 * all_tok], chip * chip_tok, chip_tok, 0)
    counts = sums[2 * all_tok :].reshape(2, NTRAJ).astype(jnp.int32)
    factor = lax.rsqrt(squares * (1.0 / depth) + NORM_EPSILON)
    factor = jnp.broadcast_to(factor[:, None], (chip_tok, 128))
    onehot = (segs.astype(jnp.int32)[:, None] == labels).astype(jnp.int32)
    n_tok = jnp.sum(onehot * counts[0], axis=1)
    lo_tok = jnp.sum(onehot * counts[1], axis=1) - chip * chip_tok + tok
    blocked = n_tok.reshape(chip_tok // BT, BT)
    bounds = jnp.stack([blocked[:, 0], blocked[:, -1]])
    n_wide = jnp.broadcast_to(n_tok[:, None], (chip_tok, 128))
    lo_wide = jnp.broadcast_to(lo_tok[:, None], (chip_tok, 128))

    q_heads = w_query.shape[1] // HD // 2
    q_cols = q_heads * HD
    kv_old = jnp.stack([prefix_keys, prefix_values])

    def query_cols(j):
        return lax.dynamic_slice_in_dim(w_query, j * q_cols, q_cols, 1)

    def old_rows(j):
        head = lax.dynamic_index_in_dim(kv_old, 2 * z + j, 1, keepdims=False)
        n = head.shape[1] // 2
        return jnp.concatenate([head[0, :n], head[0, n:], head[1, :n], head[1, n:]], axis=1)

    def kv_rows(j):
        both = jnp.concatenate(
            [lax.dynamic_slice_in_dim(w, (2 * z + j) * HD, HD, 1) for w in (w_key, w_value)], axis=1
        )
        n = both.shape[0] // 2
        return jnp.concatenate([both[:n], both[n:]], axis=1)

    def piece(q):
        n = w_out.shape[0] // 4
        rows = lax.dynamic_slice_in_dim(w_out, q * n, n, 0)
        return jnp.concatenate([rows[:, :q_cols], rows[:, q_cols:]], axis=0)

    def share(place):
        return lax.dynamic_slice_in_dim(pending[0], jnp.clip(place, 0, N_TP - 1) * feat, feat, 1)

    wq, old, wkv = query_cols(core), old_rows(core), kv_rows(core)
    n_q, n_old = wq.shape[0], old.shape[0]
    n_both = n_q + n_old

    gain = lax.dynamic_slice_in_dim(norm_gain, z * feat, feat, 0).astype(jnp.float32)
    scaled = (wide * gain[None, :]).astype(jnp.bfloat16)

    every = (0, 1, 2)
    u1, d1 = hop_up(scaled, every), hop_down(scaled, every)
    x1 = swap(jnp.concatenate([wq, old, piece(chip ^ 1)], axis=0), 2)
    y1 = swap(jnp.concatenate([wq, old, piece(chip ^ 2)], axis=0), 4)
    given = swap(
        jnp.concatenate([query_cols(1 - core), old_rows(1 - core), kv_rows(1 - core)], axis=0), 1
    )
    end1 = none_of(u1, d1, x1, y1, given)

    u2 = hop_up(after(jnp.where(z == 0, share(z + 3), u1), end1), every)
    d2 = hop_down(after(jnp.where(z == 3, share(z - 3), d1), end1), every)
    far = piece(chip ^ 3)
    n_far = far.shape[0] // 2
    x2 = swap(after(jnp.concatenate([given[:n_both], far[:n_far]], axis=0), end1), 2)
    y2 = swap(after(jnp.concatenate([given[:n_both], far[n_far:]], axis=0), end1), 4)
    near = jnp.where(z < 2, d1, u1)
    over1 = swap(after(jnp.concatenate([scaled, near], axis=0), end1), 1)
    end2 = none_of(u2, d2, x2, y2, over1)

    u3 = hop_up(
        after(jnp.where(z == 2, u2, share(z + 2) + jnp.where(z == 1, u2, 0)), end2), every
    )
    d3 = hop_down(
        after(jnp.where(z == 1, d2, share(z - 2) + jnp.where(z == 2, d2, 0)), end2), every
    )
    far_own = swap(after(jnp.concatenate([x1[:n_both], x2[n_both:]], axis=0), end2), 4)
    far_other = swap(after(y2, end2), 2)
    second = jnp.where(z < 2, d2, u2)
    over2 = swap(after(second, end2), 1)
    end3 = none_of(u3, d3, far_own, far_other, over2)

    parts, places = line_parts(z, (u1, d1), (u2, d2), (u3, d3))
    ids = jnp.concatenate([jnp.stack([chip, core]), places]).astype(jnp.int32)
    third = parts[2]
    xs = [scaled, over1, near, over1, second, over2, third, swap(third, 1)]
    own_rows = (wq, given, x1, x2, y1, y2, far_own, far_other)
    old_parts = (old,) + tuple(rows[n_q:n_both] for rows in own_rows[1:])
    span = 2 * n_old
    kv = jnp.zeros((2, N_CTX * span, HD), jnp.bfloat16)
    for index, part in enumerate(old_parts):
        from_ctx = ((chip ^ (index // 2)) * 2 + (core ^ (index % 2))) * span
        cut = [part[:, i * HD : (i + 1) * HD] for i in range(4)]
        part = jnp.stack(
            [jnp.concatenate(cut[:2], axis=0), jnp.concatenate(cut[2:], axis=0)], axis=0
        )
        kv = lax.dynamic_update_slice(kv, part, (0, from_ctx, 0))

    by_chip = jnp.stack(
        [
            piece(chip),
            x1[n_both:],
            y1[n_both:],
            jnp.concatenate([far_own[n_both:], far_other[n_both:]], axis=0),
        ]
    )

    def of_chip(q):
        return lax.dynamic_index_in_dim(by_chip, q ^ chip, 0, keepdims=False)

    swapped = none_of(xs[7]) + end3
    pieces = [of_chip(z)]
    for r in (1, 2, 3):
        pieces.append(
            lax.ppermute(after(of_chip(z ^ r), swapped), "tp", [(i, i ^ r) for i in range(N_TP)])
        )
    cores = [[2 * k + j for k in range(4)] for j in range(2)]
    wkv_all = lax.all_gather(
        after(jnp.concatenate([wkv, given[n_both:]], axis=0), end3),
        "ctx",
        axis_index_groups=cores,
    )
    n_kv = wkv.shape[0]
    wkv_parts = []
    for m in range(4):
        block = lax.dynamic_index_in_dim(wkv_all, chip ^ m, 0, keepdims=False)
        for rows in (block[:n_kv], block[n_kv:]):
            cut = rows.shape[1] // 2
            wkv_parts.append(jnp.concatenate([rows[:, :cut], rows[:, cut:]], axis=0))

    token_index = chip * chip_tok + jnp.arange(chip_tok, dtype=jnp.int32)
    positions = stretch_offset[0].astype(jnp.float32) + token_index.astype(jnp.float32)
    angles = positions[:, None] * inverse_freqs(HD)
    cosine, sinus = jnp.cos(angles), jnp.sin(angles)
    cosine = jnp.concatenate([cosine, cosine], axis=1)
    sinus = jnp.concatenate([-sinus, sinus], axis=1)

    scale = math.log2(math.e) / math.sqrt(HD)
    q = project(ids, xs, own_rows, factor, cosine, sinus, q_heads, q_heads, scale)
    part_a = attend_prefix(bounds, q, 0, n_wide, kv)
    end4 = none_of(part_a[0], *pieces[1:])
    kv_new = project(ids, xs, wkv_parts, factor + end4, cosine, sinus, 2, 1, 1.0)
    made = none_of(kv_new)
    before = lax.ppermute(kv_new[:, tok:], "ctx", [(i, i + 2) for i in range(N_CTX - 2)])
    haloed = none_of(before)

    u4 = hop_up(after(share(z + 1) + jnp.where(z == 0, 0, u3), made), every)
    d4 = hop_down(after(share(z - 1) + jnp.where(z == 3, 0, d3), made), every)
    n_piece = pieces[0].shape[0] // 2
    block = after(
        jnp.concatenate(
            [jnp.concatenate([p[:n_piece], p[n_piece:]], axis=1) for p in pieces], axis=0
        ),
        haloed,
    )
    half = block.shape[0] // 2
    wo_x, wo_y = swap(block, 2), swap(block, 4)
    part_b = attend_prefix(bounds + haloed.astype(jnp.int32), q, 1, n_wide, kv)
    k_near = jnp.concatenate([before[0], kv_new[0]], axis=0)
    v_near = jnp.concatenate([before[1], kv_new[1]], axis=0)
    attended = attend_new(q, lo_wide, k_near, v_near, part_a + part_b)

    attended = after(attended, none_of(u4, d4))
    u1, d1 = hop_up(attended, every), hop_down(attended, every)
    end6 = none_of(u1, d1, wo_x, wo_y)
    u2, d2 = hop_up(after(u1, end6), (1, 2)), hop_down(after(d1, end6), (1, 2))
    wo_parts = (
        block,
        wo_x,
        wo_y,
        swap(after(wo_x[:half], end6), 4),
        swap(after(wo_y[half:], end6), 2),
    )
    u3, d3 = hop_up(u2, (2,)), hop_down(d2, (2,))
    heads_parts, _ = line_parts(z, (u1, d1), (u2, d2), (u3, d3))
    hs = []
    for part in (attended,) + heads_parts:
        hs += [part, swap(part, 1)]
    projected = out_project(ids, hs, wo_parts)
    mine = lax.dynamic_slice_in_dim(projected, core * tok, tok, 0)
    theirs = swap(lax.dynamic_slice_in_dim(projected, (1 - core) * tok, tok, 0), 1)
    head_share = jnp.where(
        first,
        jnp.concatenate([mine, theirs], axis=1),
        jnp.concatenate([theirs, mine], axis=1),
    ).astype(jnp.float32)
    pending_share = (
        share(z).astype(jnp.float32)
        + jnp.where(z == 0, 0, u4).astype(jnp.float32)
        + jnp.where(z == 3, 0, d4).astype(jnp.float32)
    )
    return (wide + (head_share + pending_share)).astype(jnp.bfloat16)


def solution(mesh):
    in_specs = (
        P("ctx", "tp"),
        P("tp", "ctx", None),
        P(),
        P("ctx", "tp"),
        P("ctx", None),
        P("ctx", None),
        P("tp", "ctx"),
        P(None, "ctx", None),
        P(None, "ctx", None),
        P("ctx"),
        P("ctx"),
        P(),
    )
    out_specs = P("ctx", "tp")
    small = mesh.shape["ctx"] == N_CTX and mesh.shape["tp"] == N_TP
    return jax.shard_map(
        per_device if small else per_device_any,
        mesh=mesh,
        in_specs=in_specs,
        out_specs=out_specs,
        check_vma=False,
    )
```

```python
import functools
import math

import jax
import jax.numpy as jnp
from jax import lax
from jax.experimental import pallas as pl
from jax.experimental.pallas import tpu as pltpu
from jax.sharding import PartitionSpec as P

HQ = 32
KVH = 8
HD = 128
NTRAJ = 16


ROPE_BASE = 500000.0
ROPE_FACTOR = 8.0
LOW_FREQ = 1.0
HIGH_FREQ = 4.0
INITIAL_SPAN = 8192.0
NORM_EPSILON = 1e-05
MASKED = -1e30


def inverse_freqs(head_width):
    pair_index = jnp.arange(head_width // 2, dtype=jnp.float32)
    base_freq = ROPE_BASE ** (-2.0 * pair_index / head_width)
    wavelength = 2.0 * math.pi / base_freq
    smooth = (INITIAL_SPAN / wavelength - LOW_FREQ) / (HIGH_FREQ - LOW_FREQ)
    blended = (1.0 - smooth) * base_freq / ROPE_FACTOR + smooth * base_freq
    return jnp.where(
        wavelength < INITIAL_SPAN / HIGH_FREQ,
        base_freq,
        jnp.where(wavelength > INITIAL_SPAN / LOW_FREQ, base_freq / ROPE_FACTOR, blended),
    )


def rotate(vectors, positions):
    head_width = vectors.shape[-1]
    angles = positions[..., None] * inverse_freqs(head_width)
    cosine = jnp.cos(angles)
    sinus = jnp.sin(angles)
    first_half = vectors[..., : head_width // 2]
    second_half = vectors[..., head_width // 2 :]
    return jnp.concatenate(
        [first_half * cosine - second_half * sinus, second_half * cosine + first_half * sinus],
        axis=-1,
    )


def visibility(key_labels, is_prefix, key_pos, query_segs, query_index):
    earlier = key_labels[None, :] <= query_segs[:, None]
    same = (key_labels[None, :] == query_segs[:, None]) & (key_pos[None, :] <= query_index[:, None])
    return jnp.where(is_prefix[None, :], earlier, same)


def attend_whole(grouped, key_block, value_block, seen):
    scores = jnp.einsum("hrd,hnd->hrn", grouped, key_block, preferred_element_type=jnp.float32) * (
        1.0 / math.sqrt(HD)
    )
    scores = jnp.where(seen[None], scores, MASKED)
    new_max = jnp.max(scores, axis=2)
    weights = jnp.where(seen[None], jnp.exp(scores - new_max[..., None]), 0.0)
    totals = jnp.sum(weights, axis=2)
    numerator = jnp.einsum(
        "hrn,hnd->hrd",
        weights.astype(jnp.bfloat16),
        value_block,
        preferred_element_type=jnp.float32,
    )
    return numerator / totals[..., None]


def per_device_any(
    stream,
    pending,
    norm_gain,
    w_query,
    w_key,
    w_value,
    w_out,
    prefix_keys,
    prefix_values,
    prefix_segments,
    stretch_segments,
    stretch_offset,
):
    tok_rows = stream.shape[0]
    prefix_rows = prefix_keys.shape[1]
    ctx_index = lax.axis_index("ctx")
    tp_index = lax.axis_index("tp")
    gain_wide = norm_gain.astype(jnp.float32)
    whole = lax.all_gather(stream, "tp", axis=1, tiled=True).astype(jnp.float32)
    mean_square = jnp.mean(whole * whole, axis=1, keepdims=True)
    normed = (whole * lax.rsqrt(mean_square + NORM_EPSILON) * gain_wide).astype(jnp.bfloat16)
    q_cols = w_query.shape[1]
    q_heads = q_cols // HD
    full_group = HQ // KVH
    kv_heads = max(1, q_heads // full_group)
    group_size = q_heads // kv_heads
    head_start = tp_index * q_heads // full_group
    kv_cols = kv_heads * HD
    key_slice = lax.dynamic_slice_in_dim(w_key, head_start * HD, kv_cols, 1)
    value_slice = lax.dynamic_slice_in_dim(w_value, head_start * HD, kv_cols, 1)
    pieces = (
        lax.all_gather(w_query, "ctx", axis=0, tiled=True),
        lax.all_gather(key_slice, "ctx", axis=0, tiled=True),
        lax.all_gather(value_slice, "ctx", axis=0, tiled=True),
    )
    query_raw, key_full, value_full = tuple(
        (jnp.dot(normed, piece_rows, preferred_element_type=jnp.float32) for piece_rows in pieces)
    )
    token_index = ctx_index * tok_rows + jnp.arange(tok_rows, dtype=jnp.int32)
    positions = stretch_offset[0].astype(jnp.float32) + token_index.astype(jnp.float32)
    query_rows = rotate(query_raw.reshape(tok_rows, q_heads, HD), positions[:, None]).astype(
        jnp.bfloat16
    )
    new_keys = jnp.transpose(
        rotate(key_full.reshape(tok_rows, kv_heads, HD), positions[:, None]).astype(jnp.bfloat16),
        (1, 0, 2),
    )
    new_values = jnp.transpose(
        value_full.astype(jnp.bfloat16).reshape(tok_rows, kv_heads, HD), (1, 0, 2)
    )
    old_keys = lax.dynamic_slice_in_dim(prefix_keys, head_start, kv_heads, 0)
    old_values = lax.dynamic_slice_in_dim(prefix_values, head_start, kv_heads, 0)
    local_keys = jnp.concatenate([old_keys, new_keys], 1)
    local_values = jnp.concatenate([old_values, new_values], 1)
    key_labels = jnp.concatenate([prefix_segments, stretch_segments])
    key_span = prefix_rows + tok_rows
    grouped = jnp.transpose(
        query_rows.reshape(tok_rows, kv_heads, group_size, HD), (1, 0, 2, 3)
    ).reshape(kv_heads, tok_rows * group_size, HD)
    query_index = jnp.repeat(token_index, group_size)
    query_segs = jnp.repeat(stretch_segments, group_size)
    both = jnp.stack([local_keys, local_values])
    kv_block = lax.all_gather(both, "ctx", axis=2, tiled=True)
    label_block = lax.all_gather(key_labels[None, None, :], "ctx", axis=2, tiled=True)
    key_count = kv_block.shape[2]
    absolute = jnp.arange(key_count, dtype=jnp.int32)
    within = absolute % key_span
    key_pos = absolute // key_span * tok_rows + within - prefix_rows
    seen = visibility(label_block[0, 0], within < prefix_rows, key_pos, query_segs, query_index)
    attended_heads = attend_whole(grouped, kv_block[0], kv_block[1], seen).astype(jnp.bfloat16)
    attended = jnp.transpose(
        attended_heads.reshape(kv_heads, tok_rows, group_size, HD), (1, 0, 2, 3)
    ).reshape(tok_rows, q_cols)
    head_terms = jnp.dot(
        attended,
        lax.all_gather(w_out, "ctx", axis=1, tiled=True),
        preferred_element_type=jnp.float32,
    )
    head_share, pending_share = (
        lax.psum_scatter(
            head_terms.astype(jnp.bfloat16), "tp", scatter_dimension=1, tiled=True
        ).astype(jnp.float32),
        lax.psum_scatter(
            pending[0].astype(jnp.float32).astype(jnp.bfloat16),
            "tp",
            scatter_dimension=1,
            tiled=True,
        ).astype(jnp.float32),
    )
    block_share = head_share + pending_share
    return (stream.astype(jnp.float32) + block_share).astype(jnp.bfloat16)


N_CTX = 8
N_TP = 4
MIB = 1024 * 1024


def swap(x, bit):
    return lax.ppermute(x, "ctx", [(c, c ^ bit) for c in range(N_CTX)])


def hop_up(v, pairs):
    return lax.ppermute(v, "tp", [(i, i + 1) for i in pairs])


def hop_down(v, pairs):
    return lax.ppermute(v, "tp", [(N_TP - 1 - i, N_TP - 2 - i) for i in pairs])


def rotated(v, cosine, sinus):
    return v * cosine + pltpu.roll(v, HD // 2, 1) * sinus


HBM = pl.BlockSpec(memory_space=pltpu.HBM)
VMEM = pl.BlockSpec(memory_space=pltpu.VMEM)
SMEM = pl.BlockSpec(memory_space=pltpu.SMEM)
ANY = pl.BlockSpec(memory_space=pl.ANY)
LITTLE = pl.CostEstimate(flops=0, bytes_accessed=1024, transcendentals=0)


def specs_of(arrays):
    return [HBM if a.size > 200000 else ANY for a in arrays]


def move(plan, shapes, ids, sources, arrived=()):
    count = len(sources)

    def kernel(ids_ref, *refs):
        outs, sems = refs[count + len(arrived) : -1], refs[-1]
        waits = []
        for at, (choices, dst) in enumerate(plan(ids_ref, refs[:count], outs)):
            for cond, src in choices:
                copy = pltpu.make_async_copy(src, dst, sems.at[at])
                if cond is None:
                    copy.start()
                else:
                    pl.when(cond)(copy.start)
            waits.append(copy)
        for copy in waits:
            copy.wait()

    return pl.pallas_call(
        kernel,
        out_shape=tuple(jax.ShapeDtypeStruct(shape, jnp.bfloat16) for shape in shapes),
        in_specs=[SMEM] + [HBM] * count + specs_of(arrived),
        out_specs=tuple(VMEM for _ in shapes),
        scratch_shapes=[pltpu.SemaphoreType.DMA((40,))],
        compiler_params=pltpu.CompilerParams(vmem_limit_bytes=40 * MIB),
        cost_estimate=LITTLE,
        name=plan.__name__,
    )(ids, *sources, *arrived)


def gate(x, *arrived):
    return pl.pallas_call(
        lambda *refs: None,
        out_shape=jax.ShapeDtypeStruct(x.shape, x.dtype),
        in_specs=[HBM] + specs_of(arrived),
        out_specs=HBM,
        input_output_aliases={0: 0},
        compiler_params=pltpu.CompilerParams(vmem_limit_bytes=40 * MIB),
        cost_estimate=LITTLE,
        name="gate",
    )(x, *arrived)


def pick(z, options, ids, arrived=()):
    distinct = list({id(o): o for o in options}.values())

    def pick_plan(at, src, out):
        yield (
            [(at[2] == i, src[[o is d for d in distinct].index(True)]) for i, o in enumerate(options)],
            out[0],
        )

    return move(pick_plan, (options[0].shape,), ids, distinct, arrived)[0]


def hops(ids, pending, up, down, offset, relay, both, arrived=()):
    tok, feat = up.shape

    def kernel(ids_ref, pending_ref, up_ref, down_ref, *refs):
        out_up, out_down, buf, sems = refs[len(arrived) :]
        z = ids_ref[2]
        todo = []
        for i, (src, out, step, at) in enumerate(
            ((up_ref, out_up, offset, z), (down_ref, out_down, -offset, N_TP - 1 - z))
        ):
            is_relay = functools.reduce(jnp.logical_or, [at == p for p in relay], at < 0)
            is_both = functools.reduce(jnp.logical_or, [at == p for p in both], at < 0)
            place = jnp.clip(z + step, 0, N_TP - 1)
            share = pltpu.make_async_copy(
                pending_ref.at[0, :, pl.ds(multiple(place, feat), feat)], out, sems.at[i]
            )
            passed = pltpu.make_async_copy(src, out, sems.at[i])
            added = pltpu.make_async_copy(src, buf.at[i], sems.at[2 + i])
            pl.when(is_relay)(passed.start)
            pl.when(jnp.logical_not(is_relay))(share.start)
            pl.when(is_both)(added.start)
            todo.append((passed, added, is_both, out, i))
        for passed, added, is_both, out, i in todo:
            passed.wait()

            @pl.when(is_both)
            def _():
                added.wait()
                out[...] += buf[i]

    shape = jax.ShapeDtypeStruct((tok, feat), jnp.bfloat16)
    return pl.pallas_call(
        kernel,
        out_shape=(shape, shape),
        in_specs=[SMEM, HBM, HBM, HBM] + specs_of(arrived),
        out_specs=(VMEM, VMEM),
        scratch_shapes=[
            pltpu.VMEM((2, tok, feat), jnp.bfloat16),
            pltpu.SemaphoreType.DMA((4,)),
        ],
        compiler_params=pltpu.CompilerParams(vmem_limit_bytes=40 * MIB),
        cost_estimate=LITTLE,
        name="hops",
    )(ids, pending, up, down, *arrived)


def one(src, dst):
    return ([(None, src)], dst)


def multiple(value, of=128):
    return pl.multiple_of(value * of, of)


def project_kernel(heads, rot_heads, scale, skip, ids_ref, *refs):
    xs, count = refs[:8], len(refs) - 16 - skip
    ws = refs[8 : 8 + count]
    factor_ref, cos_ref, sin_ref, out_ref, x_buf, w_buf, x_sem, w_sem = refs[8 + count + skip :]
    chip, core = ids_ref[0], ids_ref[1]
    tok, half, cols = xs[0].shape[0], x_buf.shape[-1], w_buf.shape[-1]
    mine = pl.multiple_of(core * tok, 128)
    theirs = pl.multiple_of((1 - core) * tok, 128)
    waits = []
    for r in range(4):
        place = ids_ref[3 + r]
        for h in range(2):
            at = 2 * r + h
            waits.append([])
            if count == 8:
                for m in range(4):
                    src = ws[2 * m + h]
                    if src.shape[1] > cols:
                        src = src.at[:, pl.ds(multiple(core, cols), cols)]
                    else:
                        src = src.at[pl.ds(0, half)]
                    copy = pltpu.make_async_copy(src, w_buf.at[at], w_sem.at[2 * at])
                    pl.when((place ^ chip) == m)(copy.start)
                waits[at].append(copy)
            else:
                fold = half // 2
                for f in range(2):
                    src = ws[0].at[place, pl.ds(h * fold, fold), pl.ds(f * cols, cols)]
                    to = w_buf.at[at, pl.ds(f * fold, fold)]
                    copy = pltpu.make_async_copy(src, to, w_sem.at[2 * at + f])
                    copy.start()
                    waits[at].append(copy)
            features = pl.ds(pl.multiple_of((core ^ h) * half, 128), half)
            for s, rows in ((0, mine), (1, theirs)):
                copy = pltpu.make_async_copy(
                    xs[2 * r + s].at[:, features],
                    x_buf.at[at, pl.ds(rows, tok)],
                    x_sem.at[2 * at + s],
                )
                copy.start()
                waits[at].append(copy)
    acc = 0.0
    for at in range(8):
        for copy in waits[at]:
            copy.wait()
        acc = acc + jnp.dot(x_buf[at], w_buf[at], preferred_element_type=jnp.float32)
    factor = factor_ref[...]
    for h in range(heads):
        v = acc[:, h * HD : (h + 1) * HD] * factor
        if h < rot_heads:
            v = rotated(v, cos_ref[...], sin_ref[...]) * scale
        out_ref[h] = v.astype(jnp.bfloat16)


def project(ids, xs, weights, factor, cosine, sinus, heads, rot_heads, scale, arrived=()):
    tok, feat = xs[0].shape
    cols = heads * HD
    half = feat // 2
    return pl.pallas_call(
        functools.partial(project_kernel, heads, rot_heads, scale, len(arrived)),
        out_shape=jax.ShapeDtypeStruct((heads, 2 * tok, HD), jnp.bfloat16),
        in_specs=[SMEM] + [HBM] * (8 + len(weights)) + specs_of(arrived) + [VMEM] * 3,
        out_specs=VMEM,
        scratch_shapes=[
            pltpu.VMEM((8, 2 * tok, half), jnp.bfloat16),
            pltpu.VMEM((8, half, cols), jnp.bfloat16),
            pltpu.SemaphoreType.DMA((16,)),
            pltpu.SemaphoreType.DMA((16,)),
        ],
        compiler_params=pltpu.CompilerParams(vmem_limit_bytes=48 * MIB),
        cost_estimate=LITTLE,
        name="project",
    )(ids, *xs, *weights, *arrived, factor, cosine, sinus)


BT = 256
BK = 512
UNROLL = 2
CHAIN = 2


def scores(q, k):
    return lax.dot_general(q, k, (((1,), (1,)), ((), ())), preferred_element_type=jnp.float32)


def absorb(s, v_ext, m, acc):
    new = jnp.maximum(m, jnp.max(s, axis=1, keepdims=True))
    p = jnp.exp2(s - new).astype(jnp.bfloat16)
    acc = acc * jnp.exp2(m - new) + jnp.dot(p, v_ext, preferred_element_type=jnp.float32)
    return new, acc


def prefix_kernel(bound_ref, q_ref, n_ref, kv_ref, *refs):
    m_out, acc_out, v_ext, s_ref, m_ref, acc_ref = refs[-6:]
    b = pl.program_id(0)
    heads, bt = q_ref.shape[0], q_ref.shape[1]
    rows, chains = CHAIN * bt, heads // CHAIN
    big = UNROLL * BK
    last = kv_ref.shape[1] // big - 1

    @pl.when(b == 0)
    def _():
        v_ext[:, :HD] = kv_ref[1]
        v_ext[:, HD:] = jnp.ones_like(kv_ref[1])

    m_ref[...] = jnp.full_like(m_ref, MASKED)
    acc_ref[...] = jnp.zeros_like(acc_ref)
    n_rows = jnp.concatenate([n_ref[:, :1]] * CHAIN, axis=0)

    def query(g):
        return q_ref[g * CHAIN : (g + 1) * CHAIN].reshape(rows, HD)

    s_ref[...] = scores(query(0), kv_ref[0, :BK, :])
    items = [(u, g) for u in range(UNROLL) for g in range(chains)]

    def body(kb, masked):
        start = pl.multiple_of(kb * big, big)
        follow = pl.multiple_of(jnp.minimum(kb + 1, last) * big, big)
        ms = [m_ref[g][:, :1] for g in range(chains)]
        accs = [acc_ref[g] for g in range(chains)]
        s = s_ref[...]
        for t, (u, g) in enumerate(items):
            if t + 1 < len(items):
                at, who = start + items[t + 1][0] * BK, items[t + 1][1]
            else:
                at, who = follow, 0
            ahead = scores(query(who), kv_ref[0, pl.ds(at, BK), :])
            if masked:
                col = lax.broadcasted_iota(jnp.int32, s.shape, 1) + (start + u * BK)
                s = jnp.where(col < n_rows, s, MASKED)
            v = v_ext[pl.ds(start + u * BK, BK), :]
            ms[g], accs[g] = absorb(s, v, ms[g], accs[g])
            s = ahead
        s_ref[...] = s
        for g in range(chains):
            m_ref[g] = jnp.broadcast_to(ms[g], (rows, 128))
            acc_ref[g] = accs[g]

    full = bound_ref[0, b] // big
    some = (bound_ref[1, b] + big - 1) // big
    lax.fori_loop(0, full, lambda kb, c: (body(kb, False), c)[1], 0)
    lax.fori_loop(full, some, lambda kb, c: (body(kb, True), c)[1], 0)
    m_out[0] = m_ref[...]
    acc_out[0] = acc_ref[...]


def attend_prefix(bounds, q, group, n_tok, kv, arrived=()):
    heads, tokens = CHAIN, q.shape[1]
    blocks = tokens // BT
    chains, rows = heads // CHAIN, CHAIN * BT
    keys = kv.shape[1]
    return pl.pallas_call(
        prefix_kernel,
        out_shape=(
            jax.ShapeDtypeStruct((blocks, chains, rows, 128), jnp.float32),
            jax.ShapeDtypeStruct((blocks, chains, rows, 2 * HD), jnp.float32),
        ),
        grid_spec=pltpu.PrefetchScalarGridSpec(
            num_scalar_prefetch=1,
            grid=(blocks,),
            in_specs=[
                pl.BlockSpec((heads, BT, HD), lambda b, *_: (group, b, 0)),
                pl.BlockSpec((BT, 128), lambda b, *_: (b, 0)),
                pl.BlockSpec((2, keys, HD), lambda b, *_: (0, 0, 0)),
            ]
            + specs_of(arrived),
            out_specs=(
                pl.BlockSpec((1, chains, rows, 128), lambda b, *_: (b, 0, 0, 0)),
                pl.BlockSpec((1, chains, rows, 2 * HD), lambda b, *_: (b, 0, 0, 0)),
            ),
            scratch_shapes=[
                pltpu.VMEM((keys, 2 * HD), jnp.bfloat16),
                pltpu.VMEM((rows, BK), jnp.float32),
                pltpu.VMEM((chains, rows, 128), jnp.float32),
                pltpu.VMEM((chains, rows, 2 * HD), jnp.float32),
            ],
        ),
        compiler_params=pltpu.CompilerParams(vmem_limit_bytes=40 * MIB),
        cost_estimate=LITTLE,
        name="attend_prefix",
    )(bounds, q, n_tok, kv, *arrived)


def new_kernel(halo, q_ref, lo_ref, k_ref, v_ref, *refs):
    states, out_ref = refs[:-1], refs[-1]
    b = pl.program_id(0)
    heads, bt = q_ref.shape[0], q_ref.shape[1]
    rows = CHAIN * bt
    span = halo + bt
    start = pl.multiple_of(b * bt, bt)
    k = k_ref[pl.ds(start, span), :]
    v = v_ref[pl.ds(start, span), :]
    v_ext = jnp.concatenate([v, jnp.ones_like(v)], axis=1)
    lo = jnp.concatenate([lo_ref[:, :1]] * CHAIN, axis=0)

    def hide(s):
        col = lax.broadcasted_iota(jnp.int32, s.shape, 1)
        row = lax.broadcasted_iota(jnp.int32, s.shape, 0) % bt
        return jnp.where((col + start >= lo) & (col <= row + halo), s, MASKED)

    for g in range(heads // CHAIN):
        q = q_ref[g * CHAIN : (g + 1) * CHAIN].reshape(rows, HD)
        _, acc = absorb(
            hide(scores(q, k)), v_ext, states[2 * g][0, 0][:, :1], states[2 * g + 1][0, 0]
        )
        mixed = (acc[:, :HD] / acc[:, HD:]).astype(jnp.bfloat16)
        for h in range(CHAIN):
            at = (g * CHAIN + h) * HD
            out_ref[:, at : at + HD] = mixed[h * bt : (h + 1) * bt]


def attend_new(q, lo_tok, k, v, states):
    heads, tokens, _ = q.shape
    blocks = tokens // BT
    chains, rows = heads // CHAIN, CHAIN * BT
    halo = k.shape[0] - tokens
    whole = lambda b: (0, 0)
    return pl.pallas_call(
        functools.partial(new_kernel, halo),
        out_shape=jax.ShapeDtypeStruct((tokens, heads * HD), jnp.bfloat16),
        grid=(blocks,),
        in_specs=[
            pl.BlockSpec((heads, BT, HD), lambda b: (0, b, 0)),
            pl.BlockSpec((BT, 128), lambda b: (b, 0)),
            pl.BlockSpec(k.shape, whole),
            pl.BlockSpec(v.shape, whole),
        ]
        + [
            pl.BlockSpec((1, 1, rows, 128), lambda b: (b, 0, 0, 0)),
            pl.BlockSpec((1, 1, rows, 2 * HD), lambda b: (b, 0, 0, 0)),
        ]
        * chains,
        out_specs=pl.BlockSpec((BT, heads * HD), lambda b: (b, 0)),
        compiler_params=pltpu.CompilerParams(vmem_limit_bytes=40 * MIB),
        cost_estimate=LITTLE,
        name="attend_new",
    )(q, lo_tok, k, v, *states)


def out_kernel(ids_ref, *refs):
    xs, ws = refs[:8], refs[8:13]
    out_ref, x_buf, w_buf, x_sem, w_sem = refs[13:]
    chip, core, z = ids_ref[0], ids_ref[1], ids_ref[2]
    width = xs[0].shape[1]
    rows = w_buf.shape[1] // 4
    top = ws[3].shape[0]
    for r in range(4):
        near = ids_ref[3 + r] ^ z
        for m in range(4):
            to = w_buf.at[r, pl.ds(pl.multiple_of((chip ^ m) * rows, 128), rows)]
            sem = w_sem.at[4 * r + m]
            if m < 3:
                src = ws[m].at[pl.ds(pl.multiple_of(near * rows, 128), rows)]
                pltpu.make_async_copy(src, to, sem).start()
            else:

                @pl.when(near < 2)
                def _():
                    src = ws[3].at[pl.ds(pl.multiple_of(near * rows, 128), rows)]
                    pltpu.make_async_copy(src, to, sem).start()

                @pl.when(near >= 2)
                def _():
                    src = ws[4].at[pl.ds(pl.multiple_of(near * rows - top, 128), rows)]
                    pltpu.make_async_copy(src, to, sem).start()

        for s in range(2):
            at = pl.multiple_of((core ^ s) * width, 128)
            pltpu.make_async_copy(
                xs[2 * r + s], x_buf.at[r, :, pl.ds(at, width)], x_sem.at[2 * r + s]
            ).start()
    acc = None
    for r in range(4):
        for m in range(4):
            pltpu.make_async_copy(
                ws[0].at[pl.ds(0, rows)], w_buf.at[r, pl.ds(0, rows)], w_sem.at[4 * r + m]
            ).wait()
        for s in range(2):
            pltpu.make_async_copy(
                xs[0], x_buf.at[r, :, pl.ds(0, width)], x_sem.at[2 * r + s]
            ).wait()
        term = jnp.dot(x_buf[r], w_buf[r], preferred_element_type=jnp.float32)
        acc = term if acc is None else acc + term
    out_ref[...] = acc.astype(jnp.bfloat16)


def out_project(ids, xs, ws):
    tokens, width = xs[0].shape
    depth, cols = ws[0].shape
    return pl.pallas_call(
        out_kernel,
        out_shape=jax.ShapeDtypeStruct((tokens, cols), jnp.bfloat16),
        in_specs=[SMEM] + [HBM] * 13,
        out_specs=VMEM,
        scratch_shapes=[
            pltpu.VMEM((4, tokens, 2 * width), jnp.bfloat16),
            pltpu.VMEM((4, depth, cols), jnp.bfloat16),
            pltpu.SemaphoreType.DMA((8,)),
            pltpu.SemaphoreType.DMA((16,)),
        ],
        compiler_params=pltpu.CompilerParams(vmem_limit_bytes=40 * MIB),
        cost_estimate=LITTLE,
        name="out_project",
    )(ids, *xs, *ws)


def per_device(
    stream,
    pending,
    norm_gain,
    w_query,
    w_key,
    w_value,
    w_out,
    prefix_keys,
    prefix_values,
    prefix_segments,
    stretch_segments,
    stretch_offset,
):
    tok, feat = stream.shape
    chip_tok = 2 * tok
    c = lax.axis_index("ctx")
    z = lax.axis_index("tp")
    chip, core = c // 2, c % 2
    first = core == 0
    depth = feat * N_TP

    wide = stream.astype(jnp.float32)
    here = jnp.stack([chip, core, z]).astype(jnp.int32)
    every = (0, 1, 2)

    gain = lax.dynamic_slice_in_dim(norm_gain, z * feat, feat, 0).astype(jnp.float32)
    scaled = (wide * gain[None, :]).astype(jnp.bfloat16)
    u1, d1 = hop_up(scaled, every), hop_down(scaled, every)

    labels = jnp.arange(NTRAJ, dtype=jnp.int32)
    counts = jnp.stack(
        [
            jnp.sum((prefix_segments[:, None] <= labels).astype(jnp.int32), axis=0),
            jnp.sum((stretch_segments[:, None] < labels).astype(jnp.int32), axis=0),
        ]
    )
    other_segs = swap(stretch_segments, 1)
    for bit in (1, 2, 4):
        counts = counts + swap(counts, bit)
    segs = jnp.where(
        first,
        jnp.concatenate([stretch_segments, other_segs]),
        jnp.concatenate([other_segs, stretch_segments]),
    )
    onehot = (segs[:, None] == labels).astype(jnp.int32)
    n_tok = jnp.sum(onehot * counts[0], axis=1)
    lo_tok = jnp.sum(onehot * counts[1], axis=1) - chip * chip_tok + tok
    blocked = n_tok.reshape(chip_tok // BT, BT)
    bounds = jnp.stack([blocked[:, 0], blocked[:, -1]])
    n_wide = jnp.broadcast_to(n_tok[:, None], (chip_tok, 128))
    lo_wide = jnp.broadcast_to(lo_tok[:, None], (chip_tok, 128))

    token_index = chip * chip_tok + jnp.arange(chip_tok, dtype=jnp.int32)
    positions = stretch_offset[0].astype(jnp.float32) + token_index.astype(jnp.float32)
    angles = positions[:, None] * inverse_freqs(HD)
    cosine, sinus = jnp.cos(angles), jnp.sin(angles)
    cosine = jnp.concatenate([cosine, cosine], axis=1)
    sinus = jnp.concatenate([-sinus, sinus], axis=1)

    def squares(part, place):
        g = lax.dynamic_slice_in_dim(norm_gain, place * feat, feat, 0).astype(jnp.float32)
        return jnp.sum(jnp.square(part.astype(jnp.float32) / g[None, :]), axis=1, keepdims=True)

    q_heads = w_query.shape[1] // HD // 2
    q_cols = q_heads * HD
    n_q = w_query.shape[0]
    fold = prefix_keys.shape[1] // 2
    n_both = n_q + fold
    n_kv = w_key.shape[0] // 2
    n_piece = w_out.shape[0] // 4

    def first_plan(at, src, out):
        w_q, w_k, w_v, w_o, keys, values = src
        to_x, to_y, give, old_out, kv_out = out
        chip, core, z = at[0], at[1], at[2]

        def old_rows(j, dst, row):
            for i, a in enumerate((keys, keys, values, values)):
                part = a.at[2 * z + j, pl.ds((i % 2) * fold, fold)]
                yield one(part, dst.at[pl.ds(row, fold), pl.ds(i * HD, HD)])

        def kv_rows(j, dst, row):
            lanes = pl.ds(multiple(2 * z + j), HD)
            for i, a in enumerate((w_k, w_v, w_k, w_v)):
                part = a.at[pl.ds((i // 2) * n_kv, n_kv), lanes]
                yield one(part, dst.at[pl.ds(row, n_kv), pl.ds(i * HD, HD)])

        for dst, j in ((to_x, core), (to_y, core), (give, 1 - core)):
            cols = pl.ds(multiple(j, q_cols), q_cols)
            yield one(w_q.at[:, cols], dst.at[pl.ds(0, n_q)])
            yield from old_rows(j, dst, n_q)
        for dst, bit in ((to_x, 1), (to_y, 2)):
            rows = pl.ds(multiple(chip ^ bit, n_piece), n_piece)
            for i in range(2):
                part = w_o.at[rows, pl.ds(i * q_cols, q_cols)]
                yield one(part, dst.at[pl.ds(n_both + i * n_piece, n_piece)])
        yield from kv_rows(1 - core, give, n_both)
        yield from old_rows(core, old_out, 0)
        yield from kv_rows(core, kv_out, 0)

    bundle = (n_both + 2 * n_piece, q_cols)
    to_x, to_y, give, old, wkv = move(
        first_plan,
        (bundle, bundle, bundle, (fold, q_cols), (n_kv, q_cols)),
        here,
        (w_query, w_key, w_value, w_out, prefix_keys, prefix_values),
        (),
    )

    places = jnp.stack(
        [z, jnp.where(z < 2, z + 1, z - 1), jnp.where(z < 2, z + 2, z - 2), jnp.where(z % 2 == 1, 0, 3)]
    ).astype(jnp.int32)
    ids = jnp.concatenate([here, places])

    x1, y1, given = swap(to_x, 2), swap(to_y, 4), swap(give, 1)
    mine = squares(scaled, z)
    near = pick(z, (d1, d1, u1, u1), here, (cosine, sinus, n_wide, lo_wide, bounds, mine))
    over1 = swap(near, 1)

    up, down = hops(here, pending, u1, d1, 3, (1, 2, 3), (), (x1, y1, given, over1))
    u2, d2 = hop_up(up, every), hop_down(down, every)

    def second_plan(at, src, out):
        given_rows, w_o = src
        rows = pl.ds(multiple(at[0] ^ 3, n_piece), n_piece)
        for i, dst in enumerate(out[:2]):
            yield one(given_rows.at[pl.ds(0, n_both)], dst.at[pl.ds(0, n_both)])
            part = w_o.at[rows, pl.ds(i * q_cols, q_cols)]
            yield one(part, dst.at[pl.ds(n_both, n_piece)])

    short = (n_both + n_piece, q_cols)
    to_x, to_y = move(
        second_plan, (short, short), here, (given, w_out), (u1, d1, x1, y1, over1, up)
    )
    x2, y2, over0 = swap(to_x, 2), swap(to_y, 4), swap(scaled, 1)
    mine = mine + squares(near, places[1])
    theirs = squares(over1, places[1])
    second = pick(z, (d2, d2, u2, u2), here, (over0, mine, theirs))

    up, down = hops(here, pending, u2, d2, 2, (2,), (1,), (x2, y2, over0, second))
    u3, d3 = hop_up(up, every), hop_down(down, every)

    def third_plan(at, src, out):
        from_x1, from_x2, from_y2 = src
        yield one(from_x1.at[pl.ds(0, n_both)], out[0].at[pl.ds(0, n_both)])
        yield one(from_x2.at[pl.ds(n_both, n_piece)], out[0].at[pl.ds(n_both, n_piece)])
        yield one(from_y2, out[1])

    to_y, to_x = move(third_plan, (short, short), here, (x1, x2, y2), (u2, d2, over0, second, up))
    far_own, far_other = swap(to_y, 4), swap(to_x, 2)
    over2 = swap(second, 1)
    mine = mine + squares(second, places[2])
    theirs = theirs + squares(over0, z)
    third = pick(z, (d3, u1, d1, u3), here, (over2, mine, theirs))
    over3 = swap(third, 1)
    mine = mine + squares(third, places[3])
    theirs = theirs + squares(over2, places[2]) + squares(over3, places[3])
    total = jnp.where(first, jnp.concatenate([mine, theirs]), jnp.concatenate([theirs, mine]))
    factor = lax.rsqrt(total * (1.0 / depth) + NORM_EPSILON)
    factor = jnp.broadcast_to(factor, (chip_tok, 128))
    xs = [scaled, over0, near, over1, second, over2, third, over3]
    own_rows = (w_query, given, x1, x2, y1, y2, far_own, far_other)

    def prefix_plan(at, src, out):
        for m in range(4):
            for j in range(2):
                start = ((at[0] ^ m) * 2 + (at[1] ^ j)) * 2 * fold
                rows = src[2 * m + j]
                row = 0 if rows.shape[0] == fold else n_q
                for i in range(4):
                    dst = out[0].at[i // 2, pl.ds(pl.multiple_of(start + (i % 2) * fold, 128), fold)]
                    yield one(rows.at[pl.ds(row, fold), pl.ds(i * HD, HD)], dst)

    (kv,) = move(prefix_plan, ((2, N_CTX * 2 * fold, HD),), here, (old,) + own_rows[1:])

    def kv_plan(at, src, out):
        yield one(src[0], out[0].at[pl.ds(0, n_kv)])
        yield one(src[1].at[pl.ds(n_both, n_kv)], out[0].at[pl.ds(n_kv, n_kv)])

    (wkv,) = move(
        kv_plan, ((2 * n_kv, q_cols),), here, (wkv, given), (u3, d3, far_own, far_other, over2)
    )
    wkv_all = lax.all_gather(
        wkv, "ctx", axis_index_groups=[[2 * k + j for k in range(4)] for j in range(2)]
    )

    def pieces_plan(at, src, out):
        w_o, from_x, from_y, own_half, other_half = src
        chip, z = at[0], at[2]
        rows = pl.ds(multiple(chip, n_piece), n_piece)
        for r, dst in enumerate(out):
            near = (z ^ r) ^ chip
            for i in range(2):
                part = pl.ds(n_both + i * n_piece, n_piece)
                far = (own_half, other_half)[i].at[pl.ds(n_both, n_piece)]
                yield (
                    [
                        (near == 0, w_o.at[rows, pl.ds(i * q_cols, q_cols)]),
                        (near == 1, from_x.at[part]),
                        (near == 2, from_y.at[part]),
                        (near == 3, far),
                    ],
                    dst.at[pl.ds(i * n_piece, n_piece)],
                )

    pieces = list(
        move(
            pieces_plan,
            ((2 * n_piece, q_cols),) * 4,
            here,
            (w_out, x1, y1, far_own, far_other),
            (xs[7],),
        )
    )
    for r in (1, 2, 3):
        pieces[r] = lax.ppermute(pieces[r], "tp", [(i, i ^ r) for i in range(N_TP)])

    scale = math.log2(math.e) / math.sqrt(HD)
    q = project(ids, xs, own_rows, factor, cosine, sinus, q_heads, q_heads, scale)
    part_a = attend_prefix(bounds, q, 0, n_wide, kv)
    kv_new = project(
        ids, xs, (wkv_all,), factor, cosine, sinus, 2, 1, 1.0, (part_a[0],) + tuple(pieces[1:])
    )
    before = lax.ppermute(kv_new[:, tok:], "ctx", [(i, i + 2) for i in range(N_CTX - 2)])

    up, down = hops(here, pending, u3, d3, 1, (), (1, 2, 3), (kv_new,))
    u4, d4 = hop_up(up, every), hop_down(down, every)

    def block_plan(at, src, out):
        for r, part in enumerate(src):
            for i in range(2):
                dst = out[0].at[pl.ds(r * n_piece, n_piece), pl.ds(i * q_cols, q_cols)]
                yield one(part.at[pl.ds(i * n_piece, n_piece)], dst)

    (block,) = move(block_plan, ((4 * n_piece, 2 * q_cols),), here, pieces, (before,))
    half = block.shape[0] // 2
    wo_x, wo_y = swap(block, 2), swap(block, 4)
    part_b = attend_prefix(bounds, q, 1, n_wide, kv, (before,))
    k_near = jnp.concatenate([before[0], kv_new[0]], axis=0)
    v_near = jnp.concatenate([before[1], kv_new[1]], axis=0)
    attended = attend_new(q, lo_wide, k_near, v_near, part_a + part_b)

    attended = gate(attended, u4, d4)
    u1, d1 = hop_up(attended, every), hop_down(attended, every)
    near = pick(z, (d1, d1, u1, u1), here, (wo_x, wo_y))

    def far_plan(at, src, out):
        yield one(src[0].at[pl.ds(0, half)], out[0])
        yield one(src[1].at[pl.ds(half, half)], out[1])

    to_y, to_x = move(
        far_plan, ((half, block.shape[1]),) * 2, here, (wo_x, wo_y), (near,)
    )
    wo_parts = (block, wo_x, wo_y, swap(to_y, 4), swap(to_x, 2))
    u2, d2 = hop_up(gate(u1, near), (1, 2)), hop_down(gate(d1, near), (1, 2))
    second = pick(z, (d2, d2, u2, u2), here)
    u3, d3 = hop_up(u2, (2,)), hop_down(d2, (2,))
    third = pick(z, (d3, u1, d1, u3), here)
    hs = []
    for part in (attended, near, second, third):
        hs += [part, swap(part, 1)]
    projected = out_project(ids, hs, wo_parts)
    mine = lax.dynamic_slice_in_dim(projected, core * tok, tok, 0)
    theirs = swap(lax.dynamic_slice_in_dim(projected, (1 - core) * tok, tok, 0), 1)
    head_share = jnp.where(
        first,
        jnp.concatenate([mine, theirs], axis=1),
        jnp.concatenate([theirs, mine], axis=1),
    ).astype(jnp.float32)
    pending_share = (
        lax.dynamic_slice_in_dim(pending[0], z * feat, feat, 1).astype(jnp.float32)
        + jnp.where(z == 0, 0, u4).astype(jnp.float32)
        + jnp.where(z == 3, 0, d4).astype(jnp.float32)
    )
    return (wide + (head_share + pending_share)).astype(jnp.bfloat16)


def solution(mesh):
    in_specs = (
        P("ctx", "tp"),
        P("tp", "ctx", None),
        P(),
        P("ctx", "tp"),
        P("ctx", None),
        P("ctx", None),
        P("tp", "ctx"),
        P(None, "ctx", None),
        P(None, "ctx", None),
        P("ctx"),
        P("ctx"),
        P(),
    )
    out_specs = P("ctx", "tp")
    small = mesh.shape["ctx"] == N_CTX and mesh.shape["tp"] == N_TP
    return jax.shard_map(
        per_device if small else per_device_any,
        mesh=mesh,
        in_specs=in_specs,
        out_specs=out_specs,
        check_vma=False,
    )
```

```python
import functools
import math

import jax
import jax.numpy as jnp
from jax import lax
from jax.experimental import pallas as pl
from jax.experimental.pallas import tpu as pltpu
from jax.sharding import PartitionSpec as P

HQ = 32
KVH = 8
HD = 128
NTRAJ = 16


ROPE_BASE = 500000.0
ROPE_FACTOR = 8.0
LOW_FREQ = 1.0
HIGH_FREQ = 4.0
INITIAL_SPAN = 8192.0
NORM_EPSILON = 1e-05
MASKED = -1e30


def inverse_freqs(head_width):
    pair_index = jnp.arange(head_width // 2, dtype=jnp.float32)
    base_freq = ROPE_BASE ** (-2.0 * pair_index / head_width)
    wavelength = 2.0 * math.pi / base_freq
    smooth = (INITIAL_SPAN / wavelength - LOW_FREQ) / (HIGH_FREQ - LOW_FREQ)
    blended = (1.0 - smooth) * base_freq / ROPE_FACTOR + smooth * base_freq
    return jnp.where(
        wavelength < INITIAL_SPAN / HIGH_FREQ,
        base_freq,
        jnp.where(wavelength > INITIAL_SPAN / LOW_FREQ, base_freq / ROPE_FACTOR, blended),
    )


def rotate(vectors, positions):
    head_width = vectors.shape[-1]
    angles = positions[..., None] * inverse_freqs(head_width)
    cosine = jnp.cos(angles)
    sinus = jnp.sin(angles)
    first_half = vectors[..., : head_width // 2]
    second_half = vectors[..., head_width // 2 :]
    return jnp.concatenate(
        [first_half * cosine - second_half * sinus, second_half * cosine + first_half * sinus],
        axis=-1,
    )


def visibility(key_labels, is_prefix, key_pos, query_segs, query_index):
    earlier = key_labels[None, :] <= query_segs[:, None]
    same = (key_labels[None, :] == query_segs[:, None]) & (key_pos[None, :] <= query_index[:, None])
    return jnp.where(is_prefix[None, :], earlier, same)


def attend_whole(grouped, key_block, value_block, seen):
    scores = jnp.einsum("hrd,hnd->hrn", grouped, key_block, preferred_element_type=jnp.float32) * (
        1.0 / math.sqrt(HD)
    )
    scores = jnp.where(seen[None], scores, MASKED)
    new_max = jnp.max(scores, axis=2)
    weights = jnp.where(seen[None], jnp.exp(scores - new_max[..., None]), 0.0)
    totals = jnp.sum(weights, axis=2)
    numerator = jnp.einsum(
        "hrn,hnd->hrd",
        weights.astype(jnp.bfloat16),
        value_block,
        preferred_element_type=jnp.float32,
    )
    return numerator / totals[..., None]


def per_device_any(
    stream,
    pending,
    norm_gain,
    w_query,
    w_key,
    w_value,
    w_out,
    prefix_keys,
    prefix_values,
    prefix_segments,
    stretch_segments,
    stretch_offset,
):
    tok_rows = stream.shape[0]
    prefix_rows = prefix_keys.shape[1]
    ctx_index = lax.axis_index("ctx")
    tp_index = lax.axis_index("tp")
    gain_wide = norm_gain.astype(jnp.float32)
    whole = lax.all_gather(stream, "tp", axis=1, tiled=True).astype(jnp.float32)
    mean_square = jnp.mean(whole * whole, axis=1, keepdims=True)
    normed = (whole * lax.rsqrt(mean_square + NORM_EPSILON) * gain_wide).astype(jnp.bfloat16)
    q_cols = w_query.shape[1]
    q_heads = q_cols // HD
    full_group = HQ // KVH
    kv_heads = max(1, q_heads // full_group)
    group_size = q_heads // kv_heads
    head_start = tp_index * q_heads // full_group
    kv_cols = kv_heads * HD
    key_slice = lax.dynamic_slice_in_dim(w_key, head_start * HD, kv_cols, 1)
    value_slice = lax.dynamic_slice_in_dim(w_value, head_start * HD, kv_cols, 1)
    pieces = (
        lax.all_gather(w_query, "ctx", axis=0, tiled=True),
        lax.all_gather(key_slice, "ctx", axis=0, tiled=True),
        lax.all_gather(value_slice, "ctx", axis=0, tiled=True),
    )
    query_raw, key_full, value_full = tuple(
        (jnp.dot(normed, piece_rows, preferred_element_type=jnp.float32) for piece_rows in pieces)
    )
    token_index = ctx_index * tok_rows + jnp.arange(tok_rows, dtype=jnp.int32)
    positions = stretch_offset[0].astype(jnp.float32) + token_index.astype(jnp.float32)
    query_rows = rotate(query_raw.reshape(tok_rows, q_heads, HD), positions[:, None]).astype(
        jnp.bfloat16
    )
    new_keys = jnp.transpose(
        rotate(key_full.reshape(tok_rows, kv_heads, HD), positions[:, None]).astype(jnp.bfloat16),
        (1, 0, 2),
    )
    new_values = jnp.transpose(
        value_full.astype(jnp.bfloat16).reshape(tok_rows, kv_heads, HD), (1, 0, 2)
    )
    old_keys = lax.dynamic_slice_in_dim(prefix_keys, head_start, kv_heads, 0)
    old_values = lax.dynamic_slice_in_dim(prefix_values, head_start, kv_heads, 0)
    local_keys = jnp.concatenate([old_keys, new_keys], 1)
    local_values = jnp.concatenate([old_values, new_values], 1)
    key_labels = jnp.concatenate([prefix_segments, stretch_segments])
    key_span = prefix_rows + tok_rows
    grouped = jnp.transpose(
        query_rows.reshape(tok_rows, kv_heads, group_size, HD), (1, 0, 2, 3)
    ).reshape(kv_heads, tok_rows * group_size, HD)
    query_index = jnp.repeat(token_index, group_size)
    query_segs = jnp.repeat(stretch_segments, group_size)
    both = jnp.stack([local_keys, local_values])
    kv_block = lax.all_gather(both, "ctx", axis=2, tiled=True)
    label_block = lax.all_gather(key_labels[None, None, :], "ctx", axis=2, tiled=True)
    key_count = kv_block.shape[2]
    absolute = jnp.arange(key_count, dtype=jnp.int32)
    within = absolute % key_span
    key_pos = absolute // key_span * tok_rows + within - prefix_rows
    seen = visibility(label_block[0, 0], within < prefix_rows, key_pos, query_segs, query_index)
    attended_heads = attend_whole(grouped, kv_block[0], kv_block[1], seen).astype(jnp.bfloat16)
    attended = jnp.transpose(
        attended_heads.reshape(kv_heads, tok_rows, group_size, HD), (1, 0, 2, 3)
    ).reshape(tok_rows, q_cols)
    head_terms = jnp.dot(
        attended,
        lax.all_gather(w_out, "ctx", axis=1, tiled=True),
        preferred_element_type=jnp.float32,
    )
    head_share, pending_share = (
        lax.psum_scatter(
            head_terms.astype(jnp.bfloat16), "tp", scatter_dimension=1, tiled=True
        ).astype(jnp.float32),
        lax.psum_scatter(
            pending[0].astype(jnp.float32).astype(jnp.bfloat16),
            "tp",
            scatter_dimension=1,
            tiled=True,
        ).astype(jnp.float32),
    )
    block_share = head_share + pending_share
    return (stream.astype(jnp.float32) + block_share).astype(jnp.bfloat16)


N_CTX = 8
N_TP = 4
GRANT = 60 * 1024 * 1024


def swap(x, bit):
    return lax.ppermute(x, "ctx", [(c, c ^ bit) for c in range(N_CTX)])


def hop_up(v, pairs):
    return lax.ppermute(v, "tp", [(i, i + 1) for i in pairs])


def hop_down(v, pairs):
    return lax.ppermute(v, "tp", [(N_TP - 1 - i, N_TP - 2 - i) for i in pairs])


def rotated(v, cosine, sinus):
    return v * cosine + pltpu.roll(v, HD // 2, 1) * sinus


HBM = pl.BlockSpec(memory_space=pltpu.HBM)
VMEM = pl.BlockSpec(memory_space=pltpu.VMEM)
SMEM = pl.BlockSpec(memory_space=pltpu.SMEM)
ANY = pl.BlockSpec(memory_space=pl.ANY)
LITTLE = pl.CostEstimate(flops=0, bytes_accessed=1024, transcendentals=0)


def specs_of(arrays):
    return [HBM if a.size > 200000 else ANY for a in arrays]


def move(plan, shapes, ids, sources, arrived=()):
    count = len(sources)

    def kernel(ids_ref, *refs):
        outs, sems = refs[count + len(arrived) : -1], refs[-1]
        waits = []
        for at, (choices, dst) in enumerate(plan(ids_ref, refs[:count], outs)):
            for cond, src in choices:
                copy = pltpu.make_async_copy(src, dst, sems.at[at])
                if cond is None:
                    copy.start()
                else:
                    pl.when(cond)(copy.start)
            waits.append(copy)
        for copy in waits:
            copy.wait()

    return pl.pallas_call(
        kernel,
        out_shape=tuple(jax.ShapeDtypeStruct(shape, jnp.bfloat16) for shape in shapes),
        in_specs=[SMEM] + [HBM] * count + specs_of(arrived),
        out_specs=tuple(VMEM for _ in shapes),
        scratch_shapes=[pltpu.SemaphoreType.DMA((40,))],
        compiler_params=pltpu.CompilerParams(vmem_limit_bytes=GRANT),
        cost_estimate=LITTLE,
        name=plan.__name__,
    )(ids, *sources, *arrived)


def gate(x, *arrived):
    return pl.pallas_call(
        lambda *refs: None,
        out_shape=jax.ShapeDtypeStruct(x.shape, x.dtype),
        in_specs=[HBM] + specs_of(arrived),
        out_specs=HBM,
        input_output_aliases={0: 0},
        compiler_params=pltpu.CompilerParams(vmem_limit_bytes=GRANT),
        cost_estimate=LITTLE,
        name="gate",
    )(x, *arrived)


def pick(z, options, ids, arrived=()):
    distinct = list({id(o): o for o in options}.values())

    def pick_plan(at, src, out):
        yield (
            [(at[2] == i, src[[o is d for d in distinct].index(True)]) for i, o in enumerate(options)],
            out[0],
        )

    return move(pick_plan, (options[0].shape,), ids, distinct, arrived)[0]


def hops(ids, pending, up, down, offset, relay, both, arrived=()):
    tok, feat = up.shape

    def kernel(ids_ref, pending_ref, up_ref, down_ref, *refs):
        out_up, out_down, buf, sems = refs[len(arrived) :]
        z = ids_ref[2]
        todo = []
        for i, (src, out, step, at) in enumerate(
            ((up_ref, out_up, offset, z), (down_ref, out_down, -offset, N_TP - 1 - z))
        ):
            is_relay = functools.reduce(jnp.logical_or, [at == p for p in relay], at < 0)
            is_both = functools.reduce(jnp.logical_or, [at == p for p in both], at < 0)
            place = jnp.clip(z + step, 0, N_TP - 1)
            share = pltpu.make_async_copy(
                pending_ref.at[0, :, pl.ds(multiple(place, feat), feat)], out, sems.at[i]
            )
            passed = pltpu.make_async_copy(src, out, sems.at[i])
            added = pltpu.make_async_copy(src, buf.at[i], sems.at[2 + i])
            pl.when(is_relay)(passed.start)
            pl.when(jnp.logical_not(is_relay))(share.start)
            pl.when(is_both)(added.start)
            todo.append((passed, added, is_both, out, i))
        for passed, added, is_both, out, i in todo:
            passed.wait()

            @pl.when(is_both)
            def _():
                added.wait()
                out[...] += buf[i]

    shape = jax.ShapeDtypeStruct((tok, feat), jnp.bfloat16)
    return pl.pallas_call(
        kernel,
        out_shape=(shape, shape),
        in_specs=[SMEM, HBM, HBM, HBM] + specs_of(arrived),
        out_specs=(VMEM, VMEM),
        scratch_shapes=[
            pltpu.VMEM((2, tok, feat), jnp.bfloat16),
            pltpu.SemaphoreType.DMA((4,)),
        ],
        compiler_params=pltpu.CompilerParams(vmem_limit_bytes=GRANT),
        cost_estimate=LITTLE,
        name="hops",
    )(ids, pending, up, down, *arrived)


def one(src, dst):
    return ([(None, src)], dst)


def multiple(value, of=128):
    return pl.multiple_of(value * of, of)


def project_kernel(scale, at_kv, ids_ref, *refs):
    xs, ws = refs[:8], refs[8:16]
    factor_ref, cos_ref, sin_ref, q_ref, kv_ref, x_buf, w_buf, x_sem, w_sem = refs[16:]
    chip, core = ids_ref[0], ids_ref[1]
    tok, half, cols = xs[0].shape[0], x_buf.shape[-1], ws[0].shape[1]
    fold = half // 2
    mine = pl.multiple_of(core * tok, 128)
    theirs = pl.multiple_of((1 - core) * tok, 128)
    waits = []
    for r in range(4):
        place = ids_ref[3 + r]
        for h in range(2):
            at = 2 * r + h
            waits.append([])
            for i in range(3):
                for m in range(4):
                    src, dst = ws[2 * m + h], w_buf.at[at]
                    if i == 0:
                        src, dst = src.at[pl.ds(0, half)], dst.at[:, pl.ds(0, cols)]
                    else:
                        lanes = pl.ds((i - 1) * 2 * HD, 2 * HD)
                        src = src.at[pl.ds(at_kv, fold), lanes]
                        dst = dst.at[pl.ds((i - 1) * fold, fold), pl.ds(cols, 2 * HD)]
                    copy = pltpu.make_async_copy(src, dst, w_sem.at[3 * at + i])
                    pl.when((place ^ chip) == m)(copy.start)
                waits[at].append(copy)
            features = pl.ds(pl.multiple_of((core ^ h) * half, 128), half)
            for s, rows in ((0, mine), (1, theirs)):
                copy = pltpu.make_async_copy(
                    xs[2 * r + s].at[:, features],
                    x_buf.at[at, pl.ds(rows, tok)],
                    x_sem.at[2 * at + s],
                )
                copy.start()
                waits[at].append(copy)
    acc = 0.0
    for at in range(8):
        for copy in waits[at]:
            copy.wait()
        acc = acc + jnp.dot(x_buf[at], w_buf[at], preferred_element_type=jnp.float32)
    factor = factor_ref[...]
    heads = q_ref.shape[0]
    for h in range(heads + 2):
        v = acc[:, h * HD : (h + 1) * HD] * factor
        if h <= heads:
            v = rotated(v, cos_ref[...], sin_ref[...])
        if h < heads:
            q_ref[h] = (v * scale).astype(jnp.bfloat16)
        else:
            kv_ref[h - heads] = v.astype(jnp.bfloat16)


def project(ids, xs, weights, at_kv, factor, cosine, sinus, scale):
    tok, feat = xs[0].shape
    cols = weights[0].shape[1]
    half = feat // 2
    return pl.pallas_call(
        functools.partial(project_kernel, scale, at_kv),
        out_shape=(
            jax.ShapeDtypeStruct((cols // HD, 2 * tok, HD), jnp.bfloat16),
            jax.ShapeDtypeStruct((2, 2 * tok, HD), jnp.bfloat16),
        ),
        in_specs=[SMEM] + [HBM] * 16 + [VMEM] * 3,
        out_specs=(VMEM, VMEM),
        scratch_shapes=[
            pltpu.VMEM((8, 2 * tok, half), jnp.bfloat16),
            pltpu.VMEM((8, half, cols + 2 * HD), jnp.bfloat16),
            pltpu.SemaphoreType.DMA((16,)),
            pltpu.SemaphoreType.DMA((24,)),
        ],
        compiler_params=pltpu.CompilerParams(vmem_limit_bytes=GRANT),
        cost_estimate=LITTLE,
        name="project",
    )(ids, *xs, *weights, factor, cosine, sinus)


BT = 256
BK = 512
UNROLL = 2
CHAIN = 2


def scores(q, k):
    return lax.dot_general(q, k, (((1,), (1,)), ((), ())), preferred_element_type=jnp.float32)


def absorb(s, v_ext, m, acc):
    new = jnp.maximum(m, jnp.max(s, axis=1, keepdims=True))
    p = jnp.exp2(s - new).astype(jnp.bfloat16)
    acc = acc * jnp.exp2(m - new) + jnp.dot(p, v_ext, preferred_element_type=jnp.float32)
    return new, acc


def prefix_kernel(bound_ref, q_ref, n_ref, kv_ref, *refs):
    m_out, acc_out, v_ext, s_ref, m_ref, acc_ref = refs[-6:]
    b = pl.program_id(0)
    heads, bt = q_ref.shape[0], q_ref.shape[1]
    rows, chains = CHAIN * bt, heads // CHAIN
    big = UNROLL * BK
    last = kv_ref.shape[1] // big - 1

    @pl.when(b == 0)
    def _():
        v_ext[:, :HD] = kv_ref[1]
        v_ext[:, HD:] = jnp.ones_like(kv_ref[1])

    m_ref[...] = jnp.full_like(m_ref, MASKED)
    acc_ref[...] = jnp.zeros_like(acc_ref)
    n_rows = jnp.concatenate([n_ref[:, :1]] * CHAIN, axis=0)

    def query(g):
        return q_ref[g * CHAIN : (g + 1) * CHAIN].reshape(rows, HD)

    s_ref[...] = scores(query(0), kv_ref[0, :BK, :])
    items = [(u, g) for u in range(UNROLL) for g in range(chains)]

    def body(kb, masked):
        start = pl.multiple_of(kb * big, big)
        follow = pl.multiple_of(jnp.minimum(kb + 1, last) * big, big)
        ms = [m_ref[g][:, :1] for g in range(chains)]
        accs = [acc_ref[g] for g in range(chains)]
        s = s_ref[...]
        for t, (u, g) in enumerate(items):
            if t + 1 < len(items):
                at, who = start + items[t + 1][0] * BK, items[t + 1][1]
            else:
                at, who = follow, 0
            ahead = scores(query(who), kv_ref[0, pl.ds(at, BK), :])
            if masked:
                col = lax.broadcasted_iota(jnp.int32, s.shape, 1) + (start + u * BK)
                s = jnp.where(col < n_rows, s, MASKED)
            v = v_ext[pl.ds(start + u * BK, BK), :]
            ms[g], accs[g] = absorb(s, v, ms[g], accs[g])
            s = ahead
        s_ref[...] = s
        for g in range(chains):
            m_ref[g] = jnp.broadcast_to(ms[g], (rows, 128))
            acc_ref[g] = accs[g]

    full = bound_ref[0, b] // big
    some = (bound_ref[1, b] + big - 1) // big
    lax.fori_loop(0, full, lambda kb, c: (body(kb, False), c)[1], 0)
    lax.fori_loop(full, some, lambda kb, c: (body(kb, True), c)[1], 0)
    m_out[0] = m_ref[...]
    acc_out[0] = acc_ref[...]


def attend_prefix(bounds, q, group, n_tok, kv, arrived=()):
    heads, tokens = CHAIN, q.shape[1]
    blocks = tokens // BT
    chains, rows = heads // CHAIN, CHAIN * BT
    keys = kv.shape[1]
    return pl.pallas_call(
        prefix_kernel,
        out_shape=(
            jax.ShapeDtypeStruct((blocks, chains, rows, 128), jnp.float32),
            jax.ShapeDtypeStruct((blocks, chains, rows, 2 * HD), jnp.float32),
        ),
        grid_spec=pltpu.PrefetchScalarGridSpec(
            num_scalar_prefetch=1,
            grid=(blocks,),
            in_specs=[
                pl.BlockSpec((heads, BT, HD), lambda b, *_: (group, b, 0)),
                pl.BlockSpec((BT, 128), lambda b, *_: (b, 0)),
                pl.BlockSpec((2, keys, HD), lambda b, *_: (0, 0, 0)),
            ]
            + specs_of(arrived),
            out_specs=(
                pl.BlockSpec((1, chains, rows, 128), lambda b, *_: (b, 0, 0, 0)),
                pl.BlockSpec((1, chains, rows, 2 * HD), lambda b, *_: (b, 0, 0, 0)),
            ),
            scratch_shapes=[
                pltpu.VMEM((keys, 2 * HD), jnp.bfloat16),
                pltpu.VMEM((rows, BK), jnp.float32),
                pltpu.VMEM((chains, rows, 128), jnp.float32),
                pltpu.VMEM((chains, rows, 2 * HD), jnp.float32),
            ],
        ),
        compiler_params=pltpu.CompilerParams(vmem_limit_bytes=GRANT),
        cost_estimate=LITTLE,
        name="attend_prefix",
    )(bounds, q, n_tok, kv, *arrived)


def new_kernel(halo, q_ref, lo_ref, k_ref, v_ref, *refs):
    states, out_ref = refs[:-1], refs[-1]
    b = pl.program_id(0)
    heads, bt = q_ref.shape[0], q_ref.shape[1]
    rows = CHAIN * bt
    span = halo + bt
    start = pl.multiple_of(b * bt, bt)
    k = k_ref[pl.ds(start, span), :]
    v = v_ref[pl.ds(start, span), :]
    v_ext = jnp.concatenate([v, jnp.ones_like(v)], axis=1)
    lo = jnp.concatenate([lo_ref[:, :1]] * CHAIN, axis=0)

    def hide(s):
        col = lax.broadcasted_iota(jnp.int32, s.shape, 1)
        row = lax.broadcasted_iota(jnp.int32, s.shape, 0) % bt
        return jnp.where((col + start >= lo) & (col <= row + halo), s, MASKED)

    for g in range(heads // CHAIN):
        q = q_ref[g * CHAIN : (g + 1) * CHAIN].reshape(rows, HD)
        _, acc = absorb(
            hide(scores(q, k)), v_ext, states[2 * g][0, 0][:, :1], states[2 * g + 1][0, 0]
        )
        mixed = (acc[:, :HD] / acc[:, HD:]).astype(jnp.bfloat16)
        for h in range(CHAIN):
            at = (g * CHAIN + h) * HD
            out_ref[:, at : at + HD] = mixed[h * bt : (h + 1) * bt]


def attend_new(q, lo_tok, k, v, states):
    heads, tokens, _ = q.shape
    blocks = tokens // BT
    chains, rows = heads // CHAIN, CHAIN * BT
    halo = k.shape[0] - tokens
    whole = lambda b: (0, 0)
    return pl.pallas_call(
        functools.partial(new_kernel, halo),
        out_shape=jax.ShapeDtypeStruct((tokens, heads * HD), jnp.bfloat16),
        grid=(blocks,),
        in_specs=[
            pl.BlockSpec((heads, BT, HD), lambda b: (0, b, 0)),
            pl.BlockSpec((BT, 128), lambda b: (b, 0)),
            pl.BlockSpec(k.shape, whole),
            pl.BlockSpec(v.shape, whole),
        ]
        + [
            pl.BlockSpec((1, 1, rows, 128), lambda b: (b, 0, 0, 0)),
            pl.BlockSpec((1, 1, rows, 2 * HD), lambda b: (b, 0, 0, 0)),
        ]
        * chains,
        out_specs=pl.BlockSpec((BT, heads * HD), lambda b: (b, 0)),
        compiler_params=pltpu.CompilerParams(vmem_limit_bytes=GRANT),
        cost_estimate=LITTLE,
        name="attend_new",
    )(q, lo_tok, k, v, *states)


def out_kernel(ids_ref, *refs):
    xs, ws = refs[:8], refs[8:13]
    out_ref, x_buf, w_buf, x_sem, w_sem = refs[13:]
    chip, core, z = ids_ref[0], ids_ref[1], ids_ref[2]
    width = xs[0].shape[1]
    rows = w_buf.shape[1] // 4
    top = ws[3].shape[0]
    for r in range(4):
        near = ids_ref[3 + r] ^ z
        for m in range(4):
            to = w_buf.at[r, pl.ds(pl.multiple_of((chip ^ m) * rows, 128), rows)]
            sem = w_sem.at[4 * r + m]
            if m < 3:
                src = ws[m].at[pl.ds(pl.multiple_of(near * rows, 128), rows)]
                pltpu.make_async_copy(src, to, sem).start()
            else:

                @pl.when(near < 2)
                def _():
                    src = ws[3].at[pl.ds(pl.multiple_of(near * rows, 128), rows)]
                    pltpu.make_async_copy(src, to, sem).start()

                @pl.when(near >= 2)
                def _():
                    src = ws[4].at[pl.ds(pl.multiple_of(near * rows - top, 128), rows)]
                    pltpu.make_async_copy(src, to, sem).start()

        for s in range(2):
            at = pl.multiple_of((core ^ s) * width, 128)
            pltpu.make_async_copy(
                xs[2 * r + s], x_buf.at[r, :, pl.ds(at, width)], x_sem.at[2 * r + s]
            ).start()
    acc = None
    for r in range(4):
        for m in range(4):
            pltpu.make_async_copy(
                ws[0].at[pl.ds(0, rows)], w_buf.at[r, pl.ds(0, rows)], w_sem.at[4 * r + m]
            ).wait()
        for s in range(2):
            pltpu.make_async_copy(
                xs[0], x_buf.at[r, :, pl.ds(0, width)], x_sem.at[2 * r + s]
            ).wait()
        term = jnp.dot(x_buf[r], w_buf[r], preferred_element_type=jnp.float32)
        acc = term if acc is None else acc + term
    out_ref[...] = acc.astype(jnp.bfloat16)


def out_project(ids, xs, ws):
    tokens, width = xs[0].shape
    depth, cols = ws[0].shape
    return pl.pallas_call(
        out_kernel,
        out_shape=jax.ShapeDtypeStruct((tokens, cols), jnp.bfloat16),
        in_specs=[SMEM] + [HBM] * 13,
        out_specs=VMEM,
        scratch_shapes=[
            pltpu.VMEM((4, tokens, 2 * width), jnp.bfloat16),
            pltpu.VMEM((4, depth, cols), jnp.bfloat16),
            pltpu.SemaphoreType.DMA((8,)),
            pltpu.SemaphoreType.DMA((16,)),
        ],
        compiler_params=pltpu.CompilerParams(vmem_limit_bytes=GRANT),
        cost_estimate=LITTLE,
        name="out_project",
    )(ids, *xs, *ws)


def per_device(
    stream,
    pending,
    norm_gain,
    w_query,
    w_key,
    w_value,
    w_out,
    prefix_keys,
    prefix_values,
    prefix_segments,
    stretch_segments,
    stretch_offset,
):
    tok, feat = stream.shape
    chip_tok = 2 * tok
    c = lax.axis_index("ctx")
    z = lax.axis_index("tp")
    chip, core = c // 2, c % 2
    first = core == 0
    depth = feat * N_TP

    wide = stream.astype(jnp.float32)
    here = jnp.stack([chip, core, z]).astype(jnp.int32)
    every = (0, 1, 2)

    gain = lax.dynamic_slice_in_dim(norm_gain, z * feat, feat, 0).astype(jnp.float32)
    scaled = (wide * gain[None, :]).astype(jnp.bfloat16)
    u1, d1 = hop_up(scaled, every), hop_down(scaled, every)

    labels = jnp.arange(NTRAJ, dtype=jnp.int32)
    counts = jnp.concatenate(
        [
            jnp.sum((prefix_segments[:, None] <= labels).astype(jnp.int32), axis=0),
            jnp.sum((stretch_segments[:, None] < labels).astype(jnp.int32), axis=0),
        ]
    )
    notes = jnp.concatenate([counts // 32, counts % 32])
    cols = w_query.shape[1] // 2
    notes = jnp.stack(
        [jnp.pad(v, (0, cols - v.shape[0])) for v in (stretch_segments, notes)]
        + [jnp.zeros((cols,), jnp.int32)] * 14
    ).astype(jnp.bfloat16)

    token_index = chip * chip_tok + jnp.arange(chip_tok, dtype=jnp.int32)
    positions = stretch_offset[0].astype(jnp.float32) + token_index.astype(jnp.float32)
    angles = positions[:, None] * inverse_freqs(HD)
    cosine, sinus = jnp.cos(angles), jnp.sin(angles)
    cosine = jnp.concatenate([cosine, cosine], axis=1)
    sinus = jnp.concatenate([-sinus, sinus], axis=1)

    def squares(part, place):
        g = lax.dynamic_slice_in_dim(norm_gain, place * feat, feat, 0).astype(jnp.float32)
        return jnp.sum(jnp.square(part.astype(jnp.float32) / g[None, :]), axis=1, keepdims=True)

    q_heads = w_query.shape[1] // HD // 2
    q_cols = q_heads * HD
    n_q = w_query.shape[0]
    fold = prefix_keys.shape[1] // 2
    n_both = n_q + fold
    n_kv = w_key.shape[0] // 2
    n_piece = w_out.shape[0] // 4

    def first_plan(at, src, out):
        w_q, w_k, w_v, keys, values, said = src
        for dst, j in ((out[0], at[1]), (out[1], 1 - at[1])):
            head = 2 * at[2] + j
            yield one(w_q.at[:, pl.ds(multiple(j, q_cols), q_cols)], dst.at[pl.ds(0, n_q)])
            for i, a in enumerate((keys, keys, values, values)):
                part = a.at[head, pl.ds((i % 2) * fold, fold)]
                yield one(part, dst.at[pl.ds(n_q, fold), pl.ds(i * HD, HD)])
            for i, a in enumerate((w_k, w_v, w_k, w_v)):
                part = a.at[pl.ds((i // 2) * n_kv, n_kv), pl.ds(multiple(head), HD)]
                yield one(part, dst.at[pl.ds(n_both, n_kv), pl.ds(i * HD, HD)])
            yield one(said, dst.at[pl.ds(n_both + n_kv, said.shape[0])])

    own, give = move(
        first_plan,
        ((n_both + n_kv + notes.shape[0], q_cols),) * 2,
        here,
        (w_query, w_key, w_value, prefix_keys, prefix_values, notes),
    )
    places = jnp.stack(
        [z, jnp.where(z < 2, z + 1, z - 1), jnp.where(z < 2, z + 2, z - 2), jnp.where(z % 2 == 1, 0, 3)]
    ).astype(jnp.int32)
    ids = jnp.concatenate([here, places])

    x1, y1, given = swap(own, 2), swap(own, 4), swap(give, 1)
    mine = squares(scaled, z)
    near = pick(z, (d1, d1, u1, u1), here, (cosine, sinus, mine))
    over1 = swap(near, 1)

    up, down = hops(here, pending, u1, d1, 3, (1, 2, 3), (), (x1, y1, given, over1))
    u2, d2 = hop_up(up, every), hop_down(down, every)

    given = gate(given, u1, d1, x1, y1, over1)
    x2, y2, over0 = swap(given, 2), swap(given, 4), swap(gate(scaled, given), 1)
    mine = mine + squares(near, places[1])
    theirs = squares(over1, places[1])
    second = pick(z, (d2, d2, u2, u2), here, (over0, mine, theirs))

    up, down = hops(here, pending, u2, d2, 2, (2,), (1,), (x2, y2, over0, second))
    u3, d3 = hop_up(up, every), hop_down(down, every)

    x1, y2 = gate(x1, u2, d2, x2, over0, second), gate(y2, u2, d2, x2, over0, second)
    far_own, far_other = swap(x1, 4), swap(y2, 2)
    over2 = swap(second, 1)
    mine = mine + squares(second, places[2])
    theirs = theirs + squares(over0, z)
    up, down = hops(here, pending, u3, d3, 1, (), (1, 2, 3), (over2,))
    u4, d4 = hop_up(up, every), hop_down(down, every)
    third = pick(z, (d3, u1, d1, u3), here, (up, mine, theirs))
    over3 = swap(third, 1)

    mine = mine + squares(third, places[3])
    theirs = theirs + squares(over2, places[2]) + squares(over3, places[3])
    total = jnp.where(first, jnp.concatenate([mine, theirs]), jnp.concatenate([theirs, mine]))
    factor = lax.rsqrt(total * (1.0 / depth) + NORM_EPSILON)
    factor = jnp.broadcast_to(factor, (chip_tok, 128))
    xs = [scaled, over0, near, over1, second, over2, third, over3]
    own_rows = (own, given, x1, x2, y1, y2, far_own, far_other)

    said = [rows[n_both + n_kv : n_both + n_kv + 2].astype(jnp.float32) for rows in own_rows]
    total = sum(v[1, : 4 * NTRAJ] for v in said).astype(jnp.int32)
    total = total[: 2 * NTRAJ] * 32 + total[2 * NTRAJ :]
    segs = [v[0, :tok].astype(jnp.int32) for v in said[:2]]
    segs = jnp.where(first, jnp.concatenate(segs), jnp.concatenate(segs[::-1]))
    onehot = (segs[:, None] == labels).astype(jnp.int32)
    n_tok = jnp.sum(onehot * total[:NTRAJ], axis=1)
    lo_tok = jnp.sum(onehot * total[NTRAJ:], axis=1) - chip * chip_tok + tok
    blocked = n_tok.reshape(chip_tok // BT, BT)
    bounds = jnp.stack([blocked[:, 0], blocked[:, -1]])
    n_wide = jnp.broadcast_to(n_tok[:, None], (chip_tok, 128))
    lo_wide = jnp.broadcast_to(lo_tok[:, None], (chip_tok, 128))

    def prefix_plan(at, src, out):
        for m in range(4):
            for j in range(2):
                start = ((at[0] ^ m) * 2 + (at[1] ^ j)) * 2 * fold
                rows = src[2 * m + j]
                for i in range(4):
                    dst = out[0].at[i // 2, pl.ds(pl.multiple_of(start + (i % 2) * fold, 128), fold)]
                    yield one(rows.at[pl.ds(n_q, fold), pl.ds(i * HD, HD)], dst)

    (kv,) = move(prefix_plan, ((2, N_CTX * 2 * fold, HD),), here, own_rows, (third,))

    def piece_plan(at, src, out):
        for r, dst in enumerate(out):
            rows = pl.ds(multiple(at[0] ^ r, n_piece), n_piece)
            for i in range(2):
                part = src[0].at[rows, pl.ds(i * q_cols, q_cols)]
                yield one(part, dst.at[pl.ds(i * n_piece, n_piece)])

    by_chip = move(
        piece_plan, ((2 * n_piece, q_cols),) * 4, here, (w_out,), (far_own, far_other, third, kv)
    )
    by_chip = (by_chip[0],) + tuple(swap(by_chip[r], 2 * r) for r in (1, 2, 3))

    scale = math.log2(math.e) / math.sqrt(HD)
    q, kv_new = project(ids, xs, own_rows, n_both, factor, cosine, sinus, scale)
    before = lax.ppermute(kv_new[:, tok:], "ctx", [(i, i + 2) for i in range(N_CTX - 2)])

    def pieces_plan(at, src, out):
        for r, dst in enumerate(out):
            near = (at[2] ^ r) ^ at[0]
            yield ([(near == m, src[m]) for m in range(4)], dst)

    pieces = list(move(pieces_plan, ((2 * n_piece, q_cols),) * 4, here, by_chip, (q,)))
    for r in (1, 2, 3):
        pieces[r] = lax.ppermute(pieces[r], "tp", [(i, i ^ r) for i in range(N_TP)])
    part_a = attend_prefix(bounds, q, 0, n_wide, kv, (pieces[0],))
    part_b = attend_prefix(bounds, q, 1, n_wide, kv, (part_a[0], before, u4, d4))
    k_near = jnp.concatenate([before[0], kv_new[0]], axis=0)
    v_near = jnp.concatenate([before[1], kv_new[1]], axis=0)
    attended = attend_new(q, lo_wide, k_near, v_near, part_a + part_b)

    def block_plan(at, src, out):
        for r, part in enumerate(src):
            for i in range(2):
                dst = out[0].at[pl.ds(r * n_piece, n_piece), pl.ds(i * q_cols, q_cols)]
                yield one(part.at[pl.ds(i * n_piece, n_piece)], dst)

    (block,) = move(block_plan, ((4 * n_piece, 2 * q_cols),), here, pieces, (part_b[0],))
    half = block.shape[0] // 2
    wo_x, wo_y = swap(block, 2), swap(block, 4)
    u1, d1 = hop_up(attended, every), hop_down(attended, every)
    near = pick(z, (d1, d1, u1, u1), here, (wo_x, wo_y))

    def far_plan(at, src, out):
        yield one(src[0].at[pl.ds(0, half)], out[0])
        yield one(src[1].at[pl.ds(half, half)], out[1])

    to_y, to_x = move(
        far_plan, ((half, block.shape[1]),) * 2, here, (wo_x, wo_y), (near,)
    )
    wo_parts = (block, wo_x, wo_y, swap(to_y, 4), swap(to_x, 2))
    u2, d2 = hop_up(gate(u1, near), (1, 2)), hop_down(gate(d1, near), (1, 2))
    second = pick(z, (d2, d2, u2, u2), here)
    u3, d3 = hop_up(gate(u2, *wo_parts[3:]), (2,)), hop_down(gate(d2, *wo_parts[3:]), (2,))
    third = pick(z, (d3, u1, d1, u3), here)
    hs = []
    for part in (attended, near, second, third):
        hs += [part, swap(part, 1)]
    projected = out_project(ids, hs, wo_parts)
    mine = lax.dynamic_slice_in_dim(projected, core * tok, tok, 0)
    theirs = swap(lax.dynamic_slice_in_dim(projected, (1 - core) * tok, tok, 0), 1)
    head_share = jnp.where(
        first,
        jnp.concatenate([mine, theirs], axis=1),
        jnp.concatenate([theirs, mine], axis=1),
    ).astype(jnp.float32)
    pending_share = (
        lax.dynamic_slice_in_dim(pending[0], z * feat, feat, 1).astype(jnp.float32)
        + jnp.where(z == 0, 0, u4).astype(jnp.float32)
        + jnp.where(z == 3, 0, d4).astype(jnp.float32)
    )
    return (wide + (head_share + pending_share)).astype(jnp.bfloat16)


def solution(mesh):
    in_specs = (
        P("ctx", "tp"),
        P("tp", "ctx", None),
        P(),
        P("ctx", "tp"),
        P("ctx", None),
        P("ctx", None),
        P("tp", "ctx"),
        P(None, "ctx", None),
        P(None, "ctx", None),
        P("ctx"),
        P("ctx"),
        P(),
    )
    out_specs = P("ctx", "tp")
    small = mesh.shape["ctx"] == N_CTX and mesh.shape["tp"] == N_TP
    return jax.shard_map(
        per_device if small else per_device_any,
        mesh=mesh,
        in_specs=in_specs,
        out_specs=out_specs,
        check_vma=False,
    )
```

```python
import functools
import math

import jax
import jax.numpy as jnp
from jax import lax
from jax.experimental import pallas as pl
from jax.experimental.pallas import tpu as pltpu
from jax.sharding import PartitionSpec as P

HQ = 32
KVH = 8
HD = 128
NTRAJ = 16


ROPE_BASE = 500000.0
ROPE_FACTOR = 8.0
LOW_FREQ = 1.0
HIGH_FREQ = 4.0
INITIAL_SPAN = 8192.0
NORM_EPSILON = 1e-05
MASKED = -1e30


def inverse_freqs(head_width):
    pair_index = jnp.arange(head_width // 2, dtype=jnp.float32)
    base_freq = ROPE_BASE ** (-2.0 * pair_index / head_width)
    wavelength = 2.0 * math.pi / base_freq
    smooth = (INITIAL_SPAN / wavelength - LOW_FREQ) / (HIGH_FREQ - LOW_FREQ)
    blended = (1.0 - smooth) * base_freq / ROPE_FACTOR + smooth * base_freq
    return jnp.where(
        wavelength < INITIAL_SPAN / HIGH_FREQ,
        base_freq,
        jnp.where(wavelength > INITIAL_SPAN / LOW_FREQ, base_freq / ROPE_FACTOR, blended),
    )


def rotate(vectors, positions):
    head_width = vectors.shape[-1]
    angles = positions[..., None] * inverse_freqs(head_width)
    cosine = jnp.cos(angles)
    sinus = jnp.sin(angles)
    first_half = vectors[..., : head_width // 2]
    second_half = vectors[..., head_width // 2 :]
    return jnp.concatenate(
        [first_half * cosine - second_half * sinus, second_half * cosine + first_half * sinus],
        axis=-1,
    )


def visibility(key_labels, is_prefix, key_pos, query_segs, query_index):
    earlier = key_labels[None, :] <= query_segs[:, None]
    same = (key_labels[None, :] == query_segs[:, None]) & (key_pos[None, :] <= query_index[:, None])
    return jnp.where(is_prefix[None, :], earlier, same)


def attend_whole(grouped, key_block, value_block, seen):
    scores = jnp.einsum("hrd,hnd->hrn", grouped, key_block, preferred_element_type=jnp.float32) * (
        1.0 / math.sqrt(HD)
    )
    scores = jnp.where(seen[None], scores, MASKED)
    new_max = jnp.max(scores, axis=2)
    weights = jnp.where(seen[None], jnp.exp(scores - new_max[..., None]), 0.0)
    totals = jnp.sum(weights, axis=2)
    numerator = jnp.einsum(
        "hrn,hnd->hrd",
        weights.astype(jnp.bfloat16),
        value_block,
        preferred_element_type=jnp.float32,
    )
    return numerator / totals[..., None]


def per_device_any(
    stream,
    pending,
    norm_gain,
    w_query,
    w_key,
    w_value,
    w_out,
    prefix_keys,
    prefix_values,
    prefix_segments,
    stretch_segments,
    stretch_offset,
):
    tok_rows = stream.shape[0]
    prefix_rows = prefix_keys.shape[1]
    ctx_index = lax.axis_index("ctx")
    tp_index = lax.axis_index("tp")
    gain_wide = norm_gain.astype(jnp.float32)
    whole = lax.all_gather(stream, "tp", axis=1, tiled=True).astype(jnp.float32)
    mean_square = jnp.mean(whole * whole, axis=1, keepdims=True)
    normed = (whole * lax.rsqrt(mean_square + NORM_EPSILON) * gain_wide).astype(jnp.bfloat16)
    q_cols = w_query.shape[1]
    q_heads = q_cols // HD
    full_group = HQ // KVH
    kv_heads = max(1, q_heads // full_group)
    group_size = q_heads // kv_heads
    head_start = tp_index * q_heads // full_group
    kv_cols = kv_heads * HD
    key_slice = lax.dynamic_slice_in_dim(w_key, head_start * HD, kv_cols, 1)
    value_slice = lax.dynamic_slice_in_dim(w_value, head_start * HD, kv_cols, 1)
    pieces = (
        lax.all_gather(w_query, "ctx", axis=0, tiled=True),
        lax.all_gather(key_slice, "ctx", axis=0, tiled=True),
        lax.all_gather(value_slice, "ctx", axis=0, tiled=True),
    )
    query_raw, key_full, value_full = tuple(
        (jnp.dot(normed, piece_rows, preferred_element_type=jnp.float32) for piece_rows in pieces)
    )
    token_index = ctx_index * tok_rows + jnp.arange(tok_rows, dtype=jnp.int32)
    positions = stretch_offset[0].astype(jnp.float32) + token_index.astype(jnp.float32)
    query_rows = rotate(query_raw.reshape(tok_rows, q_heads, HD), positions[:, None]).astype(
        jnp.bfloat16
    )
    new_keys = jnp.transpose(
        rotate(key_full.reshape(tok_rows, kv_heads, HD), positions[:, None]).astype(jnp.bfloat16),
        (1, 0, 2),
    )
    new_values = jnp.transpose(
        value_full.astype(jnp.bfloat16).reshape(tok_rows, kv_heads, HD), (1, 0, 2)
    )
    old_keys = lax.dynamic_slice_in_dim(prefix_keys, head_start, kv_heads, 0)
    old_values = lax.dynamic_slice_in_dim(prefix_values, head_start, kv_heads, 0)
    local_keys = jnp.concatenate([old_keys, new_keys], 1)
    local_values = jnp.concatenate([old_values, new_values], 1)
    key_labels = jnp.concatenate([prefix_segments, stretch_segments])
    key_span = prefix_rows + tok_rows
    grouped = jnp.transpose(
        query_rows.reshape(tok_rows, kv_heads, group_size, HD), (1, 0, 2, 3)
    ).reshape(kv_heads, tok_rows * group_size, HD)
    query_index = jnp.repeat(token_index, group_size)
    query_segs = jnp.repeat(stretch_segments, group_size)
    both = jnp.stack([local_keys, local_values])
    kv_block = lax.all_gather(both, "ctx", axis=2, tiled=True)
    label_block = lax.all_gather(key_labels[None, None, :], "ctx", axis=2, tiled=True)
    key_count = kv_block.shape[2]
    absolute = jnp.arange(key_count, dtype=jnp.int32)
    within = absolute % key_span
    key_pos = absolute // key_span * tok_rows + within - prefix_rows
    seen = visibility(label_block[0, 0], within < prefix_rows, key_pos, query_segs, query_index)
    attended_heads = attend_whole(grouped, kv_block[0], kv_block[1], seen).astype(jnp.bfloat16)
    attended = jnp.transpose(
        attended_heads.reshape(kv_heads, tok_rows, group_size, HD), (1, 0, 2, 3)
    ).reshape(tok_rows, q_cols)
    head_terms = jnp.dot(
        attended,
        lax.all_gather(w_out, "ctx", axis=1, tiled=True),
        preferred_element_type=jnp.float32,
    )
    head_share, pending_share = (
        lax.psum_scatter(
            head_terms.astype(jnp.bfloat16), "tp", scatter_dimension=1, tiled=True
        ).astype(jnp.float32),
        lax.psum_scatter(
            pending[0].astype(jnp.float32).astype(jnp.bfloat16),
            "tp",
            scatter_dimension=1,
            tiled=True,
        ).astype(jnp.float32),
    )
    block_share = head_share + pending_share
    return (stream.astype(jnp.float32) + block_share).astype(jnp.bfloat16)


N_CTX = 8
N_TP = 4
GRANT = 60 * 1024 * 1024


def swap(x, bit):
    return lax.ppermute(x, "ctx", [(c, c ^ bit) for c in range(N_CTX)])


def hop_up(v, pairs):
    return lax.ppermute(v, "tp", [(i, i + 1) for i in pairs])


def hop_down(v, pairs):
    return lax.ppermute(v, "tp", [(N_TP - 1 - i, N_TP - 2 - i) for i in pairs])


def rotated(v, cosine, sinus):
    return v * cosine + pltpu.roll(v, HD // 2, 1) * sinus


HBM = pl.BlockSpec(memory_space=pltpu.HBM)
VMEM = pl.BlockSpec(memory_space=pltpu.VMEM)
SMEM = pl.BlockSpec(memory_space=pltpu.SMEM)
ANY = pl.BlockSpec(memory_space=pl.ANY)
LITTLE = pl.CostEstimate(flops=0, bytes_accessed=1024, transcendentals=0)


def specs_of(arrays):
    return [HBM if a.size > 200000 else ANY for a in arrays]


def move(plan, shapes, ids, sources, arrived=()):
    count = len(sources)

    def kernel(ids_ref, *refs):
        outs, sems = refs[count + len(arrived) : -1], refs[-1]
        waits = []
        for at, (choices, dst) in enumerate(plan(ids_ref, refs[:count], outs)):
            for cond, src in choices:
                copy = pltpu.make_async_copy(src, dst, sems.at[at])
                if cond is None:
                    copy.start()
                else:
                    pl.when(cond)(copy.start)
            waits.append(copy)
        for copy in waits:
            copy.wait()

    return pl.pallas_call(
        kernel,
        out_shape=tuple(jax.ShapeDtypeStruct(shape, jnp.bfloat16) for shape in shapes),
        in_specs=[SMEM] + [HBM] * count + specs_of(arrived),
        out_specs=tuple(VMEM for _ in shapes),
        scratch_shapes=[pltpu.SemaphoreType.DMA((40,))],
        compiler_params=pltpu.CompilerParams(vmem_limit_bytes=GRANT),
        cost_estimate=LITTLE,
        name=plan.__name__,
    )(ids, *sources, *arrived)


def gate(x, *arrived):
    return pl.pallas_call(
        lambda *refs: None,
        out_shape=jax.ShapeDtypeStruct(x.shape, x.dtype),
        in_specs=[HBM] + specs_of(arrived),
        out_specs=HBM,
        input_output_aliases={0: 0},
        compiler_params=pltpu.CompilerParams(vmem_limit_bytes=GRANT),
        cost_estimate=LITTLE,
        name="gate",
    )(x, *arrived)


def pick(z, options, ids, arrived=()):
    distinct = list({id(o): o for o in options}.values())

    def pick_plan(at, src, out):
        yield (
            [(at[2] == i, src[[o is d for d in distinct].index(True)]) for i, o in enumerate(options)],
            out[0],
        )

    return move(pick_plan, (options[0].shape,), ids, distinct, arrived)[0]


def hops(ids, pending, up, down, offset, relay, both, arrived=()):
    tok, feat = up.shape

    def kernel(ids_ref, pending_ref, up_ref, down_ref, *refs):
        out_up, out_down, buf, sems = refs[len(arrived) :]
        z = ids_ref[2]
        todo = []
        for i, (src, out, step, at) in enumerate(
            ((up_ref, out_up, offset, z), (down_ref, out_down, -offset, N_TP - 1 - z))
        ):
            is_relay = functools.reduce(jnp.logical_or, [at == p for p in relay], at < 0)
            is_both = functools.reduce(jnp.logical_or, [at == p for p in both], at < 0)
            place = jnp.clip(z + step, 0, N_TP - 1)
            share = pltpu.make_async_copy(
                pending_ref.at[0, :, pl.ds(multiple(place, feat), feat)], out, sems.at[i]
            )
            passed = pltpu.make_async_copy(src, out, sems.at[i])
            added = pltpu.make_async_copy(src, buf.at[i], sems.at[2 + i])
            pl.when(is_relay)(passed.start)
            pl.when(jnp.logical_not(is_relay))(share.start)
            pl.when(is_both)(added.start)
            todo.append((passed, added, is_both, out, i))
        for passed, added, is_both, out, i in todo:
            passed.wait()

            @pl.when(is_both)
            def _():
                added.wait()
                out[...] += buf[i]

    shape = jax.ShapeDtypeStruct((tok, feat), jnp.bfloat16)
    return pl.pallas_call(
        kernel,
        out_shape=(shape, shape),
        in_specs=[SMEM, HBM, HBM, HBM] + specs_of(arrived),
        out_specs=(VMEM, VMEM),
        scratch_shapes=[
            pltpu.VMEM((2, tok, feat), jnp.bfloat16),
            pltpu.SemaphoreType.DMA((4,)),
        ],
        compiler_params=pltpu.CompilerParams(vmem_limit_bytes=GRANT),
        cost_estimate=LITTLE,
        name="hops",
    )(ids, pending, up, down, *arrived)


def one(src, dst):
    return ([(None, src)], dst)


def multiple(value, of=128):
    return pl.multiple_of(value * of, of)


AHEAD = 3


def project_kernel(scale, at_kv, ids_ref, *refs):
    xs, ws = refs[:8], refs[8:16]
    factor_ref, cos_ref, sin_ref, q_ref, kv_ref, x_buf, w_buf, x_sem, w_sem = refs[16:]
    chip, core = ids_ref[0], ids_ref[1]
    tok, half, cols = xs[7].shape[0], x_buf.shape[-1], ws[0].shape[1]
    fold = half // 2
    mine = pl.multiple_of(core * tok, 128)
    theirs = pl.multiple_of((1 - core) * tok, 128)

    def fetch(at):
        r, h = at // 2, at % 2
        place = ids_ref[3 + r]
        waits = []
        for i in range(3):
            for m in range(4):
                src, dst = ws[2 * m + h], w_buf.at[at]
                if i == 0:
                    src, dst = src.at[pl.ds(0, half)], dst.at[:, pl.ds(0, cols)]
                else:
                    lanes = pl.ds((i - 1) * 2 * HD, 2 * HD)
                    src = src.at[pl.ds(at_kv, fold), lanes]
                    dst = dst.at[pl.ds((i - 1) * fold, fold), pl.ds(cols, 2 * HD)]
                copy = pltpu.make_async_copy(src, dst, w_sem.at[3 * at + i])
                pl.when((place ^ chip) == m)(copy.start)
            waits.append(copy)
        features = pl.ds(pl.multiple_of((core ^ h) * half, 128), half)
        for s, rows in ((0, mine), (1, theirs)):
            src = xs[2 * r + s].at[pl.ds(tok if r == 1 else 0, tok), features]
            copy = pltpu.make_async_copy(src, x_buf.at[at, pl.ds(rows, tok)], x_sem.at[2 * at + s])
            copy.start()
            waits.append(copy)
        return waits

    ahead = [fetch(at) for at in range(AHEAD)]
    acc = 0.0
    for at in range(8):
        for copy in ahead[at]:
            copy.wait()
        if at + AHEAD < 8:
            ahead.append(fetch(at + AHEAD))
        acc = acc + jnp.dot(x_buf[at], w_buf[at], preferred_element_type=jnp.float32)
    factor = factor_ref[...]
    heads = q_ref.shape[0]
    for h in range(heads + 2):
        v = acc[:, h * HD : (h + 1) * HD] * factor
        if h <= heads:
            v = rotated(v, cos_ref[...], sin_ref[...])
        if h < heads:
            q_ref[h] = (v * scale).astype(jnp.bfloat16)
        else:
            kv_ref[h - heads] = v.astype(jnp.bfloat16)


def project(ids, xs, weights, at_kv, factor, cosine, sinus, scale):
    tok, feat = xs[7].shape
    cols = weights[0].shape[1]
    half = feat // 2
    return pl.pallas_call(
        functools.partial(project_kernel, scale, at_kv),
        out_shape=(
            jax.ShapeDtypeStruct((cols // HD, 2 * tok, HD), jnp.bfloat16),
            jax.ShapeDtypeStruct((2, 2 * tok, HD), jnp.bfloat16),
        ),
        in_specs=[SMEM] + [HBM] * 16 + [VMEM] * 3,
        out_specs=(VMEM, VMEM),
        scratch_shapes=[
            pltpu.VMEM((8, 2 * tok, half), jnp.bfloat16),
            pltpu.VMEM((8, half, cols + 2 * HD), jnp.bfloat16),
            pltpu.SemaphoreType.DMA((16,)),
            pltpu.SemaphoreType.DMA((24,)),
        ],
        compiler_params=pltpu.CompilerParams(vmem_limit_bytes=GRANT),
        cost_estimate=LITTLE,
        name="project",
    )(ids, *xs, *weights, factor, cosine, sinus)


BT = 256
BK = 1024
CHAIN = 2


def scores(q, k):
    return lax.dot_general(q, k, (((1,), (1,)), ((), ())), preferred_element_type=jnp.float32)


def absorb(s, v_ext, m, acc):
    new = jnp.maximum(m, jnp.max(s, axis=1, keepdims=True))
    p = jnp.exp2(s - new).astype(jnp.bfloat16)
    acc = acc * jnp.exp2(m - new) + jnp.dot(p, v_ext, preferred_element_type=jnp.float32)
    return new, acc


def attend_kernel(
    halo, bound_ref, q_ref, n_ref, lo_ref, kv_ref, k_ref, v_ref, out_ref, v_ext, s_ref, m_ref, acc_ref
):
    b = pl.program_id(0)
    heads, bt = q_ref.shape[0], q_ref.shape[1]
    rows, chains = CHAIN * bt, heads // CHAIN
    last = kv_ref.shape[1] // BK - 1

    @pl.when(b == 0)
    def _():
        v_ext[:, :HD] = kv_ref[1]
        v_ext[:, HD:] = jnp.ones_like(kv_ref[1])

    m_ref[...] = jnp.full_like(m_ref, MASKED)
    acc_ref[...] = jnp.zeros_like(acc_ref)

    def query(g):
        return q_ref[g * CHAIN : (g + 1) * CHAIN].reshape(rows, HD)

    s_ref[...] = scores(query(0), kv_ref[0, :BK, :])

    def body(kb, masked):
        start = pl.multiple_of(kb * BK, BK)
        follow = pl.multiple_of(jnp.minimum(kb + 1, last) * BK, BK)
        ms = [m_ref[g][:, :1] for g in range(chains)]
        accs = [acc_ref[g] for g in range(chains)]
        s = s_ref[...]
        v = v_ext[pl.ds(start, BK), :]
        for g in range(chains):
            at, who = (start, g + 1) if g + 1 < chains else (follow, 0)
            ahead = scores(query(who), kv_ref[0, pl.ds(at, BK), :])
            if masked:
                n_rows = jnp.concatenate([n_ref[:, :1]] * CHAIN, axis=0)
                col = lax.broadcasted_iota(jnp.int32, s.shape, 1) + start
                s = jnp.where(col < n_rows, s, MASKED)
            ms[g], accs[g] = absorb(s, v, ms[g], accs[g])
            s = ahead
        s_ref[...] = s
        for g in range(chains):
            m_ref[g] = jnp.broadcast_to(ms[g], (rows, 128))
            acc_ref[g] = accs[g]

    full = bound_ref[0, b] // BK
    some = (bound_ref[1, b] + BK - 1) // BK
    lax.fori_loop(0, full, lambda kb, c: (body(kb, False), c)[1], 0)
    lax.fori_loop(full, some, lambda kb, c: (body(kb, True), c)[1], 0)

    span = halo + bt
    start = pl.multiple_of(b * bt, bt)
    k = k_ref[pl.ds(start, span), :]
    v = v_ref[pl.ds(start, span), :]
    v = jnp.concatenate([v, jnp.ones_like(v)], axis=1)
    lo = jnp.concatenate([lo_ref[:, :1]] * CHAIN, axis=0)
    col = lax.broadcasted_iota(jnp.int32, (rows, span), 1)
    row = lax.broadcasted_iota(jnp.int32, (rows, span), 0) % bt
    seen = (col + start >= lo) & (col <= row + halo)
    for g in range(chains):
        s = jnp.where(seen, scores(query(g), k), MASKED)
        _, acc = absorb(s, v, m_ref[g][:, :1], acc_ref[g])
        mixed = (acc[:, :HD] / acc[:, HD:]).astype(jnp.bfloat16)
        for h in range(CHAIN):
            at = (g * CHAIN + h) * HD
            out_ref[:, at : at + HD] = mixed[h * bt : (h + 1) * bt]


def attend(bounds, q, n_tok, lo_tok, kv, k, v, arrived=()):
    heads, tokens = q.shape[:2]
    chains, rows = heads // CHAIN, CHAIN * BT
    keys = kv.shape[1]
    halo = k.shape[0] - tokens
    count = len(arrived)

    def kernel(*refs):
        attend_kernel(halo, *refs[:7], *refs[7 + count :])

    return pl.pallas_call(
        kernel,
        out_shape=jax.ShapeDtypeStruct((tokens, heads * HD), jnp.bfloat16),
        grid_spec=pltpu.PrefetchScalarGridSpec(
            num_scalar_prefetch=1,
            grid=(tokens // BT,),
            in_specs=[
                pl.BlockSpec((heads, BT, HD), lambda b, *_: (0, b, 0)),
                pl.BlockSpec((BT, 128), lambda b, *_: (b, 0)),
                pl.BlockSpec((BT, 128), lambda b, *_: (b, 0)),
                pl.BlockSpec((2, keys, HD), lambda b, *_: (0, 0, 0)),
                pl.BlockSpec(k.shape, lambda b, *_: (0, 0)),
                pl.BlockSpec(v.shape, lambda b, *_: (0, 0)),
            ]
            + specs_of(arrived),
            out_specs=pl.BlockSpec((BT, heads * HD), lambda b, *_: (b, 0)),
            scratch_shapes=[
                pltpu.VMEM((keys, 2 * HD), jnp.bfloat16),
                pltpu.VMEM((rows, BK), jnp.float32),
                pltpu.VMEM((chains, rows, 128), jnp.float32),
                pltpu.VMEM((chains, rows, 2 * HD), jnp.float32),
            ],
        ),
        compiler_params=pltpu.CompilerParams(vmem_limit_bytes=GRANT),
        cost_estimate=LITTLE,
        name="attend",
    )(bounds, q, n_tok, lo_tok, kv, k, v, *arrived)


def out_kernel(ids_ref, *refs):
    xs, ws = refs[:8], refs[8:13]
    keep_ref, give_ref, x_buf, w_buf, o_buf, x_sem, w_sem = refs[13:]
    chip, core, z = ids_ref[0], ids_ref[1], ids_ref[2]
    width = xs[0].shape[1]
    rows = w_buf.shape[1] // 4
    top = ws[3].shape[0]
    for r in range(4):
        near = ids_ref[3 + r] ^ z
        for m in range(4):
            to = w_buf.at[r, pl.ds(pl.multiple_of((chip ^ m) * rows, 128), rows)]
            sem = w_sem.at[4 * r + m]
            if m < 3:
                src = ws[m].at[pl.ds(pl.multiple_of(near * rows, 128), rows)]
                pltpu.make_async_copy(src, to, sem).start()
            else:

                @pl.when(near < 2)
                def _():
                    src = ws[3].at[pl.ds(pl.multiple_of(near * rows, 128), rows)]
                    pltpu.make_async_copy(src, to, sem).start()

                @pl.when(near >= 2)
                def _():
                    src = ws[4].at[pl.ds(pl.multiple_of(near * rows - top, 128), rows)]
                    pltpu.make_async_copy(src, to, sem).start()

        for s in range(2):
            at = pl.multiple_of((core ^ s) * width, 128)
            pltpu.make_async_copy(
                xs[2 * r + s], x_buf.at[r, :, pl.ds(at, width)], x_sem.at[2 * r + s]
            ).start()
    acc = None
    for r in range(4):
        for m in range(4):
            pltpu.make_async_copy(
                ws[0].at[pl.ds(0, rows)], w_buf.at[r, pl.ds(0, rows)], w_sem.at[4 * r + m]
            ).wait()
        for s in range(2):
            pltpu.make_async_copy(
                xs[0], x_buf.at[r, :, pl.ds(0, width)], x_sem.at[2 * r + s]
            ).wait()
        term = jnp.dot(x_buf[r], w_buf[r], preferred_element_type=jnp.float32)
        acc = term if acc is None else acc + term
    o_buf[...] = acc.astype(jnp.bfloat16)
    half = keep_ref.shape[0]
    keep_ref[...] = o_buf[pl.ds(pl.multiple_of(core * half, 128), half)]
    give_ref[...] = o_buf[pl.ds(pl.multiple_of((1 - core) * half, 128), half)]


def out_project(ids, xs, ws):
    tokens, width = xs[0].shape
    depth, cols = ws[0].shape
    return pl.pallas_call(
        out_kernel,
        out_shape=(jax.ShapeDtypeStruct((tokens // 2, cols), jnp.bfloat16),) * 2,
        in_specs=[SMEM] + [HBM] * 13,
        out_specs=(VMEM, VMEM),
        scratch_shapes=[
            pltpu.VMEM((4, tokens, 2 * width), jnp.bfloat16),
            pltpu.VMEM((4, depth, cols), jnp.bfloat16),
            pltpu.VMEM((tokens, cols), jnp.bfloat16),
            pltpu.SemaphoreType.DMA((8,)),
            pltpu.SemaphoreType.DMA((16,)),
        ],
        compiler_params=pltpu.CompilerParams(vmem_limit_bytes=GRANT),
        cost_estimate=LITTLE,
        name="out_project",
    )(ids, *xs, *ws)


def per_device(
    stream,
    pending,
    norm_gain,
    w_query,
    w_key,
    w_value,
    w_out,
    prefix_keys,
    prefix_values,
    prefix_segments,
    stretch_segments,
    stretch_offset,
):
    tok, feat = stream.shape
    chip_tok = 2 * tok
    c = lax.axis_index("ctx")
    z = lax.axis_index("tp")
    chip, core = c // 2, c % 2
    first = core == 0
    depth = feat * N_TP

    wide = stream.astype(jnp.float32)
    here = jnp.stack([chip, core, z]).astype(jnp.int32)
    every = (0, 1, 2)

    gain = lax.dynamic_slice_in_dim(norm_gain, z * feat, feat, 0).astype(jnp.float32)
    scaled = (wide * gain[None, :]).astype(jnp.bfloat16)
    u1, d1 = hop_up(scaled, every), hop_down(scaled, every)

    labels = jnp.arange(NTRAJ, dtype=jnp.int32)
    counts = jnp.concatenate(
        [
            jnp.sum((prefix_segments[:, None] <= labels).astype(jnp.int32), axis=0),
            jnp.sum((stretch_segments[:, None] < labels).astype(jnp.int32), axis=0),
        ]
    )
    notes = jnp.concatenate([counts // 32, counts % 32])
    cols = w_query.shape[1] // 2
    notes = jnp.stack(
        [jnp.pad(v, (0, cols - v.shape[0])) for v in (stretch_segments, notes)]
        + [jnp.zeros((cols,), jnp.int32)] * 14
    ).astype(jnp.bfloat16)

    token_index = chip * chip_tok + jnp.arange(chip_tok, dtype=jnp.int32)
    positions = stretch_offset[0].astype(jnp.float32) + token_index.astype(jnp.float32)
    angles = positions[:, None] * inverse_freqs(HD)
    cosine, sinus = jnp.cos(angles), jnp.sin(angles)
    cosine = jnp.concatenate([cosine, cosine], axis=1)
    sinus = jnp.concatenate([-sinus, sinus], axis=1)

    def squares(part, place):
        g = lax.dynamic_slice_in_dim(norm_gain, place * feat, feat, 0).astype(jnp.float32)
        return jnp.sum(jnp.square(part.astype(jnp.float32) / g[None, :]), axis=1, keepdims=True)

    q_heads = w_query.shape[1] // HD // 2
    q_cols = q_heads * HD
    n_q = w_query.shape[0]
    fold = prefix_keys.shape[1] // 2
    n_both = n_q + fold
    n_kv = w_key.shape[0] // 2
    n_piece = w_out.shape[0] // 4

    def first_plan(at, src, out):
        w_q, w_k, w_v, keys, values, said = src
        for dst, j in ((out[0], at[1]), (out[1], 1 - at[1])):
            head = 2 * at[2] + j
            yield one(w_q.at[:, pl.ds(multiple(j, q_cols), q_cols)], dst.at[pl.ds(0, n_q)])
            for i, a in enumerate((keys, keys, values, values)):
                part = a.at[head, pl.ds((i % 2) * fold, fold)]
                yield one(part, dst.at[pl.ds(n_q, fold), pl.ds(i * HD, HD)])
            for i, a in enumerate((w_k, w_v, w_k, w_v)):
                part = a.at[pl.ds((i // 2) * n_kv, n_kv), pl.ds(multiple(head), HD)]
                yield one(part, dst.at[pl.ds(n_both, n_kv), pl.ds(i * HD, HD)])
            yield one(said, dst.at[pl.ds(n_both + n_kv, said.shape[0])])

    own, give = move(
        first_plan,
        ((n_both + n_kv + notes.shape[0], q_cols),) * 2,
        here,
        (w_query, w_key, w_value, prefix_keys, prefix_values, notes),
    )
    places = jnp.stack(
        [z, jnp.where(z < 2, z + 1, z - 1), jnp.where(z < 2, z + 2, z - 2), jnp.where(z % 2 == 1, 0, 3)]
    ).astype(jnp.int32)
    ids = jnp.concatenate([here, places])

    x1, y1, given = swap(own, 2), swap(own, 4), swap(give, 1)
    mine = squares(scaled, z)

    up, down = hops(here, pending, u1, d1, 3, (1, 2, 3), (), (cosine, sinus, mine, given))
    u2, d2 = hop_up(up, every), hop_down(down, every)

    given = gate(given, x1, y1)
    x2, y2 = swap(given, 2), swap(given, 4)

    def near_plan(at, src, out):
        yield one(src[0], out[0].at[pl.ds(0, tok)])
        yield ([(at[2] < 2, src[1]), (at[2] >= 2, src[2])], out[0].at[pl.ds(tok, tok)])

    (near,) = move(near_plan, ((chip_tok, feat),), here, (scaled, d1, u1), (up,))
    over1 = swap(near, 1)
    mine = mine + squares(near[tok:], places[1])
    theirs = squares(over1[:tok], z) + squares(over1[tok:], places[1])

    up, down = hops(here, pending, u2, d2, 2, (2,), (1,))
    turn = swap(gate(notes, x2, y2), 1)
    u3, d3 = hop_up(gate(up, turn), every), hop_down(gate(down, turn), every)

    x1, y2 = gate(x1, x2, y2), gate(y2, x2)
    far_own, far_other = swap(x1, 4), swap(y2, 2)
    def piece_plan(at, src, out):
        for r, dst in enumerate(out):
            rows = pl.ds(multiple(at[0] ^ r, n_piece), n_piece)
            for i in range(2):
                part = src[0].at[rows, pl.ds(i * q_cols, q_cols)]
                yield one(part, dst.at[pl.ds(i * n_piece, n_piece)])

    by_chip = move(piece_plan, ((2 * n_piece, q_cols),) * 4, here, (w_out,), (up,))
    second = pick(z, (d2, d2, u2, u2), here, (up, by_chip[0]))
    over2 = swap(second, 1)
    mine = mine + squares(second, places[2])
    up, down = hops(here, pending, u3, d3, 1, (), (1, 2, 3))
    u4, d4 = hop_up(up, every), hop_down(down, every)
    third = pick(z, (d3, u1, d1, u3), here, (up, mine, theirs))
    over3 = swap(third, 1)

    mine = mine + squares(third, places[3])
    theirs = theirs + squares(over2, places[2]) + squares(over3, places[3])
    total = jnp.where(first, jnp.concatenate([mine, theirs]), jnp.concatenate([theirs, mine]))
    factor = lax.rsqrt(total * (1.0 / depth) + NORM_EPSILON)
    factor = jnp.broadcast_to(factor, (chip_tok, 128))
    xs = [near, over1, near, over1, second, over2, third, over3]
    own_rows = (own, given, x1, x2, y1, y2, far_own, far_other)

    said = [rows[n_both + n_kv : n_both + n_kv + 2].astype(jnp.float32) for rows in own_rows]
    total = sum(v[1, : 4 * NTRAJ] for v in said).astype(jnp.int32)
    total = total[: 2 * NTRAJ] * 32 + total[2 * NTRAJ :]
    segs = [v[0, :tok].astype(jnp.int32) for v in said[:2]]
    segs = jnp.where(first, jnp.concatenate(segs), jnp.concatenate(segs[::-1]))
    onehot = (segs[:, None] == labels).astype(jnp.int32)
    n_tok = jnp.sum(onehot * total[:NTRAJ], axis=1)
    lo_tok = jnp.sum(onehot * total[NTRAJ:], axis=1) - chip * chip_tok + tok
    blocked = n_tok.reshape(chip_tok // BT, BT)
    bounds = jnp.stack([blocked[:, 0], blocked[:, -1]])
    n_wide = jnp.broadcast_to(n_tok[:, None], (chip_tok, 128))
    lo_wide = jnp.broadcast_to(lo_tok[:, None], (chip_tok, 128))

    def prefix_plan(at, src, out):
        for m in range(4):
            for j in range(2):
                start = ((at[0] ^ m) * 2 + (at[1] ^ j)) * 2 * fold
                rows = src[2 * m + j]
                for i in range(4):
                    dst = out[0].at[i // 2, pl.ds(pl.multiple_of(start + (i % 2) * fold, 128), fold)]
                    yield one(rows.at[pl.ds(n_q, fold), pl.ds(i * HD, HD)], dst)

    (kv,) = move(prefix_plan, ((2, N_CTX * 2 * fold, HD),), here, own_rows, (third,))

    by_chip = (by_chip[0],) + tuple(
        swap(gate(by_chip[r], far_own, far_other, over2), 2 * r) for r in (1, 2, 3)
    )
    scale = math.log2(math.e) / math.sqrt(HD)
    q, kv_new = project(ids, xs, own_rows, n_both, factor, cosine, sinus, scale)
    before = lax.ppermute(kv_new[:, tok:], "ctx", [(i, i + 2) for i in range(N_CTX - 2)])

    def pieces_plan(at, src, out):
        for r, dst in enumerate(out):
            near = (at[2] ^ r) ^ at[0]
            yield ([(near == m, src[m]) for m in range(4)], dst)

    pieces = list(move(pieces_plan, ((2 * n_piece, q_cols),) * 4, here, by_chip, (q, u4, d4)))
    for r in (1, 2, 3):
        pieces[r] = lax.ppermute(pieces[r], "tp", [(i, i ^ r) for i in range(N_TP)])
    k_near = jnp.concatenate([before[0], kv_new[0]], axis=0)
    v_near = jnp.concatenate([before[1], kv_new[1]], axis=0)
    attended = attend(bounds, q, n_wide, lo_wide, kv, k_near, v_near, (pieces[0],))

    def block_plan(at, src, out):
        for r, part in enumerate(src):
            for i in range(2):
                dst = out[0].at[pl.ds(r * n_piece, n_piece), pl.ds(i * q_cols, q_cols)]
                yield one(part.at[pl.ds(i * n_piece, n_piece)], dst)

    (block,) = move(block_plan, ((4 * n_piece, 2 * q_cols),), here, pieces, (attended,))
    half = block.shape[0] // 2
    wo_x, wo_y = swap(block, 2), swap(block, 4)
    u1, d1 = hop_up(attended, every), hop_down(attended, every)
    near = pick(z, (d1, d1, u1, u1), here)

    def far_plan(at, src, out):
        yield one(src[0].at[pl.ds(0, half)], out[0])
        yield one(src[1].at[pl.ds(half, half)], out[1])

    to_y, to_x = move(
        far_plan, ((half, block.shape[1]),) * 2, here, (wo_x, wo_y), (near, u4, d4)
    )
    wo_parts = (block, wo_x, wo_y, swap(to_y, 4), swap(to_x, 2))
    u2, d2 = hop_up(u1, (1, 2)), hop_down(d1, (1, 2))
    second = pick(z, (d2, d2, u2, u2), here)
    u3, d3 = hop_up(gate(u2, to_y), (2,)), hop_down(gate(d2, to_y), (2,))
    third = pick(z, (d3, u1, d1, u3), here)
    hs = []
    for part in (attended, near, second, third):
        hs += [part, swap(part, 1)]
    mine, theirs = out_project(ids, hs, wo_parts)
    theirs = swap(theirs, 1)
    head_share = jnp.where(
        first,
        jnp.concatenate([mine, theirs], axis=1),
        jnp.concatenate([theirs, mine], axis=1),
    ).astype(jnp.float32)
    pending_share = (
        lax.dynamic_slice_in_dim(pending[0], z * feat, feat, 1).astype(jnp.float32)
        + jnp.where(z == 0, 0, u4).astype(jnp.float32)
        + jnp.where(z == 3, 0, d4).astype(jnp.float32)
    )
    return (wide + (head_share + pending_share)).astype(jnp.bfloat16)


def solution(mesh):
    in_specs = (
        P("ctx", "tp"),
        P("tp", "ctx", None),
        P(),
        P("ctx", "tp"),
        P("ctx", None),
        P("ctx", None),
        P("tp", "ctx"),
        P(None, "ctx", None),
        P(None, "ctx", None),
        P("ctx"),
        P("ctx"),
        P(),
    )
    out_specs = P("ctx", "tp")
    small = mesh.shape["ctx"] == N_CTX and mesh.shape["tp"] == N_TP
    return jax.shard_map(
        per_device if small else per_device_any,
        mesh=mesh,
        in_specs=in_specs,
        out_specs=out_specs,
        check_vma=False,
    )
```

```python
import functools
import math

import jax
import jax.numpy as jnp
from jax import lax
from jax.experimental import pallas as pl
from jax.experimental.pallas import tpu as pltpu
from jax.sharding import PartitionSpec as P

HQ = 32
KVH = 8
HD = 128
NTRAJ = 16


ROPE_BASE = 500000.0
ROPE_FACTOR = 8.0
LOW_FREQ = 1.0
HIGH_FREQ = 4.0
INITIAL_SPAN = 8192.0
NORM_EPSILON = 1e-05
MASKED = -1e30


def inverse_freqs(head_width):
    pair_index = jnp.arange(head_width // 2, dtype=jnp.float32)
    base_freq = ROPE_BASE ** (-2.0 * pair_index / head_width)
    wavelength = 2.0 * math.pi / base_freq
    smooth = (INITIAL_SPAN / wavelength - LOW_FREQ) / (HIGH_FREQ - LOW_FREQ)
    blended = (1.0 - smooth) * base_freq / ROPE_FACTOR + smooth * base_freq
    return jnp.where(
        wavelength < INITIAL_SPAN / HIGH_FREQ,
        base_freq,
        jnp.where(wavelength > INITIAL_SPAN / LOW_FREQ, base_freq / ROPE_FACTOR, blended),
    )


def rotate(vectors, positions):
    head_width = vectors.shape[-1]
    angles = positions[..., None] * inverse_freqs(head_width)
    cosine = jnp.cos(angles)
    sinus = jnp.sin(angles)
    first_half = vectors[..., : head_width // 2]
    second_half = vectors[..., head_width // 2 :]
    return jnp.concatenate(
        [first_half * cosine - second_half * sinus, second_half * cosine + first_half * sinus],
        axis=-1,
    )


def visibility(key_labels, is_prefix, key_pos, query_segs, query_index):
    earlier = key_labels[None, :] <= query_segs[:, None]
    same = (key_labels[None, :] == query_segs[:, None]) & (key_pos[None, :] <= query_index[:, None])
    return jnp.where(is_prefix[None, :], earlier, same)


def attend_whole(grouped, key_block, value_block, seen):
    scores = jnp.einsum("hrd,hnd->hrn", grouped, key_block, preferred_element_type=jnp.float32) * (
        1.0 / math.sqrt(HD)
    )
    scores = jnp.where(seen[None], scores, MASKED)
    new_max = jnp.max(scores, axis=2)
    weights = jnp.where(seen[None], jnp.exp(scores - new_max[..., None]), 0.0)
    totals = jnp.sum(weights, axis=2)
    numerator = jnp.einsum(
        "hrn,hnd->hrd",
        weights.astype(jnp.bfloat16),
        value_block,
        preferred_element_type=jnp.float32,
    )
    return numerator / totals[..., None]


def per_device_any(
    stream,
    pending,
    norm_gain,
    w_query,
    w_key,
    w_value,
    w_out,
    prefix_keys,
    prefix_values,
    prefix_segments,
    stretch_segments,
    stretch_offset,
):
    tok_rows = stream.shape[0]
    prefix_rows = prefix_keys.shape[1]
    ctx_index = lax.axis_index("ctx")
    tp_index = lax.axis_index("tp")
    gain_wide = norm_gain.astype(jnp.float32)
    whole = lax.all_gather(stream, "tp", axis=1, tiled=True).astype(jnp.float32)
    mean_square = jnp.mean(whole * whole, axis=1, keepdims=True)
    normed = (whole * lax.rsqrt(mean_square + NORM_EPSILON) * gain_wide).astype(jnp.bfloat16)
    q_cols = w_query.shape[1]
    q_heads = q_cols // HD
    full_group = HQ // KVH
    kv_heads = max(1, q_heads // full_group)
    group_size = q_heads // kv_heads
    head_start = tp_index * q_heads // full_group
    kv_cols = kv_heads * HD
    key_slice = lax.dynamic_slice_in_dim(w_key, head_start * HD, kv_cols, 1)
    value_slice = lax.dynamic_slice_in_dim(w_value, head_start * HD, kv_cols, 1)
    pieces = (
        lax.all_gather(w_query, "ctx", axis=0, tiled=True),
        lax.all_gather(key_slice, "ctx", axis=0, tiled=True),
        lax.all_gather(value_slice, "ctx", axis=0, tiled=True),
    )
    query_raw, key_full, value_full = tuple(
        (jnp.dot(normed, piece_rows, preferred_element_type=jnp.float32) for piece_rows in pieces)
    )
    token_index = ctx_index * tok_rows + jnp.arange(tok_rows, dtype=jnp.int32)
    positions = stretch_offset[0].astype(jnp.float32) + token_index.astype(jnp.float32)
    query_rows = rotate(query_raw.reshape(tok_rows, q_heads, HD), positions[:, None]).astype(
        jnp.bfloat16
    )
    new_keys = jnp.transpose(
        rotate(key_full.reshape(tok_rows, kv_heads, HD), positions[:, None]).astype(jnp.bfloat16),
        (1, 0, 2),
    )
    new_values = jnp.transpose(
        value_full.astype(jnp.bfloat16).reshape(tok_rows, kv_heads, HD), (1, 0, 2)
    )
    old_keys = lax.dynamic_slice_in_dim(prefix_keys, head_start, kv_heads, 0)
    old_values = lax.dynamic_slice_in_dim(prefix_values, head_start, kv_heads, 0)
    local_keys = jnp.concatenate([old_keys, new_keys], 1)
    local_values = jnp.concatenate([old_values, new_values], 1)
    key_labels = jnp.concatenate([prefix_segments, stretch_segments])
    key_span = prefix_rows + tok_rows
    grouped = jnp.transpose(
        query_rows.reshape(tok_rows, kv_heads, group_size, HD), (1, 0, 2, 3)
    ).reshape(kv_heads, tok_rows * group_size, HD)
    query_index = jnp.repeat(token_index, group_size)
    query_segs = jnp.repeat(stretch_segments, group_size)
    both = jnp.stack([local_keys, local_values])
    kv_block = lax.all_gather(both, "ctx", axis=2, tiled=True)
    label_block = lax.all_gather(key_labels[None, None, :], "ctx", axis=2, tiled=True)
    key_count = kv_block.shape[2]
    absolute = jnp.arange(key_count, dtype=jnp.int32)
    within = absolute % key_span
    key_pos = absolute // key_span * tok_rows + within - prefix_rows
    seen = visibility(label_block[0, 0], within < prefix_rows, key_pos, query_segs, query_index)
    attended_heads = attend_whole(grouped, kv_block[0], kv_block[1], seen).astype(jnp.bfloat16)
    attended = jnp.transpose(
        attended_heads.reshape(kv_heads, tok_rows, group_size, HD), (1, 0, 2, 3)
    ).reshape(tok_rows, q_cols)
    head_terms = jnp.dot(
        attended,
        lax.all_gather(w_out, "ctx", axis=1, tiled=True),
        preferred_element_type=jnp.float32,
    )
    head_share, pending_share = (
        lax.psum_scatter(
            head_terms.astype(jnp.bfloat16), "tp", scatter_dimension=1, tiled=True
        ).astype(jnp.float32),
        lax.psum_scatter(
            pending[0].astype(jnp.float32).astype(jnp.bfloat16),
            "tp",
            scatter_dimension=1,
            tiled=True,
        ).astype(jnp.float32),
    )
    block_share = head_share + pending_share
    return (stream.astype(jnp.float32) + block_share).astype(jnp.bfloat16)


N_CTX = 8
N_TP = 4
GRANT = 60 * 1024 * 1024


def swap(x, bit):
    return lax.ppermute(x, "ctx", [(c, c ^ bit) for c in range(N_CTX)])


def hop_up(v, pairs):
    return lax.ppermute(v, "tp", [(i, i + 1) for i in pairs])


def hop_down(v, pairs):
    return lax.ppermute(v, "tp", [(N_TP - 1 - i, N_TP - 2 - i) for i in pairs])


def rotated(v, cosine, sinus):
    return v * cosine + pltpu.roll(v, HD // 2, 1) * sinus


HBM = pl.BlockSpec(memory_space=pltpu.HBM)
VMEM = pl.BlockSpec(memory_space=pltpu.VMEM)
SMEM = pl.BlockSpec(memory_space=pltpu.SMEM)
ANY = pl.BlockSpec(memory_space=pl.ANY)
LITTLE = pl.CostEstimate(flops=0, bytes_accessed=1024, transcendentals=0)


def specs_of(arrays):
    return [HBM if a.size > 200000 else ANY for a in arrays]


def move(plan, shapes, ids, sources, arrived=()):
    count = len(sources)

    def kernel(ids_ref, *refs):
        outs, sems = refs[count + len(arrived) : -1], refs[-1]
        waits = []
        for at, (choices, dst) in enumerate(plan(ids_ref, refs[:count], outs)):
            for cond, src in choices:
                copy = pltpu.make_async_copy(src, dst, sems.at[at])
                if cond is None:
                    copy.start()
                else:
                    pl.when(cond)(copy.start)
            waits.append(copy)
        for copy in waits:
            copy.wait()

    return pl.pallas_call(
        kernel,
        out_shape=tuple(jax.ShapeDtypeStruct(shape, jnp.bfloat16) for shape in shapes),
        in_specs=[SMEM] + [HBM] * count + specs_of(arrived),
        out_specs=tuple(VMEM for _ in shapes),
        scratch_shapes=[pltpu.SemaphoreType.DMA((40,))],
        compiler_params=pltpu.CompilerParams(vmem_limit_bytes=GRANT),
        cost_estimate=LITTLE,
        name=plan.__name__,
    )(ids, *sources, *arrived)


def gate(x, *arrived):
    return pl.pallas_call(
        lambda *refs: None,
        out_shape=jax.ShapeDtypeStruct(x.shape, x.dtype),
        in_specs=[HBM] + specs_of(arrived),
        out_specs=HBM,
        input_output_aliases={0: 0},
        compiler_params=pltpu.CompilerParams(vmem_limit_bytes=GRANT),
        cost_estimate=LITTLE,
        name="gate",
    )(x, *arrived)


def pick(z, options, ids, arrived=()):
    distinct = list({id(o): o for o in options}.values())

    def pick_plan(at, src, out):
        yield (
            [(at[2] == i, src[[o is d for d in distinct].index(True)]) for i, o in enumerate(options)],
            out[0],
        )

    return move(pick_plan, (options[0].shape,), ids, distinct, arrived)[0]


def hops(ids, pending, up, down, offset, relay, both, arrived=()):
    tok, feat = up.shape

    def kernel(ids_ref, pending_ref, up_ref, down_ref, *refs):
        out_up, out_down, buf, sems = refs[len(arrived) :]
        z = ids_ref[2]
        todo = []
        for i, (src, out, step, at) in enumerate(
            ((up_ref, out_up, offset, z), (down_ref, out_down, -offset, N_TP - 1 - z))
        ):
            is_relay = functools.reduce(jnp.logical_or, [at == p for p in relay], at < 0)
            is_both = functools.reduce(jnp.logical_or, [at == p for p in both], at < 0)
            place = jnp.clip(z + step, 0, N_TP - 1)
            share = pltpu.make_async_copy(
                pending_ref.at[0, :, pl.ds(multiple(place, feat), feat)], out, sems.at[i]
            )
            passed = pltpu.make_async_copy(src, out, sems.at[i])
            added = pltpu.make_async_copy(src, buf.at[i], sems.at[2 + i])
            pl.when(is_relay)(passed.start)
            pl.when(jnp.logical_not(is_relay))(share.start)
            pl.when(is_both)(added.start)
            todo.append((passed, added, is_both, out, i))
        for passed, added, is_both, out, i in todo:
            passed.wait()

            @pl.when(is_both)
            def _():
                added.wait()
                out[...] += buf[i]

    shape = jax.ShapeDtypeStruct((tok, feat), jnp.bfloat16)
    return pl.pallas_call(
        kernel,
        out_shape=(shape, shape),
        in_specs=[SMEM, HBM, HBM, HBM] + specs_of(arrived),
        out_specs=(VMEM, VMEM),
        scratch_shapes=[
            pltpu.VMEM((2, tok, feat), jnp.bfloat16),
            pltpu.SemaphoreType.DMA((4,)),
        ],
        compiler_params=pltpu.CompilerParams(vmem_limit_bytes=GRANT),
        cost_estimate=LITTLE,
        name="hops",
    )(ids, pending, up, down, *arrived)


def one(src, dst):
    return ([(None, src)], dst)


def multiple(value, of=128):
    return pl.multiple_of(value * of, of)


AHEAD = 3


def part_choices(r, z):
    return (
        [(None, 0, 0)],
        [(None, 0, 1)],
        [(None, 1, 0)],
        [(z == 0, 3, 0), (z == 3, 2, 0), ((z == 1) | (z == 2), 0, 2)],
    )[r]


def project_kernel(scale, at_kv, ids_ref, *refs):
    xs, ws = refs[:8], refs[8:16]
    factor_ref, cos_ref, sin_ref, q_ref, kv_ref, x_buf, w_buf, x_sem, w_sem = refs[16:]
    chip, core, z = ids_ref[0], ids_ref[1], ids_ref[2]
    tok, half, cols = xs[7].shape[0], x_buf.shape[-1], ws[0].shape[1]
    fold = half // 2
    mine = pl.multiple_of(core * tok, 128)
    theirs = pl.multiple_of((1 - core) * tok, 128)

    def fetch(at):
        r, h = at // 2, at % 2
        place = ids_ref[3 + r]
        waits = []
        for i in range(3):
            for m in range(4):
                src, dst = ws[2 * m + h], w_buf.at[at]
                if i == 0:
                    src, dst = src.at[pl.ds(0, half)], dst.at[:, pl.ds(0, cols)]
                else:
                    lanes = pl.ds((i - 1) * 2 * HD, 2 * HD)
                    src = src.at[pl.ds(at_kv, fold), lanes]
                    dst = dst.at[pl.ds((i - 1) * fold, fold), pl.ds(cols, 2 * HD)]
                copy = pltpu.make_async_copy(src, dst, w_sem.at[3 * at + i])
                pl.when((place ^ chip) == m)(copy.start)
            waits.append(copy)
        features = pl.ds(pl.multiple_of((core ^ h) * half, 128), half)
        for s, rows in ((0, mine), (1, theirs)):
            for cond, index, group in part_choices(r, z):
                src = xs[2 * index + s].at[pl.ds(group * tok, tok), features]
                copy = pltpu.make_async_copy(
                    src, x_buf.at[at, pl.ds(rows, tok)], x_sem.at[2 * at + s]
                )
                if cond is None:
                    copy.start()
                else:
                    pl.when(cond)(copy.start)
            waits.append(copy)
        return waits

    ahead = [fetch(at) for at in range(AHEAD)]
    acc = 0.0
    for at in range(8):
        for copy in ahead[at]:
            copy.wait()
        if at + AHEAD < 8:
            ahead.append(fetch(at + AHEAD))
        acc = acc + jnp.dot(x_buf[at], w_buf[at], preferred_element_type=jnp.float32)
    factor = factor_ref[...]
    heads = q_ref.shape[0]
    for h in range(heads + 2):
        v = acc[:, h * HD : (h + 1) * HD] * factor
        if h <= heads:
            v = rotated(v, cos_ref[...], sin_ref[...])
        if h < heads:
            q_ref[h] = (v * scale).astype(jnp.bfloat16)
        else:
            kv_ref[h - heads] = v.astype(jnp.bfloat16)


def project(ids, xs, weights, at_kv, factor, cosine, sinus, scale):
    tok, feat = xs[7].shape
    cols = weights[0].shape[1]
    half = feat // 2
    return pl.pallas_call(
        functools.partial(project_kernel, scale, at_kv),
        out_shape=(
            jax.ShapeDtypeStruct((cols // HD, 2 * tok, HD), jnp.bfloat16),
            jax.ShapeDtypeStruct((2, 2 * tok, HD), jnp.bfloat16),
        ),
        in_specs=[SMEM] + [HBM] * 16 + [VMEM] * 3,
        out_specs=(VMEM, VMEM),
        scratch_shapes=[
            pltpu.VMEM((8, 2 * tok, half), jnp.bfloat16),
            pltpu.VMEM((8, half, cols + 2 * HD), jnp.bfloat16),
            pltpu.SemaphoreType.DMA((16,)),
            pltpu.SemaphoreType.DMA((24,)),
        ],
        compiler_params=pltpu.CompilerParams(vmem_limit_bytes=GRANT),
        cost_estimate=LITTLE,
        name="project",
    )(ids, *xs, *weights, factor, cosine, sinus)


BT = 256
BK = 1024
CHAIN = 2


def scores(q, k):
    return lax.dot_general(q, k, (((1,), (1,)), ((), ())), preferred_element_type=jnp.float32)


def absorb(s, v_ext, m, acc):
    new = jnp.maximum(m, jnp.max(s, axis=1, keepdims=True))
    p = jnp.exp2(s - new).astype(jnp.bfloat16)
    acc = acc * jnp.exp2(m - new) + jnp.dot(p, v_ext, preferred_element_type=jnp.float32)
    return new, acc


def attend_kernel(halo, at_old, bound_ref, ids_ref, q_ref, n_ref, lo_ref, k_ref, v_ref, *refs):
    bundles, (out_ref, k_old, v_ext, s_ref, m_ref, acc_ref, sems) = refs[:8], refs[-7:]
    b = pl.program_id(0)
    heads, bt = q_ref.shape[0], q_ref.shape[1]
    rows, chains = CHAIN * bt, heads // CHAIN
    last = k_old.shape[0] // BK - 1
    fold = k_old.shape[0] // (2 * N_CTX)

    @pl.when(b == 0)
    def _():
        copies = []
        for index, bundle in enumerate(bundles):
            place = ((ids_ref[0] ^ (index // 2)) * 2 + (ids_ref[1] ^ (index % 2))) * 2 * fold
            for i in range(4):
                dst = (k_old, v_ext)[i // 2]
                to = pl.ds(pl.multiple_of(place + (i % 2) * fold, 128), fold)
                copies.append(
                    pltpu.make_async_copy(
                        bundle.at[pl.ds(at_old, fold), pl.ds(i * HD, HD)],
                        dst.at[to, pl.ds(0, HD)],
                        sems.at[4 * index + i],
                    )
                )
        for copy in copies:
            copy.start()
        v_ext[:, HD:] = jnp.ones((v_ext.shape[0], HD), jnp.bfloat16)
        for copy in copies:
            copy.wait()

    m_ref[...] = jnp.full_like(m_ref, MASKED)
    acc_ref[...] = jnp.zeros_like(acc_ref)

    def query(g):
        return q_ref[g * CHAIN : (g + 1) * CHAIN].reshape(rows, HD)

    s_ref[...] = scores(query(0), k_old[:BK, :])

    def body(kb, masked):
        start = pl.multiple_of(kb * BK, BK)
        follow = pl.multiple_of(jnp.minimum(kb + 1, last) * BK, BK)
        ms = [m_ref[g][:, :1] for g in range(chains)]
        accs = [acc_ref[g] for g in range(chains)]
        s = s_ref[...]
        v = v_ext[pl.ds(start, BK), :]
        for g in range(chains):
            at, who = (start, g + 1) if g + 1 < chains else (follow, 0)
            ahead = scores(query(who), k_old[pl.ds(at, BK), :])
            if masked:
                n_rows = jnp.concatenate([n_ref[:, :1]] * CHAIN, axis=0)
                col = lax.broadcasted_iota(jnp.int32, s.shape, 1) + start
                s = jnp.where(col < n_rows, s, MASKED)
            ms[g], accs[g] = absorb(s, v, ms[g], accs[g])
            s = ahead
        s_ref[...] = s
        for g in range(chains):
            m_ref[g] = jnp.broadcast_to(ms[g], (rows, 128))
            acc_ref[g] = accs[g]

    full = bound_ref[0, b] // BK
    some = (bound_ref[1, b] + BK - 1) // BK
    lax.fori_loop(0, full, lambda kb, c: (body(kb, False), c)[1], 0)
    lax.fori_loop(full, some, lambda kb, c: (body(kb, True), c)[1], 0)

    span = halo + bt
    start = pl.multiple_of(b * bt, bt)
    k = k_ref[pl.ds(start, span), :]
    v = v_ref[pl.ds(start, span), :]
    v = jnp.concatenate([v, jnp.ones_like(v)], axis=1)
    lo = jnp.concatenate([lo_ref[:, :1]] * CHAIN, axis=0)
    col = lax.broadcasted_iota(jnp.int32, (rows, span), 1)
    row = lax.broadcasted_iota(jnp.int32, (rows, span), 0) % bt
    seen = (col + start >= lo) & (col <= row + halo)
    for g in range(chains):
        s = jnp.where(seen, scores(query(g), k), MASKED)
        _, acc = absorb(s, v, m_ref[g][:, :1], acc_ref[g])
        mixed = (acc[:, :HD] / acc[:, HD:]).astype(jnp.bfloat16)
        for h in range(CHAIN):
            at = (g * CHAIN + h) * HD
            out_ref[:, at : at + HD] = mixed[h * bt : (h + 1) * bt]


def attend(bounds, ids, q, n_tok, lo_tok, k, v, bundles, at_old, keys, arrived=()):
    heads, tokens = q.shape[:2]
    chains, rows = heads // CHAIN, CHAIN * BT
    halo = k.shape[0] - tokens
    return pl.pallas_call(
        functools.partial(attend_kernel, halo, at_old),
        out_shape=jax.ShapeDtypeStruct((tokens, heads * HD), jnp.bfloat16),
        grid_spec=pltpu.PrefetchScalarGridSpec(
            num_scalar_prefetch=2,
            grid=(tokens // BT,),
            in_specs=[
                pl.BlockSpec((heads, BT, HD), lambda b, *_: (0, b, 0)),
                pl.BlockSpec((BT, 128), lambda b, *_: (b, 0)),
                pl.BlockSpec((BT, 128), lambda b, *_: (b, 0)),
                pl.BlockSpec(k.shape, lambda b, *_: (0, 0)),
                pl.BlockSpec(v.shape, lambda b, *_: (0, 0)),
            ]
            + [HBM] * 8
            + specs_of(arrived),
            out_specs=pl.BlockSpec((BT, heads * HD), lambda b, *_: (b, 0)),
            scratch_shapes=[
                pltpu.VMEM((keys, HD), jnp.bfloat16),
                pltpu.VMEM((keys, 2 * HD), jnp.bfloat16),
                pltpu.VMEM((rows, BK), jnp.float32),
                pltpu.VMEM((chains, rows, 128), jnp.float32),
                pltpu.VMEM((chains, rows, 2 * HD), jnp.float32),
                pltpu.SemaphoreType.DMA((32,)),
            ],
        ),
        compiler_params=pltpu.CompilerParams(vmem_limit_bytes=GRANT),
        cost_estimate=LITTLE,
        name="attend",
    )(bounds, ids, q, n_tok, lo_tok, k, v, *bundles, *arrived)


def out_kernel(ids_ref, *refs):
    xs, ws = refs[:8], refs[8:16]
    keep_ref, give_ref, x_buf, w_buf, o_buf, x_sem, w_sem = refs[16:]
    chip, core, z = ids_ref[0], ids_ref[1], ids_ref[2]
    width = xs[0].shape[1]
    rows = w_buf.shape[1] // 4
    for r in range(4):
        near = ids_ref[3 + r] ^ z
        for m in range(4):
            to = w_buf.at[r, pl.ds(pl.multiple_of((chip ^ m) * rows, 128), rows)]
            for i in range(2):
                src = ws[2 * m + i].at[pl.ds(pl.multiple_of((near % 2) * rows, 128), rows)]
                copy = pltpu.make_async_copy(src, to, w_sem.at[4 * r + m])
                pl.when(near // 2 == i)(copy.start)
        for s in range(2):
            at = pl.multiple_of((core ^ s) * width, 128)
            pltpu.make_async_copy(
                xs[2 * r + s], x_buf.at[r, :, pl.ds(at, width)], x_sem.at[2 * r + s]
            ).start()
    acc = None
    for r in range(4):
        for m in range(4):
            pltpu.make_async_copy(
                ws[0].at[pl.ds(0, rows)], w_buf.at[r, pl.ds(0, rows)], w_sem.at[4 * r + m]
            ).wait()
        for s in range(2):
            pltpu.make_async_copy(
                xs[0], x_buf.at[r, :, pl.ds(0, width)], x_sem.at[2 * r + s]
            ).wait()
        term = jnp.dot(x_buf[r], w_buf[r], preferred_element_type=jnp.float32)
        acc = term if acc is None else acc + term
    o_buf[...] = acc.astype(jnp.bfloat16)
    half = keep_ref.shape[0]
    keep_ref[...] = o_buf[pl.ds(pl.multiple_of(core * half, 128), half)]
    give_ref[...] = o_buf[pl.ds(pl.multiple_of((1 - core) * half, 128), half)]


def out_project(ids, xs, ws):
    tokens, width = xs[0].shape
    depth, cols = 2 * ws[0].shape[0], ws[0].shape[1]
    return pl.pallas_call(
        out_kernel,
        out_shape=(jax.ShapeDtypeStruct((tokens // 2, cols), jnp.bfloat16),) * 2,
        in_specs=[SMEM] + [HBM] * 16,
        out_specs=(VMEM, VMEM),
        scratch_shapes=[
            pltpu.VMEM((4, tokens, 2 * width), jnp.bfloat16),
            pltpu.VMEM((4, depth, cols), jnp.bfloat16),
            pltpu.VMEM((tokens, cols), jnp.bfloat16),
            pltpu.SemaphoreType.DMA((8,)),
            pltpu.SemaphoreType.DMA((16,)),
        ],
        compiler_params=pltpu.CompilerParams(vmem_limit_bytes=GRANT),
        cost_estimate=LITTLE,
        name="out_project",
    )(ids, *xs, *ws)


def per_device(
    stream,
    pending,
    norm_gain,
    w_query,
    w_key,
    w_value,
    w_out,
    prefix_keys,
    prefix_values,
    prefix_segments,
    stretch_segments,
    stretch_offset,
):
    tok, feat = stream.shape
    chip_tok = 2 * tok
    c = lax.axis_index("ctx")
    z = lax.axis_index("tp")
    chip, core = c // 2, c % 2
    first = core == 0
    depth = feat * N_TP

    wide = stream.astype(jnp.float32)
    here = jnp.stack([chip, core, z]).astype(jnp.int32)
    every = (0, 1, 2)

    gain = lax.dynamic_slice_in_dim(norm_gain, z * feat, feat, 0).astype(jnp.float32)
    scaled = (wide * gain[None, :]).astype(jnp.bfloat16)

    labels = jnp.arange(NTRAJ, dtype=jnp.int32)
    counts = jnp.concatenate(
        [
            jnp.sum((prefix_segments[:, None] <= labels).astype(jnp.int32), axis=0),
            jnp.sum((stretch_segments[:, None] < labels).astype(jnp.int32), axis=0),
        ]
    )
    notes = jnp.concatenate([counts // 32, counts % 32])
    cols = w_query.shape[1] // 2
    notes = jnp.stack(
        [jnp.pad(v, (0, cols - v.shape[0])) for v in (stretch_segments, notes)]
        + [jnp.zeros((cols,), jnp.int32)] * 14
    ).astype(jnp.bfloat16)

    token_index = chip * chip_tok + jnp.arange(chip_tok, dtype=jnp.int32)
    positions = stretch_offset[0].astype(jnp.float32) + token_index.astype(jnp.float32)
    angles = positions[:, None] * inverse_freqs(HD)
    cosine, sinus = jnp.cos(angles), jnp.sin(angles)
    cosine = jnp.concatenate([cosine, cosine], axis=1)
    sinus = jnp.concatenate([-sinus, sinus], axis=1)

    def squares(part, place):
        g = lax.dynamic_slice_in_dim(norm_gain, place * feat, feat, 0).astype(jnp.float32)
        return jnp.sum(jnp.square(part.astype(jnp.float32) / g[None, :]), axis=1, keepdims=True)

    q_heads = w_query.shape[1] // HD // 2
    q_cols = q_heads * HD
    n_q = w_query.shape[0]
    fold = prefix_keys.shape[1] // 2
    n_both = n_q + fold
    n_kv = w_key.shape[0] // 2
    n_piece = w_out.shape[0] // 4

    def first_plan(at, src, out):
        w_q, w_k, w_v, keys, values, said = src
        for dst, j in ((out[0], at[1]), (out[1], 1 - at[1])):
            head = 2 * at[2] + j
            yield one(w_q.at[:, pl.ds(multiple(j, q_cols), q_cols)], dst.at[pl.ds(0, n_q)])
            for i, a in enumerate((keys, keys, values, values)):
                part = a.at[head, pl.ds((i % 2) * fold, fold)]
                yield one(part, dst.at[pl.ds(n_q, fold), pl.ds(i * HD, HD)])
            for i, a in enumerate((w_k, w_v, w_k, w_v)):
                part = a.at[pl.ds((i // 2) * n_kv, n_kv), pl.ds(multiple(head), HD)]
                yield one(part, dst.at[pl.ds(n_both, n_kv), pl.ds(i * HD, HD)])
            yield one(said, dst.at[pl.ds(n_both + n_kv, said.shape[0])])

    own, give = move(
        first_plan,
        ((n_both + n_kv + notes.shape[0], q_cols),) * 2,
        here,
        (w_query, w_key, w_value, prefix_keys, prefix_values, notes),
    )
    places = jnp.stack(
        [z, jnp.where(z < 2, z + 1, z - 1), jnp.where(z < 2, z + 2, z - 2), jnp.where(z % 2 == 1, 0, 3)]
    ).astype(jnp.int32)
    ids = jnp.concatenate([here, places])

    x1, y1, given = swap(own, 2), swap(own, 4), swap(give, 1)
    turn = swap(gate(notes, own), 1)
    scaled = gate(scaled, turn)
    u1, d1 = hop_up(scaled, every), hop_down(scaled, every)
    mine = squares(scaled, z)

    def piece_plan(at, src, out):
        for r, dst in enumerate(out):
            rows = pl.ds(multiple(at[0] ^ r, n_piece), n_piece)
            for i in range(2):
                part = src[0].at[rows, pl.ds(i * q_cols, q_cols)]
                yield one(part, dst.at[pl.ds(i * n_piece, n_piece)])

    by_chip = move(
        piece_plan,
        ((2 * n_piece, q_cols),) * 4,
        here,
        (w_out,),
        (own,),
    )
    up, down = hops(here, pending, u1, d1, 3, (1, 2, 3), (), (cosine, sinus, mine, given, by_chip[0]))
    u2, d2 = hop_up(up, every), hop_down(down, every)

    def near_plan(at, src, out):
        own_part, up_part, down_part = src
        low = at[2] < 2
        high = at[2] >= 2
        yield one(own_part, out[0].at[pl.ds(0, tok)])
        yield ([(low, down_part), (high, up_part)], out[0].at[pl.ds(tok, tok)])
        yield ([(low, up_part), (high, down_part)], out[0].at[pl.ds(2 * tok, tok)])

    (near,) = move(near_plan, ((3 * tok, feat),), here, (scaled, u1, d1), (up,))
    given = gate(given, x1, y1, near)
    x2, y2 = swap(given, 2), swap(given, 4)
    over1 = swap(near, 1)
    mine = mine + squares(near[tok : 2 * tok], places[1])
    theirs = squares(over1[:tok], z) + squares(over1[tok : 2 * tok], places[1])
    mine_near = squares(near[2 * tok :], places[3])
    theirs_near = squares(over1[2 * tok :], places[3])

    up, down = hops(here, pending, u2, d2, 2, (2,), (1,))
    second = pick(z, (d2, d2, u2, u2), here, (up,))
    u3, d3 = hop_up(gate(up, second), every), hop_down(gate(down, second), every)
    x1, y2 = gate(x1, x2, y2), gate(y2, x2)
    far_own, far_other = swap(x1, 4), swap(y2, 2)

    over2 = swap(second, 1)
    mine = mine + squares(second, places[2])
    theirs = theirs + squares(over2, places[2])

    su3, sd3 = swap(u3, 1), swap(d3, 1)
    up, down = hops(here, pending, u3, d3, 1, (), (1, 2, 3), (over2, mine, theirs))
    u4, d4 = hop_up(up, every), hop_down(down, every)
    mine = mine + jnp.where(
        z == 0, squares(d3, places[3]), jnp.where(z == 3, squares(u3, places[3]), mine_near)
    )
    theirs = theirs + jnp.where(
        z == 0, squares(sd3, places[3]), jnp.where(z == 3, squares(su3, places[3]), theirs_near)
    )
    total = jnp.where(first, jnp.concatenate([mine, theirs]), jnp.concatenate([theirs, mine]))
    factor = lax.rsqrt(total * (1.0 / depth) + NORM_EPSILON)
    factor = jnp.broadcast_to(factor, (chip_tok, 128))
    xs = [near, over1, second, over2, u3, su3, d3, sd3]
    own_rows = (own, given, x1, x2, y1, y2, far_own, far_other)

    said = [rows[n_both + n_kv : n_both + n_kv + 2].astype(jnp.float32) for rows in own_rows]
    total = sum(v[1, : 4 * NTRAJ] for v in said).astype(jnp.int32)
    total = total[: 2 * NTRAJ] * 32 + total[2 * NTRAJ :]
    segs = [v[0, :tok].astype(jnp.int32) for v in said[:2]]
    segs = jnp.where(first, jnp.concatenate(segs), jnp.concatenate(segs[::-1]))
    onehot = (segs[:, None] == labels).astype(jnp.int32)
    n_tok = jnp.sum(onehot * total[:NTRAJ], axis=1)
    lo_tok = jnp.sum(onehot * total[NTRAJ:], axis=1) - chip * chip_tok + tok
    blocked = n_tok.reshape(chip_tok // BT, BT)
    bounds = jnp.stack([blocked[:, 0], blocked[:, -1]])
    n_wide = jnp.broadcast_to(n_tok[:, None], (chip_tok, 128))
    lo_wide = jnp.broadcast_to(lo_tok[:, None], (chip_tok, 128))

    by_chip = (by_chip[0],) + tuple(
        swap(gate(by_chip[r], far_own, far_other), 2 * r) for r in (1, 2, 3)
    )
    scale = math.log2(math.e) / math.sqrt(HD)
    q, kv_new = project(ids, xs, own_rows, n_both, factor, cosine, sinus, scale)
    before = lax.ppermute(kv_new[:, tok:], "ctx", [(i, i + 2) for i in range(N_CTX - 2)])

    def pieces_plan(at, src, out):
        for r, dst in enumerate(out):
            near = (at[2] ^ r) ^ at[0]
            yield ([(near == m, src[m]) for m in range(4)], dst)

    pieces = list(move(pieces_plan, ((2 * n_piece, q_cols),) * 4, here, by_chip, (q, u4, d4)))
    for r in (1, 2, 3):
        pieces[r] = lax.ppermute(pieces[r], "tp", [(i, i ^ r) for i in range(N_TP)])
    k_near = jnp.concatenate([before[0], kv_new[0]], axis=0)
    v_near = jnp.concatenate([before[1], kv_new[1]], axis=0)
    attended = attend(
        bounds,
        here,
        q,
        n_wide,
        lo_wide,
        k_near,
        v_near,
        own_rows,
        n_q,
        N_CTX * prefix_keys.shape[1],
        (pieces[0],),
    )

    def block_plan(at, src, out):
        for r, part in enumerate(src):
            for i in range(2):
                dst = out[r // 2].at[pl.ds((r % 2) * n_piece, n_piece), pl.ds(i * q_cols, q_cols)]
                yield one(part.at[pl.ds(i * n_piece, n_piece)], dst)

    wo_a, wo_b = move(block_plan, ((2 * n_piece, 2 * q_cols),) * 2, here, pieces, (attended,))
    wo_xa, wo_yb = swap(wo_a, 2), swap(wo_b, 4)
    wo_xb, wo_ya = swap(wo_b, 2), swap(wo_a, 4)

    attended = gate(attended, *pieces[1:])
    u1, d1 = hop_up(attended, every), hop_down(attended, every)
    near = pick(z, (d1, d1, u1, u1), here)

    wo_parts = (wo_a, wo_b, wo_xa, wo_xb, wo_ya, wo_yb, swap(wo_xa, 4), swap(wo_yb, 2))
    u2, d2 = hop_up(gate(u1, wo_xa, wo_yb), (1, 2)), hop_down(gate(d1, wo_xa, wo_yb), (1, 2))
    second = pick(z, (d2, d2, u2, u2), here)
    u3, d3 = hop_up(gate(u2, wo_xb, wo_ya), (2,)), hop_down(gate(d2, wo_xb, wo_ya), (2,))
    third = pick(z, (d3, u1, d1, u3), here, wo_parts[6:])
    hs = []
    for part in (attended, near, second, third):
        hs += [part, swap(part, 1)]
    mine, theirs = out_project(ids, hs, wo_parts)
    theirs = swap(theirs, 1)
    head_share = jnp.where(
        first,
        jnp.concatenate([mine, theirs], axis=1),
        jnp.concatenate([theirs, mine], axis=1),
    ).astype(jnp.float32)
    pending_share = (
        lax.dynamic_slice_in_dim(pending[0], z * feat, feat, 1).astype(jnp.float32)
        + jnp.where(z == 0, 0, u4).astype(jnp.float32)
        + jnp.where(z == 3, 0, d4).astype(jnp.float32)
    )
    return (wide + (head_share + pending_share)).astype(jnp.bfloat16)


def solution(mesh):
    in_specs = (
        P("ctx", "tp"),
        P("tp", "ctx", None),
        P(),
        P("ctx", "tp"),
        P("ctx", None),
        P("ctx", None),
        P("tp", "ctx"),
        P(None, "ctx", None),
        P(None, "ctx", None),
        P("ctx"),
        P("ctx"),
        P(),
    )
    out_specs = P("ctx", "tp")
    small = mesh.shape["ctx"] == N_CTX and mesh.shape["tp"] == N_TP
    return jax.shard_map(
        per_device if small else per_device_any,
        mesh=mesh,
        in_specs=in_specs,
        out_specs=out_specs,
        check_vma=False,
    )
```

```python
import functools
import math

import jax
import jax.numpy as jnp
from jax import lax
from jax.experimental import pallas as pl
from jax.experimental.pallas import tpu as pltpu
from jax.sharding import PartitionSpec as P

HQ = 32
KVH = 8
HD = 128
NTRAJ = 16


ROPE_BASE = 500000.0
ROPE_FACTOR = 8.0
LOW_FREQ = 1.0
HIGH_FREQ = 4.0
INITIAL_SPAN = 8192.0
NORM_EPSILON = 1e-05
MASKED = -1e30


def inverse_freqs(head_width):
    pair_index = jnp.arange(head_width // 2, dtype=jnp.float32)
    base_freq = ROPE_BASE ** (-2.0 * pair_index / head_width)
    wavelength = 2.0 * math.pi / base_freq
    smooth = (INITIAL_SPAN / wavelength - LOW_FREQ) / (HIGH_FREQ - LOW_FREQ)
    blended = (1.0 - smooth) * base_freq / ROPE_FACTOR + smooth * base_freq
    return jnp.where(
        wavelength < INITIAL_SPAN / HIGH_FREQ,
        base_freq,
        jnp.where(wavelength > INITIAL_SPAN / LOW_FREQ, base_freq / ROPE_FACTOR, blended),
    )


def rotate(vectors, positions):
    head_width = vectors.shape[-1]
    angles = positions[..., None] * inverse_freqs(head_width)
    cosine = jnp.cos(angles)
    sinus = jnp.sin(angles)
    first_half = vectors[..., : head_width // 2]
    second_half = vectors[..., head_width // 2 :]
    return jnp.concatenate(
        [first_half * cosine - second_half * sinus, second_half * cosine + first_half * sinus],
        axis=-1,
    )


def visibility(key_labels, is_prefix, key_pos, query_segs, query_index):
    earlier = key_labels[None, :] <= query_segs[:, None]
    same = (key_labels[None, :] == query_segs[:, None]) & (key_pos[None, :] <= query_index[:, None])
    return jnp.where(is_prefix[None, :], earlier, same)


def attend_whole(grouped, key_block, value_block, seen):
    scores = jnp.einsum("hrd,hnd->hrn", grouped, key_block, preferred_element_type=jnp.float32) * (
        1.0 / math.sqrt(HD)
    )
    scores = jnp.where(seen[None], scores, MASKED)
    new_max = jnp.max(scores, axis=2)
    weights = jnp.where(seen[None], jnp.exp(scores - new_max[..., None]), 0.0)
    totals = jnp.sum(weights, axis=2)
    numerator = jnp.einsum(
        "hrn,hnd->hrd",
        weights.astype(jnp.bfloat16),
        value_block,
        preferred_element_type=jnp.float32,
    )
    return numerator / totals[..., None]


def per_device_any(
    stream,
    pending,
    norm_gain,
    w_query,
    w_key,
    w_value,
    w_out,
    prefix_keys,
    prefix_values,
    prefix_segments,
    stretch_segments,
    stretch_offset,
):
    tok_rows = stream.shape[0]
    prefix_rows = prefix_keys.shape[1]
    ctx_index = lax.axis_index("ctx")
    tp_index = lax.axis_index("tp")
    gain_wide = norm_gain.astype(jnp.float32)
    whole = lax.all_gather(stream, "tp", axis=1, tiled=True).astype(jnp.float32)
    mean_square = jnp.mean(whole * whole, axis=1, keepdims=True)
    normed = (whole * lax.rsqrt(mean_square + NORM_EPSILON) * gain_wide).astype(jnp.bfloat16)
    q_cols = w_query.shape[1]
    q_heads = q_cols // HD
    full_group = HQ // KVH
    kv_heads = max(1, q_heads // full_group)
    group_size = q_heads // kv_heads
    head_start = tp_index * q_heads // full_group
    kv_cols = kv_heads * HD
    key_slice = lax.dynamic_slice_in_dim(w_key, head_start * HD, kv_cols, 1)
    value_slice = lax.dynamic_slice_in_dim(w_value, head_start * HD, kv_cols, 1)
    pieces = (
        lax.all_gather(w_query, "ctx", axis=0, tiled=True),
        lax.all_gather(key_slice, "ctx", axis=0, tiled=True),
        lax.all_gather(value_slice, "ctx", axis=0, tiled=True),
    )
    query_raw, key_full, value_full = tuple(
        (jnp.dot(normed, piece_rows, preferred_element_type=jnp.float32) for piece_rows in pieces)
    )
    token_index = ctx_index * tok_rows + jnp.arange(tok_rows, dtype=jnp.int32)
    positions = stretch_offset[0].astype(jnp.float32) + token_index.astype(jnp.float32)
    query_rows = rotate(query_raw.reshape(tok_rows, q_heads, HD), positions[:, None]).astype(
        jnp.bfloat16
    )
    new_keys = jnp.transpose(
        rotate(key_full.reshape(tok_rows, kv_heads, HD), positions[:, None]).astype(jnp.bfloat16),
        (1, 0, 2),
    )
    new_values = jnp.transpose(
        value_full.astype(jnp.bfloat16).reshape(tok_rows, kv_heads, HD), (1, 0, 2)
    )
    old_keys = lax.dynamic_slice_in_dim(prefix_keys, head_start, kv_heads, 0)
    old_values = lax.dynamic_slice_in_dim(prefix_values, head_start, kv_heads, 0)
    local_keys = jnp.concatenate([old_keys, new_keys], 1)
    local_values = jnp.concatenate([old_values, new_values], 1)
    key_labels = jnp.concatenate([prefix_segments, stretch_segments])
    key_span = prefix_rows + tok_rows
    grouped = jnp.transpose(
        query_rows.reshape(tok_rows, kv_heads, group_size, HD), (1, 0, 2, 3)
    ).reshape(kv_heads, tok_rows * group_size, HD)
    query_index = jnp.repeat(token_index, group_size)
    query_segs = jnp.repeat(stretch_segments, group_size)
    both = jnp.stack([local_keys, local_values])
    kv_block = lax.all_gather(both, "ctx", axis=2, tiled=True)
    label_block = lax.all_gather(key_labels[None, None, :], "ctx", axis=2, tiled=True)
    key_count = kv_block.shape[2]
    absolute = jnp.arange(key_count, dtype=jnp.int32)
    within = absolute % key_span
    key_pos = absolute // key_span * tok_rows + within - prefix_rows
    seen = visibility(label_block[0, 0], within < prefix_rows, key_pos, query_segs, query_index)
    attended_heads = attend_whole(grouped, kv_block[0], kv_block[1], seen).astype(jnp.bfloat16)
    attended = jnp.transpose(
        attended_heads.reshape(kv_heads, tok_rows, group_size, HD), (1, 0, 2, 3)
    ).reshape(tok_rows, q_cols)
    head_terms = jnp.dot(
        attended,
        lax.all_gather(w_out, "ctx", axis=1, tiled=True),
        preferred_element_type=jnp.float32,
    )
    head_share, pending_share = (
        lax.psum_scatter(
            head_terms.astype(jnp.bfloat16), "tp", scatter_dimension=1, tiled=True
        ).astype(jnp.float32),
        lax.psum_scatter(
            pending[0].astype(jnp.float32).astype(jnp.bfloat16),
            "tp",
            scatter_dimension=1,
            tiled=True,
        ).astype(jnp.float32),
    )
    block_share = head_share + pending_share
    return (stream.astype(jnp.float32) + block_share).astype(jnp.bfloat16)


N_CTX = 8
N_TP = 4
GRANT = 60 * 1024 * 1024


def swap(x, bit):
    return lax.ppermute(x, "ctx", [(c, c ^ bit) for c in range(N_CTX)])


def hop_up(v, pairs):
    return lax.ppermute(v, "tp", [(i, i + 1) for i in pairs])


def hop_down(v, pairs):
    return lax.ppermute(v, "tp", [(N_TP - 1 - i, N_TP - 2 - i) for i in pairs])


def rotated(v, cosine, sinus):
    return v * cosine + pltpu.roll(v, HD // 2, 1) * sinus


HBM = pl.BlockSpec(memory_space=pltpu.HBM)
VMEM = pl.BlockSpec(memory_space=pltpu.VMEM)
SMEM = pl.BlockSpec(memory_space=pltpu.SMEM)
ANY = pl.BlockSpec(memory_space=pl.ANY)
LITTLE = pl.CostEstimate(flops=0, bytes_accessed=1024, transcendentals=0)


def specs_of(arrays):
    return [HBM if a.size > 200000 else ANY for a in arrays]


def move(plan, shapes, ids, sources, arrived=()):
    count = len(sources)

    def kernel(ids_ref, *refs):
        outs, sems = refs[count + len(arrived) : -1], refs[-1]
        waits = []
        for at, (choices, dst) in enumerate(plan(ids_ref, refs[:count], outs)):
            for cond, src in choices:
                copy = pltpu.make_async_copy(src, dst, sems.at[at])
                if cond is None:
                    copy.start()
                else:
                    pl.when(cond)(copy.start)
            waits.append(copy)
        for copy in waits:
            copy.wait()

    return pl.pallas_call(
        kernel,
        out_shape=tuple(jax.ShapeDtypeStruct(shape, jnp.bfloat16) for shape in shapes),
        in_specs=[SMEM] + [HBM] * count + specs_of(arrived),
        out_specs=tuple(VMEM for _ in shapes),
        scratch_shapes=[pltpu.SemaphoreType.DMA((40,))],
        compiler_params=pltpu.CompilerParams(vmem_limit_bytes=GRANT),
        cost_estimate=LITTLE,
        name=plan.__name__,
    )(ids, *sources, *arrived)


def gate(x, *arrived):
    return pl.pallas_call(
        lambda *refs: None,
        out_shape=jax.ShapeDtypeStruct(x.shape, x.dtype),
        in_specs=[HBM] + specs_of(arrived),
        out_specs=HBM,
        input_output_aliases={0: 0},
        compiler_params=pltpu.CompilerParams(vmem_limit_bytes=GRANT),
        cost_estimate=LITTLE,
        name="gate",
    )(x, *arrived)


def pick(z, options, ids, arrived=()):
    distinct = list({id(o): o for o in options}.values())

    def pick_plan(at, src, out):
        yield (
            [(at[2] == i, src[[o is d for d in distinct].index(True)]) for i, o in enumerate(options)],
            out[0],
        )

    return move(pick_plan, (options[0].shape,), ids, distinct, arrived)[0]


def hops(ids, pending, up, down, offset, relay, both, rows, arrived=()):
    tok, feat = pending.shape[1], up.shape[1]

    def kernel(ids_ref, pending_ref, up_ref, down_ref, *refs):
        out_up, out_down, buf, sems = refs[len(arrived) :]
        z = ids_ref[2]
        todo = []
        for i, (src, out, step, at) in enumerate(
            ((up_ref, out_up, offset, z), (down_ref, out_down, -offset, N_TP - 1 - z))
        ):
            is_relay = functools.reduce(jnp.logical_or, [at == p for p in relay], at < 0)
            is_both = functools.reduce(jnp.logical_or, [at == p for p in both], at < 0)
            place = jnp.clip(z + step, 0, N_TP - 1)
            share = pltpu.make_async_copy(
                pending_ref.at[0, :, pl.ds(multiple(place, feat), feat)],
                out.at[pl.ds(0, tok)],
                sems.at[i],
            )
            passed = pltpu.make_async_copy(src.at[pl.ds(0, rows)], out, sems.at[i])
            added = pltpu.make_async_copy(src.at[pl.ds(0, tok)], buf.at[i], sems.at[2 + i])
            pl.when(is_relay)(passed.start)

            @pl.when(jnp.logical_not(is_relay))
            def _():
                if rows > tok:
                    out[tok:] = jnp.zeros((rows - tok, feat), jnp.bfloat16)
                share.start()

            pl.when(is_both)(added.start)
            todo.append((passed, share, added, is_relay, is_both, out, i))
        for passed, share, added, is_relay, is_both, out, i in todo:
            pl.when(is_relay)(passed.wait)
            pl.when(jnp.logical_not(is_relay))(share.wait)

            @pl.when(is_both)
            def _():
                added.wait()
                out[:tok] += buf[i]

    shape = jax.ShapeDtypeStruct((rows, feat), jnp.bfloat16)
    return pl.pallas_call(
        kernel,
        out_shape=(shape, shape),
        in_specs=[SMEM, HBM, HBM, HBM] + specs_of(arrived),
        out_specs=(VMEM, VMEM),
        scratch_shapes=[
            pltpu.VMEM((2, tok, feat), jnp.bfloat16),
            pltpu.SemaphoreType.DMA((4,)),
        ],
        compiler_params=pltpu.CompilerParams(vmem_limit_bytes=GRANT),
        cost_estimate=LITTLE,
        name="hops",
    )(ids, pending, up, down, *arrived)


def one(src, dst):
    return ([(None, src)], dst)


def multiple(value, of=128):
    return pl.multiple_of(value * of, of)


AHEAD = 3
PARTS = ((0, 0), (0, 1), (1, 0), (2, 0))


def project_kernel(slots, x_count, w_count, tok, rows, scale, at_kv, ids_ref, *refs):
    last = scale is not None
    xs, ws, refs = refs[:x_count], refs[x_count : x_count + w_count], refs[x_count + w_count :]
    x_buf, w_buf, x_sem, w_sem = refs[-4:]
    chip, core = ids_ref[0], ids_ref[1]
    half, cols = x_buf.shape[-1], ws[0].shape[1]
    fold = half // 2
    mine = pl.multiple_of(core * tok, 128)
    theirs = pl.multiple_of((1 - core) * tok, 128)

    def fetch(at):
        part, h = ids_ref[7 + slots[at // 2]], at % 2
        place = ids_ref[3 + part]
        waits = []
        for i in range(3):
            for m in range(w_count // 2):
                src, dst = ws[2 * m + h], w_buf.at[at]
                if i == 0:
                    src, dst = src.at[pl.ds(0, half)], dst.at[:, pl.ds(0, cols)]
                else:
                    lanes = pl.ds((i - 1) * 2 * HD, 2 * HD)
                    src = src.at[pl.ds(at_kv, fold), lanes]
                    dst = dst.at[pl.ds((i - 1) * fold, fold), pl.ds(cols, 2 * HD)]
                copy = pltpu.make_async_copy(src, dst, w_sem.at[3 * at + i])
                pl.when((place ^ chip) == m)(copy.start)
            waits.append(copy)
        features = pl.ds(pl.multiple_of((core ^ h) * half, 128), half)
        for s, to in ((0, mine), (1, theirs)):
            for r, (index, group) in enumerate(PARTS):
                if 2 * index < x_count:
                    src = xs[2 * index + s].at[pl.ds(group * rows, tok), features]
                    dst = x_buf.at[at, pl.ds(to, tok)]
                    copy = pltpu.make_async_copy(src, dst, x_sem.at[2 * at + s])
                    pl.when(part == r)(copy.start)
            waits.append(copy)
        return waits

    ahead = [fetch(at) for at in range(AHEAD)]
    acc = refs[0][...] if last else 0.0
    for at in range(4):
        for copy in ahead[at]:
            copy.wait()
        if at + AHEAD < 4:
            ahead.append(fetch(at + AHEAD))
        acc = acc + jnp.dot(x_buf[at], w_buf[at], preferred_element_type=jnp.float32)
    if not last:
        refs[0][...] = acc
        return
    factor_ref, cos_ref, sin_ref, q_ref, kv_ref, tail_ref = refs[1:7]
    factor = factor_ref[...]
    heads = q_ref.shape[0]
    for h in range(heads + 2):
        v = acc[:, h * HD : (h + 1) * HD] * factor
        if h <= heads:
            v = rotated(v, cos_ref[...], sin_ref[...])
        if h < heads:
            q_ref[h] = (v * scale).astype(jnp.bfloat16)
        else:
            kv_ref[h - heads] = v.astype(jnp.bfloat16)
            tail_ref[h - heads] = v[tok:].astype(jnp.bfloat16)


def project(ids, slots, xs, weights, tok, at_kv, tables=(), scale=None):
    rows = xs[0].shape[0] // 2
    feat = xs[0].shape[1]
    cols = weights[0].shape[1]
    half = feat // 2
    sums = jax.ShapeDtypeStruct((2 * tok, cols + 2 * HD), jnp.float32)
    results = (
        jax.ShapeDtypeStruct((cols // HD, 2 * tok, HD), jnp.bfloat16),
        jax.ShapeDtypeStruct((2, 2 * tok, HD), jnp.bfloat16),
        jax.ShapeDtypeStruct((2, tok, HD), jnp.bfloat16),
    )
    return pl.pallas_call(
        functools.partial(
            project_kernel, slots, len(xs), len(weights), tok, rows, scale, at_kv
        ),
        out_shape=results if tables else sums,
        in_specs=[SMEM] + [HBM] * (len(xs) + len(weights)) + [VMEM] * len(tables),
        out_specs=(VMEM,) * 3 if tables else VMEM,
        scratch_shapes=[
            pltpu.VMEM((4, 2 * tok, half), jnp.bfloat16),
            pltpu.VMEM((4, half, cols + 2 * HD), jnp.bfloat16),
            pltpu.SemaphoreType.DMA((8,)),
            pltpu.SemaphoreType.DMA((12,)),
        ],
        compiler_params=pltpu.CompilerParams(vmem_limit_bytes=GRANT),
        cost_estimate=LITTLE,
        name="project",
    )(ids, *xs, *weights, *tables)


BT = 256
BK = 1024
CHAIN = 2


def scores(q, k):
    return lax.dot_general(q, k, (((1,), (1,)), ((), ())), preferred_element_type=jnp.float32)


def absorb(s, v_ext, m, acc):
    new = jnp.maximum(m, jnp.max(s, axis=1, keepdims=True))
    p = jnp.exp2(s - new).astype(jnp.bfloat16)
    acc = acc * jnp.exp2(m - new) + jnp.dot(p, v_ext, preferred_element_type=jnp.float32)
    return new, acc


def attend_kernel(at_old, bound_ref, ids_ref, q_ref, n_ref, lo_ref, before_ref, new_ref, *refs):
    bundles, (out_ref, k_old, v_ext, kv_near, s_ref, m_ref, acc_ref, sems) = refs[:8], refs[-8:]
    halo = before_ref.shape[1]
    b = pl.program_id(0)
    heads, bt = q_ref.shape[0], q_ref.shape[1]
    rows, chains = CHAIN * bt, heads // CHAIN
    last = k_old.shape[0] // BK - 1
    fold = k_old.shape[0] // (2 * N_CTX)

    @pl.when(b == 0)
    def _():
        copies = []
        for index, bundle in enumerate(bundles):
            place = ((ids_ref[0] ^ (index // 2)) * 2 + (ids_ref[1] ^ (index % 2))) * 2 * fold
            for i in range(4):
                dst = (k_old, v_ext)[i // 2]
                to = pl.ds(pl.multiple_of(place + (i % 2) * fold, 128), fold)
                copies.append(
                    pltpu.make_async_copy(
                        bundle.at[pl.ds(at_old, fold), pl.ds(i * HD, HD)],
                        dst.at[to, pl.ds(0, HD)],
                        sems.at[4 * index + i],
                    )
                )
        for copy in copies:
            copy.start()
        v_ext[:, HD:] = jnp.ones((v_ext.shape[0], HD), jnp.bfloat16)
        kv_near[:, :halo] = before_ref[...]
        kv_near[:, halo:] = new_ref[...]
        for copy in copies:
            copy.wait()

    m_ref[...] = jnp.full_like(m_ref, MASKED)
    acc_ref[...] = jnp.zeros_like(acc_ref)

    def query(g):
        return q_ref[g * CHAIN : (g + 1) * CHAIN].reshape(rows, HD)

    s_ref[...] = scores(query(0), k_old[:BK, :])

    def body(kb, masked):
        start = pl.multiple_of(kb * BK, BK)
        follow = pl.multiple_of(jnp.minimum(kb + 1, last) * BK, BK)
        ms = [m_ref[g][:, :1] for g in range(chains)]
        accs = [acc_ref[g] for g in range(chains)]
        s = s_ref[...]
        v = v_ext[pl.ds(start, BK), :]
        for g in range(chains):
            at, who = (start, g + 1) if g + 1 < chains else (follow, 0)
            ahead = scores(query(who), k_old[pl.ds(at, BK), :])
            if masked:
                n_rows = jnp.concatenate([n_ref[:, :1]] * CHAIN, axis=0)
                col = lax.broadcasted_iota(jnp.int32, s.shape, 1) + start
                s = jnp.where(col < n_rows, s, MASKED)
            ms[g], accs[g] = absorb(s, v, ms[g], accs[g])
            s = ahead
        s_ref[...] = s
        for g in range(chains):
            m_ref[g] = jnp.broadcast_to(ms[g], (rows, 128))
            acc_ref[g] = accs[g]

    full = bound_ref[0, b] // BK
    some = (bound_ref[1, b] + BK - 1) // BK
    lax.fori_loop(0, full, lambda kb, c: (body(kb, False), c)[1], 0)
    lax.fori_loop(full, some, lambda kb, c: (body(kb, True), c)[1], 0)

    span = halo + bt
    start = pl.multiple_of(b * bt, bt)
    k = kv_near[0, pl.ds(start, span), :]
    v = kv_near[1, pl.ds(start, span), :]
    v = jnp.concatenate([v, jnp.ones_like(v)], axis=1)
    lo = jnp.concatenate([lo_ref[:, :1]] * CHAIN, axis=0)
    col = lax.broadcasted_iota(jnp.int32, (rows, span), 1)
    row = lax.broadcasted_iota(jnp.int32, (rows, span), 0) % bt
    seen = (col + start >= lo) & (col <= row + halo)
    for g in range(chains):
        s = jnp.where(seen, scores(query(g), k), MASKED)
        _, acc = absorb(s, v, m_ref[g][:, :1], acc_ref[g])
        mixed = (acc[:, :HD] / acc[:, HD:]).astype(jnp.bfloat16)
        for h in range(CHAIN):
            at = (g * CHAIN + h) * HD
            out_ref[:, at : at + HD] = mixed[h * bt : (h + 1) * bt]


def attend(bounds, ids, q, n_tok, lo_tok, before, new, bundles, at_old, keys, arrived=()):
    heads, tokens = q.shape[:2]
    chains, rows = heads // CHAIN, CHAIN * BT
    halo = before.shape[1]
    return pl.pallas_call(
        functools.partial(attend_kernel, at_old),
        out_shape=jax.ShapeDtypeStruct((tokens, heads * HD), jnp.bfloat16),
        grid_spec=pltpu.PrefetchScalarGridSpec(
            num_scalar_prefetch=2,
            grid=(tokens // BT,),
            in_specs=[
                pl.BlockSpec((heads, BT, HD), lambda b, *_: (0, b, 0)),
                pl.BlockSpec((BT, 128), lambda b, *_: (b, 0)),
                pl.BlockSpec((BT, 128), lambda b, *_: (b, 0)),
                pl.BlockSpec(before.shape, lambda b, *_: (0, 0, 0)),
                pl.BlockSpec(new.shape, lambda b, *_: (0, 0, 0)),
            ]
            + [HBM] * 8
            + specs_of(arrived),
            out_specs=pl.BlockSpec((BT, heads * HD), lambda b, *_: (b, 0)),
            scratch_shapes=[
                pltpu.VMEM((keys, HD), jnp.bfloat16),
                pltpu.VMEM((keys, 2 * HD), jnp.bfloat16),
                pltpu.VMEM((2, halo + tokens, HD), jnp.bfloat16),
                pltpu.VMEM((rows, BK), jnp.float32),
                pltpu.VMEM((chains, rows, 128), jnp.float32),
                pltpu.VMEM((chains, rows, 2 * HD), jnp.float32),
                pltpu.SemaphoreType.DMA((32,)),
            ],
        ),
        compiler_params=pltpu.CompilerParams(vmem_limit_bytes=GRANT),
        cost_estimate=LITTLE,
        name="attend",
    )(bounds, ids, q, n_tok, lo_tok, before, new, *bundles, *arrived)


def out_kernel(ids_ref, *refs):
    xs, ws = refs[:8], refs[8:16]
    keep_ref, give_ref, x_buf, w_buf, o_buf, x_sem, w_sem = refs[16:]
    chip, core, z = ids_ref[0], ids_ref[1], ids_ref[2]
    width = xs[0].shape[1]
    rows = w_buf.shape[1] // 4
    for r in range(4):
        near = ids_ref[3 + r] ^ z
        for m in range(4):
            to = w_buf.at[r, pl.ds(pl.multiple_of((chip ^ m) * rows, 128), rows)]
            for i in range(2):
                src = ws[2 * m + i].at[pl.ds(pl.multiple_of((near % 2) * rows, 128), rows)]
                copy = pltpu.make_async_copy(src, to, w_sem.at[4 * r + m])
                pl.when(near // 2 == i)(copy.start)
        for s in range(2):
            at = pl.multiple_of((core ^ s) * width, 128)
            pltpu.make_async_copy(
                xs[2 * r + s], x_buf.at[r, :, pl.ds(at, width)], x_sem.at[2 * r + s]
            ).start()
    acc = None
    for r in range(4):
        for m in range(4):
            pltpu.make_async_copy(
                ws[0].at[pl.ds(0, rows)], w_buf.at[r, pl.ds(0, rows)], w_sem.at[4 * r + m]
            ).wait()
        for s in range(2):
            pltpu.make_async_copy(
                xs[0], x_buf.at[r, :, pl.ds(0, width)], x_sem.at[2 * r + s]
            ).wait()
        term = jnp.dot(x_buf[r], w_buf[r], preferred_element_type=jnp.float32)
        acc = term if acc is None else acc + term
    o_buf[...] = acc.astype(jnp.bfloat16)
    half = keep_ref.shape[0]
    keep_ref[...] = o_buf[pl.ds(pl.multiple_of(core * half, 128), half)]
    give_ref[...] = o_buf[pl.ds(pl.multiple_of((1 - core) * half, 128), half)]


def out_project(ids, xs, ws):
    tokens, width = xs[0].shape
    depth, cols = 2 * ws[0].shape[0], ws[0].shape[1]
    return pl.pallas_call(
        out_kernel,
        out_shape=(jax.ShapeDtypeStruct((tokens // 2, cols), jnp.bfloat16),) * 2,
        in_specs=[SMEM] + [HBM] * 16,
        out_specs=(VMEM, VMEM),
        scratch_shapes=[
            pltpu.VMEM((4, tokens, 2 * width), jnp.bfloat16),
            pltpu.VMEM((4, depth, cols), jnp.bfloat16),
            pltpu.VMEM((tokens, cols), jnp.bfloat16),
            pltpu.SemaphoreType.DMA((8,)),
            pltpu.SemaphoreType.DMA((16,)),
        ],
        compiler_params=pltpu.CompilerParams(vmem_limit_bytes=GRANT),
        cost_estimate=LITTLE,
        name="out_project",
    )(ids, *xs, *ws)


def per_device(
    stream,
    pending,
    norm_gain,
    w_query,
    w_key,
    w_value,
    w_out,
    prefix_keys,
    prefix_values,
    prefix_segments,
    stretch_segments,
    stretch_offset,
):
    tok, feat = stream.shape
    chip_tok = 2 * tok
    c = lax.axis_index("ctx")
    z = lax.axis_index("tp")
    chip, core = c // 2, c % 2
    first = core == 0
    depth = feat * N_TP

    wide = stream.astype(jnp.float32)
    here = jnp.stack([chip, core, z]).astype(jnp.int32)
    every = (0, 1, 2)

    gain = lax.dynamic_slice_in_dim(norm_gain, z * feat, feat, 0).astype(jnp.float32)
    scaled = (wide * gain[None, :]).astype(jnp.bfloat16)

    left = jnp.sum(wide * wide, axis=1)
    sums = []
    for _ in range(3):
        sums.append(lax.reduce_precision(left, 8, 7))
        left = left - sums[-1]
    sums = jnp.pad(jnp.stack(sums), ((0, 13), (0, feat - tok))).astype(jnp.bfloat16)
    scaled = jnp.concatenate([scaled, sums], axis=0)
    n_rows = scaled.shape[0]

    def squares(part, group=0):
        at = group * n_rows + tok
        return jnp.sum(part[at : at + 3, :tok].astype(jnp.float32), axis=0)


    labels = jnp.arange(NTRAJ, dtype=jnp.int32)
    counts = jnp.concatenate(
        [
            jnp.sum((prefix_segments[:, None] <= labels).astype(jnp.int32), axis=0),
            jnp.sum((stretch_segments[:, None] < labels).astype(jnp.int32), axis=0),
        ]
    )
    notes = jnp.concatenate([counts // 32, counts % 32])
    cols = w_query.shape[1] // 2
    notes = jnp.stack(
        [jnp.pad(v, (0, cols - v.shape[0])) for v in (stretch_segments, notes)]
        + [jnp.zeros((cols,), jnp.int32)] * 14
    ).astype(jnp.bfloat16)

    token_index = chip * chip_tok + jnp.arange(chip_tok, dtype=jnp.int32)
    positions = stretch_offset[0].astype(jnp.float32) + token_index.astype(jnp.float32)
    angles = positions[:, None] * inverse_freqs(HD)
    cosine, sinus = jnp.cos(angles), jnp.sin(angles)
    cosine = jnp.concatenate([cosine, cosine], axis=1)
    sinus = jnp.concatenate([-sinus, sinus], axis=1)

    q_heads = w_query.shape[1] // HD // 2
    q_cols = q_heads * HD
    n_q = w_query.shape[0]
    fold = prefix_keys.shape[1] // 2
    n_both = n_q + fold
    n_kv = w_key.shape[0] // 2
    n_piece = w_out.shape[0] // 4

    def first_plan(at, src, out):
        w_q, w_k, w_v, keys, values, said = src
        for dst, j in ((out[0], at[1]), (out[1], 1 - at[1])):
            head = 2 * at[2] + j
            yield one(w_q.at[:, pl.ds(multiple(j, q_cols), q_cols)], dst.at[pl.ds(0, n_q)])
            for i, a in enumerate((keys, keys, values, values)):
                part = a.at[head, pl.ds((i % 2) * fold, fold)]
                yield one(part, dst.at[pl.ds(n_q, fold), pl.ds(i * HD, HD)])
            for i, a in enumerate((w_k, w_v, w_k, w_v)):
                part = a.at[pl.ds((i // 2) * n_kv, n_kv), pl.ds(multiple(head), HD)]
                yield one(part, dst.at[pl.ds(n_both, n_kv), pl.ds(i * HD, HD)])
            yield one(said, dst.at[pl.ds(n_both + n_kv, said.shape[0])])

    own, give = move(
        first_plan,
        ((n_both + n_kv + notes.shape[0], q_cols),) * 2,
        here,
        (w_query, w_key, w_value, prefix_keys, prefix_values, notes),
    )
    places = jnp.stack(
        [z, jnp.where(z < 2, z + 1, z - 1), jnp.where(z < 2, z + 2, z - 2), jnp.where(z % 2 == 1, 0, 3)]
    ).astype(jnp.int32)
    skip = jnp.sum(jnp.where(places == (chip ^ 3), jnp.arange(N_TP), 0))
    order = jnp.stack(
        [
            jnp.where(skip == 0, 1, 0),
            jnp.where(skip < 2, 2, 1),
            jnp.minimum(skip, 2),
            jnp.full((), 3),
        ]
    )
    ids = jnp.concatenate([here, places, order]).astype(jnp.int32)

    x1, y1, given = swap(own, 2), swap(own, 4), swap(give, 1)
    turn = swap(gate(notes, own), 1)
    scaled = gate(scaled, turn)
    u1, d1 = hop_up(scaled, every), hop_down(scaled, every)

    def piece_plan(at, src, out):
        for r, dst in enumerate(out):
            rows = pl.ds(multiple(at[0] ^ r, n_piece), n_piece)
            for i in range(2):
                part = src[0].at[rows, pl.ds(i * q_cols, q_cols)]
                yield one(part, dst.at[pl.ds(i * n_piece, n_piece)])

    by_chip = move(
        piece_plan,
        ((2 * n_piece, q_cols),) * 4,
        here,
        (w_out,),
        (own,),
    )
    given = gate(given, x1, y1)
    up, down = hops(here, pending, u1, d1, 3, (1, 2, 3), (), n_rows, (cosine, sinus, given))
    u2, d2 = hop_up(up, every), hop_down(down, every)
    x2, y2 = swap(given, 2), swap(given, 4)

    def near_plan(at, src, out):
        own_part, up_part, down_part = src
        yield one(own_part, out[0].at[pl.ds(0, n_rows)])
        near = [(at[2] < 2, down_part), (at[2] >= 2, up_part)]
        yield (near, out[0].at[pl.ds(n_rows, n_rows)])

    (near,) = move(near_plan, ((2 * n_rows, feat),), here, (scaled, u1, d1), (by_chip[0],))
    near = gate(near, x1, y1)
    over1 = swap(near, 1)

    up, down = hops(here, pending, u2, d2, 2, (2,), (1,), n_rows)
    u3, d3 = hop_up(gate(up, x2), every), hop_down(gate(down, y2), every)
    x1, y2 = gate(x1, x2, y2), gate(y2, x2)
    far_own, far_other = swap(x1, 4), swap(y2, 2)
    second = pick(z, (d2, d2, u2, u2), here)
    over2 = swap(second, 1)
    own_rows = (own, given, x1, x2, y1, y2, far_own, far_other)
    xs = [near, over1, second, over2]
    sums = project(ids, (0, 1), xs, own_rows[:6], tok, n_both)

    third = pick(z, (d3, u1, d1, u3), here, (sums, far_own, far_other))
    over3 = swap(third, 1)
    up, down = hops(here, pending, u3, d3, 1, (), (1, 2, 3), tok, (third,))
    u4, d4 = hop_up(up, every), hop_down(down, every)
    mine, theirs = (
        squares(a) + squares(a, 1) + squares(b) + squares(c)
        for a, b, c in ((near, second, third), (over1, over2, over3))
    )
    total = jnp.where(first, jnp.concatenate([mine, theirs]), jnp.concatenate([theirs, mine]))
    factor = lax.rsqrt(total * (1.0 / depth) + NORM_EPSILON)
    factor = jnp.broadcast_to(factor[:, None], (chip_tok, 128))
    xs += [third, over3]

    said = [rows[n_both + n_kv : n_both + n_kv + 2].astype(jnp.float32) for rows in own_rows]
    total = sum(v[1, : 4 * NTRAJ] for v in said).astype(jnp.int32)
    total = total[: 2 * NTRAJ] * 32 + total[2 * NTRAJ :]
    segs = [v[0, :tok].astype(jnp.int32) for v in said[:2]]
    segs = jnp.where(first, jnp.concatenate(segs), jnp.concatenate(segs[::-1]))
    onehot = (segs[:, None] == labels).astype(jnp.int32)
    n_tok = jnp.sum(onehot * total[:NTRAJ], axis=1)
    lo_tok = jnp.sum(onehot * total[NTRAJ:], axis=1) - chip * chip_tok + tok
    blocked = n_tok.reshape(chip_tok // BT, BT)
    bounds = jnp.stack([blocked[:, 0], blocked[:, -1]])
    n_wide = jnp.broadcast_to(n_tok[:, None], (chip_tok, 128))
    lo_wide = jnp.broadcast_to(lo_tok[:, None], (chip_tok, 128))

    by_chip = (by_chip[0],) + tuple(
        swap(gate(by_chip[r], far_own, far_other), 2 * r) for r in (1, 2, 3)
    )
    scale = math.log2(math.e) / math.sqrt(HD)
    q, kv_new, tail = project(
        ids, (2, 3), xs, own_rows, tok, n_both, (sums, factor, cosine, sinus), scale
    )
    before = lax.ppermute(tail, "ctx", [(i, i + 2) for i in range(N_CTX - 2)])

    def pieces_plan(at, src, out):
        for r, dst in enumerate(out):
            near = (at[2] ^ r) ^ at[0]
            yield ([(near == m, src[m]) for m in range(4)], dst)

    pieces = list(move(pieces_plan, ((2 * n_piece, q_cols),) * 4, here, by_chip, (q,)))
    for r in (1, 2, 3):
        pieces[r] = lax.ppermute(pieces[r], "tp", [(i, i ^ r) for i in range(N_TP)])
    attended = attend(
        bounds,
        here,
        q,
        n_wide,
        lo_wide,
        before,
        kv_new,
        own_rows,
        n_q,
        N_CTX * prefix_keys.shape[1],
        (pieces[0],),
    )

    def block_plan(at, src, out):
        for r, part in enumerate(src):
            for i in range(2):
                dst = out[r // 2].at[pl.ds((r % 2) * n_piece, n_piece), pl.ds(i * q_cols, q_cols)]
                yield one(part.at[pl.ds(i * n_piece, n_piece)], dst)

    wo_a, wo_b = move(block_plan, ((2 * n_piece, 2 * q_cols),) * 2, here, pieces, (attended,))
    wo_xa, wo_yb = swap(wo_a, 2), swap(wo_b, 4)
    wo_xb, wo_ya = swap(wo_b, 2), swap(wo_a, 4)

    attended = gate(attended, u4, d4, *pieces[1:])
    u1, d1 = hop_up(attended, every), hop_down(attended, every)
    near = pick(z, (d1, d1, u1, u1), here)

    wo_parts = (wo_a, wo_b, wo_xa, wo_xb, wo_ya, wo_yb, swap(wo_xa, 4), swap(wo_yb, 2))
    u2, d2 = hop_up(gate(u1, wo_xa, wo_yb), (1, 2)), hop_down(gate(d1, wo_xa, wo_yb), (1, 2))
    second = pick(z, (d2, d2, u2, u2), here)
    u3, d3 = hop_up(gate(u2, wo_xb, wo_ya), (2,)), hop_down(gate(d2, wo_xb, wo_ya), (2,))
    third = pick(z, (d3, u1, d1, u3), here, wo_parts[6:])
    hs = []
    for part in (attended, near, second, third):
        hs += [part, swap(part, 1)]
    mine, theirs = out_project(ids, hs, wo_parts)
    theirs = swap(theirs, 1)
    head_share = jnp.where(
        first,
        jnp.concatenate([mine, theirs], axis=1),
        jnp.concatenate([theirs, mine], axis=1),
    ).astype(jnp.float32)
    pending_share = (
        lax.dynamic_slice_in_dim(pending[0], z * feat, feat, 1).astype(jnp.float32)
        + jnp.where(z == 0, 0, u4).astype(jnp.float32)
        + jnp.where(z == 3, 0, d4).astype(jnp.float32)
    )
    return (wide + (head_share + pending_share)).astype(jnp.bfloat16)


def solution(mesh):
    in_specs = (
        P("ctx", "tp"),
        P("tp", "ctx", None),
        P(),
        P("ctx", "tp"),
        P("ctx", None),
        P("ctx", None),
        P("tp", "ctx"),
        P(None, "ctx", None),
        P(None, "ctx", None),
        P("ctx"),
        P("ctx"),
        P(),
    )
    out_specs = P("ctx", "tp")
    small = mesh.shape["ctx"] == N_CTX and mesh.shape["tp"] == N_TP
    return jax.shard_map(
        per_device if small else per_device_any,
        mesh=mesh,
        in_specs=in_specs,
        out_specs=out_specs,
        check_vma=False,
    )
```

```python
import functools
import math

import jax
import jax.numpy as jnp
from jax import lax
from jax.experimental import pallas as pl
from jax.experimental.pallas import tpu as pltpu
from jax.sharding import PartitionSpec as P

HQ = 32
KVH = 8
HD = 128
NTRAJ = 16


ROPE_BASE = 500000.0
ROPE_FACTOR = 8.0
LOW_FREQ = 1.0
HIGH_FREQ = 4.0
INITIAL_SPAN = 8192.0
NORM_EPSILON = 1e-05
MASKED = -1e30


def inverse_freqs(head_width):
    pair_index = jnp.arange(head_width // 2, dtype=jnp.float32)
    base_freq = ROPE_BASE ** (-2.0 * pair_index / head_width)
    wavelength = 2.0 * math.pi / base_freq
    smooth = (INITIAL_SPAN / wavelength - LOW_FREQ) / (HIGH_FREQ - LOW_FREQ)
    blended = (1.0 - smooth) * base_freq / ROPE_FACTOR + smooth * base_freq
    return jnp.where(
        wavelength < INITIAL_SPAN / HIGH_FREQ,
        base_freq,
        jnp.where(wavelength > INITIAL_SPAN / LOW_FREQ, base_freq / ROPE_FACTOR, blended),
    )


def rotate(vectors, positions):
    head_width = vectors.shape[-1]
    angles = positions[..., None] * inverse_freqs(head_width)
    cosine = jnp.cos(angles)
    sinus = jnp.sin(angles)
    first_half = vectors[..., : head_width // 2]
    second_half = vectors[..., head_width // 2 :]
    return jnp.concatenate(
        [first_half * cosine - second_half * sinus, second_half * cosine + first_half * sinus],
        axis=-1,
    )


def visibility(key_labels, is_prefix, key_pos, query_segs, query_index):
    earlier = key_labels[None, :] <= query_segs[:, None]
    same = (key_labels[None, :] == query_segs[:, None]) & (key_pos[None, :] <= query_index[:, None])
    return jnp.where(is_prefix[None, :], earlier, same)


def attend_whole(grouped, key_block, value_block, seen):
    scores = jnp.einsum("hrd,hnd->hrn", grouped, key_block, preferred_element_type=jnp.float32) * (
        1.0 / math.sqrt(HD)
    )
    scores = jnp.where(seen[None], scores, MASKED)
    new_max = jnp.max(scores, axis=2)
    weights = jnp.where(seen[None], jnp.exp(scores - new_max[..., None]), 0.0)
    totals = jnp.sum(weights, axis=2)
    numerator = jnp.einsum(
        "hrn,hnd->hrd",
        weights.astype(jnp.bfloat16),
        value_block,
        preferred_element_type=jnp.float32,
    )
    return numerator / totals[..., None]


def per_device_any(
    stream,
    pending,
    norm_gain,
    w_query,
    w_key,
    w_value,
    w_out,
    prefix_keys,
    prefix_values,
    prefix_segments,
    stretch_segments,
    stretch_offset,
):
    tok_rows = stream.shape[0]
    prefix_rows = prefix_keys.shape[1]
    ctx_index = lax.axis_index("ctx")
    tp_index = lax.axis_index("tp")
    gain_wide = norm_gain.astype(jnp.float32)
    whole = lax.all_gather(stream, "tp", axis=1, tiled=True).astype(jnp.float32)
    mean_square = jnp.mean(whole * whole, axis=1, keepdims=True)
    normed = (whole * lax.rsqrt(mean_square + NORM_EPSILON) * gain_wide).astype(jnp.bfloat16)
    q_cols = w_query.shape[1]
    q_heads = q_cols // HD
    full_group = HQ // KVH
    kv_heads = max(1, q_heads // full_group)
    group_size = q_heads // kv_heads
    head_start = tp_index * q_heads // full_group
    kv_cols = kv_heads * HD
    key_slice = lax.dynamic_slice_in_dim(w_key, head_start * HD, kv_cols, 1)
    value_slice = lax.dynamic_slice_in_dim(w_value, head_start * HD, kv_cols, 1)
    pieces = (
        lax.all_gather(w_query, "ctx", axis=0, tiled=True),
        lax.all_gather(key_slice, "ctx", axis=0, tiled=True),
        lax.all_gather(value_slice, "ctx", axis=0, tiled=True),
    )
    query_raw, key_full, value_full = tuple(
        (jnp.dot(normed, piece_rows, preferred_element_type=jnp.float32) for piece_rows in pieces)
    )
    token_index = ctx_index * tok_rows + jnp.arange(tok_rows, dtype=jnp.int32)
    positions = stretch_offset[0].astype(jnp.float32) + token_index.astype(jnp.float32)
    query_rows = rotate(query_raw.reshape(tok_rows, q_heads, HD), positions[:, None]).astype(
        jnp.bfloat16
    )
    new_keys = jnp.transpose(
        rotate(key_full.reshape(tok_rows, kv_heads, HD), positions[:, None]).astype(jnp.bfloat16),
        (1, 0, 2),
    )
    new_values = jnp.transpose(
        value_full.astype(jnp.bfloat16).reshape(tok_rows, kv_heads, HD), (1, 0, 2)
    )
    old_keys = lax.dynamic_slice_in_dim(prefix_keys, head_start, kv_heads, 0)
    old_values = lax.dynamic_slice_in_dim(prefix_values, head_start, kv_heads, 0)
    local_keys = jnp.concatenate([old_keys, new_keys], 1)
    local_values = jnp.concatenate([old_values, new_values], 1)
    key_labels = jnp.concatenate([prefix_segments, stretch_segments])
    key_span = prefix_rows + tok_rows
    grouped = jnp.transpose(
        query_rows.reshape(tok_rows, kv_heads, group_size, HD), (1, 0, 2, 3)
    ).reshape(kv_heads, tok_rows * group_size, HD)
    query_index = jnp.repeat(token_index, group_size)
    query_segs = jnp.repeat(stretch_segments, group_size)
    both = jnp.stack([local_keys, local_values])
    kv_block = lax.all_gather(both, "ctx", axis=2, tiled=True)
    label_block = lax.all_gather(key_labels[None, None, :], "ctx", axis=2, tiled=True)
    key_count = kv_block.shape[2]
    absolute = jnp.arange(key_count, dtype=jnp.int32)
    within = absolute % key_span
    key_pos = absolute // key_span * tok_rows + within - prefix_rows
    seen = visibility(label_block[0, 0], within < prefix_rows, key_pos, query_segs, query_index)
    attended_heads = attend_whole(grouped, kv_block[0], kv_block[1], seen).astype(jnp.bfloat16)
    attended = jnp.transpose(
        attended_heads.reshape(kv_heads, tok_rows, group_size, HD), (1, 0, 2, 3)
    ).reshape(tok_rows, q_cols)
    head_terms = jnp.dot(
        attended,
        lax.all_gather(w_out, "ctx", axis=1, tiled=True),
        preferred_element_type=jnp.float32,
    )
    head_share, pending_share = (
        lax.psum_scatter(
            head_terms.astype(jnp.bfloat16), "tp", scatter_dimension=1, tiled=True
        ).astype(jnp.float32),
        lax.psum_scatter(
            pending[0].astype(jnp.float32).astype(jnp.bfloat16),
            "tp",
            scatter_dimension=1,
            tiled=True,
        ).astype(jnp.float32),
    )
    block_share = head_share + pending_share
    return (stream.astype(jnp.float32) + block_share).astype(jnp.bfloat16)


N_CTX = 8
N_TP = 4
GRANT = 60 * 1024 * 1024


def swap(x, bit):
    return lax.ppermute(x, "ctx", [(c, c ^ bit) for c in range(N_CTX)])


def hop_up(v, pairs):
    return lax.ppermute(v, "tp", [(i, i + 1) for i in pairs])


def hop_down(v, pairs):
    return lax.ppermute(v, "tp", [(N_TP - 1 - i, N_TP - 2 - i) for i in pairs])


def rotated(v, cosine, sinus):
    return v * cosine + pltpu.roll(v, HD // 2, 1) * sinus


HBM = pl.BlockSpec(memory_space=pltpu.HBM)
VMEM = pl.BlockSpec(memory_space=pltpu.VMEM)
SMEM = pl.BlockSpec(memory_space=pltpu.SMEM)
ANY = pl.BlockSpec(memory_space=pl.ANY)
LITTLE = pl.CostEstimate(flops=0, bytes_accessed=1024, transcendentals=0)


def specs_of(arrays):
    return [HBM if a.size > 200000 else ANY for a in arrays]


def move(plan, shapes, ids, sources, arrived=()):
    count = len(sources)

    def kernel(ids_ref, *refs):
        outs, sems = refs[count + len(arrived) : -1], refs[-1]
        waits = []
        for at, (choices, dst) in enumerate(plan(ids_ref, refs[:count], outs)):
            for cond, src in choices:
                copy = pltpu.make_async_copy(src, dst, sems.at[at])
                if cond is None:
                    copy.start()
                else:
                    pl.when(cond)(copy.start)
            waits.append(copy)
        for copy in waits:
            copy.wait()

    return pl.pallas_call(
        kernel,
        out_shape=tuple(jax.ShapeDtypeStruct(shape, jnp.bfloat16) for shape in shapes),
        in_specs=[SMEM] + [HBM] * count + specs_of(arrived),
        out_specs=tuple(VMEM for _ in shapes),
        scratch_shapes=[pltpu.SemaphoreType.DMA((40,))],
        compiler_params=pltpu.CompilerParams(vmem_limit_bytes=GRANT),
        cost_estimate=LITTLE,
        name=plan.__name__,
    )(ids, *sources, *arrived)


def gate(x, *arrived):
    return pl.pallas_call(
        lambda *refs: None,
        out_shape=jax.ShapeDtypeStruct(x.shape, x.dtype),
        in_specs=[HBM] + specs_of(arrived),
        out_specs=HBM,
        input_output_aliases={0: 0},
        compiler_params=pltpu.CompilerParams(vmem_limit_bytes=GRANT),
        cost_estimate=LITTLE,
        name="gate",
    )(x, *arrived)


def pick(z, options, ids, arrived=()):
    distinct = list({id(o): o for o in options}.values())

    def pick_plan(at, src, out):
        yield (
            [(at[2] == i, src[[o is d for d in distinct].index(True)]) for i, o in enumerate(options)],
            out[0],
        )

    return move(pick_plan, (options[0].shape,), ids, distinct, arrived)[0]


def hops(ids, pending, up, down, offset, relay, both, rows, arrived=()):
    tok, feat = pending.shape[1], up.shape[1]

    def kernel(ids_ref, pending_ref, up_ref, down_ref, *refs):
        out_up, out_down, buf, sems = refs[len(arrived) :]
        z = ids_ref[2]
        todo = []
        for i, (src, out, step, at) in enumerate(
            ((up_ref, out_up, offset, z), (down_ref, out_down, -offset, N_TP - 1 - z))
        ):
            is_relay = functools.reduce(jnp.logical_or, [at == p for p in relay], at < 0)
            is_both = functools.reduce(jnp.logical_or, [at == p for p in both], at < 0)
            place = jnp.clip(z + step, 0, N_TP - 1)
            share = pltpu.make_async_copy(
                pending_ref.at[0, :, pl.ds(multiple(place, feat), feat)],
                out.at[pl.ds(0, tok)],
                sems.at[i],
            )
            passed = pltpu.make_async_copy(src.at[pl.ds(0, rows)], out, sems.at[i])
            added = pltpu.make_async_copy(src.at[pl.ds(0, tok)], buf.at[i], sems.at[2 + i])
            pl.when(is_relay)(passed.start)

            @pl.when(jnp.logical_not(is_relay))
            def _():
                if rows > tok:
                    out[tok:] = jnp.zeros((rows - tok, feat), jnp.bfloat16)
                share.start()

            pl.when(is_both)(added.start)
            todo.append((passed, share, added, is_relay, is_both, out, i))
        for passed, share, added, is_relay, is_both, out, i in todo:
            pl.when(is_relay)(passed.wait)
            pl.when(jnp.logical_not(is_relay))(share.wait)

            @pl.when(is_both)
            def _():
                added.wait()
                out[:tok] += buf[i]

    shape = jax.ShapeDtypeStruct((rows, feat), jnp.bfloat16)
    return pl.pallas_call(
        kernel,
        out_shape=(shape, shape),
        in_specs=[SMEM, HBM, HBM, HBM] + specs_of(arrived),
        out_specs=(VMEM, VMEM),
        scratch_shapes=[
            pltpu.VMEM((2, tok, feat), jnp.bfloat16),
            pltpu.SemaphoreType.DMA((4,)),
        ],
        compiler_params=pltpu.CompilerParams(vmem_limit_bytes=GRANT),
        cost_estimate=LITTLE,
        name="hops",
    )(ids, pending, up, down, *arrived)


def one(src, dst):
    return ([(None, src)], dst)


def multiple(value, of=128):
    return pl.multiple_of(value * of, of)


AHEAD = 3
PARTS = ((0, 0), (0, 1), (1, 0), (2, 0))


def project_kernel(slots, x_count, w_count, tok, rows, scale, at_kv, ids_ref, *refs):
    last = scale is not None
    xs, ws, refs = refs[:x_count], refs[x_count : x_count + w_count], refs[x_count + w_count :]
    x_buf, w_buf, x_sem, w_sem = refs[-4:]
    chip, core = ids_ref[0], ids_ref[1]
    half, cols = x_buf.shape[-1], ws[0].shape[1]
    fold = half // 2
    mine = pl.multiple_of(core * tok, 128)
    theirs = pl.multiple_of((1 - core) * tok, 128)

    def fetch(at):
        part, h = ids_ref[7 + slots[at // 2]], at % 2
        place = ids_ref[3 + part]
        waits = []
        for i in range(3):
            for m in range(w_count // 2):
                src, dst = ws[2 * m + h], w_buf.at[at]
                if i == 0:
                    src, dst = src.at[pl.ds(0, half)], dst.at[:, pl.ds(0, cols)]
                else:
                    lanes = pl.ds((i - 1) * 2 * HD, 2 * HD)
                    src = src.at[pl.ds(at_kv, fold), lanes]
                    dst = dst.at[pl.ds((i - 1) * fold, fold), pl.ds(cols, 2 * HD)]
                copy = pltpu.make_async_copy(src, dst, w_sem.at[3 * at + i])
                pl.when((place ^ chip) == m)(copy.start)
            waits.append(copy)
        features = pl.ds(pl.multiple_of((core ^ h) * half, 128), half)
        for s, to in ((0, mine), (1, theirs)):
            for r, (index, group) in enumerate(PARTS):
                if 2 * index < x_count:
                    src = xs[2 * index + s].at[pl.ds(group * rows, tok), features]
                    dst = x_buf.at[at, pl.ds(to, tok)]
                    copy = pltpu.make_async_copy(src, dst, x_sem.at[2 * at + s])
                    pl.when(part == r)(copy.start)
            waits.append(copy)
        return waits

    ahead = [fetch(at) for at in range(AHEAD)]
    acc = refs[0][...] if last else 0.0
    for at in range(4):
        for copy in ahead[at]:
            copy.wait()
        if at + AHEAD < 4:
            ahead.append(fetch(at + AHEAD))
        acc = acc + jnp.dot(x_buf[at], w_buf[at], preferred_element_type=jnp.float32)
    if not last:
        refs[0][...] = acc
        return
    factor_ref, cos_ref, sin_ref, q_ref, kv_ref, tail_ref = refs[1:7]
    factor = factor_ref[...]
    heads = q_ref.shape[0]
    for h in range(heads + 2):
        v = acc[:, h * HD : (h + 1) * HD] * factor
        if h <= heads:
            v = rotated(v, cos_ref[...], sin_ref[...])
        if h < heads:
            q_ref[h] = (v * scale).astype(jnp.bfloat16)
        else:
            kv_ref[h - heads] = v.astype(jnp.bfloat16)
            tail_ref[h - heads] = v[tok:].astype(jnp.bfloat16)


def project(ids, slots, xs, weights, tok, at_kv, tables=(), scale=None):
    rows = xs[0].shape[0] // 2
    feat = xs[0].shape[1]
    cols = weights[0].shape[1]
    half = feat // 2
    sums = jax.ShapeDtypeStruct((2 * tok, cols + 2 * HD), jnp.float32)
    results = (
        jax.ShapeDtypeStruct((cols // HD, 2 * tok, HD), jnp.bfloat16),
        jax.ShapeDtypeStruct((2, 2 * tok, HD), jnp.bfloat16),
        jax.ShapeDtypeStruct((2, tok, HD), jnp.bfloat16),
    )
    return pl.pallas_call(
        functools.partial(
            project_kernel, slots, len(xs), len(weights), tok, rows, scale, at_kv
        ),
        out_shape=results if tables else sums,
        in_specs=[SMEM] + [HBM] * (len(xs) + len(weights)) + [VMEM] * len(tables),
        out_specs=(VMEM,) * 3 if tables else VMEM,
        scratch_shapes=[
            pltpu.VMEM((4, 2 * tok, half), jnp.bfloat16),
            pltpu.VMEM((4, half, cols + 2 * HD), jnp.bfloat16),
            pltpu.SemaphoreType.DMA((8,)),
            pltpu.SemaphoreType.DMA((12,)),
        ],
        compiler_params=pltpu.CompilerParams(vmem_limit_bytes=GRANT),
        cost_estimate=LITTLE,
        name="project",
    )(ids, *xs, *weights, *tables)


BT = 384
BK = 1024
CHAIN = 2


def scores(q, k):
    return lax.dot_general(q, k, (((1,), (1,)), ((), ())), preferred_element_type=jnp.float32)


def absorb(s, v_ext, m, acc):
    new = jnp.maximum(m, jnp.max(s, axis=1, keepdims=True))
    p = jnp.exp2(s - new).astype(jnp.bfloat16)
    acc = acc * jnp.exp2(m - new) + jnp.dot(p, v_ext, preferred_element_type=jnp.float32)
    return new, acc


def attend_kernel(at_old, bound_ref, ids_ref, q_ref, n_ref, lo_ref, before_ref, new_ref, *refs):
    bundles, (out_ref, k_old, v_ext, kv_near, s_ref, m_ref, acc_ref, sems) = refs[:8], refs[-8:]
    halo = before_ref.shape[1]
    b = pl.program_id(0)
    heads, bt = q_ref.shape[0], q_ref.shape[1]
    rows, chains = CHAIN * bt, heads // CHAIN
    last = k_old.shape[0] // BK - 1
    fold = k_old.shape[0] // (2 * N_CTX)

    @pl.when(b == 0)
    def _():
        copies = []
        for index, bundle in enumerate(bundles):
            place = ((ids_ref[0] ^ (index // 2)) * 2 + (ids_ref[1] ^ (index % 2))) * 2 * fold
            for i in range(4):
                dst = (k_old, v_ext)[i // 2]
                to = pl.ds(pl.multiple_of(place + (i % 2) * fold, 128), fold)
                copies.append(
                    pltpu.make_async_copy(
                        bundle.at[pl.ds(at_old, fold), pl.ds(i * HD, HD)],
                        dst.at[to, pl.ds(0, HD)],
                        sems.at[4 * index + i],
                    )
                )
        for copy in copies:
            copy.start()
        v_ext[:, HD:] = jnp.ones((v_ext.shape[0], HD), jnp.bfloat16)
        kv_near[:, :halo] = before_ref[...]
        kv_near[:, halo:] = new_ref[...]
        for copy in copies:
            copy.wait()

    m_ref[...] = jnp.full_like(m_ref, MASKED)
    acc_ref[...] = jnp.zeros_like(acc_ref)

    def query(g):
        return q_ref[g * CHAIN : (g + 1) * CHAIN].reshape(rows, HD)

    s_ref[...] = scores(query(0), k_old[:BK, :])

    def body(kb, masked):
        start = pl.multiple_of(kb * BK, BK)
        follow = pl.multiple_of(jnp.minimum(kb + 1, last) * BK, BK)
        ms = [m_ref[g][:, :1] for g in range(chains)]
        accs = [acc_ref[g] for g in range(chains)]
        s = s_ref[...]
        v = v_ext[pl.ds(start, BK), :]
        for g in range(chains):
            at, who = (start, g + 1) if g + 1 < chains else (follow, 0)
            ahead = scores(query(who), k_old[pl.ds(at, BK), :])
            if masked:
                n_rows = jnp.concatenate([n_ref[:, :1]] * CHAIN, axis=0)
                col = lax.broadcasted_iota(jnp.int32, s.shape, 1) + start
                s = jnp.where(col < n_rows, s, MASKED)
            ms[g], accs[g] = absorb(s, v, ms[g], accs[g])
            s = ahead
        s_ref[...] = s
        for g in range(chains):
            m_ref[g] = jnp.broadcast_to(ms[g], (rows, 128))
            acc_ref[g] = accs[g]

    full = bound_ref[0, b] // BK
    some = (bound_ref[1, b] + BK - 1) // BK
    lax.fori_loop(0, full, lambda kb, c: (body(kb, False), c)[1], 0)
    lax.fori_loop(full, some, lambda kb, c: (body(kb, True), c)[1], 0)

    span = halo + bt
    start = pl.multiple_of(b * bt, bt)
    k = kv_near[0, pl.ds(start, span), :]
    v = kv_near[1, pl.ds(start, span), :]
    v = jnp.concatenate([v, jnp.ones_like(v)], axis=1)
    lo = jnp.concatenate([lo_ref[:, :1]] * CHAIN, axis=0)
    col = lax.broadcasted_iota(jnp.int32, (rows, span), 1)
    row = lax.broadcasted_iota(jnp.int32, (rows, span), 0) % bt
    seen = (col + start >= lo) & (col <= row + halo)
    for g in range(chains):
        s = jnp.where(seen, scores(query(g), k), MASKED)
        _, acc = absorb(s, v, m_ref[g][:, :1], acc_ref[g])
        mixed = (acc[:, :HD] / acc[:, HD:]).astype(jnp.bfloat16)
        for h in range(CHAIN):
            at = (g * CHAIN + h) * HD
            out_ref[:, at : at + HD] = mixed[h * bt : (h + 1) * bt]


def attend(bounds, ids, q, n_tok, lo_tok, before, new, bundles, at_old, keys, arrived=()):
    heads, tokens = q.shape[:2]
    chains, rows = heads // CHAIN, CHAIN * BT
    halo = before.shape[1]
    return pl.pallas_call(
        functools.partial(attend_kernel, at_old),
        out_shape=jax.ShapeDtypeStruct((tokens, heads * HD), jnp.bfloat16),
        grid_spec=pltpu.PrefetchScalarGridSpec(
            num_scalar_prefetch=2,
            grid=(tokens // BT,),
            in_specs=[
                pl.BlockSpec((heads, BT, HD), lambda b, *_: (0, b, 0)),
                pl.BlockSpec((BT, 128), lambda b, *_: (b, 0)),
                pl.BlockSpec((BT, 128), lambda b, *_: (b, 0)),
                pl.BlockSpec(before.shape, lambda b, *_: (0, 0, 0)),
                pl.BlockSpec(new.shape, lambda b, *_: (0, 0, 0)),
            ]
            + [HBM] * 8
            + specs_of(arrived),
            out_specs=pl.BlockSpec((BT, heads * HD), lambda b, *_: (b, 0)),
            scratch_shapes=[
                pltpu.VMEM((keys, HD), jnp.bfloat16),
                pltpu.VMEM((keys, 2 * HD), jnp.bfloat16),
                pltpu.VMEM((2, halo + tokens, HD), jnp.bfloat16),
                pltpu.VMEM((rows, BK), jnp.float32),
                pltpu.VMEM((chains, rows, 128), jnp.float32),
                pltpu.VMEM((chains, rows, 2 * HD), jnp.float32),
                pltpu.SemaphoreType.DMA((32,)),
            ],
        ),
        compiler_params=pltpu.CompilerParams(vmem_limit_bytes=GRANT),
        cost_estimate=LITTLE,
        name="attend",
    )(bounds, ids, q, n_tok, lo_tok, before, new, *bundles, *arrived)


def out_kernel(ids_ref, *refs):
    xs, ws = refs[:8], refs[8:16]
    keep_ref, give_ref, x_buf, w_buf, o_buf, x_sem, w_sem = refs[16:]
    chip, core, z = ids_ref[0], ids_ref[1], ids_ref[2]
    width = xs[0].shape[1]
    rows = w_buf.shape[1] // 4
    for r in range(4):
        near = ids_ref[3 + r] ^ z
        for m in range(4):
            to = w_buf.at[r, pl.ds(pl.multiple_of((chip ^ m) * rows, 128), rows)]
            for i in range(2):
                src = ws[2 * m + i].at[pl.ds(pl.multiple_of((near % 2) * rows, 128), rows)]
                copy = pltpu.make_async_copy(src, to, w_sem.at[4 * r + m])
                pl.when(near // 2 == i)(copy.start)
        for s in range(2):
            at = pl.multiple_of((core ^ s) * width, 128)
            pltpu.make_async_copy(
                xs[2 * r + s], x_buf.at[r, :, pl.ds(at, width)], x_sem.at[2 * r + s]
            ).start()
    acc = None
    for r in range(4):
        for m in range(4):
            pltpu.make_async_copy(
                ws[0].at[pl.ds(0, rows)], w_buf.at[r, pl.ds(0, rows)], w_sem.at[4 * r + m]
            ).wait()
        for s in range(2):
            pltpu.make_async_copy(
                xs[0], x_buf.at[r, :, pl.ds(0, width)], x_sem.at[2 * r + s]
            ).wait()
        term = jnp.dot(x_buf[r], w_buf[r], preferred_element_type=jnp.float32)
        acc = term if acc is None else acc + term
    o_buf[...] = acc.astype(jnp.bfloat16)
    half = keep_ref.shape[0]
    keep_ref[...] = o_buf[pl.ds(pl.multiple_of(core * half, 128), half)]
    give_ref[...] = o_buf[pl.ds(pl.multiple_of((1 - core) * half, 128), half)]


def out_project(ids, xs, ws):
    tokens, width = xs[0].shape
    depth, cols = 2 * ws[0].shape[0], ws[0].shape[1]
    return pl.pallas_call(
        out_kernel,
        out_shape=(jax.ShapeDtypeStruct((tokens // 2, cols), jnp.bfloat16),) * 2,
        in_specs=[SMEM] + [HBM] * 16,
        out_specs=(VMEM, VMEM),
        scratch_shapes=[
            pltpu.VMEM((4, tokens, 2 * width), jnp.bfloat16),
            pltpu.VMEM((4, depth, cols), jnp.bfloat16),
            pltpu.VMEM((tokens, cols), jnp.bfloat16),
            pltpu.SemaphoreType.DMA((8,)),
            pltpu.SemaphoreType.DMA((16,)),
        ],
        compiler_params=pltpu.CompilerParams(vmem_limit_bytes=GRANT),
        cost_estimate=LITTLE,
        name="out_project",
    )(ids, *xs, *ws)


def per_device(
    stream,
    pending,
    norm_gain,
    w_query,
    w_key,
    w_value,
    w_out,
    prefix_keys,
    prefix_values,
    prefix_segments,
    stretch_segments,
    stretch_offset,
):
    tok, feat = stream.shape
    chip_tok = 2 * tok
    c = lax.axis_index("ctx")
    z = lax.axis_index("tp")
    chip, core = c // 2, c % 2
    first = core == 0
    depth = feat * N_TP

    wide = stream.astype(jnp.float32)
    here = jnp.stack([chip, core, z]).astype(jnp.int32)
    every = (0, 1, 2)

    gain = lax.dynamic_slice_in_dim(norm_gain, z * feat, feat, 0).astype(jnp.float32)
    scaled = (wide * gain[None, :]).astype(jnp.bfloat16)

    left = jnp.sum(wide * wide, axis=1)
    sums = []
    for _ in range(3):
        sums.append(lax.reduce_precision(left, 8, 7))
        left = left - sums[-1]
    sums = jnp.pad(jnp.stack(sums), ((0, 13), (0, feat - tok))).astype(jnp.bfloat16)
    scaled = jnp.concatenate([scaled, sums], axis=0)
    n_rows = scaled.shape[0]

    def squares(part, group=0):
        at = group * n_rows + tok
        return jnp.sum(part[at : at + 3, :tok].astype(jnp.float32), axis=0)


    labels = jnp.arange(NTRAJ, dtype=jnp.int32)
    counts = jnp.concatenate(
        [
            jnp.sum((prefix_segments[:, None] <= labels).astype(jnp.int32), axis=0),
            jnp.sum((stretch_segments[:, None] < labels).astype(jnp.int32), axis=0),
        ]
    )
    notes = jnp.concatenate([counts // 32, counts % 32])
    cols = w_query.shape[1] // 2
    notes = jnp.stack(
        [jnp.pad(v, (0, cols - v.shape[0])) for v in (stretch_segments, notes)]
        + [jnp.zeros((cols,), jnp.int32)] * 14
    ).astype(jnp.bfloat16)

    token_index = chip * chip_tok + jnp.arange(chip_tok, dtype=jnp.int32)
    positions = stretch_offset[0].astype(jnp.float32) + token_index.astype(jnp.float32)
    angles = positions[:, None] * inverse_freqs(HD)
    cosine, sinus = jnp.cos(angles), jnp.sin(angles)
    cosine = jnp.concatenate([cosine, cosine], axis=1)
    sinus = jnp.concatenate([-sinus, sinus], axis=1)

    q_heads = w_query.shape[1] // HD // 2
    q_cols = q_heads * HD
    n_q = w_query.shape[0]
    fold = prefix_keys.shape[1] // 2
    n_both = n_q + fold
    n_kv = w_key.shape[0] // 2
    n_piece = w_out.shape[0] // 4

    def first_plan(at, src, out):
        w_q, w_k, w_v, keys, values, said = src
        for dst, j in ((out[0], at[1]), (out[1], 1 - at[1])):
            head = 2 * at[2] + j
            yield one(w_q.at[:, pl.ds(multiple(j, q_cols), q_cols)], dst.at[pl.ds(0, n_q)])
            for i, a in enumerate((keys, keys, values, values)):
                part = a.at[head, pl.ds((i % 2) * fold, fold)]
                yield one(part, dst.at[pl.ds(n_q, fold), pl.ds(i * HD, HD)])
            for i, a in enumerate((w_k, w_v, w_k, w_v)):
                part = a.at[pl.ds((i // 2) * n_kv, n_kv), pl.ds(multiple(head), HD)]
                yield one(part, dst.at[pl.ds(n_both, n_kv), pl.ds(i * HD, HD)])
            yield one(said, dst.at[pl.ds(n_both + n_kv, said.shape[0])])

    own, give = move(
        first_plan,
        ((n_both + n_kv + notes.shape[0], q_cols),) * 2,
        here,
        (w_query, w_key, w_value, prefix_keys, prefix_values, notes),
    )
    places = jnp.stack(
        [z, jnp.where(z < 2, z + 1, z - 1), jnp.where(z < 2, z + 2, z - 2), jnp.where(z % 2 == 1, 0, 3)]
    ).astype(jnp.int32)
    skip = jnp.sum(jnp.where(places == (chip ^ 3), jnp.arange(N_TP), 0))
    order = jnp.stack(
        [
            jnp.where(skip == 0, 1, 0),
            jnp.where(skip < 2, 2, 1),
            jnp.minimum(skip, 2),
            jnp.full((), 3),
        ]
    )
    ids = jnp.concatenate([here, places, order]).astype(jnp.int32)

    x1, y1, given = swap(own, 2), swap(own, 4), swap(give, 1)
    turn = swap(gate(notes, own), 1)
    scaled = gate(scaled, turn)
    u1, d1 = hop_up(scaled, every), hop_down(scaled, every)

    def piece_plan(at, src, out):
        for r, dst in enumerate(out):
            rows = pl.ds(multiple(at[0] ^ r, n_piece), n_piece)
            for i in range(2):
                part = src[0].at[rows, pl.ds(i * q_cols, q_cols)]
                yield one(part, dst.at[pl.ds(i * n_piece, n_piece)])

    by_chip = move(
        piece_plan,
        ((2 * n_piece, q_cols),) * 4,
        here,
        (w_out,),
        (own,),
    )
    given = gate(given, x1, y1)
    up, down = hops(here, pending, u1, d1, 3, (1, 2, 3), (), n_rows, (cosine, sinus, given))
    u2, d2 = hop_up(up, every), hop_down(down, every)
    x2, y2 = swap(given, 2), swap(given, 4)

    def near_plan(at, src, out):
        own_part, up_part, down_part = src
        yield one(own_part, out[0].at[pl.ds(0, n_rows)])
        near = [(at[2] < 2, down_part), (at[2] >= 2, up_part)]
        yield (near, out[0].at[pl.ds(n_rows, n_rows)])

    (near,) = move(near_plan, ((2 * n_rows, feat),), here, (scaled, u1, d1), (by_chip[0],))
    near = gate(near, x1, y1)
    over1 = swap(near, 1)

    up, down = hops(here, pending, u2, d2, 2, (2,), (1,), n_rows)
    u3, d3 = hop_up(gate(up, x2), every), hop_down(gate(down, y2), every)
    x1, y2 = gate(x1, x2, y2), gate(y2, x2)
    far_own, far_other = swap(x1, 4), swap(y2, 2)
    second = pick(z, (d2, d2, u2, u2), here)
    over2 = swap(second, 1)
    own_rows = (own, given, x1, x2, y1, y2, far_own, far_other)
    xs = [near, over1, second, over2]
    sums = project(ids, (0, 1), xs, own_rows[:6], tok, n_both)

    third = pick(z, (d3, u1, d1, u3), here, (sums, far_own, far_other))
    over3 = swap(third, 1)
    last_up, last_down = u3, d3
    mine, theirs = (
        squares(a) + squares(a, 1) + squares(b) + squares(c)
        for a, b, c in ((near, second, third), (over1, over2, over3))
    )
    total = jnp.where(first, jnp.concatenate([mine, theirs]), jnp.concatenate([theirs, mine]))
    factor = lax.rsqrt(total * (1.0 / depth) + NORM_EPSILON)
    factor = jnp.broadcast_to(factor[:, None], (chip_tok, 128))
    xs += [third, over3]

    said = [rows[n_both + n_kv : n_both + n_kv + 2].astype(jnp.float32) for rows in own_rows]
    total = sum(v[1, : 4 * NTRAJ] for v in said).astype(jnp.int32)
    total = total[: 2 * NTRAJ] * 32 + total[2 * NTRAJ :]
    segs = [v[0, :tok].astype(jnp.int32) for v in said[:2]]
    segs = jnp.where(first, jnp.concatenate(segs), jnp.concatenate(segs[::-1]))
    onehot = (segs[:, None] == labels).astype(jnp.int32)
    n_tok = jnp.sum(onehot * total[:NTRAJ], axis=1)
    lo_tok = jnp.sum(onehot * total[NTRAJ:], axis=1) - chip * chip_tok + tok
    blocked = n_tok.reshape(chip_tok // BT, BT)
    bounds = jnp.stack([blocked[:, 0], blocked[:, -1]])
    n_wide = jnp.broadcast_to(n_tok[:, None], (chip_tok, 128))
    lo_wide = jnp.broadcast_to(lo_tok[:, None], (chip_tok, 128))

    by_chip = (by_chip[0],) + tuple(
        swap(gate(by_chip[r], far_own, far_other), 2 * r) for r in (1, 2, 3)
    )
    scale = math.log2(math.e) / math.sqrt(HD)
    q, kv_new, tail = project(
        ids, (2, 3), xs, own_rows, tok, n_both, (sums, factor, cosine, sinus), scale
    )
    before = lax.ppermute(tail, "ctx", [(i, i + 2) for i in range(N_CTX - 2)])

    def pieces_plan(at, src, out):
        for r, dst in enumerate(out):
            near = (at[2] ^ r) ^ at[0]
            yield ([(near == m, src[m]) for m in range(4)], dst)

    pieces = list(move(pieces_plan, ((2 * n_piece, q_cols),) * 4, here, by_chip, (q,)))
    for r in (1, 2, 3):
        pieces[r] = lax.ppermute(
            gate(pieces[r], before), "tp", [(i, i ^ r) for i in range(N_TP)]
        )
    attended = attend(
        bounds,
        here,
        q,
        n_wide,
        lo_wide,
        before,
        kv_new,
        own_rows,
        n_q,
        N_CTX * prefix_keys.shape[1],
        (pieces[0],),
    )

    def block_plan(at, src, out):
        for r, part in enumerate(src):
            for i in range(2):
                dst = out[r // 2].at[pl.ds((r % 2) * n_piece, n_piece), pl.ds(i * q_cols, q_cols)]
                yield one(part.at[pl.ds(i * n_piece, n_piece)], dst)

    wo_a, wo_b = move(block_plan, ((2 * n_piece, 2 * q_cols),) * 2, here, pieces, (attended,))
    wo_xa, wo_yb = swap(wo_a, 2), swap(wo_b, 4)
    wo_xb, wo_ya = swap(wo_b, 2), swap(wo_a, 4)

    attended = gate(attended, *pieces[1:])
    u1, d1 = hop_up(attended, every), hop_down(attended, every)
    near = pick(z, (d1, d1, u1, u1), here)

    wo_parts = (wo_a, wo_b, wo_xa, wo_xb, wo_ya, wo_yb, swap(wo_xa, 4), swap(wo_yb, 2))
    u2, d2 = hop_up(gate(u1, wo_xa, wo_yb), (1, 2)), hop_down(gate(d1, wo_xa, wo_yb), (1, 2))
    second = pick(z, (d2, d2, u2, u2), here)
    u3, d3 = hop_up(gate(u2, wo_xb, wo_ya), (2,)), hop_down(gate(d2, wo_xb, wo_ya), (2,))
    third = pick(z, (d3, u1, d1, u3), here, wo_parts[6:])

    up, down = hops(here, pending, last_up, last_down, 1, (), (1, 2, 3), tok, (second,))
    u4, d4 = hop_up(up, every), hop_down(down, every)
    hs = []
    for part in (attended, near, second, third):
        hs += [part, swap(part, 1)]
    mine, theirs = out_project(ids, hs, wo_parts)
    theirs = swap(theirs, 1)
    head_share = jnp.where(
        first,
        jnp.concatenate([mine, theirs], axis=1),
        jnp.concatenate([theirs, mine], axis=1),
    ).astype(jnp.float32)
    pending_share = (
        lax.dynamic_slice_in_dim(pending[0], z * feat, feat, 1).astype(jnp.float32)
        + jnp.where(z == 0, 0, u4).astype(jnp.float32)
        + jnp.where(z == 3, 0, d4).astype(jnp.float32)
    )
    return (wide + (head_share + pending_share)).astype(jnp.bfloat16)


def solution(mesh):
    in_specs = (
        P("ctx", "tp"),
        P("tp", "ctx", None),
        P(),
        P("ctx", "tp"),
        P("ctx", None),
        P("ctx", None),
        P("tp", "ctx"),
        P(None, "ctx", None),
        P(None, "ctx", None),
        P("ctx"),
        P("ctx"),
        P(),
    )
    out_specs = P("ctx", "tp")
    small = mesh.shape["ctx"] == N_CTX and mesh.shape["tp"] == N_TP
    return jax.shard_map(
        per_device if small else per_device_any,
        mesh=mesh,
        in_specs=in_specs,
        out_specs=out_specs,
        check_vma=False,
    )
```

```python
import functools
import math

import jax
import jax.numpy as jnp
from jax import lax
from jax.experimental import pallas as pl
from jax.experimental.pallas import tpu as pltpu
from jax.sharding import PartitionSpec as P

HQ = 32
KVH = 8
HD = 128
NTRAJ = 16


ROPE_BASE = 500000.0
ROPE_FACTOR = 8.0
LOW_FREQ = 1.0
HIGH_FREQ = 4.0
INITIAL_SPAN = 8192.0
NORM_EPSILON = 1e-05
MASKED = -1e30


def inverse_freqs(head_width):
    pair_index = jnp.arange(head_width // 2, dtype=jnp.float32)
    base_freq = ROPE_BASE ** (-2.0 * pair_index / head_width)
    wavelength = 2.0 * math.pi / base_freq
    smooth = (INITIAL_SPAN / wavelength - LOW_FREQ) / (HIGH_FREQ - LOW_FREQ)
    blended = (1.0 - smooth) * base_freq / ROPE_FACTOR + smooth * base_freq
    return jnp.where(
        wavelength < INITIAL_SPAN / HIGH_FREQ,
        base_freq,
        jnp.where(wavelength > INITIAL_SPAN / LOW_FREQ, base_freq / ROPE_FACTOR, blended),
    )


def rotate(vectors, positions):
    head_width = vectors.shape[-1]
    angles = positions[..., None] * inverse_freqs(head_width)
    cosine = jnp.cos(angles)
    sinus = jnp.sin(angles)
    first_half = vectors[..., : head_width // 2]
    second_half = vectors[..., head_width // 2 :]
    return jnp.concatenate(
        [first_half * cosine - second_half * sinus, second_half * cosine + first_half * sinus],
        axis=-1,
    )


def visibility(key_labels, is_prefix, key_pos, query_segs, query_index):
    earlier = key_labels[None, :] <= query_segs[:, None]
    same = (key_labels[None, :] == query_segs[:, None]) & (key_pos[None, :] <= query_index[:, None])
    return jnp.where(is_prefix[None, :], earlier, same)


def attend_whole(grouped, key_block, value_block, seen):
    scores = jnp.einsum("hrd,hnd->hrn", grouped, key_block, preferred_element_type=jnp.float32) * (
        1.0 / math.sqrt(HD)
    )
    scores = jnp.where(seen[None], scores, MASKED)
    new_max = jnp.max(scores, axis=2)
    weights = jnp.where(seen[None], jnp.exp(scores - new_max[..., None]), 0.0)
    totals = jnp.sum(weights, axis=2)
    numerator = jnp.einsum(
        "hrn,hnd->hrd",
        weights.astype(jnp.bfloat16),
        value_block,
        preferred_element_type=jnp.float32,
    )
    return numerator / totals[..., None]


def per_device_any(
    stream,
    pending,
    norm_gain,
    w_query,
    w_key,
    w_value,
    w_out,
    prefix_keys,
    prefix_values,
    prefix_segments,
    stretch_segments,
    stretch_offset,
):
    tok_rows = stream.shape[0]
    prefix_rows = prefix_keys.shape[1]
    ctx_index = lax.axis_index("ctx")
    tp_index = lax.axis_index("tp")
    gain_wide = norm_gain.astype(jnp.float32)
    whole = lax.all_gather(stream, "tp", axis=1, tiled=True).astype(jnp.float32)
    mean_square = jnp.mean(whole * whole, axis=1, keepdims=True)
    normed = (whole * lax.rsqrt(mean_square + NORM_EPSILON) * gain_wide).astype(jnp.bfloat16)
    q_cols = w_query.shape[1]
    q_heads = q_cols // HD
    full_group = HQ // KVH
    kv_heads = max(1, q_heads // full_group)
    group_size = q_heads // kv_heads
    head_start = tp_index * q_heads // full_group
    kv_cols = kv_heads * HD
    key_slice = lax.dynamic_slice_in_dim(w_key, head_start * HD, kv_cols, 1)
    value_slice = lax.dynamic_slice_in_dim(w_value, head_start * HD, kv_cols, 1)
    pieces = (
        lax.all_gather(w_query, "ctx", axis=0, tiled=True),
        lax.all_gather(key_slice, "ctx", axis=0, tiled=True),
        lax.all_gather(value_slice, "ctx", axis=0, tiled=True),
    )
    query_raw, key_full, value_full = tuple(
        (jnp.dot(normed, piece_rows, preferred_element_type=jnp.float32) for piece_rows in pieces)
    )
    token_index = ctx_index * tok_rows + jnp.arange(tok_rows, dtype=jnp.int32)
    positions = stretch_offset[0].astype(jnp.float32) + token_index.astype(jnp.float32)
    query_rows = rotate(query_raw.reshape(tok_rows, q_heads, HD), positions[:, None]).astype(
        jnp.bfloat16
    )
    new_keys = jnp.transpose(
        rotate(key_full.reshape(tok_rows, kv_heads, HD), positions[:, None]).astype(jnp.bfloat16),
        (1, 0, 2),
    )
    new_values = jnp.transpose(
        value_full.astype(jnp.bfloat16).reshape(tok_rows, kv_heads, HD), (1, 0, 2)
    )
    old_keys = lax.dynamic_slice_in_dim(prefix_keys, head_start, kv_heads, 0)
    old_values = lax.dynamic_slice_in_dim(prefix_values, head_start, kv_heads, 0)
    local_keys = jnp.concatenate([old_keys, new_keys], 1)
    local_values = jnp.concatenate([old_values, new_values], 1)
    key_labels = jnp.concatenate([prefix_segments, stretch_segments])
    key_span = prefix_rows + tok_rows
    grouped = jnp.transpose(
        query_rows.reshape(tok_rows, kv_heads, group_size, HD), (1, 0, 2, 3)
    ).reshape(kv_heads, tok_rows * group_size, HD)
    query_index = jnp.repeat(token_index, group_size)
    query_segs = jnp.repeat(stretch_segments, group_size)
    both = jnp.stack([local_keys, local_values])
    kv_block = lax.all_gather(both, "ctx", axis=2, tiled=True)
    label_block = lax.all_gather(key_labels[None, None, :], "ctx", axis=2, tiled=True)
    key_count = kv_block.shape[2]
    absolute = jnp.arange(key_count, dtype=jnp.int32)
    within = absolute % key_span
    key_pos = absolute // key_span * tok_rows + within - prefix_rows
    seen = visibility(label_block[0, 0], within < prefix_rows, key_pos, query_segs, query_index)
    attended_heads = attend_whole(grouped, kv_block[0], kv_block[1], seen).astype(jnp.bfloat16)
    attended = jnp.transpose(
        attended_heads.reshape(kv_heads, tok_rows, group_size, HD), (1, 0, 2, 3)
    ).reshape(tok_rows, q_cols)
    head_terms = jnp.dot(
        attended,
        lax.all_gather(w_out, "ctx", axis=1, tiled=True),
        preferred_element_type=jnp.float32,
    )
    head_share, pending_share = (
        lax.psum_scatter(
            head_terms.astype(jnp.bfloat16), "tp", scatter_dimension=1, tiled=True
        ).astype(jnp.float32),
        lax.psum_scatter(
            pending[0].astype(jnp.float32).astype(jnp.bfloat16),
            "tp",
            scatter_dimension=1,
            tiled=True,
        ).astype(jnp.float32),
    )
    block_share = head_share + pending_share
    return (stream.astype(jnp.float32) + block_share).astype(jnp.bfloat16)


N_CTX = 8
N_TP = 4
GRANT = 60 * 1024 * 1024


def swap(x, bit):
    return lax.ppermute(x, "ctx", [(c, c ^ bit) for c in range(N_CTX)])


def hop_up(v, pairs):
    return lax.ppermute(v, "tp", [(i, i + 1) for i in pairs])


def hop_down(v, pairs):
    return lax.ppermute(v, "tp", [(N_TP - 1 - i, N_TP - 2 - i) for i in pairs])


def rotated(v, cosine, sinus):
    return v * cosine + pltpu.roll(v, HD // 2, 1) * sinus


HBM = pl.BlockSpec(memory_space=pltpu.HBM)
VMEM = pl.BlockSpec(memory_space=pltpu.VMEM)
SMEM = pl.BlockSpec(memory_space=pltpu.SMEM)
ANY = pl.BlockSpec(memory_space=pl.ANY)
LITTLE = pl.CostEstimate(flops=0, bytes_accessed=1024, transcendentals=0)


def specs_of(arrays):
    return [HBM if a.size > 200000 else ANY for a in arrays]


def move(plan, shapes, ids, sources, arrived=()):
    count = len(sources)

    def kernel(ids_ref, *refs):
        outs, sems = refs[count + len(arrived) : -1], refs[-1]
        waits = []
        for at, (choices, dst) in enumerate(plan(ids_ref, refs[:count], outs)):
            for cond, src in choices:
                copy = pltpu.make_async_copy(src, dst, sems.at[at])
                if cond is None:
                    copy.start()
                else:
                    pl.when(cond)(copy.start)
            waits.append(copy)
        for copy in waits:
            copy.wait()

    return pl.pallas_call(
        kernel,
        out_shape=tuple(jax.ShapeDtypeStruct(shape, jnp.bfloat16) for shape in shapes),
        in_specs=[SMEM] + [HBM] * count + specs_of(arrived),
        out_specs=tuple(VMEM for _ in shapes),
        scratch_shapes=[pltpu.SemaphoreType.DMA((40,))],
        compiler_params=pltpu.CompilerParams(vmem_limit_bytes=GRANT),
        cost_estimate=LITTLE,
        name=plan.__name__,
    )(ids, *sources, *arrived)


def gate(x, *arrived):
    return pl.pallas_call(
        lambda *refs: None,
        out_shape=jax.ShapeDtypeStruct(x.shape, x.dtype),
        in_specs=[HBM] + specs_of(arrived),
        out_specs=HBM,
        input_output_aliases={0: 0},
        compiler_params=pltpu.CompilerParams(vmem_limit_bytes=GRANT),
        cost_estimate=LITTLE,
        name="gate",
    )(x, *arrived)


def pick(z, options, ids, arrived=()):
    distinct = list({id(o): o for o in options}.values())

    def pick_plan(at, src, out):
        yield (
            [(at[2] == i, src[[o is d for d in distinct].index(True)]) for i, o in enumerate(options)],
            out[0],
        )

    return move(pick_plan, (options[0].shape,), ids, distinct, arrived)[0]


def hops(ids, pending, up, down, offset, relay, both, rows, arrived=()):
    tok, feat = pending.shape[1], up.shape[1]

    def kernel(ids_ref, pending_ref, up_ref, down_ref, *refs):
        out_up, out_down, buf, sems = refs[len(arrived) :]
        z = ids_ref[2]
        todo = []
        for i, (src, out, step, at) in enumerate(
            ((up_ref, out_up, offset, z), (down_ref, out_down, -offset, N_TP - 1 - z))
        ):
            is_relay = functools.reduce(jnp.logical_or, [at == p for p in relay], at < 0)
            is_both = functools.reduce(jnp.logical_or, [at == p for p in both], at < 0)
            place = jnp.clip(z + step, 0, N_TP - 1)
            share = pltpu.make_async_copy(
                pending_ref.at[0, :, pl.ds(multiple(place, feat), feat)],
                out.at[pl.ds(0, tok)],
                sems.at[i],
            )
            passed = pltpu.make_async_copy(src.at[pl.ds(0, rows)], out, sems.at[i])
            added = pltpu.make_async_copy(src.at[pl.ds(0, tok)], buf.at[i], sems.at[2 + i])
            pl.when(is_relay)(passed.start)

            @pl.when(jnp.logical_not(is_relay))
            def _():
                if rows > tok:
                    out[tok:] = jnp.zeros((rows - tok, feat), jnp.bfloat16)
                share.start()

            pl.when(is_both)(added.start)
            todo.append((passed, share, added, is_relay, is_both, out, i))
        for passed, share, added, is_relay, is_both, out, i in todo:
            pl.when(is_relay)(passed.wait)
            pl.when(jnp.logical_not(is_relay))(share.wait)

            @pl.when(is_both)
            def _():
                added.wait()
                out[:tok] += buf[i]

    shape = jax.ShapeDtypeStruct((rows, feat), jnp.bfloat16)
    return pl.pallas_call(
        kernel,
        out_shape=(shape, shape),
        in_specs=[SMEM, HBM, HBM, HBM] + specs_of(arrived),
        out_specs=(VMEM, VMEM),
        scratch_shapes=[
            pltpu.VMEM((2, tok, feat), jnp.bfloat16),
            pltpu.SemaphoreType.DMA((4,)),
        ],
        compiler_params=pltpu.CompilerParams(vmem_limit_bytes=GRANT),
        cost_estimate=LITTLE,
        name="hops",
    )(ids, pending, up, down, *arrived)


def one(src, dst):
    return ([(None, src)], dst)


def multiple(value, of=128):
    return pl.multiple_of(value * of, of)


AHEAD = 3
PARTS = ((0, 0), (0, 1), (1, 0), (2, 0))


def project_kernel(slots, x_count, w_count, tok, rows, scale, at_kv, ids_ref, *refs):
    last = scale is not None
    xs, ws, refs = refs[:x_count], refs[x_count : x_count + w_count], refs[x_count + w_count :]
    x_buf, w_buf, x_sem, w_sem = refs[-4:]
    chip, core = ids_ref[0], ids_ref[1]
    half, cols = x_buf.shape[-1], ws[0].shape[1]
    fold = half // 2
    mine = pl.multiple_of(core * tok, 128)
    theirs = pl.multiple_of((1 - core) * tok, 128)

    def fetch(at):
        part, h = ids_ref[7 + slots[at // 2]], at % 2
        place = ids_ref[3 + part]
        waits = []
        for i in range(3):
            for m in range(w_count // 2):
                src, dst = ws[2 * m + h], w_buf.at[at]
                if i == 0:
                    src, dst = src.at[pl.ds(0, half)], dst.at[:, pl.ds(0, cols)]
                else:
                    lanes = pl.ds((i - 1) * 2 * HD, 2 * HD)
                    src = src.at[pl.ds(at_kv, fold), lanes]
                    dst = dst.at[pl.ds((i - 1) * fold, fold), pl.ds(cols, 2 * HD)]
                copy = pltpu.make_async_copy(src, dst, w_sem.at[3 * at + i])
                pl.when((place ^ chip) == m)(copy.start)
            waits.append(copy)
        features = pl.ds(pl.multiple_of((core ^ h) * half, 128), half)
        for s, to in ((0, mine), (1, theirs)):
            for r, (index, group) in enumerate(PARTS):
                if 2 * index < x_count:
                    src = xs[2 * index + s].at[pl.ds(group * rows, tok), features]
                    dst = x_buf.at[at, pl.ds(to, tok)]
                    copy = pltpu.make_async_copy(src, dst, x_sem.at[2 * at + s])
                    pl.when(part == r)(copy.start)
            waits.append(copy)
        return waits

    ahead = [fetch(at) for at in range(AHEAD)]
    acc = refs[0][...] if last else 0.0
    for at in range(4):
        for copy in ahead[at]:
            copy.wait()
        if at + AHEAD < 4:
            ahead.append(fetch(at + AHEAD))
        acc = acc + jnp.dot(x_buf[at], w_buf[at], preferred_element_type=jnp.float32)
    if not last:
        refs[0][...] = acc
        return
    factor_ref, cos_ref, sin_ref, q_ref, kv_ref, tail_ref = refs[1:7]
    factor = factor_ref[...]
    heads = q_ref.shape[0]
    for h in range(heads + 2):
        v = acc[:, h * HD : (h + 1) * HD] * factor
        if h <= heads:
            v = rotated(v, cos_ref[...], sin_ref[...])
        if h < heads:
            q_ref[h] = (v * scale).astype(jnp.bfloat16)
        else:
            kv_ref[h - heads] = v.astype(jnp.bfloat16)
            tail_ref[h - heads] = v[tok:].astype(jnp.bfloat16)


def project(ids, slots, xs, weights, tok, at_kv, tables=(), scale=None):
    rows = xs[0].shape[0] // 2
    feat = xs[0].shape[1]
    cols = weights[0].shape[1]
    half = feat // 2
    sums = jax.ShapeDtypeStruct((2 * tok, cols + 2 * HD), jnp.float32)
    results = (
        jax.ShapeDtypeStruct((cols // HD, 2 * tok, HD), jnp.bfloat16),
        jax.ShapeDtypeStruct((2, 2 * tok, HD), jnp.bfloat16),
        jax.ShapeDtypeStruct((2, tok, HD), jnp.bfloat16),
    )
    return pl.pallas_call(
        functools.partial(
            project_kernel, slots, len(xs), len(weights), tok, rows, scale, at_kv
        ),
        out_shape=results if tables else sums,
        in_specs=[SMEM] + [HBM] * (len(xs) + len(weights)) + [VMEM] * len(tables),
        out_specs=(VMEM,) * 3 if tables else VMEM,
        scratch_shapes=[
            pltpu.VMEM((4, 2 * tok, half), jnp.bfloat16),
            pltpu.VMEM((4, half, cols + 2 * HD), jnp.bfloat16),
            pltpu.SemaphoreType.DMA((8,)),
            pltpu.SemaphoreType.DMA((12,)),
        ],
        compiler_params=pltpu.CompilerParams(vmem_limit_bytes=GRANT),
        cost_estimate=LITTLE,
        name="project",
    )(ids, *xs, *weights, *tables)


BT = 256
BK = 1024
CHAIN = 2


def scores(q, k):
    return lax.dot_general(q, k, (((1,), (1,)), ((), ())), preferred_element_type=jnp.float32)


def absorb(s, v_ext, m, acc):
    new = jnp.maximum(m, jnp.max(s, axis=1, keepdims=True))
    p = jnp.exp2(s - new).astype(jnp.bfloat16)
    acc = acc * jnp.exp2(m - new) + jnp.dot(p, v_ext, preferred_element_type=jnp.float32)
    return new, acc


def attend_kernel(at_old, bound_ref, ids_ref, q_ref, n_ref, lo_ref, before_ref, new_ref, *refs):
    bundles, (out_ref, k_old, v_ext, kv_near, s_ref, m_ref, acc_ref, sems) = refs[:8], refs[-8:]
    halo = before_ref.shape[1]
    b = pl.program_id(0)
    heads, bt = q_ref.shape[0], q_ref.shape[1]
    rows, chains = CHAIN * bt, heads // CHAIN
    last = k_old.shape[0] // BK - 1
    fold = k_old.shape[0] // (2 * N_CTX)

    @pl.when(b == 0)
    def _():
        copies = []
        for index, bundle in enumerate(bundles):
            place = ((ids_ref[0] ^ (index // 2)) * 2 + (ids_ref[1] ^ (index % 2))) * 2 * fold
            for i in range(4):
                dst = (k_old, v_ext)[i // 2]
                to = pl.ds(pl.multiple_of(place + (i % 2) * fold, 128), fold)
                copies.append(
                    pltpu.make_async_copy(
                        bundle.at[pl.ds(at_old, fold), pl.ds(i * HD, HD)],
                        dst.at[to, pl.ds(0, HD)],
                        sems.at[4 * index + i],
                    )
                )
        for copy in copies:
            copy.start()
        v_ext[:, HD:] = jnp.ones((v_ext.shape[0], HD), jnp.bfloat16)
        kv_near[:, :halo] = before_ref[...]
        kv_near[:, halo:] = new_ref[...]
        for copy in copies:
            copy.wait()

    m_ref[...] = jnp.full_like(m_ref, MASKED)
    acc_ref[...] = jnp.zeros_like(acc_ref)

    def query(g):
        return q_ref[g * CHAIN : (g + 1) * CHAIN].reshape(rows, HD)

    s_ref[...] = scores(query(0), k_old[:BK, :])

    def body(kb, masked):
        start = pl.multiple_of(kb * BK, BK)
        follow = pl.multiple_of(jnp.minimum(kb + 1, last) * BK, BK)
        ms = [m_ref[g][:, :1] for g in range(chains)]
        accs = [acc_ref[g] for g in range(chains)]
        s = s_ref[...]
        v = v_ext[pl.ds(start, BK), :]
        for g in range(chains):
            at, who = (start, g + 1) if g + 1 < chains else (follow, 0)
            ahead = scores(query(who), k_old[pl.ds(at, BK), :])
            if masked:
                n_rows = jnp.concatenate([n_ref[:, :1]] * CHAIN, axis=0)
                col = lax.broadcasted_iota(jnp.int32, s.shape, 1) + start
                s = jnp.where(col < n_rows, s, MASKED)
            ms[g], accs[g] = absorb(s, v, ms[g], accs[g])
            s = ahead
        s_ref[...] = s
        for g in range(chains):
            m_ref[g] = jnp.broadcast_to(ms[g], (rows, 128))
            acc_ref[g] = accs[g]

    full = bound_ref[0, b] // BK
    some = (bound_ref[1, b] + BK - 1) // BK
    lax.fori_loop(0, full, lambda kb, c: (body(kb, False), c)[1], 0)
    lax.fori_loop(full, some, lambda kb, c: (body(kb, True), c)[1], 0)

    span = halo + bt
    start = pl.multiple_of(b * bt, bt)
    k = kv_near[0, pl.ds(start, span), :]
    v = kv_near[1, pl.ds(start, span), :]
    v = jnp.concatenate([v, jnp.ones_like(v)], axis=1)
    lo = jnp.concatenate([lo_ref[:, :1]] * CHAIN, axis=0)
    col = lax.broadcasted_iota(jnp.int32, (rows, span), 1)
    row = lax.broadcasted_iota(jnp.int32, (rows, span), 0) % bt
    seen = (col + start >= lo) & (col <= row + halo)
    for g in range(chains):
        s = jnp.where(seen, scores(query(g), k), MASKED)
        _, acc = absorb(s, v, m_ref[g][:, :1], acc_ref[g])
        mixed = (acc[:, :HD] / acc[:, HD:]).astype(jnp.bfloat16)
        for h in range(CHAIN):
            at = (g * CHAIN + h) * HD
            out_ref[:, at : at + HD] = mixed[h * bt : (h + 1) * bt]


def attend(bounds, ids, q, n_tok, lo_tok, before, new, bundles, at_old, keys, arrived=()):
    heads, tokens = q.shape[:2]
    chains, rows = heads // CHAIN, CHAIN * BT
    halo = before.shape[1]
    return pl.pallas_call(
        functools.partial(attend_kernel, at_old),
        out_shape=jax.ShapeDtypeStruct((tokens, heads * HD), jnp.bfloat16),
        grid_spec=pltpu.PrefetchScalarGridSpec(
            num_scalar_prefetch=2,
            grid=(tokens // BT,),
            in_specs=[
                pl.BlockSpec((heads, BT, HD), lambda b, *_: (0, b, 0)),
                pl.BlockSpec((BT, 128), lambda b, *_: (b, 0)),
                pl.BlockSpec((BT, 128), lambda b, *_: (b, 0)),
                pl.BlockSpec(before.shape, lambda b, *_: (0, 0, 0)),
                pl.BlockSpec(new.shape, lambda b, *_: (0, 0, 0)),
            ]
            + [HBM] * 8
            + specs_of(arrived),
            out_specs=pl.BlockSpec((BT, heads * HD), lambda b, *_: (b, 0)),
            scratch_shapes=[
                pltpu.VMEM((keys, HD), jnp.bfloat16),
                pltpu.VMEM((keys, 2 * HD), jnp.bfloat16),
                pltpu.VMEM((2, halo + tokens, HD), jnp.bfloat16),
                pltpu.VMEM((rows, BK), jnp.float32),
                pltpu.VMEM((chains, rows, 128), jnp.float32),
                pltpu.VMEM((chains, rows, 2 * HD), jnp.float32),
                pltpu.SemaphoreType.DMA((32,)),
            ],
        ),
        compiler_params=pltpu.CompilerParams(vmem_limit_bytes=GRANT),
        cost_estimate=LITTLE,
        name="attend",
    )(bounds, ids, q, n_tok, lo_tok, before, new, *bundles, *arrived)


def out_kernel(ids_ref, *refs):
    xs, ws = refs[:8], refs[8:16]
    keep_ref, give_ref, x_buf, w_buf, o_buf, x_sem, w_sem = refs[16:]
    chip, core, z = ids_ref[0], ids_ref[1], ids_ref[2]
    width = xs[0].shape[1]
    rows = w_buf.shape[1] // 4
    for r in range(4):
        near = ids_ref[3 + r] ^ z
        for m in range(4):
            to = w_buf.at[r, pl.ds(pl.multiple_of((chip ^ m) * rows, 128), rows)]
            for i in range(2):
                src = ws[2 * m + i].at[pl.ds(pl.multiple_of((near % 2) * rows, 128), rows)]
                copy = pltpu.make_async_copy(src, to, w_sem.at[4 * r + m])
                pl.when(near // 2 == i)(copy.start)
        for s in range(2):
            at = pl.multiple_of((core ^ s) * width, 128)
            pltpu.make_async_copy(
                xs[2 * r + s], x_buf.at[r, :, pl.ds(at, width)], x_sem.at[2 * r + s]
            ).start()
    acc = None
    for r in range(4):
        for m in range(4):
            pltpu.make_async_copy(
                ws[0].at[pl.ds(0, rows)], w_buf.at[r, pl.ds(0, rows)], w_sem.at[4 * r + m]
            ).wait()
        for s in range(2):
            pltpu.make_async_copy(
                xs[0], x_buf.at[r, :, pl.ds(0, width)], x_sem.at[2 * r + s]
            ).wait()
        term = jnp.dot(x_buf[r], w_buf[r], preferred_element_type=jnp.float32)
        acc = term if acc is None else acc + term
    o_buf[...] = acc.astype(jnp.bfloat16)
    half = keep_ref.shape[0]
    keep_ref[...] = o_buf[pl.ds(pl.multiple_of(core * half, 128), half)]
    give_ref[...] = o_buf[pl.ds(pl.multiple_of((1 - core) * half, 128), half)]


def out_project(ids, xs, ws):
    tokens, width = xs[0].shape
    depth, cols = 2 * ws[0].shape[0], ws[0].shape[1]
    return pl.pallas_call(
        out_kernel,
        out_shape=(jax.ShapeDtypeStruct((tokens // 2, cols), jnp.bfloat16),) * 2,
        in_specs=[SMEM] + [HBM] * 16,
        out_specs=(VMEM, VMEM),
        scratch_shapes=[
            pltpu.VMEM((4, tokens, 2 * width), jnp.bfloat16),
            pltpu.VMEM((4, depth, cols), jnp.bfloat16),
            pltpu.VMEM((tokens, cols), jnp.bfloat16),
            pltpu.SemaphoreType.DMA((8,)),
            pltpu.SemaphoreType.DMA((16,)),
        ],
        compiler_params=pltpu.CompilerParams(vmem_limit_bytes=GRANT),
        cost_estimate=LITTLE,
        name="out_project",
    )(ids, *xs, *ws)


def per_device(
    stream,
    pending,
    norm_gain,
    w_query,
    w_key,
    w_value,
    w_out,
    prefix_keys,
    prefix_values,
    prefix_segments,
    stretch_segments,
    stretch_offset,
):
    tok, feat = stream.shape
    chip_tok = 2 * tok
    c = lax.axis_index("ctx")
    z = lax.axis_index("tp")
    chip, core = c // 2, c % 2
    first = core == 0
    depth = feat * N_TP

    wide = stream.astype(jnp.float32)
    here = jnp.stack([chip, core, z]).astype(jnp.int32)
    every = (0, 1, 2)

    gain = lax.dynamic_slice_in_dim(norm_gain, z * feat, feat, 0).astype(jnp.float32)
    scaled = (wide * gain[None, :]).astype(jnp.bfloat16)

    left = jnp.sum(wide * wide, axis=1)
    sums = []
    for _ in range(3):
        sums.append(lax.reduce_precision(left, 8, 7))
        left = left - sums[-1]
    sums = jnp.pad(jnp.stack(sums), ((0, 13), (0, feat - tok))).astype(jnp.bfloat16)
    scaled = jnp.concatenate([scaled, sums], axis=0)
    n_rows = scaled.shape[0]

    def squares(part, group=0):
        at = group * n_rows + tok
        return jnp.sum(part[at : at + 3, :tok].astype(jnp.float32), axis=0)


    labels = jnp.arange(NTRAJ, dtype=jnp.int32)
    counts = jnp.concatenate(
        [
            jnp.sum((prefix_segments[:, None] <= labels).astype(jnp.int32), axis=0),
            jnp.sum((stretch_segments[:, None] < labels).astype(jnp.int32), axis=0),
        ]
    )
    notes = jnp.concatenate([counts // 32, counts % 32])
    cols = w_query.shape[1] // 2
    notes = jnp.stack(
        [jnp.pad(v, (0, cols - v.shape[0])) for v in (stretch_segments, notes)]
        + [jnp.zeros((cols,), jnp.int32)] * 14
    ).astype(jnp.bfloat16)

    token_index = chip * chip_tok + jnp.arange(chip_tok, dtype=jnp.int32)
    positions = stretch_offset[0].astype(jnp.float32) + token_index.astype(jnp.float32)
    angles = positions[:, None] * inverse_freqs(HD)
    cosine, sinus = jnp.cos(angles), jnp.sin(angles)
    cosine = jnp.concatenate([cosine, cosine], axis=1)
    sinus = jnp.concatenate([-sinus, sinus], axis=1)

    q_heads = w_query.shape[1] // HD // 2
    q_cols = q_heads * HD
    n_q = w_query.shape[0]
    fold = prefix_keys.shape[1] // 2
    n_both = n_q + fold
    n_kv = w_key.shape[0] // 2
    n_piece = w_out.shape[0] // 4

    def first_plan(at, src, out):
        w_q, w_k, w_v, keys, values, said = src
        for dst, j in ((out[0], at[1]), (out[1], 1 - at[1])):
            head = 2 * at[2] + j
            yield one(w_q.at[:, pl.ds(multiple(j, q_cols), q_cols)], dst.at[pl.ds(0, n_q)])
            for i, a in enumerate((keys, keys, values, values)):
                part = a.at[head, pl.ds((i % 2) * fold, fold)]
                yield one(part, dst.at[pl.ds(n_q, fold), pl.ds(i * HD, HD)])
            for i, a in enumerate((w_k, w_v, w_k, w_v)):
                part = a.at[pl.ds((i // 2) * n_kv, n_kv), pl.ds(multiple(head), HD)]
                yield one(part, dst.at[pl.ds(n_both, n_kv), pl.ds(i * HD, HD)])
            yield one(said, dst.at[pl.ds(n_both + n_kv, said.shape[0])])

    own, give = move(
        first_plan,
        ((n_both + n_kv + notes.shape[0], q_cols),) * 2,
        here,
        (w_query, w_key, w_value, prefix_keys, prefix_values, notes),
    )
    places = jnp.stack(
        [z, jnp.where(z < 2, z + 1, z - 1), jnp.where(z < 2, z + 2, z - 2), jnp.where(z % 2 == 1, 0, 3)]
    ).astype(jnp.int32)
    skip = jnp.sum(jnp.where(places == (chip ^ 3), jnp.arange(N_TP), 0))
    order = jnp.stack(
        [
            jnp.where(skip == 0, 1, 0),
            jnp.where(skip < 2, 2, 1),
            jnp.minimum(skip, 2),
            jnp.full((), 3),
        ]
    )
    ids = jnp.concatenate([here, places, order]).astype(jnp.int32)

    x1, y1, given = swap(own, 2), swap(own, 4), swap(give, 1)
    turn = swap(gate(notes, own), 1)
    scaled = gate(scaled, turn)
    u1, d1 = hop_up(scaled, every), hop_down(scaled, every)

    def piece_plan(at, src, out):
        for r, dst in enumerate(out):
            rows = pl.ds(multiple(at[0] ^ r, n_piece), n_piece)
            for i in range(2):
                part = src[0].at[rows, pl.ds(i * q_cols, q_cols)]
                yield one(part, dst.at[pl.ds(i * n_piece, n_piece)])

    by_chip = move(
        piece_plan,
        ((2 * n_piece, q_cols),) * 4,
        here,
        (w_out,),
        (own,),
    )
    given = gate(given, x1, y1)
    up, down = hops(here, pending, u1, d1, 3, (1, 2, 3), (), n_rows, (cosine, sinus, given, by_chip[0]))
    u2, d2 = hop_up(up, every), hop_down(down, every)
    x2, y2 = swap(given, 2), swap(given, 4)

    def near_plan(at, src, out):
        own_part, up_part, down_part = src
        yield one(own_part, out[0].at[pl.ds(0, n_rows)])
        near = [(at[2] < 2, down_part), (at[2] >= 2, up_part)]
        yield (near, out[0].at[pl.ds(n_rows, n_rows)])

    (near,) = move(near_plan, ((2 * n_rows, feat),), here, (scaled, u1, d1), (up,))

    x1, y2 = gate(x1, x2, y2, u2, d2), gate(y2, x2, u2, d2)
    up, down = hops(here, pending, u2, d2, 2, (2,), (1,), n_rows, (x1, y2, near))
    u3, d3 = hop_up(up, every), hop_down(down, every)
    far_own, far_other = swap(x1, 4), swap(y2, 2)
    near = gate(near, up)
    over1 = swap(near, 1)
    second = pick(z, (d2, d2, u2, u2), here, (up,))
    over2 = swap(second, 1)
    own_rows = (own, given, x1, x2, y1, y2, far_own, far_other)
    xs = [near, over1, second, over2]
    sums = project(ids, (0, 1), xs, own_rows[:6], tok, n_both)

    third = pick(z, (d3, u1, d1, u3), here, (sums, far_own, far_other))
    over3 = swap(third, 1)
    up, down = hops(here, pending, u3, d3, 1, (), (1, 2, 3), tok, (third,))
    u4, d4 = hop_up(up, every), hop_down(down, every)
    mine, theirs = (
        squares(a) + squares(a, 1) + squares(b) + squares(c)
        for a, b, c in ((near, second, third), (over1, over2, over3))
    )
    total = jnp.where(first, jnp.concatenate([mine, theirs]), jnp.concatenate([theirs, mine]))
    factor = lax.rsqrt(total * (1.0 / depth) + NORM_EPSILON)
    factor = jnp.broadcast_to(factor[:, None], (chip_tok, 128))
    xs += [third, over3]

    said = [rows[n_both + n_kv : n_both + n_kv + 2].astype(jnp.float32) for rows in own_rows]
    total = sum(v[1, : 4 * NTRAJ] for v in said).astype(jnp.int32)
    total = total[: 2 * NTRAJ] * 32 + total[2 * NTRAJ :]
    segs = [v[0, :tok].astype(jnp.int32) for v in said[:2]]
    segs = jnp.where(first, jnp.concatenate(segs), jnp.concatenate(segs[::-1]))
    onehot = (segs[:, None] == labels).astype(jnp.int32)
    n_tok = jnp.sum(onehot * total[:NTRAJ], axis=1)
    lo_tok = jnp.sum(onehot * total[NTRAJ:], axis=1) - chip * chip_tok + tok
    blocked = n_tok.reshape(chip_tok // BT, BT)
    bounds = jnp.stack([blocked[:, 0], blocked[:, -1]])
    n_wide = jnp.broadcast_to(n_tok[:, None], (chip_tok, 128))
    lo_wide = jnp.broadcast_to(lo_tok[:, None], (chip_tok, 128))

    by_chip = (by_chip[0],) + tuple(
        swap(gate(by_chip[r], far_own, far_other), 2 * r) for r in (1, 2, 3)
    )
    scale = math.log2(math.e) / math.sqrt(HD)
    q, kv_new, tail = project(
        ids, (2, 3), xs, own_rows, tok, n_both, (sums, factor, cosine, sinus), scale
    )
    before = lax.ppermute(tail, "ctx", [(i, i + 2) for i in range(N_CTX - 2)])

    def pieces_plan(at, src, out):
        for r, dst in enumerate(out):
            near = (at[2] ^ r) ^ at[0]
            yield ([(near == m, src[m]) for m in range(4)], dst)

    pieces = list(move(pieces_plan, ((2 * n_piece, q_cols),) * 4, here, by_chip, (q,)))
    for r in (1, 2, 3):
        pieces[r] = lax.ppermute(
            gate(pieces[r], before), "tp", [(i, i ^ r) for i in range(N_TP)]
        )
    attended = attend(
        bounds,
        here,
        q,
        n_wide,
        lo_wide,
        before,
        kv_new,
        own_rows,
        n_q,
        N_CTX * prefix_keys.shape[1],
        (pieces[0],),
    )

    def block_plan(at, src, out):
        for r, part in enumerate(src):
            for i in range(2):
                dst = out[r // 2].at[pl.ds((r % 2) * n_piece, n_piece), pl.ds(i * q_cols, q_cols)]
                yield one(part.at[pl.ds(i * n_piece, n_piece)], dst)

    wo_a, wo_b = move(block_plan, ((2 * n_piece, 2 * q_cols),) * 2, here, pieces, (attended,))
    wo_xa, wo_yb = swap(wo_a, 2), swap(wo_b, 4)
    wo_xb, wo_ya = swap(wo_b, 2), swap(wo_a, 4)

    attended = gate(attended, u4, d4, *pieces[1:])
    u1, d1 = hop_up(attended, every), hop_down(attended, every)
    near = pick(z, (d1, d1, u1, u1), here)

    wo_parts = (wo_a, wo_b, wo_xa, wo_xb, wo_ya, wo_yb, swap(wo_xa, 4), swap(wo_yb, 2))
    u2, d2 = hop_up(gate(u1, wo_xa, wo_yb), (1, 2)), hop_down(gate(d1, wo_xa, wo_yb), (1, 2))
    second = pick(z, (d2, d2, u2, u2), here)
    u3, d3 = hop_up(gate(u2, wo_ya), (2,)), hop_down(gate(d2, wo_ya), (2,))
    third = pick(z, (d3, u1, d1, u3), here, wo_parts[6:] + (wo_xb,))
    hs = []
    for part in (attended, near, second, third):
        hs += [part, swap(part, 1)]
    mine, theirs = out_project(ids, hs, wo_parts)
    theirs = swap(theirs, 1)
    head_share = jnp.where(
        first,
        jnp.concatenate([mine, theirs], axis=1),
        jnp.concatenate([theirs, mine], axis=1),
    ).astype(jnp.float32)
    pending_share = (
        lax.dynamic_slice_in_dim(pending[0], z * feat, feat, 1).astype(jnp.float32)
        + jnp.where(z == 0, 0, u4).astype(jnp.float32)
        + jnp.where(z == 3, 0, d4).astype(jnp.float32)
    )
    return (wide + (head_share + pending_share)).astype(jnp.bfloat16)


def solution(mesh):
    in_specs = (
        P("ctx", "tp"),
        P("tp", "ctx", None),
        P(),
        P("ctx", "tp"),
        P("ctx", None),
        P("ctx", None),
        P("tp", "ctx"),
        P(None, "ctx", None),
        P(None, "ctx", None),
        P("ctx"),
        P("ctx"),
        P(),
    )
    out_specs = P("ctx", "tp")
    small = mesh.shape["ctx"] == N_CTX and mesh.shape["tp"] == N_TP
    return jax.shard_map(
        per_device if small else per_device_any,
        mesh=mesh,
        in_specs=in_specs,
        out_specs=out_specs,
        check_vma=False,
    )
```

```python
import functools
import math

import jax
import jax.numpy as jnp
from jax import lax
from jax.experimental import pallas as pl
from jax.experimental.pallas import tpu as pltpu
from jax.sharding import PartitionSpec as P

HQ = 32
KVH = 8
HD = 128
NTRAJ = 16


ROPE_BASE = 500000.0
ROPE_FACTOR = 8.0
LOW_FREQ = 1.0
HIGH_FREQ = 4.0
INITIAL_SPAN = 8192.0
NORM_EPSILON = 1e-05
MASKED = -1e30


def inverse_freqs(head_width):
    pair_index = jnp.arange(head_width // 2, dtype=jnp.float32)
    base_freq = ROPE_BASE ** (-2.0 * pair_index / head_width)
    wavelength = 2.0 * math.pi / base_freq
    smooth = (INITIAL_SPAN / wavelength - LOW_FREQ) / (HIGH_FREQ - LOW_FREQ)
    blended = (1.0 - smooth) * base_freq / ROPE_FACTOR + smooth * base_freq
    return jnp.where(
        wavelength < INITIAL_SPAN / HIGH_FREQ,
        base_freq,
        jnp.where(wavelength > INITIAL_SPAN / LOW_FREQ, base_freq / ROPE_FACTOR, blended),
    )


def rotate(vectors, positions):
    head_width = vectors.shape[-1]
    angles = positions[..., None] * inverse_freqs(head_width)
    cosine = jnp.cos(angles)
    sinus = jnp.sin(angles)
    first_half = vectors[..., : head_width // 2]
    second_half = vectors[..., head_width // 2 :]
    return jnp.concatenate(
        [first_half * cosine - second_half * sinus, second_half * cosine + first_half * sinus],
        axis=-1,
    )


def visibility(key_labels, is_prefix, key_pos, query_segs, query_index):
    earlier = key_labels[None, :] <= query_segs[:, None]
    same = (key_labels[None, :] == query_segs[:, None]) & (key_pos[None, :] <= query_index[:, None])
    return jnp.where(is_prefix[None, :], earlier, same)


def attend_whole(grouped, key_block, value_block, seen):
    scores = jnp.einsum("hrd,hnd->hrn", grouped, key_block, preferred_element_type=jnp.float32) * (
        1.0 / math.sqrt(HD)
    )
    scores = jnp.where(seen[None], scores, MASKED)
    new_max = jnp.max(scores, axis=2)
    weights = jnp.where(seen[None], jnp.exp(scores - new_max[..., None]), 0.0)
    totals = jnp.sum(weights, axis=2)
    numerator = jnp.einsum(
        "hrn,hnd->hrd",
        weights.astype(jnp.bfloat16),
        value_block,
        preferred_element_type=jnp.float32,
    )
    return numerator / totals[..., None]


def per_device_any(
    stream,
    pending,
    norm_gain,
    w_query,
    w_key,
    w_value,
    w_out,
    prefix_keys,
    prefix_values,
    prefix_segments,
    stretch_segments,
    stretch_offset,
):
    tok_rows = stream.shape[0]
    prefix_rows = prefix_keys.shape[1]
    ctx_index = lax.axis_index("ctx")
    tp_index = lax.axis_index("tp")
    gain_wide = norm_gain.astype(jnp.float32)
    whole = lax.all_gather(stream, "tp", axis=1, tiled=True).astype(jnp.float32)
    mean_square = jnp.mean(whole * whole, axis=1, keepdims=True)
    normed = (whole * lax.rsqrt(mean_square + NORM_EPSILON) * gain_wide).astype(jnp.bfloat16)
    q_cols = w_query.shape[1]
    q_heads = q_cols // HD
    full_group = HQ // KVH
    kv_heads = max(1, q_heads // full_group)
    group_size = q_heads // kv_heads
    head_start = tp_index * q_heads // full_group
    kv_cols = kv_heads * HD
    key_slice = lax.dynamic_slice_in_dim(w_key, head_start * HD, kv_cols, 1)
    value_slice = lax.dynamic_slice_in_dim(w_value, head_start * HD, kv_cols, 1)
    pieces = (
        lax.all_gather(w_query, "ctx", axis=0, tiled=True),
        lax.all_gather(key_slice, "ctx", axis=0, tiled=True),
        lax.all_gather(value_slice, "ctx", axis=0, tiled=True),
    )
    query_raw, key_full, value_full = tuple(
        (jnp.dot(normed, piece_rows, preferred_element_type=jnp.float32) for piece_rows in pieces)
    )
    token_index = ctx_index * tok_rows + jnp.arange(tok_rows, dtype=jnp.int32)
    positions = stretch_offset[0].astype(jnp.float32) + token_index.astype(jnp.float32)
    query_rows = rotate(query_raw.reshape(tok_rows, q_heads, HD), positions[:, None]).astype(
        jnp.bfloat16
    )
    new_keys = jnp.transpose(
        rotate(key_full.reshape(tok_rows, kv_heads, HD), positions[:, None]).astype(jnp.bfloat16),
        (1, 0, 2),
    )
    new_values = jnp.transpose(
        value_full.astype(jnp.bfloat16).reshape(tok_rows, kv_heads, HD), (1, 0, 2)
    )
    old_keys = lax.dynamic_slice_in_dim(prefix_keys, head_start, kv_heads, 0)
    old_values = lax.dynamic_slice_in_dim(prefix_values, head_start, kv_heads, 0)
    local_keys = jnp.concatenate([old_keys, new_keys], 1)
    local_values = jnp.concatenate([old_values, new_values], 1)
    key_labels = jnp.concatenate([prefix_segments, stretch_segments])
    key_span = prefix_rows + tok_rows
    grouped = jnp.transpose(
        query_rows.reshape(tok_rows, kv_heads, group_size, HD), (1, 0, 2, 3)
    ).reshape(kv_heads, tok_rows * group_size, HD)
    query_index = jnp.repeat(token_index, group_size)
    query_segs = jnp.repeat(stretch_segments, group_size)
    both = jnp.stack([local_keys, local_values])
    kv_block = lax.all_gather(both, "ctx", axis=2, tiled=True)
    label_block = lax.all_gather(key_labels[None, None, :], "ctx", axis=2, tiled=True)
    key_count = kv_block.shape[2]
    absolute = jnp.arange(key_count, dtype=jnp.int32)
    within = absolute % key_span
    key_pos = absolute // key_span * tok_rows + within - prefix_rows
    seen = visibility(label_block[0, 0], within < prefix_rows, key_pos, query_segs, query_index)
    attended_heads = attend_whole(grouped, kv_block[0], kv_block[1], seen).astype(jnp.bfloat16)
    attended = jnp.transpose(
        attended_heads.reshape(kv_heads, tok_rows, group_size, HD), (1, 0, 2, 3)
    ).reshape(tok_rows, q_cols)
    head_terms = jnp.dot(
        attended,
        lax.all_gather(w_out, "ctx", axis=1, tiled=True),
        preferred_element_type=jnp.float32,
    )
    head_share, pending_share = (
        lax.psum_scatter(
            head_terms.astype(jnp.bfloat16), "tp", scatter_dimension=1, tiled=True
        ).astype(jnp.float32),
        lax.psum_scatter(
            pending[0].astype(jnp.float32).astype(jnp.bfloat16),
            "tp",
            scatter_dimension=1,
            tiled=True,
        ).astype(jnp.float32),
    )
    block_share = head_share + pending_share
    return (stream.astype(jnp.float32) + block_share).astype(jnp.bfloat16)


N_CTX = 8
N_TP = 4
GRANT = 60 * 1024 * 1024


def swap(x, bit):
    return lax.ppermute(x, "ctx", [(c, c ^ bit) for c in range(N_CTX)])


def hop_up(v, pairs):
    return lax.ppermute(v, "tp", [(i, i + 1) for i in pairs])


def hop_down(v, pairs):
    return lax.ppermute(v, "tp", [(N_TP - 1 - i, N_TP - 2 - i) for i in pairs])


def rotated(v, cosine, sinus):
    return v * cosine + pltpu.roll(v, HD // 2, 1) * sinus


HBM = pl.BlockSpec(memory_space=pltpu.HBM)
VMEM = pl.BlockSpec(memory_space=pltpu.VMEM)
SMEM = pl.BlockSpec(memory_space=pltpu.SMEM)
ANY = pl.BlockSpec(memory_space=pl.ANY)
LITTLE = pl.CostEstimate(flops=0, bytes_accessed=1024, transcendentals=0)


def specs_of(arrays):
    return [HBM if a.size > 200000 else ANY for a in arrays]


def move(plan, shapes, ids, sources, arrived=()):
    count = len(sources)

    def kernel(ids_ref, *refs):
        outs, sems = refs[count + len(arrived) : -1], refs[-1]
        waits = []
        for at, (choices, dst) in enumerate(plan(ids_ref, refs[:count], outs)):
            for cond, src in choices:
                copy = pltpu.make_async_copy(src, dst, sems.at[at])
                if cond is None:
                    copy.start()
                else:
                    pl.when(cond)(copy.start)
            waits.append(copy)
        for copy in waits:
            copy.wait()

    return pl.pallas_call(
        kernel,
        out_shape=tuple(jax.ShapeDtypeStruct(shape, jnp.bfloat16) for shape in shapes),
        in_specs=[SMEM] + [HBM] * count + specs_of(arrived),
        out_specs=tuple(VMEM for _ in shapes),
        scratch_shapes=[pltpu.SemaphoreType.DMA((40,))],
        compiler_params=pltpu.CompilerParams(vmem_limit_bytes=GRANT),
        cost_estimate=LITTLE,
        name=plan.__name__,
    )(ids, *sources, *arrived)


def gate(x, *arrived):
    return pl.pallas_call(
        lambda *refs: None,
        out_shape=jax.ShapeDtypeStruct(x.shape, x.dtype),
        in_specs=[HBM] + specs_of(arrived),
        out_specs=HBM,
        input_output_aliases={0: 0},
        compiler_params=pltpu.CompilerParams(vmem_limit_bytes=GRANT),
        cost_estimate=LITTLE,
        name="gate",
    )(x, *arrived)


def pick(z, options, ids, arrived=()):
    distinct = list({id(o): o for o in options}.values())

    def pick_plan(at, src, out):
        yield (
            [(at[2] == i, src[[o is d for d in distinct].index(True)]) for i, o in enumerate(options)],
            out[0],
        )

    return move(pick_plan, (options[0].shape,), ids, distinct, arrived)[0]


def hops(ids, pending, up, down, offset, relay, both, rows, arrived=()):
    tok, feat = pending.shape[1], up.shape[1]

    def kernel(ids_ref, pending_ref, up_ref, down_ref, *refs):
        out_up, out_down, buf, sems = refs[len(arrived) :]
        z = ids_ref[2]
        todo = []
        for i, (src, out, step, at) in enumerate(
            ((up_ref, out_up, offset, z), (down_ref, out_down, -offset, N_TP - 1 - z))
        ):
            is_relay = functools.reduce(jnp.logical_or, [at == p for p in relay], at < 0)
            is_both = functools.reduce(jnp.logical_or, [at == p for p in both], at < 0)
            place = jnp.clip(z + step, 0, N_TP - 1)
            share = pltpu.make_async_copy(
                pending_ref.at[0, :, pl.ds(multiple(place, feat), feat)],
                out.at[pl.ds(0, tok)],
                sems.at[i],
            )
            passed = pltpu.make_async_copy(src.at[pl.ds(0, rows)], out, sems.at[i])
            added = pltpu.make_async_copy(src.at[pl.ds(0, tok)], buf.at[i], sems.at[2 + i])
            pl.when(is_relay)(passed.start)

            @pl.when(jnp.logical_not(is_relay))
            def _():
                if rows > tok:
                    out[tok:] = jnp.zeros((rows - tok, feat), jnp.bfloat16)
                share.start()

            pl.when(is_both)(added.start)
            todo.append((passed, share, added, is_relay, is_both, out, i))
        for passed, share, added, is_relay, is_both, out, i in todo:
            pl.when(is_relay)(passed.wait)
            pl.when(jnp.logical_not(is_relay))(share.wait)

            @pl.when(is_both)
            def _():
                added.wait()
                out[:tok] += buf[i]

    shape = jax.ShapeDtypeStruct((rows, feat), jnp.bfloat16)
    return pl.pallas_call(
        kernel,
        out_shape=(shape, shape),
        in_specs=[SMEM, HBM, HBM, HBM] + specs_of(arrived),
        out_specs=(VMEM, VMEM),
        scratch_shapes=[
            pltpu.VMEM((2, tok, feat), jnp.bfloat16),
            pltpu.SemaphoreType.DMA((4,)),
        ],
        compiler_params=pltpu.CompilerParams(vmem_limit_bytes=GRANT),
        cost_estimate=LITTLE,
        name="hops",
    )(ids, pending, up, down, *arrived)


def one(src, dst):
    return ([(None, src)], dst)


def multiple(value, of=128):
    return pl.multiple_of(value * of, of)


AHEAD = 3
PARTS = ((0, 0), (0, 1), (1, 0), (2, 0))


def project_kernel(slots, x_count, w_count, tok, rows, scale, at_kv, ids_ref, *refs):
    last = scale is not None
    xs, ws, refs = refs[:x_count], refs[x_count : x_count + w_count], refs[x_count + w_count :]
    x_buf, w_buf, x_sem, w_sem = refs[-4:]
    chip, core = ids_ref[0], ids_ref[1]
    half, cols = x_buf.shape[-1], ws[0].shape[1]
    fold = half // 2
    mine = pl.multiple_of(core * tok, 128)
    theirs = pl.multiple_of((1 - core) * tok, 128)

    def fetch(at):
        part, h = ids_ref[7 + slots[at // 2]], at % 2
        place = ids_ref[3 + part]
        waits = []
        for i in range(3):
            for m in range(w_count // 2):
                src, dst = ws[2 * m + h], w_buf.at[at]
                if i == 0:
                    src, dst = src.at[pl.ds(0, half)], dst.at[:, pl.ds(0, cols)]
                else:
                    lanes = pl.ds((i - 1) * 2 * HD, 2 * HD)
                    src = src.at[pl.ds(at_kv, fold), lanes]
                    dst = dst.at[pl.ds((i - 1) * fold, fold), pl.ds(cols, 2 * HD)]
                copy = pltpu.make_async_copy(src, dst, w_sem.at[3 * at + i])
                pl.when((place ^ chip) == m)(copy.start)
            waits.append(copy)
        features = pl.ds(pl.multiple_of((core ^ h) * half, 128), half)
        for s, to in ((0, mine), (1, theirs)):
            for r, (index, group) in enumerate(PARTS):
                if 2 * index < x_count:
                    src = xs[2 * index + s].at[pl.ds(group * rows, tok), features]
                    dst = x_buf.at[at, pl.ds(to, tok)]
                    copy = pltpu.make_async_copy(src, dst, x_sem.at[2 * at + s])
                    pl.when(part == r)(copy.start)
            waits.append(copy)
        return waits

    ahead = [fetch(at) for at in range(AHEAD)]
    acc = refs[0][...] if last else 0.0
    for at in range(4):
        for copy in ahead[at]:
            copy.wait()
        if at + AHEAD < 4:
            ahead.append(fetch(at + AHEAD))
        acc = acc + jnp.dot(x_buf[at], w_buf[at], preferred_element_type=jnp.float32)
    if not last:
        refs[0][...] = acc
        return
    factor_ref, cos_ref, sin_ref, q_ref, kv_ref, tail_ref = refs[1:7]
    factor = factor_ref[...]
    heads = q_ref.shape[0]
    for h in range(heads + 2):
        v = acc[:, h * HD : (h + 1) * HD] * factor
        if h <= heads:
            v = rotated(v, cos_ref[...], sin_ref[...])
        if h < heads:
            q_ref[h] = (v * scale).astype(jnp.bfloat16)
        else:
            kv_ref[h - heads] = v.astype(jnp.bfloat16)
            tail_ref[h - heads] = v[tok:].astype(jnp.bfloat16)


def project(ids, slots, xs, weights, tok, at_kv, tables=(), scale=None):
    rows = xs[0].shape[0] // 2
    feat = xs[0].shape[1]
    cols = weights[0].shape[1]
    half = feat // 2
    sums = jax.ShapeDtypeStruct((2 * tok, cols + 2 * HD), jnp.float32)
    results = (
        jax.ShapeDtypeStruct((cols // HD, 2 * tok, HD), jnp.bfloat16),
        jax.ShapeDtypeStruct((2, 2 * tok, HD), jnp.bfloat16),
        jax.ShapeDtypeStruct((2, tok, HD), jnp.bfloat16),
    )
    return pl.pallas_call(
        functools.partial(
            project_kernel, slots, len(xs), len(weights), tok, rows, scale, at_kv
        ),
        out_shape=results if tables else sums,
        in_specs=[SMEM] + [HBM] * (len(xs) + len(weights)) + [VMEM] * len(tables),
        out_specs=(VMEM,) * 3 if tables else VMEM,
        scratch_shapes=[
            pltpu.VMEM((4, 2 * tok, half), jnp.bfloat16),
            pltpu.VMEM((4, half, cols + 2 * HD), jnp.bfloat16),
            pltpu.SemaphoreType.DMA((8,)),
            pltpu.SemaphoreType.DMA((12,)),
        ],
        compiler_params=pltpu.CompilerParams(vmem_limit_bytes=GRANT),
        cost_estimate=LITTLE,
        name="project",
    )(ids, *xs, *weights, *tables)


BT = 256
BK = 1024
CHAIN = 2


def scores(q, k):
    return lax.dot_general(q, k, (((1,), (1,)), ((), ())), preferred_element_type=jnp.float32)


def absorb(s, v_ext, m, acc):
    new = jnp.maximum(m, jnp.max(s, axis=1, keepdims=True))
    p = jnp.exp2((s - new).astype(jnp.bfloat16))
    acc = acc * jnp.exp2(m - new) + jnp.dot(p, v_ext, preferred_element_type=jnp.float32)
    return new, acc


def attend_kernel(at_old, bound_ref, ids_ref, q_ref, n_ref, lo_ref, before_ref, new_ref, *refs):
    bundles, (out_ref, k_old, v_ext, kv_near, s_ref, m_ref, acc_ref, sems) = refs[:8], refs[-8:]
    halo = before_ref.shape[1]
    b = pl.program_id(0)
    heads, bt = q_ref.shape[0], q_ref.shape[1]
    rows, chains = CHAIN * bt, heads // CHAIN
    last = k_old.shape[0] // BK - 1
    fold = k_old.shape[0] // (2 * N_CTX)

    @pl.when(b == 0)
    def _():
        copies = []
        for index, bundle in enumerate(bundles):
            place = ((ids_ref[0] ^ (index // 2)) * 2 + (ids_ref[1] ^ (index % 2))) * 2 * fold
            for i in range(4):
                dst = (k_old, v_ext)[i // 2]
                to = pl.ds(pl.multiple_of(place + (i % 2) * fold, 128), fold)
                copies.append(
                    pltpu.make_async_copy(
                        bundle.at[pl.ds(at_old, fold), pl.ds(i * HD, HD)],
                        dst.at[to, pl.ds(0, HD)],
                        sems.at[4 * index + i],
                    )
                )
        for copy in copies:
            copy.start()
        v_ext[:, HD:] = jnp.ones((v_ext.shape[0], HD), jnp.bfloat16)
        kv_near[:, :halo] = before_ref[...]
        kv_near[:, halo:] = new_ref[...]
        for copy in copies:
            copy.wait()

    m_ref[...] = jnp.full_like(m_ref, MASKED)
    acc_ref[...] = jnp.zeros_like(acc_ref)

    def query(g):
        return q_ref[g * CHAIN : (g + 1) * CHAIN].reshape(rows, HD)

    s_ref[...] = scores(query(0), k_old[:BK, :])

    def body(kb, masked):
        start = pl.multiple_of(kb * BK, BK)
        follow = pl.multiple_of(jnp.minimum(kb + 1, last) * BK, BK)
        ms = [m_ref[g][:, :1] for g in range(chains)]
        accs = [acc_ref[g] for g in range(chains)]
        s = s_ref[...]
        v = v_ext[pl.ds(start, BK), :]
        for g in range(chains):
            at, who = (start, g + 1) if g + 1 < chains else (follow, 0)
            ahead = scores(query(who), k_old[pl.ds(at, BK), :])
            if masked:
                n_rows = jnp.concatenate([n_ref[:, :1]] * CHAIN, axis=0)
                col = lax.broadcasted_iota(jnp.int32, s.shape, 1) + start
                s = jnp.where(col < n_rows, s, MASKED)
            ms[g], accs[g] = absorb(s, v, ms[g], accs[g])
            s = ahead
        s_ref[...] = s
        for g in range(chains):
            m_ref[g] = jnp.broadcast_to(ms[g], (rows, 128))
            acc_ref[g] = accs[g]

    full = bound_ref[0, b] // BK
    some = (bound_ref[1, b] + BK - 1) // BK
    lax.fori_loop(0, full, lambda kb, c: (body(kb, False), c)[1], 0)
    lax.fori_loop(full, some, lambda kb, c: (body(kb, True), c)[1], 0)

    span = halo + bt
    start = pl.multiple_of(b * bt, bt)
    k = kv_near[0, pl.ds(start, span), :]
    v = kv_near[1, pl.ds(start, span), :]
    v = jnp.concatenate([v, jnp.ones_like(v)], axis=1)
    lo = jnp.concatenate([lo_ref[:, :1]] * CHAIN, axis=0)
    col = lax.broadcasted_iota(jnp.int32, (rows, span), 1)
    row = lax.broadcasted_iota(jnp.int32, (rows, span), 0) % bt
    seen = (col + start >= lo) & (col <= row + halo)
    for g in range(chains):
        s = jnp.where(seen, scores(query(g), k), MASKED)
        _, acc = absorb(s, v, m_ref[g][:, :1], acc_ref[g])
        mixed = (acc[:, :HD] / acc[:, HD:]).astype(jnp.bfloat16)
        for h in range(CHAIN):
            at = (g * CHAIN + h) * HD
            out_ref[:, at : at + HD] = mixed[h * bt : (h + 1) * bt]


def attend(bounds, ids, q, n_tok, lo_tok, before, new, bundles, at_old, keys, arrived=()):
    heads, tokens = q.shape[:2]
    chains, rows = heads // CHAIN, CHAIN * BT
    halo = before.shape[1]
    return pl.pallas_call(
        functools.partial(attend_kernel, at_old),
        out_shape=jax.ShapeDtypeStruct((tokens, heads * HD), jnp.bfloat16),
        grid_spec=pltpu.PrefetchScalarGridSpec(
            num_scalar_prefetch=2,
            grid=(tokens // BT,),
            in_specs=[
                pl.BlockSpec((heads, BT, HD), lambda b, *_: (0, b, 0)),
                pl.BlockSpec((BT, 128), lambda b, *_: (b, 0)),
                pl.BlockSpec((BT, 128), lambda b, *_: (b, 0)),
                pl.BlockSpec(before.shape, lambda b, *_: (0, 0, 0)),
                pl.BlockSpec(new.shape, lambda b, *_: (0, 0, 0)),
            ]
            + [HBM] * 8
            + specs_of(arrived),
            out_specs=pl.BlockSpec((BT, heads * HD), lambda b, *_: (b, 0)),
            scratch_shapes=[
                pltpu.VMEM((keys, HD), jnp.bfloat16),
                pltpu.VMEM((keys, 2 * HD), jnp.bfloat16),
                pltpu.VMEM((2, halo + tokens, HD), jnp.bfloat16),
                pltpu.VMEM((rows, BK), jnp.float32),
                pltpu.VMEM((chains, rows, 128), jnp.float32),
                pltpu.VMEM((chains, rows, 2 * HD), jnp.float32),
                pltpu.SemaphoreType.DMA((32,)),
            ],
        ),
        compiler_params=pltpu.CompilerParams(vmem_limit_bytes=GRANT),
        cost_estimate=LITTLE,
        name="attend",
    )(bounds, ids, q, n_tok, lo_tok, before, new, *bundles, *arrived)


def out_kernel(ids_ref, *refs):
    xs, ws = refs[:8], refs[8:16]
    keep_ref, give_ref, x_buf, w_buf, o_buf, x_sem, w_sem = refs[16:]
    chip, core, z = ids_ref[0], ids_ref[1], ids_ref[2]
    width = xs[0].shape[1]
    rows = w_buf.shape[1] // 4
    for r in range(4):
        near = ids_ref[3 + r] ^ z
        for m in range(4):
            to = w_buf.at[r, pl.ds(pl.multiple_of((chip ^ m) * rows, 128), rows)]
            for i in range(2):
                src = ws[2 * m + i].at[pl.ds(pl.multiple_of((near % 2) * rows, 128), rows)]
                copy = pltpu.make_async_copy(src, to, w_sem.at[4 * r + m])
                pl.when(near // 2 == i)(copy.start)
        for s in range(2):
            at = pl.multiple_of((core ^ s) * width, 128)
            pltpu.make_async_copy(
                xs[2 * r + s], x_buf.at[r, :, pl.ds(at, width)], x_sem.at[2 * r + s]
            ).start()
    acc = None
    for r in range(4):
        for m in range(4):
            pltpu.make_async_copy(
                ws[0].at[pl.ds(0, rows)], w_buf.at[r, pl.ds(0, rows)], w_sem.at[4 * r + m]
            ).wait()
        for s in range(2):
            pltpu.make_async_copy(
                xs[0], x_buf.at[r, :, pl.ds(0, width)], x_sem.at[2 * r + s]
            ).wait()
        term = jnp.dot(x_buf[r], w_buf[r], preferred_element_type=jnp.float32)
        acc = term if acc is None else acc + term
    o_buf[...] = acc.astype(jnp.bfloat16)
    half = keep_ref.shape[0]
    keep_ref[...] = o_buf[pl.ds(pl.multiple_of(core * half, 128), half)]
    give_ref[...] = o_buf[pl.ds(pl.multiple_of((1 - core) * half, 128), half)]


def out_project(ids, xs, ws):
    tokens, width = xs[0].shape
    depth, cols = 2 * ws[0].shape[0], ws[0].shape[1]
    return pl.pallas_call(
        out_kernel,
        out_shape=(jax.ShapeDtypeStruct((tokens // 2, cols), jnp.bfloat16),) * 2,
        in_specs=[SMEM] + [HBM] * 16,
        out_specs=(VMEM, VMEM),
        scratch_shapes=[
            pltpu.VMEM((4, tokens, 2 * width), jnp.bfloat16),
            pltpu.VMEM((4, depth, cols), jnp.bfloat16),
            pltpu.VMEM((tokens, cols), jnp.bfloat16),
            pltpu.SemaphoreType.DMA((8,)),
            pltpu.SemaphoreType.DMA((16,)),
        ],
        compiler_params=pltpu.CompilerParams(vmem_limit_bytes=GRANT),
        cost_estimate=LITTLE,
        name="out_project",
    )(ids, *xs, *ws)


def per_device(
    stream,
    pending,
    norm_gain,
    w_query,
    w_key,
    w_value,
    w_out,
    prefix_keys,
    prefix_values,
    prefix_segments,
    stretch_segments,
    stretch_offset,
):
    tok, feat = stream.shape
    chip_tok = 2 * tok
    c = lax.axis_index("ctx")
    z = lax.axis_index("tp")
    chip, core = c // 2, c % 2
    first = core == 0
    depth = feat * N_TP

    wide = stream.astype(jnp.float32)
    here = jnp.stack([chip, core, z]).astype(jnp.int32)
    every = (0, 1, 2)

    gain = lax.dynamic_slice_in_dim(norm_gain, z * feat, feat, 0).astype(jnp.float32)
    scaled = (wide * gain[None, :]).astype(jnp.bfloat16)

    left = jnp.sum(wide * wide, axis=1)
    sums = []
    for _ in range(3):
        sums.append(lax.reduce_precision(left, 8, 7))
        left = left - sums[-1]
    sums = jnp.pad(jnp.stack(sums), ((0, 13), (0, feat - tok))).astype(jnp.bfloat16)
    scaled = jnp.concatenate([scaled, sums], axis=0)
    n_rows = scaled.shape[0]

    def squares(part, group=0):
        at = group * n_rows + tok
        return jnp.sum(part[at : at + 3, :tok].astype(jnp.float32), axis=0)


    labels = jnp.arange(NTRAJ, dtype=jnp.int32)
    counts = jnp.concatenate(
        [
            jnp.sum((prefix_segments[:, None] <= labels).astype(jnp.int32), axis=0),
            jnp.sum((stretch_segments[:, None] < labels).astype(jnp.int32), axis=0),
        ]
    )
    notes = jnp.concatenate([counts // 32, counts % 32])
    cols = w_query.shape[1] // 2
    notes = jnp.stack(
        [jnp.pad(v, (0, cols - v.shape[0])) for v in (stretch_segments, notes)]
        + [jnp.zeros((cols,), jnp.int32)] * 14
    ).astype(jnp.bfloat16)

    token_index = chip * chip_tok + jnp.arange(chip_tok, dtype=jnp.int32)
    positions = stretch_offset[0].astype(jnp.float32) + token_index.astype(jnp.float32)
    angles = positions[:, None] * inverse_freqs(HD)
    cosine, sinus = jnp.cos(angles), jnp.sin(angles)
    cosine = jnp.concatenate([cosine, cosine], axis=1)
    sinus = jnp.concatenate([-sinus, sinus], axis=1)

    q_heads = w_query.shape[1] // HD // 2
    q_cols = q_heads * HD
    n_q = w_query.shape[0]
    fold = prefix_keys.shape[1] // 2
    n_both = n_q + fold
    n_kv = w_key.shape[0] // 2
    n_piece = w_out.shape[0] // 4

    def first_plan(at, src, out):
        w_q, w_k, w_v, keys, values, said = src
        for dst, j in ((out[0], at[1]), (out[1], 1 - at[1])):
            head = 2 * at[2] + j
            yield one(w_q.at[:, pl.ds(multiple(j, q_cols), q_cols)], dst.at[pl.ds(0, n_q)])
            for i, a in enumerate((keys, keys, values, values)):
                part = a.at[head, pl.ds((i % 2) * fold, fold)]
                yield one(part, dst.at[pl.ds(n_q, fold), pl.ds(i * HD, HD)])
            for i, a in enumerate((w_k, w_v, w_k, w_v)):
                part = a.at[pl.ds((i // 2) * n_kv, n_kv), pl.ds(multiple(head), HD)]
                yield one(part, dst.at[pl.ds(n_both, n_kv), pl.ds(i * HD, HD)])
            yield one(said, dst.at[pl.ds(n_both + n_kv, said.shape[0])])

    own, give = move(
        first_plan,
        ((n_both + n_kv + notes.shape[0], q_cols),) * 2,
        here,
        (w_query, w_key, w_value, prefix_keys, prefix_values, notes),
    )
    places = jnp.stack(
        [z, jnp.where(z < 2, z + 1, z - 1), jnp.where(z < 2, z + 2, z - 2), jnp.where(z % 2 == 1, 0, 3)]
    ).astype(jnp.int32)
    skip = jnp.sum(jnp.where(places == (chip ^ 3), jnp.arange(N_TP), 0))
    order = jnp.stack(
        [
            jnp.where(skip == 0, 1, 0),
            jnp.where(skip < 2, 2, 1),
            jnp.minimum(skip, 2),
            jnp.full((), 3),
        ]
    )
    ids = jnp.concatenate([here, places, order]).astype(jnp.int32)

    x1, y1, given = swap(own, 2), swap(own, 4), swap(give, 1)
    turn = swap(gate(notes, own), 1)
    scaled = gate(scaled, turn)
    u1, d1 = hop_up(scaled, every), hop_down(scaled, every)

    def piece_plan(at, src, out):
        for r, dst in enumerate(out):
            rows = pl.ds(multiple(at[0] ^ r, n_piece), n_piece)
            for i in range(2):
                part = src[0].at[rows, pl.ds(i * q_cols, q_cols)]
                yield one(part, dst.at[pl.ds(i * n_piece, n_piece)])

    by_chip = move(
        piece_plan,
        ((2 * n_piece, q_cols),) * 4,
        here,
        (w_out,),
        (own,),
    )
    given = gate(given, x1, y1)
    up, down = hops(here, pending, u1, d1, 3, (1, 2, 3), (), n_rows, (cosine, sinus, given, by_chip[0]))
    u2, d2 = hop_up(up, every), hop_down(down, every)
    x2, y2 = swap(given, 2), swap(given, 4)

    def near_plan(at, src, out):
        own_part, up_part, down_part = src
        yield one(own_part, out[0].at[pl.ds(0, n_rows)])
        near = [(at[2] < 2, down_part), (at[2] >= 2, up_part)]
        yield (near, out[0].at[pl.ds(n_rows, n_rows)])

    (near,) = move(near_plan, ((2 * n_rows, feat),), here, (scaled, u1, d1), (up,))

    x1, y2 = gate(x1, x2, y2, u2, d2), gate(y2, x2, u2, d2)
    up, down = hops(here, pending, u2, d2, 2, (2,), (1,), n_rows, (x1, y2, near))
    u3, d3 = hop_up(up, every), hop_down(down, every)
    far_own, far_other = swap(x1, 4), swap(y2, 2)
    near = gate(near, up)
    over1 = swap(near, 1)
    second = pick(z, (d2, d2, u2, u2), here, (up,))
    over2 = swap(second, 1)
    own_rows = (own, given, x1, x2, y1, y2, far_own, far_other)
    xs = [near, over1, second, over2]
    sums = project(ids, (0, 1), xs, own_rows[:6], tok, n_both)

    third = pick(z, (d3, u1, d1, u3), here, (sums, far_own, far_other))
    over3 = swap(third, 1)
    up, down = hops(here, pending, u3, d3, 1, (), (1, 2, 3), tok, (third,))
    u4, d4 = hop_up(up, every), hop_down(down, every)
    mine, theirs = (
        squares(a) + squares(a, 1) + squares(b) + squares(c)
        for a, b, c in ((near, second, third), (over1, over2, over3))
    )
    total = jnp.where(first, jnp.concatenate([mine, theirs]), jnp.concatenate([theirs, mine]))
    factor = lax.rsqrt(total * (1.0 / depth) + NORM_EPSILON)
    factor = jnp.broadcast_to(factor[:, None], (chip_tok, 128))
    xs += [third, over3]

    said = [rows[n_both + n_kv : n_both + n_kv + 2].astype(jnp.float32) for rows in own_rows]
    total = sum(v[1, : 4 * NTRAJ] for v in said).astype(jnp.int32)
    total = total[: 2 * NTRAJ] * 32 + total[2 * NTRAJ :]
    segs = [v[0, :tok].astype(jnp.int32) for v in said[:2]]
    segs = jnp.where(first, jnp.concatenate(segs), jnp.concatenate(segs[::-1]))
    onehot = (segs[:, None] == labels).astype(jnp.int32)
    n_tok = jnp.sum(onehot * total[:NTRAJ], axis=1)
    lo_tok = jnp.sum(onehot * total[NTRAJ:], axis=1) - chip * chip_tok + tok
    blocked = n_tok.reshape(chip_tok // BT, BT)
    bounds = jnp.stack([blocked[:, 0], blocked[:, -1]])
    n_wide = jnp.broadcast_to(n_tok[:, None], (chip_tok, 128))
    lo_wide = jnp.broadcast_to(lo_tok[:, None], (chip_tok, 128))

    by_chip = (by_chip[0],) + tuple(
        swap(gate(by_chip[r], far_own, far_other), 2 * r) for r in (1, 2, 3)
    )
    scale = math.log2(math.e) / math.sqrt(HD)
    q, kv_new, tail = project(
        ids, (2, 3), xs, own_rows, tok, n_both, (sums, factor, cosine, sinus), scale
    )
    before = lax.ppermute(tail, "ctx", [(i, i + 2) for i in range(N_CTX - 2)])

    def pieces_plan(at, src, out):
        for r, dst in enumerate(out):
            near = (at[2] ^ r) ^ at[0]
            yield ([(near == m, src[m]) for m in range(4)], dst)

    pieces = list(move(pieces_plan, ((2 * n_piece, q_cols),) * 4, here, by_chip, (q,)))
    for r in (1, 2, 3):
        pieces[r] = lax.ppermute(
            gate(pieces[r], before), "tp", [(i, i ^ r) for i in range(N_TP)]
        )
    attended = attend(
        bounds,
        here,
        q,
        n_wide,
        lo_wide,
        before,
        kv_new,
        own_rows,
        n_q,
        N_CTX * prefix_keys.shape[1],
        (pieces[0],),
    )

    def block_plan(at, src, out):
        for r, part in enumerate(src):
            for i in range(2):
                dst = out[r // 2].at[pl.ds((r % 2) * n_piece, n_piece), pl.ds(i * q_cols, q_cols)]
                yield one(part.at[pl.ds(i * n_piece, n_piece)], dst)

    wo_a, wo_b = move(block_plan, ((2 * n_piece, 2 * q_cols),) * 2, here, pieces, (attended,))
    wo_xa, wo_yb = swap(wo_a, 2), swap(wo_b, 4)
    wo_xb, wo_ya = swap(wo_b, 2), swap(wo_a, 4)

    attended = gate(attended, u4, d4, *pieces[1:])
    u1, d1 = hop_up(attended, every), hop_down(attended, every)
    near = pick(z, (d1, d1, u1, u1), here)

    wo_parts = (wo_a, wo_b, wo_xa, wo_xb, wo_ya, wo_yb, swap(wo_xa, 4), swap(wo_yb, 2))
    u2, d2 = hop_up(gate(u1, wo_xa, wo_yb), (1, 2)), hop_down(gate(d1, wo_xa, wo_yb), (1, 2))
    second = pick(z, (d2, d2, u2, u2), here)
    u3, d3 = hop_up(gate(u2, wo_xb, wo_ya), (2,)), hop_down(gate(d2, wo_xb, wo_ya), (2,))
    third = pick(z, (d3, u1, d1, u3), here, wo_parts[6:])
    hs = []
    for part in (attended, near, second, third):
        hs += [part, swap(part, 1)]
    mine, theirs = out_project(ids, hs, wo_parts)
    theirs = swap(theirs, 1)
    head_share = jnp.where(
        first,
        jnp.concatenate([mine, theirs], axis=1),
        jnp.concatenate([theirs, mine], axis=1),
    ).astype(jnp.float32)
    pending_share = (
        lax.dynamic_slice_in_dim(pending[0], z * feat, feat, 1).astype(jnp.float32)
        + jnp.where(z == 0, 0, u4).astype(jnp.float32)
        + jnp.where(z == 3, 0, d4).astype(jnp.float32)
    )
    return (wide + (head_share + pending_share)).astype(jnp.bfloat16)


def solution(mesh):
    in_specs = (
        P("ctx", "tp"),
        P("tp", "ctx", None),
        P(),
        P("ctx", "tp"),
        P("ctx", None),
        P("ctx", None),
        P("tp", "ctx"),
        P(None, "ctx", None),
        P(None, "ctx", None),
        P("ctx"),
        P("ctx"),
        P(),
    )
    out_specs = P("ctx", "tp")
    small = mesh.shape["ctx"] == N_CTX and mesh.shape["tp"] == N_TP
    return jax.shard_map(
        per_device if small else per_device_any,
        mesh=mesh,
        in_specs=in_specs,
        out_specs=out_specs,
        check_vma=False,
    )
```

```python
import functools
import math

import jax
import jax.numpy as jnp
from jax import lax
from jax.experimental import pallas as pl
from jax.experimental.pallas import tpu as pltpu
from jax.sharding import PartitionSpec as P

HQ = 32
KVH = 8
HD = 128
NTRAJ = 16


ROPE_BASE = 500000.0
ROPE_FACTOR = 8.0
LOW_FREQ = 1.0
HIGH_FREQ = 4.0
INITIAL_SPAN = 8192.0
NORM_EPSILON = 1e-05
MASKED = -1e30


def inverse_freqs(head_width):
    pair_index = jnp.arange(head_width // 2, dtype=jnp.float32)
    base_freq = ROPE_BASE ** (-2.0 * pair_index / head_width)
    wavelength = 2.0 * math.pi / base_freq
    smooth = (INITIAL_SPAN / wavelength - LOW_FREQ) / (HIGH_FREQ - LOW_FREQ)
    blended = (1.0 - smooth) * base_freq / ROPE_FACTOR + smooth * base_freq
    return jnp.where(
        wavelength < INITIAL_SPAN / HIGH_FREQ,
        base_freq,
        jnp.where(wavelength > INITIAL_SPAN / LOW_FREQ, base_freq / ROPE_FACTOR, blended),
    )


def rotate(vectors, positions):
    head_width = vectors.shape[-1]
    angles = positions[..., None] * inverse_freqs(head_width)
    cosine = jnp.cos(angles)
    sinus = jnp.sin(angles)
    first_half = vectors[..., : head_width // 2]
    second_half = vectors[..., head_width // 2 :]
    return jnp.concatenate(
        [first_half * cosine - second_half * sinus, second_half * cosine + first_half * sinus],
        axis=-1,
    )


def visibility(key_labels, is_prefix, key_pos, query_segs, query_index):
    earlier = key_labels[None, :] <= query_segs[:, None]
    same = (key_labels[None, :] == query_segs[:, None]) & (key_pos[None, :] <= query_index[:, None])
    return jnp.where(is_prefix[None, :], earlier, same)


def attend_whole(grouped, key_block, value_block, seen):
    scores = jnp.einsum("hrd,hnd->hrn", grouped, key_block, preferred_element_type=jnp.float32) * (
        1.0 / math.sqrt(HD)
    )
    scores = jnp.where(seen[None], scores, MASKED)
    new_max = jnp.max(scores, axis=2)
    weights = jnp.where(seen[None], jnp.exp(scores - new_max[..., None]), 0.0)
    totals = jnp.sum(weights, axis=2)
    numerator = jnp.einsum(
        "hrn,hnd->hrd",
        weights.astype(jnp.bfloat16),
        value_block,
        preferred_element_type=jnp.float32,
    )
    return numerator / totals[..., None]


def per_device_any(
    stream,
    pending,
    norm_gain,
    w_query,
    w_key,
    w_value,
    w_out,
    prefix_keys,
    prefix_values,
    prefix_segments,
    stretch_segments,
    stretch_offset,
):
    tok_rows = stream.shape[0]
    prefix_rows = prefix_keys.shape[1]
    ctx_index = lax.axis_index("ctx")
    tp_index = lax.axis_index("tp")
    gain_wide = norm_gain.astype(jnp.float32)
    whole = lax.all_gather(stream, "tp", axis=1, tiled=True).astype(jnp.float32)
    mean_square = jnp.mean(whole * whole, axis=1, keepdims=True)
    normed = (whole * lax.rsqrt(mean_square + NORM_EPSILON) * gain_wide).astype(jnp.bfloat16)
    q_cols = w_query.shape[1]
    q_heads = q_cols // HD
    full_group = HQ // KVH
    kv_heads = max(1, q_heads // full_group)
    group_size = q_heads // kv_heads
    head_start = tp_index * q_heads // full_group
    kv_cols = kv_heads * HD
    key_slice = lax.dynamic_slice_in_dim(w_key, head_start * HD, kv_cols, 1)
    value_slice = lax.dynamic_slice_in_dim(w_value, head_start * HD, kv_cols, 1)
    pieces = (
        lax.all_gather(w_query, "ctx", axis=0, tiled=True),
        lax.all_gather(key_slice, "ctx", axis=0, tiled=True),
        lax.all_gather(value_slice, "ctx", axis=0, tiled=True),
    )
    query_raw, key_full, value_full = tuple(
        (jnp.dot(normed, piece_rows, preferred_element_type=jnp.float32) for piece_rows in pieces)
    )
    token_index = ctx_index * tok_rows + jnp.arange(tok_rows, dtype=jnp.int32)
    positions = stretch_offset[0].astype(jnp.float32) + token_index.astype(jnp.float32)
    query_rows = rotate(query_raw.reshape(tok_rows, q_heads, HD), positions[:, None]).astype(
        jnp.bfloat16
    )
    new_keys = jnp.transpose(
        rotate(key_full.reshape(tok_rows, kv_heads, HD), positions[:, None]).astype(jnp.bfloat16),
        (1, 0, 2),
    )
    new_values = jnp.transpose(
        value_full.astype(jnp.bfloat16).reshape(tok_rows, kv_heads, HD), (1, 0, 2)
    )
    old_keys = lax.dynamic_slice_in_dim(prefix_keys, head_start, kv_heads, 0)
    old_values = lax.dynamic_slice_in_dim(prefix_values, head_start, kv_heads, 0)
    local_keys = jnp.concatenate([old_keys, new_keys], 1)
    local_values = jnp.concatenate([old_values, new_values], 1)
    key_labels = jnp.concatenate([prefix_segments, stretch_segments])
    key_span = prefix_rows + tok_rows
    grouped = jnp.transpose(
        query_rows.reshape(tok_rows, kv_heads, group_size, HD), (1, 0, 2, 3)
    ).reshape(kv_heads, tok_rows * group_size, HD)
    query_index = jnp.repeat(token_index, group_size)
    query_segs = jnp.repeat(stretch_segments, group_size)
    both = jnp.stack([local_keys, local_values])
    kv_block = lax.all_gather(both, "ctx", axis=2, tiled=True)
    label_block = lax.all_gather(key_labels[None, None, :], "ctx", axis=2, tiled=True)
    key_count = kv_block.shape[2]
    absolute = jnp.arange(key_count, dtype=jnp.int32)
    within = absolute % key_span
    key_pos = absolute // key_span * tok_rows + within - prefix_rows
    seen = visibility(label_block[0, 0], within < prefix_rows, key_pos, query_segs, query_index)
    attended_heads = attend_whole(grouped, kv_block[0], kv_block[1], seen).astype(jnp.bfloat16)
    attended = jnp.transpose(
        attended_heads.reshape(kv_heads, tok_rows, group_size, HD), (1, 0, 2, 3)
    ).reshape(tok_rows, q_cols)
    head_terms = jnp.dot(
        attended,
        lax.all_gather(w_out, "ctx", axis=1, tiled=True),
        preferred_element_type=jnp.float32,
    )
    head_share, pending_share = (
        lax.psum_scatter(
            head_terms.astype(jnp.bfloat16), "tp", scatter_dimension=1, tiled=True
        ).astype(jnp.float32),
        lax.psum_scatter(
            pending[0].astype(jnp.float32).astype(jnp.bfloat16),
            "tp",
            scatter_dimension=1,
            tiled=True,
        ).astype(jnp.float32),
    )
    block_share = head_share + pending_share
    return (stream.astype(jnp.float32) + block_share).astype(jnp.bfloat16)


N_CTX = 8
N_TP = 4
GRANT = 60 * 1024 * 1024


def swap(x, bit):
    return lax.ppermute(x, "ctx", [(c, c ^ bit) for c in range(N_CTX)])


def hop_up(v, pairs):
    return lax.ppermute(v, "tp", [(i, i + 1) for i in pairs])


def hop_down(v, pairs):
    return lax.ppermute(v, "tp", [(N_TP - 1 - i, N_TP - 2 - i) for i in pairs])


def rotated(v, cosine, sinus):
    return v * cosine + pltpu.roll(v, HD // 2, 1) * sinus


HBM = pl.BlockSpec(memory_space=pltpu.HBM)
VMEM = pl.BlockSpec(memory_space=pltpu.VMEM)
SMEM = pl.BlockSpec(memory_space=pltpu.SMEM)
ANY = pl.BlockSpec(memory_space=pl.ANY)
LITTLE = pl.CostEstimate(flops=0, bytes_accessed=1024, transcendentals=0)


def specs_of(arrays):
    return [HBM if a.size > 200000 else ANY for a in arrays]


def move(plan, shapes, ids, sources, arrived=()):
    count = len(sources)

    def kernel(ids_ref, *refs):
        outs, sems = refs[count + len(arrived) : -1], refs[-1]
        waits = []
        for at, (choices, dst) in enumerate(plan(ids_ref, refs[:count], outs)):
            for cond, src in choices:
                copy = pltpu.make_async_copy(src, dst, sems.at[at])
                if cond is None:
                    copy.start()
                else:
                    pl.when(cond)(copy.start)
            waits.append(copy)
        for copy in waits:
            copy.wait()

    return pl.pallas_call(
        kernel,
        out_shape=tuple(jax.ShapeDtypeStruct(shape, jnp.bfloat16) for shape in shapes),
        in_specs=[SMEM] + [HBM] * count + specs_of(arrived),
        out_specs=tuple(VMEM for _ in shapes),
        scratch_shapes=[pltpu.SemaphoreType.DMA((40,))],
        compiler_params=pltpu.CompilerParams(vmem_limit_bytes=GRANT),
        cost_estimate=LITTLE,
        name=plan.__name__,
    )(ids, *sources, *arrived)


def gate(x, *arrived):
    return pl.pallas_call(
        lambda *refs: None,
        out_shape=jax.ShapeDtypeStruct(x.shape, x.dtype),
        in_specs=[HBM] + specs_of(arrived),
        out_specs=HBM,
        input_output_aliases={0: 0},
        compiler_params=pltpu.CompilerParams(vmem_limit_bytes=GRANT),
        cost_estimate=LITTLE,
        name="gate",
    )(x, *arrived)


def pick(z, options, ids, arrived=()):
    distinct = list({id(o): o for o in options}.values())

    def pick_plan(at, src, out):
        yield (
            [(at[2] == i, src[[o is d for d in distinct].index(True)]) for i, o in enumerate(options)],
            out[0],
        )

    return move(pick_plan, (options[0].shape,), ids, distinct, arrived)[0]


def hops(ids, pending, up, down, offset, relay, both, rows, arrived=()):
    tok, feat = pending.shape[1], up.shape[1]

    def kernel(ids_ref, pending_ref, up_ref, down_ref, *refs):
        out_up, out_down, buf, sems = refs[len(arrived) :]
        z = ids_ref[2]
        todo = []
        for i, (src, out, step, at) in enumerate(
            ((up_ref, out_up, offset, z), (down_ref, out_down, -offset, N_TP - 1 - z))
        ):
            is_relay = functools.reduce(jnp.logical_or, [at == p for p in relay], at < 0)
            is_both = functools.reduce(jnp.logical_or, [at == p for p in both], at < 0)
            place = jnp.clip(z + step, 0, N_TP - 1)
            share = pltpu.make_async_copy(
                pending_ref.at[0, :, pl.ds(multiple(place, feat), feat)],
                out.at[pl.ds(0, tok)],
                sems.at[i],
            )
            passed = pltpu.make_async_copy(src.at[pl.ds(0, rows)], out, sems.at[i])
            added = pltpu.make_async_copy(src.at[pl.ds(0, tok)], buf.at[i], sems.at[2 + i])
            pl.when(is_relay)(passed.start)

            @pl.when(jnp.logical_not(is_relay))
            def _():
                if rows > tok:
                    out[tok:] = jnp.zeros((rows - tok, feat), jnp.bfloat16)
                share.start()

            pl.when(is_both)(added.start)
            todo.append((passed, share, added, is_relay, is_both, out, i))
        for passed, share, added, is_relay, is_both, out, i in todo:
            pl.when(is_relay)(passed.wait)
            pl.when(jnp.logical_not(is_relay))(share.wait)

            @pl.when(is_both)
            def _():
                added.wait()
                out[:tok] += buf[i]

    shape = jax.ShapeDtypeStruct((rows, feat), jnp.bfloat16)
    return pl.pallas_call(
        kernel,
        out_shape=(shape, shape),
        in_specs=[SMEM, HBM, HBM, HBM] + specs_of(arrived),
        out_specs=(VMEM, VMEM),
        scratch_shapes=[
            pltpu.VMEM((2, tok, feat), jnp.bfloat16),
            pltpu.SemaphoreType.DMA((4,)),
        ],
        compiler_params=pltpu.CompilerParams(vmem_limit_bytes=GRANT),
        cost_estimate=LITTLE,
        name="hops",
    )(ids, pending, up, down, *arrived)


def one(src, dst):
    return ([(None, src)], dst)


def multiple(value, of=128):
    return pl.multiple_of(value * of, of)


AHEAD = 3
PARTS = ((0, 0), (0, 1), (1, 0), (2, 0))


def project_kernel(slots, x_count, w_count, tok, rows, scale, at_kv, ids_ref, *refs):
    last = scale is not None
    xs, ws, refs = refs[:x_count], refs[x_count : x_count + w_count], refs[x_count + w_count :]
    x_buf, w_buf, x_sem, w_sem = refs[-4:]
    chip, core = ids_ref[0], ids_ref[1]
    half, cols = x_buf.shape[-1], ws[0].shape[1]
    fold = half // 2
    mine = pl.multiple_of(core * tok, 128)
    theirs = pl.multiple_of((1 - core) * tok, 128)

    def fetch(at):
        part, h = ids_ref[7 + slots[at // 2]], at % 2
        place = ids_ref[3 + part]
        waits = []
        for i in range(3):
            for m in range(w_count // 2):
                src, dst = ws[2 * m + h], w_buf.at[at]
                if i == 0:
                    src, dst = src.at[pl.ds(0, half)], dst.at[:, pl.ds(0, cols)]
                else:
                    lanes = pl.ds((i - 1) * 2 * HD, 2 * HD)
                    src = src.at[pl.ds(at_kv, fold), lanes]
                    dst = dst.at[pl.ds((i - 1) * fold, fold), pl.ds(cols, 2 * HD)]
                copy = pltpu.make_async_copy(src, dst, w_sem.at[3 * at + i])
                pl.when((place ^ chip) == m)(copy.start)
            waits.append(copy)
        features = pl.ds(pl.multiple_of((core ^ h) * half, 128), half)
        for s, to in ((0, mine), (1, theirs)):
            for r, (index, group) in enumerate(PARTS):
                if 2 * index < x_count:
                    src = xs[2 * index + s].at[pl.ds(group * rows, tok), features]
                    dst = x_buf.at[at, pl.ds(to, tok)]
                    copy = pltpu.make_async_copy(src, dst, x_sem.at[2 * at + s])
                    pl.when(part == r)(copy.start)
            waits.append(copy)
        return waits

    ahead = [fetch(at) for at in range(AHEAD)]
    acc = refs[0][...] if last else 0.0
    for at in range(4):
        for copy in ahead[at]:
            copy.wait()
        if at + AHEAD < 4:
            ahead.append(fetch(at + AHEAD))
        acc = acc + jnp.dot(x_buf[at], w_buf[at], preferred_element_type=jnp.float32)
    if not last:
        refs[0][...] = acc
        return
    factor_ref, cos_ref, sin_ref, q_ref, kv_ref, tail_ref = refs[1:7]
    factor = factor_ref[...]
    heads = q_ref.shape[0]
    for h in range(heads + 2):
        v = acc[:, h * HD : (h + 1) * HD] * factor
        if h <= heads:
            v = rotated(v, cos_ref[...], sin_ref[...])
        if h < heads:
            q_ref[h] = (v * scale).astype(jnp.bfloat16)
        else:
            kv_ref[h - heads] = v.astype(jnp.bfloat16)
            tail_ref[h - heads] = v[tok:].astype(jnp.bfloat16)


def project(ids, slots, xs, weights, tok, at_kv, tables=(), scale=None):
    rows = xs[0].shape[0] // 2
    feat = xs[0].shape[1]
    cols = weights[0].shape[1]
    half = feat // 2
    sums = jax.ShapeDtypeStruct((2 * tok, cols + 2 * HD), jnp.float32)
    results = (
        jax.ShapeDtypeStruct((cols // HD, 2 * tok, HD), jnp.bfloat16),
        jax.ShapeDtypeStruct((2, 2 * tok, HD), jnp.bfloat16),
        jax.ShapeDtypeStruct((2, tok, HD), jnp.bfloat16),
    )
    return pl.pallas_call(
        functools.partial(
            project_kernel, slots, len(xs), len(weights), tok, rows, scale, at_kv
        ),
        out_shape=results if tables else sums,
        in_specs=[SMEM] + [HBM] * (len(xs) + len(weights)) + [VMEM] * len(tables),
        out_specs=(VMEM,) * 3 if tables else VMEM,
        scratch_shapes=[
            pltpu.VMEM((4, 2 * tok, half), jnp.bfloat16),
            pltpu.VMEM((4, half, cols + 2 * HD), jnp.bfloat16),
            pltpu.SemaphoreType.DMA((8,)),
            pltpu.SemaphoreType.DMA((12,)),
        ],
        compiler_params=pltpu.CompilerParams(vmem_limit_bytes=GRANT),
        cost_estimate=LITTLE,
        name="project",
    )(ids, *xs, *weights, *tables)


BT = 256
BK = 1024
CHAIN = 2


def scores(q, k):
    return lax.dot_general(q, k, (((1,), (1,)), ((), ())), preferred_element_type=jnp.float32)


def absorb(s, v_ext, m, acc):
    new = jnp.maximum(m, jnp.max(s, axis=1, keepdims=True))
    p = jnp.exp2(s - new).astype(jnp.bfloat16)
    acc = acc * jnp.exp2(m - new) + jnp.dot(p, v_ext, preferred_element_type=jnp.float32)
    return new, acc


def attend_kernel(at_old, bound_ref, ids_ref, q_ref, n_ref, lo_ref, before_ref, new_ref, *refs):
    bundles, (out_ref, k_old, k_turned, v_ext, kv_near, s_ref, m_ref, acc_ref, sems) = refs[:8], refs[-9:]
    halo = before_ref.shape[1]
    b = pl.program_id(0)
    heads, bt = q_ref.shape[0], q_ref.shape[1]
    rows, chains = CHAIN * bt, heads // CHAIN
    last = k_old.shape[0] // BK - 1
    fold = k_old.shape[0] // (2 * N_CTX)

    @pl.when(b == 0)
    def _():
        copies = []
        for index, bundle in enumerate(bundles):
            place = ((ids_ref[0] ^ (index // 2)) * 2 + (ids_ref[1] ^ (index % 2))) * 2 * fold
            for i in range(4):
                dst = (k_old, v_ext)[i // 2]
                to = pl.ds(pl.multiple_of(place + (i % 2) * fold, 128), fold)
                copies.append(
                    pltpu.make_async_copy(
                        bundle.at[pl.ds(at_old, fold), pl.ds(i * HD, HD)],
                        dst.at[to, pl.ds(0, HD)],
                        sems.at[4 * index + i],
                    )
                )
        for copy in copies:
            copy.start()
        v_ext[:, HD:] = jnp.ones((v_ext.shape[0], HD), jnp.bfloat16)
        kv_near[:, :halo] = before_ref[...]
        kv_near[:, halo:] = new_ref[...]
        for copy in copies:
            copy.wait()
        for at in range(0, k_old.shape[0], BK):
            k_turned[:, at : at + BK] = k_old[at : at + BK, :].T

    m_ref[...] = jnp.full_like(m_ref, MASKED)
    acc_ref[...] = jnp.zeros_like(acc_ref)

    def query(g):
        return q_ref[g * CHAIN : (g + 1) * CHAIN].reshape(rows, HD)

    s_ref[...] = jnp.dot(query(0), k_turned[:, :BK], preferred_element_type=jnp.float32)

    def body(kb, masked):
        start = pl.multiple_of(kb * BK, BK)
        follow = pl.multiple_of(jnp.minimum(kb + 1, last) * BK, BK)
        ms = [m_ref[g][:, :1] for g in range(chains)]
        accs = [acc_ref[g] for g in range(chains)]
        s = s_ref[...]
        v = v_ext[pl.ds(start, BK), :]
        for g in range(chains):
            at, who = (start, g + 1) if g + 1 < chains else (follow, 0)
            ahead = jnp.dot(
                query(who), k_turned[:, pl.ds(at, BK)], preferred_element_type=jnp.float32
            )
            if masked:
                n_rows = jnp.concatenate([n_ref[:, :1]] * CHAIN, axis=0)
                col = lax.broadcasted_iota(jnp.int32, s.shape, 1) + start
                s = jnp.where(col < n_rows, s, MASKED)
            ms[g], accs[g] = absorb(s, v, ms[g], accs[g])
            s = ahead
        s_ref[...] = s
        for g in range(chains):
            m_ref[g] = jnp.broadcast_to(ms[g], (rows, 128))
            acc_ref[g] = accs[g]

    full = bound_ref[0, b] // BK
    some = (bound_ref[1, b] + BK - 1) // BK
    lax.fori_loop(0, full, lambda kb, c: (body(kb, False), c)[1], 0)
    lax.fori_loop(full, some, lambda kb, c: (body(kb, True), c)[1], 0)

    span = halo + bt
    start = pl.multiple_of(b * bt, bt)
    k = kv_near[0, pl.ds(start, span), :]
    v = kv_near[1, pl.ds(start, span), :]
    v = jnp.concatenate([v, jnp.ones_like(v)], axis=1)
    lo = jnp.concatenate([lo_ref[:, :1]] * CHAIN, axis=0)
    col = lax.broadcasted_iota(jnp.int32, (rows, span), 1)
    row = lax.broadcasted_iota(jnp.int32, (rows, span), 0) % bt
    seen = (col + start >= lo) & (col <= row + halo)
    for g in range(chains):
        s = jnp.where(seen, scores(query(g), k), MASKED)
        _, acc = absorb(s, v, m_ref[g][:, :1], acc_ref[g])
        mixed = (acc[:, :HD] / acc[:, HD:]).astype(jnp.bfloat16)
        for h in range(CHAIN):
            at = (g * CHAIN + h) * HD
            out_ref[:, at : at + HD] = mixed[h * bt : (h + 1) * bt]


def attend(bounds, ids, q, n_tok, lo_tok, before, new, bundles, at_old, keys, arrived=()):
    heads, tokens = q.shape[:2]
    chains, rows = heads // CHAIN, CHAIN * BT
    halo = before.shape[1]
    return pl.pallas_call(
        functools.partial(attend_kernel, at_old),
        out_shape=jax.ShapeDtypeStruct((tokens, heads * HD), jnp.bfloat16),
        grid_spec=pltpu.PrefetchScalarGridSpec(
            num_scalar_prefetch=2,
            grid=(tokens // BT,),
            in_specs=[
                pl.BlockSpec((heads, BT, HD), lambda b, *_: (0, b, 0)),
                pl.BlockSpec((BT, 128), lambda b, *_: (b, 0)),
                pl.BlockSpec((BT, 128), lambda b, *_: (b, 0)),
                pl.BlockSpec(before.shape, lambda b, *_: (0, 0, 0)),
                pl.BlockSpec(new.shape, lambda b, *_: (0, 0, 0)),
            ]
            + [HBM] * 8
            + specs_of(arrived),
            out_specs=pl.BlockSpec((BT, heads * HD), lambda b, *_: (b, 0)),
            scratch_shapes=[
                pltpu.VMEM((keys, HD), jnp.bfloat16),
                pltpu.VMEM((HD, keys), jnp.bfloat16),
                pltpu.VMEM((keys, 2 * HD), jnp.bfloat16),
                pltpu.VMEM((2, halo + tokens, HD), jnp.bfloat16),
                pltpu.VMEM((rows, BK), jnp.float32),
                pltpu.VMEM((chains, rows, 128), jnp.float32),
                pltpu.VMEM((chains, rows, 2 * HD), jnp.float32),
                pltpu.SemaphoreType.DMA((32,)),
            ],
        ),
        compiler_params=pltpu.CompilerParams(vmem_limit_bytes=GRANT),
        cost_estimate=LITTLE,
        name="attend",
    )(bounds, ids, q, n_tok, lo_tok, before, new, *bundles, *arrived)


def out_kernel(ids_ref, *refs):
    xs, ws = refs[:8], refs[8:16]
    keep_ref, give_ref, x_buf, w_buf, o_buf, x_sem, w_sem = refs[16:]
    chip, core, z = ids_ref[0], ids_ref[1], ids_ref[2]
    width = xs[0].shape[1]
    rows = w_buf.shape[1] // 4
    for r in range(4):
        near = ids_ref[3 + r] ^ z
        for m in range(4):
            to = w_buf.at[r, pl.ds(pl.multiple_of((chip ^ m) * rows, 128), rows)]
            for i in range(2):
                src = ws[2 * m + i].at[pl.ds(pl.multiple_of((near % 2) * rows, 128), rows)]
                copy = pltpu.make_async_copy(src, to, w_sem.at[4 * r + m])
                pl.when(near // 2 == i)(copy.start)
        for s in range(2):
            at = pl.multiple_of((core ^ s) * width, 128)
            pltpu.make_async_copy(
                xs[2 * r + s], x_buf.at[r, :, pl.ds(at, width)], x_sem.at[2 * r + s]
            ).start()
    acc = None
    for r in range(4):
        for m in range(4):
            pltpu.make_async_copy(
                ws[0].at[pl.ds(0, rows)], w_buf.at[r, pl.ds(0, rows)], w_sem.at[4 * r + m]
            ).wait()
        for s in range(2):
            pltpu.make_async_copy(
                xs[0], x_buf.at[r, :, pl.ds(0, width)], x_sem.at[2 * r + s]
            ).wait()
        term = jnp.dot(x_buf[r], w_buf[r], preferred_element_type=jnp.float32)
        acc = term if acc is None else acc + term
    o_buf[...] = acc.astype(jnp.bfloat16)
    half = keep_ref.shape[0]
    keep_ref[...] = o_buf[pl.ds(pl.multiple_of(core * half, 128), half)]
    give_ref[...] = o_buf[pl.ds(pl.multiple_of((1 - core) * half, 128), half)]


def out_project(ids, xs, ws):
    tokens, width = xs[0].shape
    depth, cols = 2 * ws[0].shape[0], ws[0].shape[1]
    return pl.pallas_call(
        out_kernel,
        out_shape=(jax.ShapeDtypeStruct((tokens // 2, cols), jnp.bfloat16),) * 2,
        in_specs=[SMEM] + [HBM] * 16,
        out_specs=(VMEM, VMEM),
        scratch_shapes=[
            pltpu.VMEM((4, tokens, 2 * width), jnp.bfloat16),
            pltpu.VMEM((4, depth, cols), jnp.bfloat16),
            pltpu.VMEM((tokens, cols), jnp.bfloat16),
            pltpu.SemaphoreType.DMA((8,)),
            pltpu.SemaphoreType.DMA((16,)),
        ],
        compiler_params=pltpu.CompilerParams(vmem_limit_bytes=GRANT),
        cost_estimate=LITTLE,
        name="out_project",
    )(ids, *xs, *ws)


def per_device(
    stream,
    pending,
    norm_gain,
    w_query,
    w_key,
    w_value,
    w_out,
    prefix_keys,
    prefix_values,
    prefix_segments,
    stretch_segments,
    stretch_offset,
):
    tok, feat = stream.shape
    chip_tok = 2 * tok
    c = lax.axis_index("ctx")
    z = lax.axis_index("tp")
    chip, core = c // 2, c % 2
    first = core == 0
    depth = feat * N_TP

    wide = stream.astype(jnp.float32)
    here = jnp.stack([chip, core, z]).astype(jnp.int32)
    every = (0, 1, 2)

    gain = lax.dynamic_slice_in_dim(norm_gain, z * feat, feat, 0).astype(jnp.float32)
    scaled = (wide * gain[None, :]).astype(jnp.bfloat16)

    left = jnp.sum(wide * wide, axis=1)
    sums = []
    for _ in range(3):
        sums.append(lax.reduce_precision(left, 8, 7))
        left = left - sums[-1]
    sums = jnp.pad(jnp.stack(sums), ((0, 13), (0, feat - tok))).astype(jnp.bfloat16)
    scaled = jnp.concatenate([scaled, sums], axis=0)
    n_rows = scaled.shape[0]

    def squares(part, group=0):
        at = group * n_rows + tok
        return jnp.sum(part[at : at + 3, :tok].astype(jnp.float32), axis=0)


    labels = jnp.arange(NTRAJ, dtype=jnp.int32)
    counts = jnp.concatenate(
        [
            jnp.sum((prefix_segments[:, None] <= labels).astype(jnp.int32), axis=0),
            jnp.sum((stretch_segments[:, None] < labels).astype(jnp.int32), axis=0),
        ]
    )
    notes = jnp.concatenate([counts // 32, counts % 32])
    cols = w_query.shape[1] // 2
    notes = jnp.stack(
        [jnp.pad(v, (0, cols - v.shape[0])) for v in (stretch_segments, notes)]
        + [jnp.zeros((cols,), jnp.int32)] * 14
    ).astype(jnp.bfloat16)

    token_index = chip * chip_tok + jnp.arange(chip_tok, dtype=jnp.int32)
    positions = stretch_offset[0].astype(jnp.float32) + token_index.astype(jnp.float32)
    angles = positions[:, None] * inverse_freqs(HD)
    cosine, sinus = jnp.cos(angles), jnp.sin(angles)
    cosine = jnp.concatenate([cosine, cosine], axis=1)
    sinus = jnp.concatenate([-sinus, sinus], axis=1)

    q_heads = w_query.shape[1] // HD // 2
    q_cols = q_heads * HD
    n_q = w_query.shape[0]
    fold = prefix_keys.shape[1] // 2
    n_both = n_q + fold
    n_kv = w_key.shape[0] // 2
    n_piece = w_out.shape[0] // 4

    def first_plan(at, src, out):
        w_q, w_k, w_v, keys, values, said = src
        for dst, j in ((out[0], at[1]), (out[1], 1 - at[1])):
            head = 2 * at[2] + j
            yield one(w_q.at[:, pl.ds(multiple(j, q_cols), q_cols)], dst.at[pl.ds(0, n_q)])
            for i, a in enumerate((keys, keys, values, values)):
                part = a.at[head, pl.ds((i % 2) * fold, fold)]
                yield one(part, dst.at[pl.ds(n_q, fold), pl.ds(i * HD, HD)])
            for i, a in enumerate((w_k, w_v, w_k, w_v)):
                part = a.at[pl.ds((i // 2) * n_kv, n_kv), pl.ds(multiple(head), HD)]
                yield one(part, dst.at[pl.ds(n_both, n_kv), pl.ds(i * HD, HD)])
            yield one(said, dst.at[pl.ds(n_both + n_kv, said.shape[0])])

    own, give = move(
        first_plan,
        ((n_both + n_kv + notes.shape[0], q_cols),) * 2,
        here,
        (w_query, w_key, w_value, prefix_keys, prefix_values, notes),
    )
    places = jnp.stack(
        [z, jnp.where(z < 2, z + 1, z - 1), jnp.where(z < 2, z + 2, z - 2), jnp.where(z % 2 == 1, 0, 3)]
    ).astype(jnp.int32)
    skip = jnp.sum(jnp.where(places == (chip ^ 3), jnp.arange(N_TP), 0))
    order = jnp.stack(
        [
            jnp.where(skip == 0, 1, 0),
            jnp.where(skip < 2, 2, 1),
            jnp.minimum(skip, 2),
            jnp.full((), 3),
        ]
    )
    ids = jnp.concatenate([here, places, order]).astype(jnp.int32)

    x1, y1, given = swap(own, 2), swap(own, 4), swap(give, 1)
    turn = swap(gate(notes, own), 1)
    scaled = gate(scaled, turn)
    u1, d1 = hop_up(scaled, every), hop_down(scaled, every)

    def piece_plan(at, src, out):
        for r, dst in enumerate(out):
            rows = pl.ds(multiple(at[0] ^ r, n_piece), n_piece)
            for i in range(2):
                part = src[0].at[rows, pl.ds(i * q_cols, q_cols)]
                yield one(part, dst.at[pl.ds(i * n_piece, n_piece)])

    by_chip = move(
        piece_plan,
        ((2 * n_piece, q_cols),) * 4,
        here,
        (w_out,),
        (own,),
    )
    given = gate(given, x1, y1)
    up, down = hops(here, pending, u1, d1, 3, (1, 2, 3), (), n_rows, (cosine, sinus, given, by_chip[0]))
    u2, d2 = hop_up(up, every), hop_down(down, every)
    x2, y2 = swap(given, 2), swap(given, 4)

    def near_plan(at, src, out):
        own_part, up_part, down_part = src
        yield one(own_part, out[0].at[pl.ds(0, n_rows)])
        near = [(at[2] < 2, down_part), (at[2] >= 2, up_part)]
        yield (near, out[0].at[pl.ds(n_rows, n_rows)])

    (near,) = move(near_plan, ((2 * n_rows, feat),), here, (scaled, u1, d1), (up,))

    x1, y2 = gate(x1, x2, y2, u2, d2), gate(y2, x2, u2, d2)
    up, down = hops(here, pending, u2, d2, 2, (2,), (1,), n_rows, (x1, y2, near))
    u3, d3 = hop_up(up, every), hop_down(down, every)
    far_own, far_other = swap(x1, 4), swap(y2, 2)
    near = gate(near, up)
    over1 = swap(near, 1)
    second = pick(z, (d2, d2, u2, u2), here, (up,))
    over2 = swap(second, 1)
    own_rows = (own, given, x1, x2, y1, y2, far_own, far_other)
    xs = [near, over1, second, over2]
    sums = project(ids, (0, 1), xs, own_rows[:6], tok, n_both)

    third = pick(z, (d3, u1, d1, u3), here, (sums, far_own, far_other))
    over3 = swap(third, 1)
    up, down = hops(here, pending, u3, d3, 1, (), (1, 2, 3), tok, (third,))
    u4, d4 = hop_up(up, every), hop_down(down, every)
    mine, theirs = (
        squares(a) + squares(a, 1) + squares(b) + squares(c)
        for a, b, c in ((near, second, third), (over1, over2, over3))
    )
    total = jnp.where(first, jnp.concatenate([mine, theirs]), jnp.concatenate([theirs, mine]))
    factor = lax.rsqrt(total * (1.0 / depth) + NORM_EPSILON)
    factor = jnp.broadcast_to(factor[:, None], (chip_tok, 128))
    xs += [third, over3]

    said = [rows[n_both + n_kv : n_both + n_kv + 2].astype(jnp.float32) for rows in own_rows]
    total = sum(v[1, : 4 * NTRAJ] for v in said).astype(jnp.int32)
    total = total[: 2 * NTRAJ] * 32 + total[2 * NTRAJ :]
    segs = [v[0, :tok].astype(jnp.int32) for v in said[:2]]
    segs = jnp.where(first, jnp.concatenate(segs), jnp.concatenate(segs[::-1]))
    onehot = (segs[:, None] == labels).astype(jnp.int32)
    n_tok = jnp.sum(onehot * total[:NTRAJ], axis=1)
    lo_tok = jnp.sum(onehot * total[NTRAJ:], axis=1) - chip * chip_tok + tok
    blocked = n_tok.reshape(chip_tok // BT, BT)
    bounds = jnp.stack([blocked[:, 0], blocked[:, -1]])
    n_wide = jnp.broadcast_to(n_tok[:, None], (chip_tok, 128))
    lo_wide = jnp.broadcast_to(lo_tok[:, None], (chip_tok, 128))

    by_chip = (by_chip[0],) + tuple(
        swap(gate(by_chip[r], far_own, far_other), 2 * r) for r in (1, 2, 3)
    )
    scale = math.log2(math.e) / math.sqrt(HD)
    q, kv_new, tail = project(
        ids, (2, 3), xs, own_rows, tok, n_both, (sums, factor, cosine, sinus), scale
    )
    before = lax.ppermute(tail, "ctx", [(i, i + 2) for i in range(N_CTX - 2)])

    def pieces_plan(at, src, out):
        for r, dst in enumerate(out):
            near = (at[2] ^ r) ^ at[0]
            yield ([(near == m, src[m]) for m in range(4)], dst)

    pieces = list(move(pieces_plan, ((2 * n_piece, q_cols),) * 4, here, by_chip, (q,)))
    for r in (1, 2, 3):
        pieces[r] = lax.ppermute(
            gate(pieces[r], before), "tp", [(i, i ^ r) for i in range(N_TP)]
        )
    attended = attend(
        bounds,
        here,
        q,
        n_wide,
        lo_wide,
        before,
        kv_new,
        own_rows,
        n_q,
        N_CTX * prefix_keys.shape[1],
        (pieces[0],),
    )

    def block_plan(at, src, out):
        for r, part in enumerate(src):
            for i in range(2):
                dst = out[r // 2].at[pl.ds((r % 2) * n_piece, n_piece), pl.ds(i * q_cols, q_cols)]
                yield one(part.at[pl.ds(i * n_piece, n_piece)], dst)

    wo_a, wo_b = move(block_plan, ((2 * n_piece, 2 * q_cols),) * 2, here, pieces, (attended,))
    wo_xa, wo_yb = swap(wo_a, 2), swap(wo_b, 4)
    wo_xb, wo_ya = swap(wo_b, 2), swap(wo_a, 4)

    attended = gate(attended, u4, d4, *pieces[1:])
    u1, d1 = hop_up(attended, every), hop_down(attended, every)
    near = pick(z, (d1, d1, u1, u1), here)

    wo_parts = (wo_a, wo_b, wo_xa, wo_xb, wo_ya, wo_yb, swap(wo_xa, 4), swap(wo_yb, 2))
    u2, d2 = hop_up(gate(u1, wo_xa, wo_yb), (1, 2)), hop_down(gate(d1, wo_xa, wo_yb), (1, 2))
    second = pick(z, (d2, d2, u2, u2), here)
    u3, d3 = hop_up(gate(u2, wo_xb, wo_ya), (2,)), hop_down(gate(d2, wo_xb, wo_ya), (2,))
    third = pick(z, (d3, u1, d1, u3), here, wo_parts[6:])
    hs = []
    for part in (attended, near, second, third):
        hs += [part, swap(part, 1)]
    mine, theirs = out_project(ids, hs, wo_parts)
    theirs = swap(theirs, 1)
    head_share = jnp.where(
        first,
        jnp.concatenate([mine, theirs], axis=1),
        jnp.concatenate([theirs, mine], axis=1),
    ).astype(jnp.float32)
    pending_share = (
        lax.dynamic_slice_in_dim(pending[0], z * feat, feat, 1).astype(jnp.float32)
        + jnp.where(z == 0, 0, u4).astype(jnp.float32)
        + jnp.where(z == 3, 0, d4).astype(jnp.float32)
    )
    return (wide + (head_share + pending_share)).astype(jnp.bfloat16)


def solution(mesh):
    in_specs = (
        P("ctx", "tp"),
        P("tp", "ctx", None),
        P(),
        P("ctx", "tp"),
        P("ctx", None),
        P("ctx", None),
        P("tp", "ctx"),
        P(None, "ctx", None),
        P(None, "ctx", None),
        P("ctx"),
        P("ctx"),
        P(),
    )
    out_specs = P("ctx", "tp")
    small = mesh.shape["ctx"] == N_CTX and mesh.shape["tp"] == N_TP
    return jax.shard_map(
        per_device if small else per_device_any,
        mesh=mesh,
        in_specs=in_specs,
        out_specs=out_specs,
        check_vma=False,
    )
```
